32 devices in a mesh: ctx: 16 (over z, y, core), tp: 2 (over x).
Axes of the slice: x: 2, y: 2, z: 4, core: 2. Of those that a mesh axis runs over, the one named last changes fastest.
Arguments:
- layer_input: bfloat16 [2048, 2048], P('ctx'), may hold values from -6 to 6
- block_order: int32 [32], replicated, may hold values from 0 to 31, each once
- attn_gain: float32 [2048], replicated, may hold values from 0.1 to 1.9
- attn_shift: float32 [2048], replicated, may hold values from -1.75 to 1.75
- mlp_gain: float32 [2048], replicated, may hold values from 0.1 to 1.9
- mlp_shift: float32 [2048], replicated, may hold values from -1.75 to 1.75
- w_query: bfloat16 [2048, 2048], P('ctx', 'tp'), may hold values from -0.125 to 0.125
- b_query: float32 [2048], P('tp'), may hold values from -3 to 3
- w_key: bfloat16 [2048, 2048], P('ctx', 'tp'), may hold values from -0.125 to 0.125
- b_key: float32 [2048], P('tp'), may hold values from -3 to 3
- w_value: bfloat16 [2048, 2048], P('ctx', 'tp'), may hold values from -0.125 to 0.125
- b_value: float32 [2048], P('tp'), may hold values from -3 to 3
- w_out: bfloat16 [2048, 2048], P('tp', 'ctx'), may hold values from -1 to 1
- b_out: float32 [2048], replicated, may hold values from -1.75 to 1.75
- w_up: bfloat16 [2048, 8192], P('ctx', 'tp'), may hold values from -0.125 to 0.125
- b_up: float32 [8192], P('tp'), may hold values from -3 to 3
- w_down: bfloat16 [8192, 2048], P('tp', 'ctx'), may hold values from -0.0625 to 0.0625
- b_down: float32 [2048], replicated, may hold values from -1.75 to 1.75
- out_grad: bfloat16 [2048, 2048], P('ctx'), may hold values from -6 to 6
Outputs:
- layer_output: bfloat16 [2048, 2048], P('ctx')
- input_grad: float32 [2048, 2048], P('ctx')
- grad_w_query: float32 [2048, 2048], P('ctx', 'tp')
- grad_w_key: float32 [2048, 2048], P('ctx', 'tp')
- grad_w_value: float32 [2048, 2048], P('ctx', 'tp')
- grad_w_out: float32 [2048, 2048], P('tp', 'ctx')
- grad_w_up: float32 [2048, 8192], P('ctx', 'tp')
- grad_w_down: float32 [8192, 2048], P('tp', 'ctx')
- grad_b_query: float32 [2048], P('tp')
- grad_b_key: float32 [2048], P('tp')
- grad_b_value: float32 [2048], P('tp')
- grad_b_out: float32 [2048], replicated
- grad_b_up: float32 [8192], P('tp')
- grad_b_down: float32 [2048], replicated
- grad_attn_gain: float32 [2048], replicated
- grad_attn_shift: float32 [2048], replicated
- grad_mlp_gain: float32 [2048], replicated
- grad_mlp_shift: float32 [2048], replicated
The draws below stay inside these ranges and needn't reach their ends.
Inputs may be any that keep to these rules, and one draw needn't show every extreme that they name: A permutation: device i of ctx holds sequence blocks block_order[2 i] and block_order[2 i + 1] in that order, each of 64 tokens.
All inputs are finite; a program needn't handle non-finite values.
Results may differ from the reference program's by a relative error of at most 0.018.
Values may be sent and summed in bfloat16 or wider, within the bound.
A program may use at most 192 MiB of HBM per device.

```python
import math
from functools import partial
import jax
import jax.numpy as jnp
from jax import lax

D = 2048
HEADS = 8
HD = 256
ROT = 64
FF = 8192
T_DEV = 128
SEQ = 2048
N_CTX = 16


def block_scale(stream_key, dims, shards, smallest, high):
    level = 1.0
    for dim, shards_of in shards:
        steps = jax.random.uniform(jax.random.fold_in(jax.random.fold_in(stream_key, 6), dim), (shards_of,), jnp.float32, smallest / len(shards), high / len(shards))
        level = level * jnp.repeat(jnp.exp(steps), dims[dim] // shards_of).reshape((-1,) + (1,) * (len(dims) - 1 - dim))
    return level


def gaussian(own_key, extent, scale, reach, cuts=(), kind=jnp.bfloat16):
    level = block_scale(own_key, extent, cuts, -0.22, 0.18) if cuts else 1.0
    values = jax.random.normal(own_key, extent, jnp.float32) * scale * level
    return jnp.minimum(jnp.maximum(values, -reach), reach).astype(kind)


def setup_inputs(seed: int = 0) -> dict:
    streams_of = jax.random.split(jax.random.key(seed), 20)
    return {
        "layer_input": gaussian(streams_of[0], (SEQ, D), 1.0, 6.0, ((0, 16),)),
        "block_order": jax.random.permutation(streams_of[1], 2 * N_CTX).astype(jnp.int32),
        "attn_gain": jnp.clip(1.0 + 0.18 * jax.random.normal(streams_of[2], (D,), jnp.float32), 0.1, 1.9),
        "attn_shift": gaussian(streams_of[3], (D,), 0.3, 1.75, (), jnp.float32),
        "mlp_gain": jnp.clip(1.0 + 0.18 * jax.random.normal(streams_of[4], (D,), jnp.float32), 0.1, 1.9),
        "mlp_shift": gaussian(streams_of[5], (D,), 0.3, 1.75, (), jnp.float32),
        "w_query": gaussian(streams_of[6], (D, D), D ** -0.5, 0.125, ((0, 16), (1, 2))),
        "b_query": gaussian(streams_of[7], (D,), 0.5, 3.0, ((0, 2),), jnp.float32),
        "w_key": gaussian(streams_of[8], (D, D), D ** -0.5, 0.125, ((0, 16), (1, 2))),
        "b_key": gaussian(streams_of[9], (D,), 0.5, 3.0, ((0, 2),), jnp.float32),
        "w_value": gaussian(streams_of[10], (D, D), D ** -0.5, 0.125, ((0, 16), (1, 2))),
        "b_value": gaussian(streams_of[11], (D,), 0.5, 3.0, ((0, 2),), jnp.float32),
        "w_out": gaussian(streams_of[12], (D, D), (D // 64) ** -0.5, 1.0, ((0, 2), (1, 16))),
        "b_out": gaussian(streams_of[13], (D,), 0.3, 1.75, (), jnp.float32),
        "w_up": gaussian(streams_of[14], (D, FF), D ** -0.5, 0.125, ((0, 16), (1, 2))),
        "b_up": gaussian(streams_of[15], (FF,), 0.5, 3.0, ((0, 2),), jnp.float32),
        "w_down": gaussian(streams_of[16], (FF, D), FF ** -0.5, 0.0625, ((0, 2), (1, 16))),
        "b_down": gaussian(streams_of[17], (D,), 0.3, 1.75, (), jnp.float32),
        "out_grad": gaussian(streams_of[18], (SEQ, D), 1.0, 6.0, ((0, 16),)),
    }


@jax.custom_vjp
def low(v):
    return lax.optimization_barrier(v.astype(jnp.bfloat16)).astype(jnp.float32)

@jax.custom_vjp
def low_back(v):
    return v

def low_keep(v):
    return (low(v), None)

def low_pass(kept, grad):
    return (grad,)

def back_keep(v):
    return (v, None)

def back_low(kept, grad):
    return (low(grad),)
low.defvjp(low_keep, low_pass)
low_back.defvjp(back_keep, back_low)
highest = lax.Precision.HIGHEST
norm_epsilon = 1e-05

def layer_norm(values, gain, shift):
    row_mean = lax.optimization_barrier(jnp.mean(values, -1, keepdims=True))
    centered = values - row_mean
    variance = lax.optimization_barrier(jnp.mean(centered * centered, -1, keepdims=True))
    return centered * lax.rsqrt(variance + norm_epsilon) * gain + shift

def rotate(values, cosine, sine_table):
    half_rot = ROT // 2
    leading = values[..., :half_rot]
    trailing = values[..., half_rot:ROT]
    cos_rows = cosine[:, None, :]
    sin_rows = sine_table[:, None, :]
    return jnp.concatenate([leading * cos_rows - trailing * sin_rows, trailing * cos_rows + leading * sin_rows, values[..., ROT:]], -1)

def token_positions(block_order):
    row_index = jnp.arange(T_DEV * N_CTX, dtype=jnp.int32)
    half_block = T_DEV // 2
    device = row_index // T_DEV
    within = row_index % T_DEV
    slot_index = 2 * device + within // half_block
    return (jnp.take(block_order, slot_index) * half_block + within % half_block).astype(jnp.int32)

def rope_tables(positions):
    freqs = 10000.0 ** (-(2.0 * jnp.arange(ROT // 2, dtype=jnp.float32)) / ROT)
    angles = positions.astype(jnp.float32)[:, None] * freqs[None, :]
    return (jnp.cos(angles), jnp.sin(angles))

def layer_forward(positions, cosine, sine_table, layer_input, attn_gain, attn_shift, mlp_gain, mlp_shift, w_query, b_query, w_key, b_key, w_value, b_value, w_out, b_out, w_up, b_up, w_down, b_down):
    row_count = layer_input.shape[0]
    normed_attn = low(layer_norm(layer_input, attn_gain, attn_shift))
    normed_mlp = low(layer_norm(layer_input, mlp_gain, mlp_shift))

    def heads(weight, bias):
        linear = low_back(jnp.dot(normed_attn, weight, precision=highest))
        return (linear + bias).reshape(row_count, HEADS, HD)
    query = low(rotate(heads(w_query, b_query), cosine, sine_table))
    keys = low(rotate(heads(w_key, b_key), cosine, sine_table))
    values = low(heads(w_value, b_value))
    block_rows = min(512, row_count)
    block_count = row_count // block_rows
    score_scale = 1.0 / math.sqrt(HD)

    def attend(pieces):
        query_block, query_place = pieces
        scores = low_back(jnp.einsum('thd,shd->hts', query_block, keys, precision=highest)) * score_scale
        allowed = positions[None, None, :] <= query_place[None, :, None]
        scores = jnp.where(allowed, scores, -1e+30)
        probs = jax.nn.softmax(scores, axis=-1)
        return jnp.einsum('hts,shd->thd', low(probs), values, precision=highest)
    attended = lax.map(jax.checkpoint(attend), (query.reshape(block_count, block_rows, HEADS, HD), positions.reshape(block_count, block_rows)))
    attended = low(low_back(attended.reshape(row_count, D)))
    hidden_pre = low_back(jnp.dot(normed_mlp, w_up, precision=highest)) + b_up
    hidden = low(jax.nn.gelu(hidden_pre, approximate=False))
    branches = jnp.dot(attended, w_out, precision=highest) + jnp.dot(hidden, w_down, precision=highest)
    return layer_input + branches + b_out + b_down

def reference(layer_input, block_order, attn_gain, attn_shift, mlp_gain, mlp_shift, w_query, b_query, w_key, b_key, w_value, b_value, w_out, b_out, w_up, b_up, w_down, b_down, out_grad):
    positions = token_positions(block_order)
    cosine, sine_table = rope_tables(positions)
    params = (layer_input.astype(jnp.float32), attn_gain, attn_shift, mlp_gain, mlp_shift, w_query.astype(jnp.float32), b_query, w_key.astype(jnp.float32), b_key, w_value.astype(jnp.float32), b_value, w_out.astype(jnp.float32), b_out, w_up.astype(jnp.float32), b_up, w_down.astype(jnp.float32), b_down)
    result, pullback = jax.vjp(partial(layer_forward, positions, cosine, sine_table), *params)
    grads = pullback(out_grad.astype(jnp.float32))
    input_grad, grad_attn_gain, grad_attn_shift, grad_mlp_gain, grad_mlp_shift, grad_w_query, grad_b_query, grad_w_key, grad_b_key, grad_w_value, grad_b_value, grad_w_out, grad_b_out, grad_w_up, grad_b_up, grad_w_down, grad_b_down = grads
    return (result.astype(jnp.bfloat16), input_grad, grad_w_query, grad_w_key, grad_w_value, grad_w_out, grad_w_up, grad_w_down, grad_b_query, grad_b_key, grad_b_value, grad_b_out, grad_b_up, grad_b_down, grad_attn_gain, grad_attn_shift, grad_mlp_gain, grad_mlp_shift)
```

```python
import functools
import math

import jax
import jax.numpy as jnp
from jax import lax
from jax.experimental import pallas as pl
from jax.experimental.pallas import tpu as pltpu
from jax.sharding import PartitionSpec as P

HEADS = 8
HD = 256
ROT = 64
CHUNK = 256

norm_epsilon = 1e-05
BF = jnp.bfloat16
F32 = jnp.float32
MESH = pl.DeviceIdType.MESH


def mm(a, b):
    return jnp.dot(a, b, preferred_element_type=F32)


def mm_tn(a, b):
    return lax.dot_general(a, b, (((0,), (0,)), ((), ())), preferred_element_type=F32)


def mm_nt(a, b):
    return lax.dot_general(a, b, (((1,), (1,)), ((), ())), preferred_element_type=F32)


class Place:
    def __init__(self, depth_size, group):
        self.depth_size = depth_size
        self.group = group
        self.bits = group.bit_length() - 1
        self.ctx = lax.axis_index("ctx")
        self.tp = lax.axis_index("tp")
        self.depth = self.ctx // group
        self.member = self.ctx % group
        slot = 0
        for stage in range(self.bits):
            slot = slot + self.bit(stage) * 2**stage
        self.slot = slot

    def bit(self, stage):
        return (self.member // 2 ** (self.bits - 1 - stage)) % 2

    def along(self, step):
        return {"ctx": lax.rem(self.depth + step, self.depth_size) * self.group + self.member}

    def across(self, stage):
        reach = 2 ** (self.bits - 1 - stage)
        return {"ctx": self.ctx + (1 - 2 * self.bit(stage)) * reach}

    def twin(self):
        return {"tp": 1 - self.tp}

    def base(self, stage):
        return (self.slot // 2**stage) * 2**stage

    def greet(self, devices):
        barrier = pltpu.get_barrier_semaphore()
        for device in devices:
            pl.semaphore_signal(barrier, inc=1, device_id=device, device_id_type=MESH)
        pl.semaphore_wait(barrier, len(devices))

    def everyone(self):
        return (
            [self.along(step) for step in range(1, self.depth_size)]
            + [self.across(stage) for stage in range(self.bits)]
            + [self.twin()]
        )


def remote(src, dst, send, recv, device):
    copy = pltpu.make_async_remote_copy(
        src_ref=src, dst_ref=dst, send_sem=send, recv_sem=recv, device_id=device, device_id_type=MESH
    )
    copy.start()
    return copy


def local(src, dst, sem):
    copy = pltpu.make_async_copy(src, dst, sem)
    copy.start()
    return copy


def gather_kernel(depth_size, group, x_in, dy_in, w_in, x_out, dy_out, w_out, tz_s, tz_r, tx_s, tx_r, t_l, z_s, z_r, z_l, g_s, g_r):
    at = Place(depth_size, group)
    at.greet(at.everyone())
    rows, half = x_in.shape[1:]
    sent = []
    mine = pl.ds(pl.multiple_of(at.depth * rows, rows), rows)
    my_cols = pl.ds(pl.multiple_of(at.tp * half, half), half)

    def token_start(i, src, dst):
        copies = [
            remote(src.at[at.tp], dst.at[mine, my_cols], tz_s.at[i, s], tz_r.at[i, s], at.along(s))
            for s in range(1, depth_size)
        ]
        copies.append(local(src.at[at.tp], dst.at[mine, my_cols], t_l.at[i]))
        return copies

    def token_swap(i, copies, dst):
        for copy in copies[:-1]:
            copy.wait_recv()
            sent.append(copy)
        copies[-1].wait()
        return remote(dst.at[:, my_cols], dst.at[:, my_cols], tx_s.at[i], tx_r.at[i], at.twin())

    chunks = w_in.shape[0]

    def z_start(k):
        copies = [
            remote(
                w_in.at[k, lax.rem(at.depth + s, depth_size)],
                w_out.at[k, at.slot, at.depth],
                z_s.at[k, s],
                z_r.at[k, s],
                at.along(s),
            )
            for s in range(1, depth_size)
        ]
        copies.append(local(w_in.at[k, at.depth], w_out.at[k, at.slot, at.depth], z_l.at[k]))
        return copies

    def z_wait(copies):
        for copy in copies[:-1]:
            copy.wait_recv()
            sent.append(copy)
        copies[-1].wait()

    def g_start(k, stage):
        held = pl.ds(at.base(stage), 2**stage)
        return remote(
            w_out.at[k, held], w_out.at[k, held], g_s.at[k, stage], g_r.at[k, stage], at.across(stage)
        )

    ahead = 2
    tokens = [token_start(0, x_in, x_out)]
    z_copies = {k: z_start(k) for k in range(min(ahead, chunks))}
    stages = {}
    swaps = []
    for step in range(chunks + at.bits):
        if step < chunks:
            z_wait(z_copies[step])
            stages[step] = [g_start(step, 0)]
            if step + ahead < chunks:
                z_copies[step + ahead] = z_start(step + ahead)
            if step == 0:
                swaps.append(token_swap(0, tokens[0], x_out))
                tokens.append(token_start(1, dy_in, dy_out))
            if step == 1:
                swaps.append(token_swap(1, tokens[1], dy_out))
        for stage in range(1, at.bits + 1):
            k = step - stage
            if 0 <= k < chunks:
                stages[k][stage - 1].wait_recv()
                if stage < at.bits:
                    stages[k].append(g_start(k, stage))
    for swap in swaps:
        swap.wait()
    for k in range(chunks):
        for copy in stages[k]:
            copy.wait_send()
    for copy in sent:
        copy.wait_send()


def gather_all(depth_size, group, x_halves, dy_halves, weights):
    tp, rows, half = x_halves.shape
    chunks, _, depth_rows, width = weights.shape
    bits = group.bit_length() - 1
    dma = pltpu.SemaphoreType.DMA
    hbm = pl.BlockSpec(memory_space=pl.ANY)
    tokens = jax.ShapeDtypeStruct((depth_size * rows, tp * half), BF)
    return pl.pallas_call(
        functools.partial(gather_kernel, depth_size, group),
        out_shape=(
            tokens,
            tokens,
            jax.ShapeDtypeStruct((chunks, group, depth_size, depth_rows, width), BF),
        ),
        in_specs=[hbm] * 3,
        out_specs=(hbm, hbm, hbm),
        scratch_shapes=[
            dma((2, depth_size)),
            dma((2, depth_size)),
            dma((2,)),
            dma((2,)),
            dma((2,)),
            dma((chunks, depth_size)),
            dma((chunks, depth_size)),
            dma((chunks,)),
            dma((chunks, bits)),
            dma((chunks, bits)),
        ],
        compiler_params=pltpu.CompilerParams(collective_id=0, has_side_effects=True),
    )(x_halves, dy_halves, weights)


def share_kernel(depth_size, group, kv_in, kv_out, send, recv, loc):
    at = Place(depth_size, group)
    at.greet([at.across(stage) for stage in range(at.bits)])
    local(kv_in, kv_out.at[at.slot], loc).wait()
    copies = []
    for stage in range(at.bits):
        held = pl.ds(at.base(stage), 2**stage)
        copy = remote(kv_out.at[held], kv_out.at[held], send.at[stage], recv.at[stage], at.across(stage))
        copy.wait_recv()
        copies.append(copy)
    for copy in copies:
        copy.wait_send()


def share_group(depth_size, group, kv):
    bits = group.bit_length() - 1
    dma = pltpu.SemaphoreType.DMA
    hbm = pl.BlockSpec(memory_space=pl.ANY)
    return pl.pallas_call(
        functools.partial(share_kernel, depth_size, group),
        out_shape=jax.ShapeDtypeStruct((group,) + kv.shape, BF),
        in_specs=[hbm],
        out_specs=hbm,
        scratch_shapes=[dma((bits,)), dma((bits,)), dma],
        compiler_params=pltpu.CompilerParams(collective_id=1, has_side_effects=True),
    )(kv)


def fold_kernel(depth_size, group, g_in, total, landing, send, recv):
    at = Place(depth_size, group)
    at.greet([at.across(stage) for stage in range(at.bits)])
    for stage in reversed(range(at.bits)):
        size = 2**stage
        own = at.base(stage)
        other = own + (1 - 2 * at.bit(stage)) * size
        source = g_in if stage == at.bits - 1 else total
        copy = remote(
            source.at[pl.ds(other, size)],
            landing.at[pl.ds(size - 1, size)],
            send.at[stage],
            recv.at[stage],
            at.across(stage),
        )
        copy.wait()

        def add(i, _):
            total[own + i] = (
                source[own + i].astype(F32) + landing[size - 1 + i].astype(F32)
            ).astype(BF)
            return 0

        lax.fori_loop(0, size, add, 0)


def fold_group(depth_size, group, grads):
    bits = group.bit_length() - 1
    dma = pltpu.SemaphoreType.DMA
    vmem = pl.BlockSpec(memory_space=pltpu.VMEM)
    return pl.pallas_call(
        functools.partial(fold_kernel, depth_size, group),
        out_shape=jax.ShapeDtypeStruct(grads.shape, BF),
        in_specs=[vmem],
        out_specs=vmem,
        scratch_shapes=[
            pltpu.VMEM((group - 1,) + grads.shape[1:], BF),
            dma((bits,)),
            dma((bits,)),
        ],
        compiler_params=pltpu.CompilerParams(
            collective_id=2, has_side_effects=True, vmem_limit_bytes=60 << 20
        ),
    )(grads)


def reduce_kernel(depth_size, group, out_in, back_in, g_in, out_sum, back_sum, g_out, total, landing, g_s, g_r, z_s, z_r, z_l, t_acc, t_swap, t_land, tx_s, tx_r, tz_s, tz_r, ty_s, ty_r):
    at = Place(depth_size, group)
    at.greet(at.everyone())
    chunks = g_in.shape[0]
    depth_rows = g_in.shape[3]
    rows = out_sum.shape[0]
    half = t_acc.shape[2]
    last = at.bits - 1
    sent = []

    def g_start(k, stage):
        size = 2**stage
        other = at.base(stage) + (1 - 2 * at.bit(stage)) * size
        source = g_in.at[k] if stage == last else total.at[k]
        return remote(
            source.at[pl.ds(other, size)],
            landing.at[k, pl.ds(size - 1, size)],
            g_s.at[k, stage],
            g_r.at[k, stage],
            at.across(stage),
        )

    def g_finish(k, stage, copy):
        copy.wait_recv()
        sent.append(copy)
        size = 2**stage
        own = at.base(stage)
        source = g_in.at[k] if stage == last else total.at[k]

        def add(i, _):
            j = i // depth_size
            z = i % depth_size
            total[k, own + j, z] = (
                source[own + j, z].astype(F32) + landing[k, size - 1 + j, z].astype(F32)
            ).astype(BF)
            return 0

        lax.fori_loop(0, size * depth_size, add, 0)

    def z_start(k):
        copies = [
            remote(
                total.at[k, at.slot, lax.rem(at.depth + s, depth_size)],
                g_out.at[k, at.depth],
                z_s.at[k, s],
                z_r.at[k, s],
                at.along(s),
            )
            for s in range(1, depth_size)
        ]
        copies.append(local(total.at[k, at.slot, at.depth], g_out.at[k, at.depth], z_l.at[k]))
        return copies

    my_cols = pl.ds(pl.multiple_of(at.tp * half, half), half)
    her_cols = pl.ds(pl.multiple_of((1 - at.tp) * half, half), half)

    def token_first(i, src):
        return remote(src.at[:, her_cols], t_swap.at[i], tx_s.at[i], tx_r.at[i], at.twin())

    def token_second(i, src, copy):
        copy.wait_recv()
        sent.append(copy)

        def add(z, _):
            block = pl.ds(pl.multiple_of(z * rows, rows), rows)
            t_acc[i, block, :] = (
                src[block, my_cols].astype(F32) + t_swap[i, block, :].astype(F32)
            ).astype(BF)
            return 0

        lax.fori_loop(0, depth_size, add, 0)
        copies = []
        for s in range(1, depth_size):
            there = lax.rem(at.depth + s, depth_size)
            block = pl.ds(pl.multiple_of(there * rows, rows), rows)
            copies.append(
                remote(
                    t_acc.at[i, block, :], t_land.at[i, s - 1], tz_s.at[i, s], tz_r.at[i, s], at.along(s)
                )
            )
        return copies

    def token_third(i, dst, copies):
        for copy in copies:
            copy.wait_recv()
            sent.append(copy)
        mine = pl.ds(pl.multiple_of(at.depth * rows, rows), rows)
        value = t_acc[i, mine, :].astype(F32)
        for s in range(1, depth_size):
            value = value + t_land[i, s - 1].astype(F32)
        dst[:, my_cols] = value.astype(BF)
        return remote(dst.at[:, my_cols], dst.at[:, my_cols], ty_s.at[i], ty_r.at[i], at.twin())

    firsts = [token_first(0, out_in), token_first(1, back_in)]
    copies_of = {k: [g_start(k, last)] for k in range(chunks)}
    z_copies = {}
    seconds = []
    thirds = []
    for step in range(chunks + at.bits):
        for back in range(at.bits):
            k = step - back
            stage = last - back
            if 0 <= k < chunks:
                g_finish(k, stage, copies_of[k][back])
                if stage > 0:
                    copies_of[k].append(g_start(k, stage - 1))
                else:
                    z_copies[k] = z_start(k)
        if step == 1:
            seconds.append(token_second(0, out_in, firsts[0]))
        if step == 2:
            seconds.append(token_second(1, back_in, firsts[1]))
        if step == 4:
            thirds.append(token_third(0, out_sum, seconds[0]))
        if step == 5:
            thirds.append(token_third(1, back_sum, seconds[1]))
    for k in range(chunks):
        for copy in z_copies[k][:-1]:
            copy.wait()
        z_copies[k][-1].wait()
    for copy in thirds:
        copy.wait()
    for copy in sent:
        copy.wait_send()


def reduce_all(depth_size, group, out_part, back_part, grads):
    chunks, _, _, depth_rows, width = grads.shape
    all_rows, columns = out_part.shape
    rows = all_rows // depth_size
    half = columns // 2
    bits = group.bit_length() - 1
    dma = pltpu.SemaphoreType.DMA
    vmem = pl.BlockSpec(memory_space=pltpu.VMEM)
    tokens = jax.ShapeDtypeStruct((rows, columns), BF)
    return pl.pallas_call(
        functools.partial(reduce_kernel, depth_size, group),
        out_shape=(tokens, tokens, jax.ShapeDtypeStruct((chunks, depth_size, depth_rows, width), BF)),
        in_specs=[vmem] * 3,
        out_specs=(vmem, vmem, vmem),
        scratch_shapes=[
            pltpu.VMEM((chunks, group, depth_size, depth_rows, width), BF),
            pltpu.VMEM((chunks, group - 1, depth_size, depth_rows, width), BF),
            dma((chunks, bits)),
            dma((chunks, bits)),
            dma((chunks, depth_size)),
            dma((chunks, depth_size)),
            dma((chunks,)),
            pltpu.VMEM((2, all_rows, half), BF),
            pltpu.VMEM((2, all_rows, half), BF),
            pltpu.VMEM((2, depth_size - 1, rows, half), BF),
            dma((2,)),
            dma((2,)),
            dma((2, depth_size)),
            dma((2, depth_size)),
            dma((2,)),
            dma((2,)),
        ],
        compiler_params=pltpu.CompilerParams(
            collective_id=3, has_side_effects=True, vmem_limit_bytes=60 << 20
        ),
    )(out_part, back_part, grads)


def rotate(values, cosine, sine_table):
    half_rot = ROT // 2
    leading = values[..., :half_rot]
    trailing = values[..., half_rot:ROT]
    return jnp.concatenate(
        [
            leading * cosine - trailing * sine_table,
            trailing * cosine + leading * sine_table,
            values[..., ROT:],
        ],
        -1,
    )


def rope_tables(positions):
    freqs = 10000.0 ** (-(2.0 * jnp.arange(ROT // 2, dtype=F32)) / ROT)
    angles = positions.astype(F32)[:, None] * freqs[None, :]
    return (jnp.cos(angles), jnp.sin(angles))


def gelu_parts(values):
    gate = 0.5 * (1.0 + lax.erf(values * math.sqrt(0.5)))
    slope = gate + values * jnp.exp(-0.5 * values * values) * (1.0 / math.sqrt(2.0 * math.pi))
    return values * gate, slope


def shards(
    layer_input,
    block_order,
    attn_gain,
    attn_shift,
    mlp_gain,
    mlp_shift,
    w_query,
    b_query,
    w_key,
    b_key,
    w_value,
    b_value,
    w_out,
    b_out,
    w_up,
    b_up,
    w_down,
    b_down,
    out_grad,
):
    rows, width = layer_input.shape
    ctx_size = lax.axis_size("ctx")
    tp_size = lax.axis_size("tp")
    depth_size = HEADS // tp_size
    group = ctx_size // depth_size
    bits = group.bit_length() - 1
    depth_rows = width // ctx_size
    hidden_width = w_up.shape[1] // depth_size
    ff_chunks = hidden_width // CHUNK
    at = Place(depth_size, group)
    block_rows = rows // 2

    def permuted(array):
        lead = array.shape[:-1]
        n = len(lead)
        split = array.reshape(lead + (depth_size,) + (2,) * bits + (depth_rows,))
        order = tuple(range(n)) + tuple(n + 1 + b for b in reversed(range(bits))) + (n, n + 1 + bits)
        return split.transpose(order).reshape(lead + (width,))

    def restored(array):
        lead = array.shape[:-1]
        n = len(lead)
        split = array.reshape(lead + (2,) * bits + (depth_size, depth_rows))
        order = tuple(range(n)) + (n + bits,) + tuple(n + b for b in reversed(range(bits))) + (n + bits + 1,)
        return split.transpose(order).reshape(lead + (width,))

    def slot_members():
        table = []
        for slot in range(group):
            member = 0
            for stage in range(bits):
                member += ((slot >> stage) & 1) << (bits - 1 - stage)
            table.append(member)
        return table

    blocks = block_order.reshape(depth_size, group, 2)
    order = jnp.stack([blocks[:, m] for m in slot_members()], 0)
    place = order[..., None] * block_rows + jnp.arange(block_rows, dtype=jnp.int32)
    key_place = place.reshape(group * depth_size * rows)
    token_total = depth_size * rows
    query_place = lax.dynamic_slice_in_dim(key_place, at.slot * token_total, token_total)
    cosine, sine_table = rope_tables(query_place)

    inputs32 = layer_input.astype(F32)
    centered = inputs32 - jnp.mean(inputs32, -1, keepdims=True)
    inverse = lax.rsqrt(jnp.mean(centered * centered, -1, keepdims=True) + norm_epsilon)
    normal32 = centered * inverse

    def halves(array):
        return permuted(array).reshape(rows, tp_size, width // tp_size).transpose(1, 0, 2)

    def by_head(weight):
        return weight.reshape(depth_rows, depth_size, HD).transpose(1, 0, 2)

    def by_chunk(weight):
        return weight.reshape(depth_rows, depth_size, ff_chunks, CHUNK).transpose(2, 1, 0, 3)

    weights = jnp.concatenate(
        [
            jnp.concatenate([by_head(w_query), by_head(w_key)], -1)[None],
            jnp.concatenate([by_head(w_value), by_head(w_out.T)], -1)[None],
            jnp.concatenate([by_chunk(w_up), by_chunk(w_down.T)], -1),
        ],
        0,
    )
    normal, grad, gathered = gather_all(
        depth_size, group, halves(normal32.astype(BF)), halves(out_grad), weights
    )
    full = gathered.reshape(2 + ff_chunks, width, 2 * HD)
    gain_a, shift_a, gain_m, shift_m = permuted(jnp.stack([attn_gain, attn_shift, mlp_gain, mlp_shift]))
    normal_tokens = normal.astype(F32)
    attn_in = (normal_tokens * gain_a + shift_a).astype(BF)
    mlp_in = (normal_tokens * gain_m + shift_m).astype(BF)

    def own_part(vector, size):
        return lax.dynamic_slice_in_dim(vector, at.depth * size, size)

    query_key = mm(attn_in, full[0])
    query = rotate(query_key[:, :HD] + own_part(b_query, HD), cosine, sine_table).astype(BF)
    keys = rotate(query_key[:, HD:] + own_part(b_key, HD), cosine, sine_table).astype(BF)
    values = (mm(attn_in, full[1, :, :HD]) + own_part(b_value, HD)).astype(BF)
    out_t = full[1, :, HD:]
    shared = share_group(depth_size, group, jnp.concatenate([keys, values], -1))
    shared = shared.reshape(group * token_total, 2 * HD)
    all_keys, all_values = shared[:, :HD], shared[:, HD:]
    score_scale = 1.0 / math.sqrt(HD)
    scores = mm_nt(query, all_keys) * score_scale
    allowed = key_place[None, :] <= query_place[:, None]
    scores = jnp.where(allowed, scores, -1e30)
    top = jnp.max(scores, -1, keepdims=True)
    raw = jnp.exp(scores - top)
    probs = raw / jnp.sum(raw, -1, keepdims=True)
    probs_low = probs.astype(BF)
    attended = mm(probs_low, all_values)
    attn_low = attended.astype(BF)

    head_grad = mm(grad, out_t).astype(BF)
    delta = jnp.sum(head_grad.astype(F32) * attended, -1, keepdims=True)
    value_part = mm_tn(probs_low, head_grad)
    score_grad = (probs * (mm_nt(head_grad, all_values) - delta) * score_scale).astype(BF)
    query_acc = mm(score_grad, all_keys)
    key_part = mm_tn(score_grad, query)
    parts = jnp.concatenate([key_part, value_part], -1).astype(BF)
    folded = fold_group(depth_size, group, parts.reshape(group, token_total, 2 * HD))
    own_grads = lax.dynamic_index_in_dim(folded, at.slot, 0, keepdims=False).astype(F32)
    query_lin = rotate(query_acc, cosine, -sine_table)
    key_lin = rotate(own_grads[:, :HD], cosine, -sine_table)
    value_lin = own_grads[:, HD:]
    query_low, key_low, value_low = query_lin.astype(BF), key_lin.astype(BF), value_lin.astype(BF)
    query_key_low = jnp.concatenate([query_low, key_low], -1)
    attn_back = mm_nt(query_key_low, full[0]) + mm_nt(value_low, full[1, :, :HD])
    grad_chunks = [
        mm_tn(attn_in, query_key_low).astype(BF),
        jnp.concatenate([mm_tn(attn_in, value_low), mm_tn(grad, attn_low)], -1).astype(BF),
    ]

    branches = mm_nt(attn_low, out_t)
    mlp_back = jnp.zeros((token_total, width), F32)
    bias_up = own_part(b_up, hidden_width).reshape(ff_chunks, CHUNK)
    up_sums = []
    for i in range(ff_chunks):
        up, down_t = full[2 + i, :, :CHUNK], full[2 + i, :, CHUNK:]
        activated, slope = gelu_parts(mm(mlp_in, up) + bias_up[i])
        hidden = activated.astype(BF)
        up_grad = mm(grad, down_t) * slope
        up_sums.append(jnp.sum(up_grad, 0))
        up_low = up_grad.astype(BF)
        branches = branches + mm_nt(hidden, down_t)
        mlp_back = mlp_back + mm_nt(up_low, up)
        grad_chunks.append(jnp.concatenate([mm_tn(mlp_in, up_low), mm_tn(grad, hidden)], -1).astype(BF))

    normal_tokens2 = normal.astype(F32)
    back = attn_back * gain_a + mlp_back * gain_m
    grads = jnp.stack(grad_chunks).reshape(2 + ff_chunks, group, depth_size, depth_rows, 2 * HD)
    norm_sums = restored(
        jnp.stack(
            [
                jnp.sum(attn_back * normal_tokens2, 0),
                jnp.sum(attn_back, 0),
                jnp.sum(mlp_back * normal_tokens2, 0),
                jnp.sum(mlp_back, 0),
            ]
        )
    )
    own_biases = jnp.concatenate(
        [jnp.sum(query_lin, 0), jnp.sum(key_lin, 0), jnp.sum(value_lin, 0)] + up_sums
    )
    spread = jnp.where(
        jnp.arange(depth_size, dtype=jnp.int32)[:, None] == at.depth, own_biases[None, :], 0.0
    )
    norm_sums = lax.psum(norm_sums, ("ctx", "tp"))
    grad32 = out_grad.astype(F32)
    spread, bias_grad = lax.psum((spread, jnp.sum(grad32, 0)), "ctx")

    out_sum, back_sum, grad_shares = reduce_all(
        depth_size, group, branches.astype(BF), back.astype(BF), grads
    )
    layer_output = (inputs32 + restored(out_sum).astype(F32) + b_out + b_down).astype(BF)
    back_total = restored(back_sum).astype(F32)
    input_grad = grad32 + inverse * (
        back_total
        - jnp.mean(back_total, -1, keepdims=True)
        - normal32 * jnp.mean(back_total * normal32, -1, keepdims=True)
    )

    def from_head(share):
        return share.transpose(1, 0, 2).reshape(depth_rows, depth_size * HD).astype(F32)

    def from_chunk(share):
        return share.transpose(2, 1, 0, 3).reshape(depth_rows, depth_size * hidden_width).astype(F32)

    return (
        layer_output,
        input_grad,
        from_head(grad_shares[0, :, :, :HD]),
        from_head(grad_shares[0, :, :, HD:]),
        from_head(grad_shares[1, :, :, :HD]),
        from_head(grad_shares[1, :, :, HD:]).T,
        from_chunk(grad_shares[2:, :, :, :CHUNK]),
        from_chunk(grad_shares[2:, :, :, CHUNK:]).T,
        spread[:, :HD].reshape(-1),
        spread[:, HD : 2 * HD].reshape(-1),
        spread[:, 2 * HD : 3 * HD].reshape(-1),
        bias_grad,
        spread[:, 3 * HD :].reshape(-1),
        bias_grad,
        norm_sums[0],
        norm_sums[1],
        norm_sums[2],
        norm_sums[3],
    )


def solution(mesh):
    in_specs = (
        P("ctx", None),
        P(),
        P(),
        P(),
        P(),
        P(),
        P("ctx", "tp"),
        P("tp"),
        P("ctx", "tp"),
        P("tp"),
        P("ctx", "tp"),
        P("tp"),
        P("tp", "ctx"),
        P(),
        P("ctx", "tp"),
        P("tp"),
        P("tp", "ctx"),
        P(),
        P("ctx", None),
    )
    out_specs = (
        P("ctx", None),
        P("ctx", None),
        P("ctx", "tp"),
        P("ctx", "tp"),
        P("ctx", "tp"),
        P("tp", "ctx"),
        P("ctx", "tp"),
        P("tp", "ctx"),
        P("tp"),
        P("tp"),
        P("tp"),
        P(),
        P("tp"),
        P(),
        P(),
        P(),
        P(),
        P(),
    )
    return jax.shard_map(shards, mesh=mesh, in_specs=in_specs, out_specs=out_specs, check_vma=False)
```

```python
import functools
import math

import jax
import jax.numpy as jnp
from jax import lax
from jax.experimental import pallas as pl
from jax.experimental.pallas import tpu as pltpu
from jax.sharding import PartitionSpec as P

HEADS = 8
HD = 256
ROT = 64
CHUNK = 256

norm_epsilon = 1e-05
BF = jnp.bfloat16
F32 = jnp.float32
MESH = pl.DeviceIdType.MESH


def mm(a, b):
    return jnp.dot(a, b, preferred_element_type=F32)


def mm_tn(a, b):
    return lax.dot_general(a, b, (((0,), (0,)), ((), ())), preferred_element_type=F32)


def mm_nt(a, b):
    return lax.dot_general(a, b, (((1,), (1,)), ((), ())), preferred_element_type=F32)


class Place:
    def __init__(self, depth_size, group):
        self.depth_size = depth_size
        self.group = group
        self.bits = group.bit_length() - 1
        self.ctx = lax.axis_index("ctx")
        self.tp = lax.axis_index("tp")
        self.depth = self.ctx // group
        self.member = self.ctx % group
        slot = 0
        for stage in range(self.bits):
            slot = slot + self.bit(stage) * 2**stage
        self.slot = slot

    def bit(self, stage):
        return (self.member // 2 ** (self.bits - 1 - stage)) % 2

    def along(self, step):
        return {"ctx": lax.rem(self.depth + step, self.depth_size) * self.group + self.member}

    def across(self, stage):
        reach = 2 ** (self.bits - 1 - stage)
        return {"ctx": self.ctx + (1 - 2 * self.bit(stage)) * reach}

    def twin(self):
        return {"tp": 1 - self.tp}

    def base(self, stage):
        return (self.slot // 2**stage) * 2**stage

    def greet(self, devices):
        barrier = pltpu.get_barrier_semaphore()
        for device in devices:
            pl.semaphore_signal(barrier, inc=1, device_id=device, device_id_type=MESH)
        pl.semaphore_wait(barrier, len(devices))

    def everyone(self):
        return (
            [self.along(step) for step in range(1, self.depth_size)]
            + [self.across(stage) for stage in range(self.bits)]
            + [self.twin()]
        )


def remote(src, dst, send, recv, device):
    copy = pltpu.make_async_remote_copy(
        src_ref=src, dst_ref=dst, send_sem=send, recv_sem=recv, device_id=device, device_id_type=MESH
    )
    copy.start()
    return copy


def local(src, dst, sem):
    copy = pltpu.make_async_copy(src, dst, sem)
    copy.start()
    return copy


def gather_kernel(depth_size, group, x_in, dy_in, w_in, x_out, dy_out, w_out, tz_s, tz_r, tx_s, tx_r, t_l, z_s, z_r, z_l, g_s, g_r):
    at = Place(depth_size, group)
    at.greet(at.everyone())
    rows, half = x_in.shape[1:]
    sent = []
    mine = pl.ds(pl.multiple_of(at.depth * rows, rows), rows)
    my_cols = pl.ds(pl.multiple_of(at.tp * half, half), half)

    def token_start(i, src, dst):
        copies = [
            remote(src.at[at.tp], dst.at[mine, my_cols], tz_s.at[i, s], tz_r.at[i, s], at.along(s))
            for s in range(1, depth_size)
        ]
        copies.append(local(src.at[at.tp], dst.at[mine, my_cols], t_l.at[i]))
        return copies

    def token_swap(i, copies, dst):
        for copy in copies[:-1]:
            copy.wait_recv()
            sent.append(copy)
        copies[-1].wait()
        return remote(dst.at[:, my_cols], dst.at[:, my_cols], tx_s.at[i], tx_r.at[i], at.twin())

    chunks = w_in.shape[0]

    def z_start(k):
        copies = [
            remote(
                w_in.at[k, lax.rem(at.depth + s, depth_size)],
                w_out.at[k, at.slot, at.depth],
                z_s.at[k, s],
                z_r.at[k, s],
                at.along(s),
            )
            for s in range(1, depth_size)
        ]
        copies.append(local(w_in.at[k, at.depth], w_out.at[k, at.slot, at.depth], z_l.at[k]))
        return copies

    def z_wait(copies):
        for copy in copies[:-1]:
            copy.wait_recv()
            sent.append(copy)
        copies[-1].wait()

    def g_start(k, stage):
        held = pl.ds(at.base(stage), 2**stage)
        return remote(
            w_out.at[k, held], w_out.at[k, held], g_s.at[k, stage], g_r.at[k, stage], at.across(stage)
        )

    ahead = 2
    tokens = [token_start(0, x_in, x_out)]
    z_copies = {k: z_start(k) for k in range(min(ahead, chunks))}
    stages = {}
    swaps = []
    for step in range(chunks + at.bits):
        if step < chunks:
            z_wait(z_copies[step])
            stages[step] = [g_start(step, 0)]
            if step + ahead < chunks:
                z_copies[step + ahead] = z_start(step + ahead)
            if step == 0:
                swaps.append(token_swap(0, tokens[0], x_out))
                tokens.append(token_start(1, dy_in, dy_out))
            if step == 1:
                swaps.append(token_swap(1, tokens[1], dy_out))
        for stage in range(1, at.bits + 1):
            k = step - stage
            if 0 <= k < chunks:
                stages[k][stage - 1].wait_recv()
                if stage < at.bits:
                    stages[k].append(g_start(k, stage))
    for swap in swaps:
        swap.wait()
    for k in range(chunks):
        for copy in stages[k]:
            copy.wait_send()
    for copy in sent:
        copy.wait_send()


def gather_all(depth_size, group, x_halves, dy_halves, weights):
    tp, rows, half = x_halves.shape
    chunks, _, depth_rows, width = weights.shape
    bits = group.bit_length() - 1
    dma = pltpu.SemaphoreType.DMA
    hbm = pl.BlockSpec(memory_space=pl.ANY)
    tokens = jax.ShapeDtypeStruct((depth_size * rows, tp * half), BF)
    return pl.pallas_call(
        functools.partial(gather_kernel, depth_size, group),
        out_shape=(
            tokens,
            tokens,
            jax.ShapeDtypeStruct((chunks, group, depth_size, depth_rows, width), BF),
        ),
        in_specs=[hbm] * 3,
        out_specs=(hbm, hbm, hbm),
        scratch_shapes=[
            dma((2, depth_size)),
            dma((2, depth_size)),
            dma((2,)),
            dma((2,)),
            dma((2,)),
            dma((chunks, depth_size)),
            dma((chunks, depth_size)),
            dma((chunks,)),
            dma((chunks, bits)),
            dma((chunks, bits)),
        ],
        compiler_params=pltpu.CompilerParams(collective_id=0, has_side_effects=True),
    )(x_halves, dy_halves, weights)


def share_kernel(depth_size, group, kv_in, kv_out, send, recv, loc):
    at = Place(depth_size, group)
    at.greet([at.across(stage) for stage in range(at.bits)])
    local(kv_in, kv_out.at[at.slot], loc).wait()
    copies = []
    for stage in range(at.bits):
        held = pl.ds(at.base(stage), 2**stage)
        copy = remote(kv_out.at[held], kv_out.at[held], send.at[stage], recv.at[stage], at.across(stage))
        copy.wait_recv()
        copies.append(copy)
    for copy in copies:
        copy.wait_send()


def share_group(depth_size, group, kv):
    bits = group.bit_length() - 1
    dma = pltpu.SemaphoreType.DMA
    hbm = pl.BlockSpec(memory_space=pl.ANY)
    return pl.pallas_call(
        functools.partial(share_kernel, depth_size, group),
        out_shape=jax.ShapeDtypeStruct((group,) + kv.shape, BF),
        in_specs=[hbm],
        out_specs=hbm,
        scratch_shapes=[dma((bits,)), dma((bits,)), dma],
        compiler_params=pltpu.CompilerParams(collective_id=1, has_side_effects=True),
    )(kv)


def fold_kernel(depth_size, group, g_in, total, landing, send, recv):
    at = Place(depth_size, group)
    at.greet([at.across(stage) for stage in range(at.bits)])
    for stage in reversed(range(at.bits)):
        size = 2**stage
        own = at.base(stage)
        other = own + (1 - 2 * at.bit(stage)) * size
        source = g_in if stage == at.bits - 1 else total
        copy = remote(
            source.at[pl.ds(other, size)],
            landing.at[pl.ds(size - 1, size)],
            send.at[stage],
            recv.at[stage],
            at.across(stage),
        )
        copy.wait()

        def add(i, _):
            total[own + i] = (
                source[own + i].astype(F32) + landing[size - 1 + i].astype(F32)
            ).astype(BF)
            return 0

        lax.fori_loop(0, size, add, 0)


def fold_group(depth_size, group, grads):
    bits = group.bit_length() - 1
    dma = pltpu.SemaphoreType.DMA
    vmem = pl.BlockSpec(memory_space=pltpu.VMEM)
    return pl.pallas_call(
        functools.partial(fold_kernel, depth_size, group),
        out_shape=jax.ShapeDtypeStruct(grads.shape, BF),
        in_specs=[vmem],
        out_specs=vmem,
        scratch_shapes=[
            pltpu.VMEM((group - 1,) + grads.shape[1:], BF),
            dma((bits,)),
            dma((bits,)),
        ],
        compiler_params=pltpu.CompilerParams(
            collective_id=2, has_side_effects=True, vmem_limit_bytes=60 << 20
        ),
    )(grads)


def reduce_kernel(depth_size, group, out_in, back_in, g_in, out_sum, back_sum, g_out, total, landing, g_s, g_r, z_s, z_r, z_l, t_acc, t_swap, t_land, tx_s, tx_r, tz_s, tz_r, ty_s, ty_r):
    at = Place(depth_size, group)
    at.greet(at.everyone())
    chunks = g_in.shape[0]
    depth_rows = g_in.shape[3]
    rows = out_sum.shape[0]
    half = t_acc.shape[2]
    last = at.bits - 1
    sent = []

    def g_start(k, stage):
        size = 2**stage
        other = at.base(stage) + (1 - 2 * at.bit(stage)) * size
        source = g_in.at[k] if stage == last else total.at[k]
        return remote(
            source.at[pl.ds(other, size)],
            landing.at[k, pl.ds(size - 1, size)],
            g_s.at[k, stage],
            g_r.at[k, stage],
            at.across(stage),
        )

    def g_finish(k, stage, copy):
        copy.wait_recv()
        sent.append(copy)
        size = 2**stage
        own = at.base(stage)
        source = g_in.at[k] if stage == last else total.at[k]

        def add(i, _):
            j = i // depth_size
            z = i % depth_size
            total[k, own + j, z] = (
                source[own + j, z].astype(F32) + landing[k, size - 1 + j, z].astype(F32)
            ).astype(BF)
            return 0

        lax.fori_loop(0, size * depth_size, add, 0)

    def z_start(k):
        copies = [
            remote(
                total.at[k, at.slot, lax.rem(at.depth + s, depth_size)],
                g_out.at[k, at.depth],
                z_s.at[k, s],
                z_r.at[k, s],
                at.along(s),
            )
            for s in range(1, depth_size)
        ]
        copies.append(local(total.at[k, at.slot, at.depth], g_out.at[k, at.depth], z_l.at[k]))
        return copies

    my_cols = pl.ds(pl.multiple_of(at.tp * half, half), half)
    her_cols = pl.ds(pl.multiple_of((1 - at.tp) * half, half), half)

    def token_first(i, src):
        return remote(src.at[:, her_cols], t_swap.at[i], tx_s.at[i], tx_r.at[i], at.twin())

    def token_second(i, src, copy):
        copy.wait_recv()
        sent.append(copy)

        def add(z, _):
            block = pl.ds(pl.multiple_of(z * rows, rows), rows)
            t_acc[i, block, :] = (
                src[block, my_cols].astype(F32) + t_swap[i, block, :].astype(F32)
            ).astype(BF)
            return 0

        lax.fori_loop(0, depth_size, add, 0)
        copies = []
        for s in range(1, depth_size):
            there = lax.rem(at.depth + s, depth_size)
            block = pl.ds(pl.multiple_of(there * rows, rows), rows)
            copies.append(
                remote(
                    t_acc.at[i, block, :], t_land.at[i, s - 1], tz_s.at[i, s], tz_r.at[i, s], at.along(s)
                )
            )
        return copies

    def token_third(i, dst, copies):
        for copy in copies:
            copy.wait_recv()
            sent.append(copy)
        mine = pl.ds(pl.multiple_of(at.depth * rows, rows), rows)
        value = t_acc[i, mine, :].astype(F32)
        for s in range(1, depth_size):
            value = value + t_land[i, s - 1].astype(F32)
        dst[:, my_cols] = value.astype(BF)
        return remote(dst.at[:, my_cols], dst.at[:, my_cols], ty_s.at[i], ty_r.at[i], at.twin())

    firsts = [token_first(0, out_in), token_first(1, back_in)]
    copies_of = {k: [g_start(k, last)] for k in range(chunks)}
    z_copies = {}
    seconds = []
    thirds = []
    for step in range(chunks + at.bits):
        for back in range(at.bits):
            k = step - back
            stage = last - back
            if 0 <= k < chunks:
                g_finish(k, stage, copies_of[k][back])
                if stage > 0:
                    copies_of[k].append(g_start(k, stage - 1))
                else:
                    z_copies[k] = z_start(k)
        if step == 1:
            seconds.append(token_second(0, out_in, firsts[0]))
        if step == 2:
            seconds.append(token_second(1, back_in, firsts[1]))
        if step == 4:
            thirds.append(token_third(0, out_sum, seconds[0]))
        if step == 5:
            thirds.append(token_third(1, back_sum, seconds[1]))
    for k in range(chunks):
        for copy in z_copies[k][:-1]:
            copy.wait()
        z_copies[k][-1].wait()
    for copy in thirds:
        copy.wait()
    for copy in sent:
        copy.wait_send()


def reduce_all(depth_size, group, out_part, back_part, grads):
    chunks, _, _, depth_rows, width = grads.shape
    all_rows, columns = out_part.shape
    rows = all_rows // depth_size
    half = columns // 2
    bits = group.bit_length() - 1
    dma = pltpu.SemaphoreType.DMA
    vmem = pl.BlockSpec(memory_space=pltpu.VMEM)
    tokens = jax.ShapeDtypeStruct((rows, columns), BF)
    return pl.pallas_call(
        functools.partial(reduce_kernel, depth_size, group),
        out_shape=(tokens, tokens, jax.ShapeDtypeStruct((chunks, depth_size, depth_rows, width), BF)),
        in_specs=[vmem] * 3,
        out_specs=(vmem, vmem, vmem),
        scratch_shapes=[
            pltpu.VMEM((chunks, group, depth_size, depth_rows, width), BF),
            pltpu.VMEM((chunks, group - 1, depth_size, depth_rows, width), BF),
            dma((chunks, bits)),
            dma((chunks, bits)),
            dma((chunks, depth_size)),
            dma((chunks, depth_size)),
            dma((chunks,)),
            pltpu.VMEM((2, all_rows, half), BF),
            pltpu.VMEM((2, all_rows, half), BF),
            pltpu.VMEM((2, depth_size - 1, rows, half), BF),
            dma((2,)),
            dma((2,)),
            dma((2, depth_size)),
            dma((2, depth_size)),
            dma((2,)),
            dma((2,)),
        ],
        compiler_params=pltpu.CompilerParams(
            collective_id=3, has_side_effects=True, vmem_limit_bytes=60 << 20
        ),
    )(out_part, back_part, grads)


def rotate(values, cosine, sine_table):
    half_rot = ROT // 2
    leading = values[..., :half_rot]
    trailing = values[..., half_rot:ROT]
    return jnp.concatenate(
        [
            leading * cosine - trailing * sine_table,
            trailing * cosine + leading * sine_table,
            values[..., ROT:],
        ],
        -1,
    )


def rope_tables(positions):
    freqs = 10000.0 ** (-(2.0 * jnp.arange(ROT // 2, dtype=F32)) / ROT)
    angles = positions.astype(F32)[:, None] * freqs[None, :]
    return (jnp.cos(angles), jnp.sin(angles))


def gelu_parts(values):
    gate = 0.5 * (1.0 + lax.erf(values * math.sqrt(0.5)))
    slope = gate + values * jnp.exp(-0.5 * values * values) * (1.0 / math.sqrt(2.0 * math.pi))
    return values * gate, slope


SMALL_ROWS = 96
VMEM_BYTES = 64 << 20


def slot_member(slot, bits):
    member = 0
    for stage in range(bits):
        member += ((slot >> stage) & 1) << (bits - 1 - stage)
    return member


def natural_blocks(depth_size, group):
    bits = group.bit_length() - 1
    return [
        depth * group + slot_member(slot, bits) for slot in range(group) for depth in range(depth_size)
    ]


def token_places(block_order, depth_size, group, rows):
    bits = group.bit_length() - 1
    blocks = block_order.reshape(depth_size, group, 2)
    order = jnp.stack([blocks[:, slot_member(slot, bits)] for slot in range(group)], 0)
    place = order[..., None] * (rows // 2) + jnp.arange(rows // 2, dtype=jnp.int32)
    return place.reshape(group * depth_size * rows)

ROW_TILE = 256
DROP = -1e30


def layout_of(depth_size, group, depth_rows, rows, width, ff_chunks):
    tokens = depth_size * rows
    half = width // 2
    landing = (group - 1) * depth_size * depth_rows
    heads = 3 + ff_chunks
    cols = 1 + ff_chunks
    return [
        ("wr", (heads, width, CHUNK), BF),
        ("wc", (cols, CHUNK, width), BF),
        ("gr", (heads, width, CHUNK), BF),
        ("gc", (cols, CHUNK, width), BF),
        ("lr", (heads, landing, CHUNK), BF),
        ("lc", (cols, CHUNK, landing), BF),
        ("x", (tokens, width), BF),
        ("dy", (tokens, width), BF),
        ("na", (tokens, width), BF),
        ("nm", (tokens, width), BF),
        ("nmt", (width, tokens), BF),
        ("kv", (group * tokens, 2 * HD), BF),
        ("q", (tokens, HD), BF),
        ("low", (tokens, 3 * HD), BF),
        ("al", (tokens, HD), BF),
        ("hg", (tokens, HD), BF),
        ("alt", (HD, tokens), BF),
        ("att", (HD, tokens), F32),
        ("dqt", (HD, tokens), F32),
        ("stat", (8, tokens), F32),
        ("tab", (group * tokens, 128), F32),
        ("kb", (8, HD), F32),
        ("hid", (ff_chunks, tokens, CHUNK), BF),
        ("ul", (ff_chunks, tokens, CHUNK), BF),
        ("tz", (2, 2, tokens // 2, half // 2), BF),
        ("te", (2, rows, half), BF),
        ("fin", (2, rows, width), BF),
        ("mean", (tokens, 1), F32),
        ("inv", (tokens, 1), F32),
        ("gv", (8, width), F32),
        ("ps", (group.bit_length(), SMALL_ROWS, 128), F32),
        ("pl", (group.bit_length() - 1, SMALL_ROWS, 128), F32),
        ("pz", (depth_size, SMALL_ROWS, 128), F32),
        ("px", (2, SMALL_ROWS, 128), F32),
    ]


def semaphores_of(depth_size, group, items):
    bits = group.bit_length() - 1
    return [
        ("z_s", (items, 2, depth_size)),
        ("z_r", (items, 2, depth_size)),
        ("z_l", (items, 2)),
        ("g_s", (items, 2, bits)),
        ("g_r", (items, 2, bits)),
        ("t_s", (2, 3)),
        ("t_r", (2, 3)),
        ("w_s", (2, 3)),
        ("w_r", (2, 3)),
        ("kv_s", (3, bits)),
        ("kv_r", (3, bits)),
        ("f_s", (items, 2, bits)),
        ("f_r", (items, 2, bits)),
        ("e_s", (items, 2, depth_size)),
        ("e_r", (items, 2, depth_size)),
        ("e_l", (items, 2)),
        ("o_s", (2, 5)),
        ("o_r", (2, 5)),
        ("i_l", (4,)),
        ("p_s", (bits + depth_size,)),
        ("p_r", (bits + depth_size,)),
    ]


INPUTS = ("x_in", "dy_in", "vectors", "biases", "places")
INPUTS += ("w_query", "w_key", "w_value", "w_out", "w_up", "w_down")
OUTPUTS = ("layer_output", "input_grad", "g_query", "g_key", "g_value", "g_out", "g_up", "g_down")
OUTPUTS += ("norm_sums", "b_query", "b_key", "b_value", "b_up", "b_sum")


class Bag:
    pass


def fused_kernel(names, depth_size, group, *refs):
    m = Bag()
    for name, ref in zip(names, refs, strict=True):
        setattr(m, name, ref)
    at = Place(depth_size, group)
    at.greet(at.everyone())
    bits = at.bits
    rows, width = m.x_in.shape
    depth_rows = width // (depth_size * group)
    tokens = depth_size * rows
    half = width // 2
    ff_width = m.w_up.shape[1] // depth_size
    ff_chunks = ff_width // CHUNK
    block_count = width // depth_rows
    own_block = at.slot * depth_size + at.depth
    natural = natural_blocks(depth_size, group)
    sends, settled = [], []

    def blocks(first, count):
        return pl.ds(pl.multiple_of(first * depth_rows, depth_rows), count * depth_rows)

    def token_rows(depth):
        return pl.ds(pl.multiple_of(depth * rows, rows), rows)

    def peer(step):
        return lax.rem(at.depth + step, depth_size)

    my_cols = pl.ds(pl.multiple_of(at.tp * half, half), half)
    her_cols = pl.ds(pl.multiple_of((1 - at.tp) * half, half), half)

    items = [(("r", 0), ("r", 1)), (("r", 2), ("c", 0))]
    items += [(("r", 3 + i), ("c", 1 + i)) for i in range(ff_chunks)]
    row_pairs = [(m.w_query, m.g_query), (m.w_key, m.g_key), (m.w_value, m.g_value)]

    def outer(kind, a, depth, which):
        if kind == "r" and a < 3:
            return row_pairs[a][which].at[:, pl.ds(pl.multiple_of(depth * HD, HD), HD)]
        if kind == "r":
            first = pl.multiple_of(depth * ff_width + (a - 3) * CHUNK, CHUNK)
            return (m.w_up, m.g_up)[which].at[:, pl.ds(first, CHUNK)]
        if a == 0:
            return (m.w_out, m.g_out)[which].at[pl.ds(pl.multiple_of(depth * HD, HD), HD), :]
        first = pl.multiple_of(depth * ff_width + (a - 1) * CHUNK, CHUNK)
        return (m.w_down, m.g_down)[which].at[pl.ds(first, CHUNK), :]

    def part(pair, kind, a, first, count):
        if kind == "r":
            return pair[0].at[a, blocks(first, count), :]
        return pair[1].at[a, :, blocks(first, count)]

    weights, grads, landing = (m.wr, m.wc), (m.gr, m.gc), (m.lr, m.lc)

    def z_start(k):
        copies = []
        for j, (kind, a) in enumerate(items[k]):
            for s in range(1, depth_size):
                copies.append(
                    remote(
                        outer(kind, a, peer(s), 0),
                        part(weights, kind, a, own_block, 1),
                        m.z_s.at[k, j, s],
                        m.z_r.at[k, j, s],
                        at.along(s),
                    )
                )
        for j, (kind, a) in enumerate(items[k]):
            copies.append(
                local(outer(kind, a, at.depth, 0), part(weights, kind, a, own_block, 1), m.z_l.at[k, j])
            )
        return copies

    def z_wait(copies):
        for copy in copies[:-2]:
            copy.wait_recv()
        sends.extend(copies[:-2])
        for copy in copies[-2:]:
            copy.wait()

    def g_start(k, stage):
        copies = []
        for j, (kind, a) in enumerate(items[k]):
            held = part(weights, kind, a, at.base(stage) * depth_size, 2**stage * depth_size)
            copies.append(
                remote(held, held, m.g_s.at[k, j, stage], m.g_r.at[k, j, stage], at.across(stage))
            )
        return copies

    def received(copies):
        for copy in copies:
            copy.wait_recv()
        sends.extend(copies)

    def settle(copies):
        for copy in copies:
            copy.wait_send()
        settled.extend(copies)

    def fold_start(k, stage):
        size = 2**stage
        other = at.base(stage) + (1 - 2 * at.bit(stage)) * size
        return [
            remote(
                part(grads, kind, a, other * depth_size, size * depth_size),
                part(landing, kind, a, (size - 1) * depth_size, size * depth_size),
                m.f_s.at[k, j, stage],
                m.f_r.at[k, j, stage],
                at.across(stage),
            )
            for j, (kind, a) in enumerate(items[k])
        ]

    def fold_finish(k, stage, copies):
        received(copies)
        size = 2**stage
        own = at.base(stage) * depth_size
        for kind, a in items[k]:

            def add(i, _, kind=kind, a=a):
                mine = blocks(own + i, 1)
                theirs = blocks((size - 1) * depth_size + i, 1)
                if kind == "r":
                    total = m.gr[a, mine, :].astype(F32) + m.lr[a, theirs, :].astype(F32)
                    m.gr[a, mine, :] = total.astype(BF)
                else:
                    total = m.gc[a, :, mine].astype(F32) + m.lc[a, :, theirs].astype(F32)
                    m.gc[a, :, mine] = total.astype(BF)
                return 0

            lax.fori_loop(0, size * depth_size, add, 0)

    def end_start(k):
        copies = []
        for j, (kind, a) in enumerate(items[k]):
            for s in range(1, depth_size):
                copies.append(
                    remote(
                        part(grads, kind, a, at.slot * depth_size + peer(s), 1),
                        outer(kind, a, at.depth, 1),
                        m.e_s.at[k, j, s],
                        m.e_r.at[k, j, s],
                        at.along(s),
                    )
                )
        for j, (kind, a) in enumerate(items[k]):
            copies.append(
                local(part(grads, kind, a, own_block, 1), outer(kind, a, at.depth, 1), m.e_l.at[k, j])
            )
        return copies

    near = {"ctx": at.ctx + (1 - 2 * (at.depth % 2)) * group}
    far = {"ctx": at.ctx + (2 - 4 * (at.depth // 2)) * group}
    near_depth = at.depth + 1 - 2 * (at.depth % 2)
    pair_first = at.depth // 2 * 2
    my_pair = pl.ds(pl.multiple_of(pair_first * rows, rows), 2 * rows)
    her_pair = pl.ds(pl.multiple_of((2 - pair_first) * rows, rows), 2 * rows)
    quarter = half // 2
    my_quarter = pl.ds(pl.multiple_of(at.tp * half + at.depth % 2 * quarter, quarter), quarter)
    her_quarter = pl.ds(pl.multiple_of(at.tp * half + (1 - at.depth % 2) * quarter, quarter), quarter)

    def token_step(i, buffer, step, copies):
        if copies:
            received(copies[-1:])
        brought = [
            None,
            (token_rows(near_depth), my_cols),
            (her_pair, my_quarter),
            (her_pair, her_quarter),
        ]
        given = [(token_rows(at.depth), my_cols), (my_pair, my_quarter), (her_pair, my_quarter)]
        if step < 3:
            piece = buffer.at[given[step][0], given[step][1]]
            there = far if step == 1 else near
            copies.append(remote(piece, piece, m.t_s.at[i, step], m.t_r.at[i, step], there))
        if step:
            piece = buffer.at[brought[step][0], brought[step][1]]
            swapped[i].append(
                remote(piece, piece, m.w_s.at[i, step - 1], m.w_r.at[i, step - 1], at.twin())
            )
        return copies

    def kv_start(stage):
        size = 2**stage * tokens
        held = m.kv.at[pl.ds(pl.multiple_of(at.base(stage) * tokens, tokens), size), :]
        return remote(held, held, m.kv_s.at[0, stage], m.kv_r.at[0, stage], at.across(stage))

    spare = (m.lr.at[1 + ff_chunks], m.lr.at[2 + ff_chunks])

    def dkv_start(stage):
        size = 2**stage
        other = at.base(stage) + (1 - 2 * at.bit(stage)) * size
        given = pl.ds(pl.multiple_of(other * tokens, tokens), size * tokens)
        taken = pl.ds((size - 1) * tokens, size * tokens)
        return [
            remote(
                m.kv.at[given, slice(h * HD, (h + 1) * HD)],
                spare[h].at[taken, :],
                m.kv_s.at[1 + h, stage],
                m.kv_r.at[1 + h, stage],
                at.across(stage),
            )
            for h in range(2)
        ]

    def dkv_finish(stage, copies):
        received(copies)
        size = 2**stage
        own = at.base(stage) * tokens
        step = ROW_TILE

        def add(i, _):
            mine = pl.ds(pl.multiple_of(own + i * step, step), step)
            theirs = pl.ds(pl.multiple_of((size - 1) * tokens + i * step, step), step)
            for h in range(2):
                cols = slice(h * HD, (h + 1) * HD)
                total = m.kv[mine, cols].astype(F32) + spare[h][theirs, :].astype(F32)
                m.kv[mine, cols] = total.astype(BF)
            return 0

        lax.fori_loop(0, size * tokens // step, add, 0)

    def place_rows():
        mine = token_rows(at.depth)
        for b in range(block_count):
            c = natural[b]
            into = slice(b * depth_rows, (b + 1) * depth_rows)
            out_of = slice(c * depth_rows, (c + 1) * depth_rows)
            m.x[mine, into] = m.x_in[:, out_of]
            m.dy[mine, into] = m.dy_in[:, out_of]
            m.gv[:, into] = m.vectors[:, out_of]

    def affine():
        step = 32

        def stats(i, _):
            here = pl.ds(pl.multiple_of(i * step, step), step)
            x = m.x[here, :].astype(F32)
            mean = jnp.mean(x, -1, keepdims=True)
            centered = x - mean
            m.mean[here, :] = mean
            m.inv[here, :] = lax.rsqrt(jnp.mean(centered * centered, -1, keepdims=True) + norm_epsilon)
            return 0

        lax.fori_loop(0, tokens // step, stats, 0)

        def body(i, _):
            here = token_rows(i)
            for n in range(width // 512):
                cols = slice(n * 512, (n + 1) * 512)
                normal = (m.x[here, cols].astype(F32) - m.mean[here, :]) * m.inv[here, :]
                m.na[here, cols] = (normal * m.gv[0:1, cols] + m.gv[1:2, cols]).astype(BF)
                mlp = normal * m.gv[2:3, cols] + m.gv[3:4, cols]
                m.nm[here, cols] = mlp.astype(BF)
                m.nmt[cols, here] = mlp.T.astype(BF)
            return 0

        lax.fori_loop(0, depth_size, body, 0)

    lane = lax.broadcasted_iota(jnp.int32, (1, 128), 1)

    def place_column(n):
        row = jnp.broadcast_to(m.places[pl.ds(n, 1), :].astype(F32), (128, 128))
        return row.T

    def make_tables():
        def body(n, _):
            angles = place_column(n) * m.vectors[5:6, :128]
            here = pl.ds(pl.multiple_of(n * 128, 128), 128)
            m.tab[here, :] = jnp.cos(angles - m.vectors[6:7, :128])
            return 0

        lax.fori_loop(0, group * tokens // 128, body, 0)

    def turned(value, here, sign):
        head = value[:, :128]
        left = pltpu.roll(head, 128 - ROT // 2, 1)
        right = pltpu.roll(head, ROT // 2, 1)
        table = m.tab[here, :]
        cosine = jnp.where(lane < ROT, table, 1.0)
        sine = sign * pltpu.roll(table, ROT, 1)
        crossed = jnp.where(lane < ROT // 2, -left, jnp.where(lane < ROT, right, 0.0))
        return head * cosine + crossed * sine

    def project(a):
        return mm(m.na[...], m.wr[a]) + m.biases[a : a + 1, :]

    kv_own = pl.ds(pl.multiple_of(at.slot * tokens, tokens), tokens)
    score_scale = 1.0 / math.sqrt(HD)

    def make_query_key():
        query = project(0)
        head = turned(query, kv_own, 1.0)
        m.q[:, :128] = head.astype(BF)
        m.q[:, 128:] = query[:, 128:].astype(BF)
        keys = project(1)
        m.kv[kv_own, :128] = turned(keys, kv_own, 1.0).astype(BF)
        m.kv[kv_own, 128:HD] = keys[:, 128:].astype(BF)

    def make_values():
        m.kv[kv_own, HD:] = project(2).astype(BF)

    def key_rows(j):
        return pl.ds(pl.multiple_of(j * tokens, tokens), tokens)

    def masked_scores(j):
        scores = mm_nt(m.kv[key_rows(j), :HD], m.q[...]) * score_scale
        count = tokens // 128
        column = jnp.concatenate([place_column(j * count + n)[:, :1] for n in range(count)], 0)
        row = jnp.concatenate([m.places[pl.ds(at.slot * count + n, 1), :] for n in range(count)], 1)
        return jnp.where(column <= row.astype(F32), scores, DROP)

    def attend(j):
        scores = masked_scores(j)
        if j == 0:
            old = jnp.full((1, tokens), -1e20, F32)
        else:
            old = m.stat[0:1, :]
        new = jnp.maximum(old, jnp.max(scores, 0, keepdims=True))
        raw = jnp.exp(scores - new)
        total = jnp.sum(raw, 0, keepdims=True)
        value = mm(m.kv[key_rows(j), HD:].T, raw.astype(BF))
        m.stat[0:1, :] = new
        if j:
            factor = jnp.exp(old - new)
            total = total + m.stat[1:2, :] * factor
            value = value + m.att[...] * factor
        m.stat[1:2, :] = total
        m.att[...] = value
        if j == group - 1:
            m.stat[2:3, :] = new + jnp.log(total)
            value = value / total
            m.att[...] = value
            m.alt[...] = value.astype(BF)
            m.al[...] = value.T.astype(BF)

    def head_grads():
        grad = mm_nt(m.dy[...], m.wc[0])
        low = grad.astype(BF)
        m.hg[...] = low
        m.stat[3:4, :] = jnp.sum(low.astype(F32).T * m.att[...], 0, keepdims=True)

    def attend_back(j):
        probs = jnp.exp(masked_scores(j) - m.stat[2:3, :])
        value_part = mm(probs.astype(BF), m.hg[...])
        prob_grad = mm_nt(m.kv[key_rows(j), HD:], m.hg[...])
        score_grad = (probs * (prob_grad - m.stat[3:4, :]) * score_scale).astype(BF)
        query_part = mm(m.kv[key_rows(j), :HD].T, score_grad)
        key_part = mm(score_grad, m.q[...])
        head_sum = jnp.sum(turned(key_part, key_rows(j), -1.0), 0, keepdims=True)
        rest_sum = jnp.sum(key_part[:, 128:], 0, keepdims=True)
        if j:
            query_part = query_part + m.dqt[...]
            head_sum = head_sum + m.kb[0:1, :128]
            rest_sum = rest_sum + m.kb[0:1, 128:]
        m.dqt[...] = query_part
        m.kb[0:1, :128] = head_sum
        m.kb[0:1, 128:] = rest_sum
        m.kv[key_rows(j), :HD] = key_part.astype(BF)
        m.kv[key_rows(j), HD:] = value_part.astype(BF)

    def small_store(first, row):
        for n in range(row.shape[1] // 128):
            m.ps[0, first + n : first + n + 1, :] = row[:, n * 128 : (n + 1) * 128]

    def attention_grads():
        query = m.dqt[...].T
        head = turned(query, kv_own, -1.0)
        keys = m.kv[kv_own, :HD].astype(F32)
        key_head = turned(keys, kv_own, -1.0)
        m.low[:, :128] = head.astype(BF)
        m.low[:, 128:HD] = query[:, 128:].astype(BF)
        m.low[:, HD : HD + 128] = key_head.astype(BF)
        m.low[:, HD + 128 : 2 * HD] = m.kv[kv_own, 128:HD]
        m.low[:, 2 * HD :] = m.kv[kv_own, HD:]
        small_store(64, jnp.sum(head, 0, keepdims=True))
        small_store(65, jnp.sum(query[:, 128:], 0, keepdims=True))
        small_store(66, m.kb[0:1, :])
        small_store(68, jnp.sum(m.kv[kv_own, HD:].astype(F32), 0, keepdims=True))

        def body(n, _):
            tile = pl.ds(pl.multiple_of(n * ROW_TILE, ROW_TILE), ROW_TILE)
            turned_in = m.na[:, tile].T
            for a in range(3):
                m.gr[a, tile, :] = mm(turned_in, m.low[:, a * HD : (a + 1) * HD]).astype(BF)
            return 0

        lax.fori_loop(0, width // ROW_TILE, body, 0)

        def body_out(n, _):
            tile = pl.ds(pl.multiple_of(n * 512, 512), 512)
            m.gc[0, :, tile] = mm(m.alt[...], m.dy[:, tile]).astype(BF)
            return 0

        lax.fori_loop(0, width // 512, body_out, 0)

    def feed_forward(i):
        activated, slope = gelu_parts(mm(m.nm[...], m.wr[3 + i]) + m.biases[3 + i : 4 + i, :])
        m.hid[i] = activated.astype(BF)
        up_grad = mm_nt(m.dy[...], m.wc[1 + i]) * slope
        small_store(70 + 2 * i, jnp.sum(up_grad, 0, keepdims=True))
        m.ul[i] = up_grad.astype(BF)
        turned_hidden = activated.T.astype(BF)

        def body(n, _):
            tile = pl.ds(pl.multiple_of(n * 512, 512), 512)
            m.gr[3 + i, tile, :] = mm(m.nmt[tile, :], m.ul[i]).astype(BF)
            m.gc[1 + i, :, tile] = mm(turned_hidden, m.dy[:, tile]).astype(BF)
            return 0

        lax.fori_loop(0, width // 512, body, 0)

    out, back = m.na, m.dy

    def tile_of(n):
        return pl.ds(pl.multiple_of(n * ROW_TILE, ROW_TILE), ROW_TILE)

    def small_add_rows(first, n, value):
        row = jnp.sum(value, 0, keepdims=True)
        for h in range(ROW_TILE // 128):
            m.ps[0, pl.ds(first + n * (ROW_TILE // 128) + h, 1), :] = row[:, h * 128 : (h + 1) * 128]

    def end_out(n):
        tile = tile_of(n)
        total = mm(m.al[...], m.wc[0, :, tile])
        for i in range(ff_chunks):
            total += mm(m.hid[i], m.wc[1 + i, :, tile])
        out[:, tile] = total.astype(BF)

    def end_back(n):
        tile = tile_of(n)
        attn_back = mm_nt(m.low[:, :HD], m.wr[0, tile, :])
        for a in (1, 2):
            attn_back += mm_nt(m.low[:, a * HD : (a + 1) * HD], m.wr[a, tile, :])
        mlp_back = mm_nt(m.ul[0], m.wr[3, tile, :])
        for i in range(1, ff_chunks):
            mlp_back += mm_nt(m.ul[i], m.wr[3 + i, tile, :])
        normal = (m.x[:, tile].astype(F32) - m.mean[...]) * m.inv[...]
        small_add_rows(0, n, attn_back * normal)
        small_add_rows(16, n, attn_back)
        small_add_rows(32, n, mlp_back * normal)
        small_add_rows(48, n, mlp_back)
        small_add_rows(78, n, m.dy[:, tile].astype(F32))
        back[:, tile] = (attn_back * m.gv[0:1, tile] + mlp_back * m.gv[2:3, tile]).astype(BF)

    def end_half(piece, which):
        count = half // ROW_TILE

        def body(n, _):
            piece(which * count + n)
            return 0

        lax.fori_loop(0, count, body, 0)

    swap_in = (m.nm.at[:, 0:half], m.nm.at[:, half : 2 * half])

    def offer():
        pl.semaphore_signal(m.free, inc=1, device_id=at.twin(), device_id_type=MESH)

    def sum_start(i):
        if i == 0:
            pl.semaphore_wait(m.free, 1)
        return remote(ends[i].at[:, her_cols], swap_in[i], m.o_s.at[i, 0], m.o_r.at[i, 0], at.twin())

    ends = (out, back)

    def sum_step(i, step, copy):
        received([copy])
        mine = ends[i]
        if step == 0:

            def add(z, _):
                block = token_rows(z)
                total = mine[block, my_cols].astype(F32) + swap_in[i][block, :].astype(F32)
                mine[block, my_cols] = total.astype(BF)
                return 0

            lax.fori_loop(0, depth_size, add, 0)
            source, into, there = mine.at[her_pair, her_quarter], m.tz.at[i, 0], near
        elif step == 1:
            total = mine[her_pair, my_quarter].astype(F32) + m.tz[i, 0].astype(F32)
            mine[her_pair, my_quarter] = total.astype(BF)
            source, into, there = mine.at[her_pair, my_quarter], m.tz.at[i, 1], far
        elif step == 2:
            total = mine[my_pair, my_quarter].astype(F32) + m.tz[i, 1].astype(F32)
            mine[my_pair, my_quarter] = total.astype(BF)
            source, into, there = mine.at[token_rows(near_depth), my_cols], m.te.at[i], near
        else:
            total = mine[token_rows(at.depth), my_cols].astype(F32) + m.te[i].astype(F32)
            m.fin[i, :, my_cols] = total.astype(BF)
            source, into, there = m.fin.at[i, :, my_cols], m.fin.at[i, :, my_cols], at.twin()
        return remote(source, into, m.o_s.at[i, 1 + step], m.o_r.at[i, 1 + step], there)

    def stage_of(column):
        piece = column // tokens
        return (m.att, m.dqt)[piece // 2], piece % 2 * rows, column % tokens

    def finish_rows():
        step = 16

        def body(i, _):
            here = pl.ds(pl.multiple_of(i * step, step), step)
            x = m.x_in[here, :].astype(F32)
            dy = m.dy_in[here, :].astype(F32)
            here_all = pl.ds(pl.multiple_of(at.depth * rows + i * step, step), step)
            inverse = m.inv[here_all, :]
            normal = (x - m.mean[here_all, :]) * inverse
            total = jnp.zeros((step, 1), F32)
            against = jnp.zeros((step, 1), F32)
            pieces = {}
            for b in range(block_count):
                c = natural[b]
                out_of = slice(b * depth_rows, (b + 1) * depth_rows)
                into = slice(c * depth_rows, (c + 1) * depth_rows)
                m.layer_output[here, into] = (
                    x[:, into] + m.fin[0, here, out_of].astype(F32) + m.vectors[4:5, into]
                ).astype(BF)
                pieces[b] = m.fin[1, here, out_of].astype(F32)
                total += jnp.sum(pieces[b], -1, keepdims=True)
                against += jnp.sum(pieces[b] * normal[:, into], -1, keepdims=True)
            total = total / width
            against = against / width
            for b in range(block_count):
                c = natural[b]
                into = slice(c * depth_rows, (c + 1) * depth_rows)
                staged, first, cols = stage_of(c * depth_rows)
                there = pl.ds(pl.multiple_of(first + i * step, step), step)
                staged[there, cols : cols + depth_rows] = dy[:, into] + inverse * (
                    pieces[b] - total - normal[:, into] * against
                )
            return 0

        lax.fori_loop(0, rows // step, body, 0)
        copies = []
        for n in range(width // tokens):
            staged, first, _ = stage_of(n * tokens)
            copies.append(
                local(
                    staged.at[first : first + rows, :],
                    m.input_grad.at[:, n * tokens : (n + 1) * tokens],
                    m.i_l.at[n],
                )
            )
        for copy in copies:
            copy.wait()

    def small_group(stage):
        return remote(m.ps.at[stage], m.pl.at[stage], m.p_s.at[stage], m.p_r.at[stage], at.across(stage))

    def small_add(stage, copy):
        received([copy])
        m.ps[stage + 1] = m.ps[stage] + m.pl[stage]

    def small_depth():
        total = m.ps.at[bits]
        copies = [
            remote(total, m.pz.at[at.depth], m.p_s.at[bits + s], m.p_r.at[bits + s], at.along(s))
            for s in range(1, depth_size)
        ]
        m.pz[at.depth] = m.ps[bits]
        return copies

    def small_twin(copies):
        received(copies)
        value = m.pz[0]
        for z in range(1, depth_size):
            value = value + m.pz[z]
        m.px[0] = value
        return remote(m.px.at[0], m.px.at[1], m.p_s.at[bits], m.p_r.at[bits], at.twin())

    def small_finish(copy):
        received([copy])
        for v in range(4):
            for b in range(block_count):
                row = v * 16 + b
                into = v * 16 + natural[b]
                m.norm_sums[into : into + 1, :] = m.px[0, row : row + 1, :] + m.px[1, row : row + 1, :]
        for b in range(block_count):
            m.b_sum[natural[b] : natural[b] + 1, :] = m.ps[bits, 78 + b : 79 + b, :]
        for z in range(depth_size):
            m.b_query[2 * z : 2 * z + 2, :] = m.pz[z, 64:66, :]
            m.b_key[2 * z : 2 * z + 2, :] = m.pz[z, 66:68, :]
            m.b_value[2 * z : 2 * z + 2, :] = m.pz[z, 68:70, :]
            m.b_up[8 * z : 8 * z + 8, :] = m.pz[z, 70:78, :]

    live = {}
    swapped = {0: [], 1: []}
    buffers = (m.x, m.dy)

    def run(name, n):
        if name == "zs":
            live["z", n] = z_start(n)
        elif name == "zy":
            z_wait(live["z", n])
            live["g", n] = g_start(n, 0)
        elif name == "yc":
            received(live["g", n])
            live["g", n] = g_start(n, 1)
        elif name == "cw":
            received(live["g", n])
        elif name == "ta":
            live["t", n] = token_step(n, buffers[n], 0, [])
        elif name == "tb":
            token_step(n, buffers[n], 1, live["t", n])
        elif name == "tc":
            token_step(n, buffers[n], 2, live["t", n])
        elif name == "td":
            token_step(n, buffers[n], 3, live["t", n])
        elif name == "te":
            received(swapped[n])
        elif name == "norm":
            m.ps[0] = jnp.zeros_like(m.ps[0])
            place_rows()
        elif name == "tab":
            make_tables()
        elif name == "aff":
            affine()
        elif name == "qk":
            make_query_key()
        elif name == "val":
            make_values()
        elif name == "ky":
            live["k", 0] = kv_start(0)
        elif name == "kc":
            received([live["k", 0]])
            live["k", 1] = kv_start(1)
        elif name == "kw":
            received([live["k", 1]])
        elif name == "at":
            attend(n)
        elif name == "hg":
            head_grads()
        elif name == "bw":
            if n == 0:
                settle([live["k", 0], live["k", 1]])
            attend_back(n)
        elif name == "dc":
            live["d"] = dkv_start(1)
        elif name == "dy":
            dkv_finish(1, live["d"])
            live["d"] = dkv_start(0)
        elif name == "dw":
            dkv_finish(0, live["d"])
        elif name == "ag":
            attention_grads()
        elif name == "ff":
            feed_forward(n)
        elif name == "fc":
            live["f", n] = fold_start(n, 1)
        elif name == "fy":
            fold_finish(n, 1, live["f", n])
            live["f", n] = fold_start(n, 0)
        elif name == "fz":
            fold_finish(n, 0, live["f", n])
            live["e", n] = end_start(n)
        elif name == "of":
            offer()
        elif name == "eo":
            end_half(end_out, at.tp if n else 1 - at.tp)
        elif name == "eb":
            if n == 0:
                settle(live["t", 1] + swapped[1])
            end_half(end_back, at.tp if n else 1 - at.tp)
        elif name == "sx":
            live["s", n] = sum_start(n)
        elif name == "sa":
            live["s", n] = sum_step(n, 0, live["s", n])
        elif name == "sb":
            live["s", n] = sum_step(n, 1, live["s", n])
        elif name == "sc":
            live["s", n] = sum_step(n, 2, live["s", n])
        elif name == "sd":
            live["s", n] = sum_step(n, 3, live["s", n])
        elif name == "sw":
            received([live["s", n]])
        elif name == "pa":
            live["p"] = small_group(0)
        elif name == "pb":
            small_add(0, live["p"])
            live["p"] = small_group(1)
        elif name == "pc":
            small_add(1, live["p"])
            live["p"] = small_depth()
        elif name == "pd":
            live["p"] = small_twin(live["p"])
        elif name == "pe":
            small_finish(live["p"])
        elif name == "fin":
            finish_rows()
        elif name == "ew":
            received(live["e", n][:-2])
            for copy in live["e", n][-2:]:
                copy.wait()

    for entry in SCHEDULE:
        name = entry.rstrip("0123456789")
        run(name, int(entry[len(name) :] or 0))
    for copy in sends:
        if not any(copy is other for other in settled):
            copy.wait_send()


SCHEDULE = (
    "zs0", "norm", "ta0", "zy0", "zs1", "tb0", "zs2", "zs5", "zy1", "tc0", "ta1", "yc1",
    "cw1", "zy2", "td0", "tab", "yc0", "zy5", "tb1", "te0", "aff", "yc2", "cw0", "zs3",
    "qk", "val", "tc1", "yc5", "ky", "zs4", "zy3", "kc", "td1", "kw", "at0", "at1",
    "te1", "cw2", "zy4", "ff0", "at2", "fc2", "cw5", "at3", "hg", "bw0", "bw1", "bw2",
    "bw3", "dc", "ff3", "yc3", "dy", "yc4", "cw3", "fy2", "cw4", "ff2", "ff1", "fc3",
    "dw", "ag", "eo0", "of0", "sx0", "fc0", "fy3", "eb0", "fz2", "fc1", "fy0", "fz3",
    "fc4", "sx1", "eb1", "pa", "fc5", "pb", "fz0", "fy4", "ew3", "eo1", "pc", "sa0",
    "ew0", "fz4", "sb0", "sa1", "fy5", "ew4", "fy1", "sb1", "ew2", "fz5", "pd", "sc0",
    "sc1", "fz1", "sd0", "sd1", "ew5", "sw0", "pe", "sw1", "fin", "ew1",
)


def fits(depth_size, group, depth_rows, rows, width, ff_chunks):
    sizes = layout_of(depth_size, group, depth_rows, rows, width, ff_chunks)
    total = sum(math.prod(shape) * jnp.dtype(kind).itemsize for _, shape, kind in sizes)
    shaped = group == depth_size == ff_chunks == 4 and depth_rows == rows == 128
    return shaped and total < VMEM_BYTES


def fused_shards(
    layer_input,
    block_order,
    attn_gain,
    attn_shift,
    mlp_gain,
    mlp_shift,
    w_query,
    b_query,
    w_key,
    b_key,
    w_value,
    b_value,
    w_out,
    b_out,
    w_up,
    b_up,
    w_down,
    b_down,
    out_grad,
):
    rows, width = layer_input.shape
    tp_size = lax.axis_size("tp")
    depth_size = HEADS // tp_size
    group = lax.axis_size("ctx") // depth_size
    depth_rows = width // (depth_size * group)
    ff_width = w_up.shape[1] // depth_size
    ff_chunks = ff_width // CHUNK
    tokens = depth_size * rows
    at = Place(depth_size, group)

    places = token_places(block_order, depth_size, group, rows).reshape(-1, 128)
    freqs = 10000.0 ** (-(2.0 * jnp.arange(ROT // 2, dtype=F32)) / ROT)
    phases = jnp.repeat(jnp.array([0.0, math.pi / 2], F32), 64)
    vectors = jnp.stack(
        [attn_gain, attn_shift, mlp_gain, mlp_shift, b_out + b_down]
        + [jnp.tile(freqs, width // (ROT // 2)), jnp.tile(phases, width // 128), b_out]
    )
    per_head = [bias.reshape(depth_size, 1, HD) for bias in (b_query, b_key, b_value)]
    per_head += [b_up.reshape(depth_size, ff_chunks, CHUNK), jnp.zeros((depth_size, 1, CHUNK), F32)]
    biases = lax.dynamic_index_in_dim(jnp.concatenate(per_head, 1), at.depth, 0, keepdims=False)

    buffers = layout_of(depth_size, group, depth_rows, rows, width, ff_chunks)
    semaphores = semaphores_of(depth_size, group, 2 + ff_chunks)
    names = tuple(INPUTS) + tuple(OUTPUTS) + tuple(b[0] for b in buffers) + tuple(s[0] for s in semaphores) + ("free",)
    vmem = pl.BlockSpec(memory_space=pltpu.VMEM)
    hbm = pl.BlockSpec(memory_space=pl.ANY)
    shape = jax.ShapeDtypeStruct
    wide, thin = depth_size * HD, depth_size * ff_width
    results = pl.pallas_call(
        functools.partial(fused_kernel, names, depth_size, group),
        out_shape=(
            shape((rows, width), BF),
            shape((rows, width), F32),
            shape((depth_rows, wide), BF),
            shape((depth_rows, wide), BF),
            shape((depth_rows, wide), BF),
            shape((wide, depth_rows), BF),
            shape((depth_rows, thin), BF),
            shape((thin, depth_rows), BF),
            shape((4 * width // 128, 128), F32),
            shape((wide // 128, 128), F32),
            shape((wide // 128, 128), F32),
            shape((wide // 128, 128), F32),
            shape((thin // 128, 128), F32),
            shape((width // 128, 128), F32),
        ),
        in_specs=[vmem] * 5 + [hbm] * 6,
        out_specs=(vmem,) + (hbm,) * 7 + (vmem,) * 6,
        scratch_shapes=[pltpu.VMEM(s, t) for _, s, t in buffers]
        + [pltpu.SemaphoreType.DMA(s) for _, s in semaphores]
        + [pltpu.SemaphoreType.REGULAR],
        compiler_params=pltpu.CompilerParams(
            collective_id=4, has_side_effects=True, vmem_limit_bytes=VMEM_BYTES
        ),
    )(
        layer_input,
        out_grad,
        vectors,
        biases,
        places,
        w_query,
        w_key,
        w_value,
        w_out,
        w_up,
        w_down,
    )
    output, input_grad = results[:2]
    weight_grads = [grad.astype(F32) for grad in results[2:8]]
    norm_sums = results[8].reshape(4, width)
    small = [result.reshape(-1) for result in results[9:]]
    return (
        output,
        input_grad,
        *weight_grads,
        small[0],
        small[1],
        small[2],
        small[4],
        small[3],
        small[4],
        norm_sums[0],
        norm_sums[1],
        norm_sums[2],
        norm_sums[3],
    )


def shards(
    layer_input,
    block_order,
    attn_gain,
    attn_shift,
    mlp_gain,
    mlp_shift,
    w_query,
    b_query,
    w_key,
    b_key,
    w_value,
    b_value,
    w_out,
    b_out,
    w_up,
    b_up,
    w_down,
    b_down,
    out_grad,
):
    rows, width = layer_input.shape
    depth_size = HEADS // lax.axis_size("tp")
    group = lax.axis_size("ctx") // depth_size
    ff_chunks = w_up.shape[1] // depth_size // CHUNK
    whole = fits(depth_size, group, width // (depth_size * group), rows, width, ff_chunks)
    chosen = fused_shards if whole else staged_shards
    return chosen(
        layer_input, block_order, attn_gain, attn_shift, mlp_gain, mlp_shift, w_query, b_query, w_key, b_key, w_value, b_value, w_out, b_out, w_up, b_up, w_down, b_down, out_grad
    )


def staged_shards(
    layer_input,
    block_order,
    attn_gain,
    attn_shift,
    mlp_gain,
    mlp_shift,
    w_query,
    b_query,
    w_key,
    b_key,
    w_value,
    b_value,
    w_out,
    b_out,
    w_up,
    b_up,
    w_down,
    b_down,
    out_grad,
):
    rows, width = layer_input.shape
    ctx_size = lax.axis_size("ctx")
    tp_size = lax.axis_size("tp")
    depth_size = HEADS // tp_size
    group = ctx_size // depth_size
    bits = group.bit_length() - 1
    depth_rows = width // ctx_size
    hidden_width = w_up.shape[1] // depth_size
    ff_chunks = hidden_width // CHUNK
    at = Place(depth_size, group)
    block_rows = rows // 2

    def permuted(array):
        lead = array.shape[:-1]
        n = len(lead)
        split = array.reshape(lead + (depth_size,) + (2,) * bits + (depth_rows,))
        order = tuple(range(n)) + tuple(n + 1 + b for b in reversed(range(bits))) + (n, n + 1 + bits)
        return split.transpose(order).reshape(lead + (width,))

    def restored(array):
        lead = array.shape[:-1]
        n = len(lead)
        split = array.reshape(lead + (2,) * bits + (depth_size, depth_rows))
        order = tuple(range(n)) + (n + bits,) + tuple(n + b for b in reversed(range(bits))) + (n + bits + 1,)
        return split.transpose(order).reshape(lead + (width,))

    def slot_members():
        table = []
        for slot in range(group):
            member = 0
            for stage in range(bits):
                member += ((slot >> stage) & 1) << (bits - 1 - stage)
            table.append(member)
        return table

    blocks = block_order.reshape(depth_size, group, 2)
    order = jnp.stack([blocks[:, m] for m in slot_members()], 0)
    place = order[..., None] * block_rows + jnp.arange(block_rows, dtype=jnp.int32)
    key_place = place.reshape(group * depth_size * rows)
    token_total = depth_size * rows
    query_place = lax.dynamic_slice_in_dim(key_place, at.slot * token_total, token_total)
    cosine, sine_table = rope_tables(query_place)

    inputs32 = layer_input.astype(F32)
    centered = inputs32 - jnp.mean(inputs32, -1, keepdims=True)
    inverse = lax.rsqrt(jnp.mean(centered * centered, -1, keepdims=True) + norm_epsilon)
    normal32 = centered * inverse

    def halves(array):
        return permuted(array).reshape(rows, tp_size, width // tp_size).transpose(1, 0, 2)

    def by_head(weight):
        return weight.reshape(depth_rows, depth_size, HD).transpose(1, 0, 2)

    def by_chunk(weight):
        return weight.reshape(depth_rows, depth_size, ff_chunks, CHUNK).transpose(2, 1, 0, 3)

    weights = jnp.concatenate(
        [
            jnp.concatenate([by_head(w_query), by_head(w_key)], -1)[None],
            jnp.concatenate([by_head(w_value), by_head(w_out.T)], -1)[None],
            jnp.concatenate([by_chunk(w_up), by_chunk(w_down.T)], -1),
        ],
        0,
    )
    normal, grad, gathered = gather_all(
        depth_size, group, halves(normal32.astype(BF)), halves(out_grad), weights
    )
    full = gathered.reshape(2 + ff_chunks, width, 2 * HD)
    gain_a, shift_a, gain_m, shift_m = permuted(jnp.stack([attn_gain, attn_shift, mlp_gain, mlp_shift]))
    normal_tokens = normal.astype(F32)
    attn_in = (normal_tokens * gain_a + shift_a).astype(BF)
    mlp_in = (normal_tokens * gain_m + shift_m).astype(BF)

    def own_part(vector, size):
        return lax.dynamic_slice_in_dim(vector, at.depth * size, size)

    query_key = mm(attn_in, full[0])
    query = rotate(query_key[:, :HD] + own_part(b_query, HD), cosine, sine_table).astype(BF)
    keys = rotate(query_key[:, HD:] + own_part(b_key, HD), cosine, sine_table).astype(BF)
    values = (mm(attn_in, full[1, :, :HD]) + own_part(b_value, HD)).astype(BF)
    out_t = full[1, :, HD:]
    shared = share_group(depth_size, group, jnp.concatenate([keys, values], -1))
    shared = shared.reshape(group * token_total, 2 * HD)
    all_keys, all_values = shared[:, :HD], shared[:, HD:]
    score_scale = 1.0 / math.sqrt(HD)
    scores = mm_nt(query, all_keys) * score_scale
    allowed = key_place[None, :] <= query_place[:, None]
    scores = jnp.where(allowed, scores, -1e30)
    top = jnp.max(scores, -1, keepdims=True)
    raw = jnp.exp(scores - top)
    probs = raw / jnp.sum(raw, -1, keepdims=True)
    probs_low = probs.astype(BF)
    attended = mm(probs_low, all_values)
    attn_low = attended.astype(BF)

    head_grad = mm(grad, out_t).astype(BF)
    delta = jnp.sum(head_grad.astype(F32) * attended, -1, keepdims=True)
    value_part = mm_tn(probs_low, head_grad)
    score_grad = (probs * (mm_nt(head_grad, all_values) - delta) * score_scale).astype(BF)
    query_acc = mm(score_grad, all_keys)
    key_part = mm_tn(score_grad, query)
    parts = jnp.concatenate([key_part, value_part], -1).astype(BF)
    folded = fold_group(depth_size, group, parts.reshape(group, token_total, 2 * HD))
    own_grads = lax.dynamic_index_in_dim(folded, at.slot, 0, keepdims=False).astype(F32)
    query_lin = rotate(query_acc, cosine, -sine_table)
    key_lin = rotate(own_grads[:, :HD], cosine, -sine_table)
    value_lin = own_grads[:, HD:]
    query_low, key_low, value_low = query_lin.astype(BF), key_lin.astype(BF), value_lin.astype(BF)
    query_key_low = jnp.concatenate([query_low, key_low], -1)
    attn_back = mm_nt(query_key_low, full[0]) + mm_nt(value_low, full[1, :, :HD])
    grad_chunks = [
        mm_tn(attn_in, query_key_low).astype(BF),
        jnp.concatenate([mm_tn(attn_in, value_low), mm_tn(grad, attn_low)], -1).astype(BF),
    ]

    branches = mm_nt(attn_low, out_t)
    mlp_back = jnp.zeros((token_total, width), F32)
    bias_up = own_part(b_up, hidden_width).reshape(ff_chunks, CHUNK)
    up_sums = []
    for i in range(ff_chunks):
        up, down_t = full[2 + i, :, :CHUNK], full[2 + i, :, CHUNK:]
        activated, slope = gelu_parts(mm(mlp_in, up) + bias_up[i])
        hidden = activated.astype(BF)
        up_grad = mm(grad, down_t) * slope
        up_sums.append(jnp.sum(up_grad, 0))
        up_low = up_grad.astype(BF)
        branches = branches + mm_nt(hidden, down_t)
        mlp_back = mlp_back + mm_nt(up_low, up)
        grad_chunks.append(jnp.concatenate([mm_tn(mlp_in, up_low), mm_tn(grad, hidden)], -1).astype(BF))

    normal_tokens2 = normal.astype(F32)
    back = attn_back * gain_a + mlp_back * gain_m
    grads = jnp.stack(grad_chunks).reshape(2 + ff_chunks, group, depth_size, depth_rows, 2 * HD)
    norm_sums = restored(
        jnp.stack(
            [
                jnp.sum(attn_back * normal_tokens2, 0),
                jnp.sum(attn_back, 0),
                jnp.sum(mlp_back * normal_tokens2, 0),
                jnp.sum(mlp_back, 0),
            ]
        )
    )
    own_biases = jnp.concatenate(
        [jnp.sum(query_lin, 0), jnp.sum(key_lin, 0), jnp.sum(value_lin, 0)] + up_sums
    )
    spread = jnp.where(
        jnp.arange(depth_size, dtype=jnp.int32)[:, None] == at.depth, own_biases[None, :], 0.0
    )
    norm_sums = lax.psum(norm_sums, ("ctx", "tp"))
    grad32 = out_grad.astype(F32)
    spread, bias_grad = lax.psum((spread, jnp.sum(grad32, 0)), "ctx")

    out_sum, back_sum, grad_shares = reduce_all(
        depth_size, group, branches.astype(BF), back.astype(BF), grads
    )
    layer_output = (inputs32 + restored(out_sum).astype(F32) + b_out + b_down).astype(BF)
    back_total = restored(back_sum).astype(F32)
    input_grad = grad32 + inverse * (
        back_total
        - jnp.mean(back_total, -1, keepdims=True)
        - normal32 * jnp.mean(back_total * normal32, -1, keepdims=True)
    )

    def from_head(share):
        return share.transpose(1, 0, 2).reshape(depth_rows, depth_size * HD).astype(F32)

    def from_chunk(share):
        return share.transpose(2, 1, 0, 3).reshape(depth_rows, depth_size * hidden_width).astype(F32)

    return (
        layer_output,
        input_grad,
        from_head(grad_shares[0, :, :, :HD]),
        from_head(grad_shares[0, :, :, HD:]),
        from_head(grad_shares[1, :, :, :HD]),
        from_head(grad_shares[1, :, :, HD:]).T,
        from_chunk(grad_shares[2:, :, :, :CHUNK]),
        from_chunk(grad_shares[2:, :, :, CHUNK:]).T,
        spread[:, :HD].reshape(-1),
        spread[:, HD : 2 * HD].reshape(-1),
        spread[:, 2 * HD : 3 * HD].reshape(-1),
        bias_grad,
        spread[:, 3 * HD :].reshape(-1),
        bias_grad,
        norm_sums[0],
        norm_sums[1],
        norm_sums[2],
        norm_sums[3],
    )


def solution(mesh):
    in_specs = (
        P("ctx", None),
        P(),
        P(),
        P(),
        P(),
        P(),
        P("ctx", "tp"),
        P("tp"),
        P("ctx", "tp"),
        P("tp"),
        P("ctx", "tp"),
        P("tp"),
        P("tp", "ctx"),
        P(),
        P("ctx", "tp"),
        P("tp"),
        P("tp", "ctx"),
        P(),
        P("ctx", None),
    )
    out_specs = (
        P("ctx", None),
        P("ctx", None),
        P("ctx", "tp"),
        P("ctx", "tp"),
        P("ctx", "tp"),
        P("tp", "ctx"),
        P("ctx", "tp"),
        P("tp", "ctx"),
        P("tp"),
        P("tp"),
        P("tp"),
        P(),
        P("tp"),
        P(),
        P(),
        P(),
        P(),
        P(),
    )
    return jax.shard_map(shards, mesh=mesh, in_specs=in_specs, out_specs=out_specs, check_vma=False)
```

```python
import functools
import math

import jax
import jax.numpy as jnp
import numpy as np
from jax import lax
from jax.experimental import pallas as pl
from jax.experimental.pallas import tpu as pltpu
from jax.sharding import PartitionSpec as P

HEADS = 8
HD = 256
ROT = 64
CHUNK = 256

norm_epsilon = 1e-05
BF = jnp.bfloat16
F32 = jnp.float32
MESH = pl.DeviceIdType.MESH


def mm(a, b):
    return jnp.dot(a, b, preferred_element_type=F32)


def mm_tn(a, b):
    return lax.dot_general(a, b, (((0,), (0,)), ((), ())), preferred_element_type=F32)


def mm_nt(a, b):
    return lax.dot_general(a, b, (((1,), (1,)), ((), ())), preferred_element_type=F32)


class Place:
    def __init__(self, depth_size, group):
        self.depth_size = depth_size
        self.group = group
        self.bits = group.bit_length() - 1
        self.ctx = lax.axis_index("ctx")
        self.tp = lax.axis_index("tp")
        self.depth = self.ctx // group
        self.member = self.ctx % group
        slot = 0
        for stage in range(self.bits):
            slot = slot + self.bit(stage) * 2**stage
        self.slot = slot

    def bit(self, stage):
        return (self.member // 2 ** (self.bits - 1 - stage)) % 2

    def along(self, step):
        return {"ctx": lax.rem(self.depth + step, self.depth_size) * self.group + self.member}

    def across(self, stage):
        reach = 2 ** (self.bits - 1 - stage)
        return {"ctx": self.ctx + (1 - 2 * self.bit(stage)) * reach}

    def twin(self):
        return {"tp": 1 - self.tp}

    def base(self, stage):
        return (self.slot // 2**stage) * 2**stage

    def greet(self, devices):
        barrier = pltpu.get_barrier_semaphore()
        for device in devices:
            pl.semaphore_signal(barrier, inc=1, device_id=device, device_id_type=MESH)
        pl.semaphore_wait(barrier, len(devices))

    def everyone(self):
        return (
            [self.along(step) for step in range(1, self.depth_size)]
            + [self.across(stage) for stage in range(self.bits)]
            + [self.twin()]
        )


def remote(src, dst, send, recv, device):
    copy = pltpu.make_async_remote_copy(
        src_ref=src, dst_ref=dst, send_sem=send, recv_sem=recv, device_id=device, device_id_type=MESH
    )
    copy.start()
    return copy


def local(src, dst, sem):
    copy = pltpu.make_async_copy(src, dst, sem)
    copy.start()
    return copy


def gather_kernel(depth_size, group, x_in, dy_in, w_in, x_out, dy_out, w_out, tz_s, tz_r, tx_s, tx_r, t_l, z_s, z_r, z_l, g_s, g_r):
    at = Place(depth_size, group)
    at.greet(at.everyone())
    rows, half = x_in.shape[1:]
    sent = []
    mine = pl.ds(pl.multiple_of(at.depth * rows, rows), rows)
    my_cols = pl.ds(pl.multiple_of(at.tp * half, half), half)

    def token_start(i, src, dst):
        copies = [
            remote(src.at[at.tp], dst.at[mine, my_cols], tz_s.at[i, s], tz_r.at[i, s], at.along(s))
            for s in range(1, depth_size)
        ]
        copies.append(local(src.at[at.tp], dst.at[mine, my_cols], t_l.at[i]))
        return copies

    def token_swap(i, copies, dst):
        for copy in copies[:-1]:
            copy.wait_recv()
            sent.append(copy)
        copies[-1].wait()
        return remote(dst.at[:, my_cols], dst.at[:, my_cols], tx_s.at[i], tx_r.at[i], at.twin())

    chunks = w_in.shape[0]

    def z_start(k):
        copies = [
            remote(
                w_in.at[k, lax.rem(at.depth + s, depth_size)],
                w_out.at[k, at.slot, at.depth],
                z_s.at[k, s],
                z_r.at[k, s],
                at.along(s),
            )
            for s in range(1, depth_size)
        ]
        copies.append(local(w_in.at[k, at.depth], w_out.at[k, at.slot, at.depth], z_l.at[k]))
        return copies

    def z_wait(copies):
        for copy in copies[:-1]:
            copy.wait_recv()
            sent.append(copy)
        copies[-1].wait()

    def g_start(k, stage):
        held = pl.ds(at.base(stage), 2**stage)
        return remote(
            w_out.at[k, held], w_out.at[k, held], g_s.at[k, stage], g_r.at[k, stage], at.across(stage)
        )

    ahead = 2
    tokens = [token_start(0, x_in, x_out)]
    z_copies = {k: z_start(k) for k in range(min(ahead, chunks))}
    stages = {}
    swaps = []
    for step in range(chunks + at.bits):
        if step < chunks:
            z_wait(z_copies[step])
            stages[step] = [g_start(step, 0)]
            if step + ahead < chunks:
                z_copies[step + ahead] = z_start(step + ahead)
            if step == 0:
                swaps.append(token_swap(0, tokens[0], x_out))
                tokens.append(token_start(1, dy_in, dy_out))
            if step == 1:
                swaps.append(token_swap(1, tokens[1], dy_out))
        for stage in range(1, at.bits + 1):
            k = step - stage
            if 0 <= k < chunks:
                stages[k][stage - 1].wait_recv()
                if stage < at.bits:
                    stages[k].append(g_start(k, stage))
    for swap in swaps:
        swap.wait()
    for k in range(chunks):
        for copy in stages[k]:
            copy.wait_send()
    for copy in sent:
        copy.wait_send()


def gather_all(depth_size, group, x_halves, dy_halves, weights):
    tp, rows, half = x_halves.shape
    chunks, _, depth_rows, width = weights.shape
    bits = group.bit_length() - 1
    dma = pltpu.SemaphoreType.DMA
    hbm = pl.BlockSpec(memory_space=pl.ANY)
    tokens = jax.ShapeDtypeStruct((depth_size * rows, tp * half), BF)
    return pl.pallas_call(
        functools.partial(gather_kernel, depth_size, group),
        out_shape=(
            tokens,
            tokens,
            jax.ShapeDtypeStruct((chunks, group, depth_size, depth_rows, width), BF),
        ),
        in_specs=[hbm] * 3,
        out_specs=(hbm, hbm, hbm),
        scratch_shapes=[
            dma((2, depth_size)),
            dma((2, depth_size)),
            dma((2,)),
            dma((2,)),
            dma((2,)),
            dma((chunks, depth_size)),
            dma((chunks, depth_size)),
            dma((chunks,)),
            dma((chunks, bits)),
            dma((chunks, bits)),
        ],
        compiler_params=pltpu.CompilerParams(collective_id=0, has_side_effects=True),
    )(x_halves, dy_halves, weights)


def share_kernel(depth_size, group, kv_in, kv_out, send, recv, loc):
    at = Place(depth_size, group)
    at.greet([at.across(stage) for stage in range(at.bits)])
    local(kv_in, kv_out.at[at.slot], loc).wait()
    copies = []
    for stage in range(at.bits):
        held = pl.ds(at.base(stage), 2**stage)
        copy = remote(kv_out.at[held], kv_out.at[held], send.at[stage], recv.at[stage], at.across(stage))
        copy.wait_recv()
        copies.append(copy)
    for copy in copies:
        copy.wait_send()


def share_group(depth_size, group, kv):
    bits = group.bit_length() - 1
    dma = pltpu.SemaphoreType.DMA
    hbm = pl.BlockSpec(memory_space=pl.ANY)
    return pl.pallas_call(
        functools.partial(share_kernel, depth_size, group),
        out_shape=jax.ShapeDtypeStruct((group,) + kv.shape, BF),
        in_specs=[hbm],
        out_specs=hbm,
        scratch_shapes=[dma((bits,)), dma((bits,)), dma],
        compiler_params=pltpu.CompilerParams(collective_id=1, has_side_effects=True),
    )(kv)


def fold_kernel(depth_size, group, g_in, total, landing, send, recv):
    at = Place(depth_size, group)
    at.greet([at.across(stage) for stage in range(at.bits)])
    for stage in reversed(range(at.bits)):
        size = 2**stage
        own = at.base(stage)
        other = own + (1 - 2 * at.bit(stage)) * size
        source = g_in if stage == at.bits - 1 else total
        copy = remote(
            source.at[pl.ds(other, size)],
            landing.at[pl.ds(size - 1, size)],
            send.at[stage],
            recv.at[stage],
            at.across(stage),
        )
        copy.wait()

        def add(i, _):
            total[own + i] = (
                source[own + i].astype(F32) + landing[size - 1 + i].astype(F32)
            ).astype(BF)
            return 0

        lax.fori_loop(0, size, add, 0)


def fold_group(depth_size, group, grads):
    bits = group.bit_length() - 1
    dma = pltpu.SemaphoreType.DMA
    vmem = pl.BlockSpec(memory_space=pltpu.VMEM)
    return pl.pallas_call(
        functools.partial(fold_kernel, depth_size, group),
        out_shape=jax.ShapeDtypeStruct(grads.shape, BF),
        in_specs=[vmem],
        out_specs=vmem,
        scratch_shapes=[
            pltpu.VMEM((group - 1,) + grads.shape[1:], BF),
            dma((bits,)),
            dma((bits,)),
        ],
        compiler_params=pltpu.CompilerParams(
            collective_id=2, has_side_effects=True, vmem_limit_bytes=60 << 20
        ),
    )(grads)


def reduce_kernel(depth_size, group, out_in, back_in, g_in, out_sum, back_sum, g_out, total, landing, g_s, g_r, z_s, z_r, z_l, t_acc, t_swap, t_land, tx_s, tx_r, tz_s, tz_r, ty_s, ty_r):
    at = Place(depth_size, group)
    at.greet(at.everyone())
    chunks = g_in.shape[0]
    depth_rows = g_in.shape[3]
    rows = out_sum.shape[0]
    half = t_acc.shape[2]
    last = at.bits - 1
    sent = []

    def g_start(k, stage):
        size = 2**stage
        other = at.base(stage) + (1 - 2 * at.bit(stage)) * size
        source = g_in.at[k] if stage == last else total.at[k]
        return remote(
            source.at[pl.ds(other, size)],
            landing.at[k, pl.ds(size - 1, size)],
            g_s.at[k, stage],
            g_r.at[k, stage],
            at.across(stage),
        )

    def g_finish(k, stage, copy):
        copy.wait_recv()
        sent.append(copy)
        size = 2**stage
        own = at.base(stage)
        source = g_in.at[k] if stage == last else total.at[k]

        def add(i, _):
            j = i // depth_size
            z = i % depth_size
            total[k, own + j, z] = (
                source[own + j, z].astype(F32) + landing[k, size - 1 + j, z].astype(F32)
            ).astype(BF)
            return 0

        lax.fori_loop(0, size * depth_size, add, 0)

    def z_start(k):
        copies = [
            remote(
                total.at[k, at.slot, lax.rem(at.depth + s, depth_size)],
                g_out.at[k, at.depth],
                z_s.at[k, s],
                z_r.at[k, s],
                at.along(s),
            )
            for s in range(1, depth_size)
        ]
        copies.append(local(total.at[k, at.slot, at.depth], g_out.at[k, at.depth], z_l.at[k]))
        return copies

    my_cols = pl.ds(pl.multiple_of(at.tp * half, half), half)
    her_cols = pl.ds(pl.multiple_of((1 - at.tp) * half, half), half)

    def token_first(i, src):
        return remote(src.at[:, her_cols], t_swap.at[i], tx_s.at[i], tx_r.at[i], at.twin())

    def token_second(i, src, copy):
        copy.wait_recv()
        sent.append(copy)

        def add(z, _):
            block = pl.ds(pl.multiple_of(z * rows, rows), rows)
            t_acc[i, block, :] = (
                src[block, my_cols].astype(F32) + t_swap[i, block, :].astype(F32)
            ).astype(BF)
            return 0

        lax.fori_loop(0, depth_size, add, 0)
        copies = []
        for s in range(1, depth_size):
            there = lax.rem(at.depth + s, depth_size)
            block = pl.ds(pl.multiple_of(there * rows, rows), rows)
            copies.append(
                remote(
                    t_acc.at[i, block, :], t_land.at[i, s - 1], tz_s.at[i, s], tz_r.at[i, s], at.along(s)
                )
            )
        return copies

    def token_third(i, dst, copies):
        for copy in copies:
            copy.wait_recv()
            sent.append(copy)
        mine = pl.ds(pl.multiple_of(at.depth * rows, rows), rows)
        value = t_acc[i, mine, :].astype(F32)
        for s in range(1, depth_size):
            value = value + t_land[i, s - 1].astype(F32)
        dst[:, my_cols] = value.astype(BF)
        return remote(dst.at[:, my_cols], dst.at[:, my_cols], ty_s.at[i], ty_r.at[i], at.twin())

    firsts = [token_first(0, out_in), token_first(1, back_in)]
    copies_of = {k: [g_start(k, last)] for k in range(chunks)}
    z_copies = {}
    seconds = []
    thirds = []
    for step in range(chunks + at.bits):
        for back in range(at.bits):
            k = step - back
            stage = last - back
            if 0 <= k < chunks:
                g_finish(k, stage, copies_of[k][back])
                if stage > 0:
                    copies_of[k].append(g_start(k, stage - 1))
                else:
                    z_copies[k] = z_start(k)
        if step == 1:
            seconds.append(token_second(0, out_in, firsts[0]))
        if step == 2:
            seconds.append(token_second(1, back_in, firsts[1]))
        if step == 4:
            thirds.append(token_third(0, out_sum, seconds[0]))
        if step == 5:
            thirds.append(token_third(1, back_sum, seconds[1]))
    for k in range(chunks):
        for copy in z_copies[k][:-1]:
            copy.wait()
        z_copies[k][-1].wait()
    for copy in thirds:
        copy.wait()
    for copy in sent:
        copy.wait_send()


def reduce_all(depth_size, group, out_part, back_part, grads):
    chunks, _, _, depth_rows, width = grads.shape
    all_rows, columns = out_part.shape
    rows = all_rows // depth_size
    half = columns // 2
    bits = group.bit_length() - 1
    dma = pltpu.SemaphoreType.DMA
    vmem = pl.BlockSpec(memory_space=pltpu.VMEM)
    tokens = jax.ShapeDtypeStruct((rows, columns), BF)
    return pl.pallas_call(
        functools.partial(reduce_kernel, depth_size, group),
        out_shape=(tokens, tokens, jax.ShapeDtypeStruct((chunks, depth_size, depth_rows, width), BF)),
        in_specs=[vmem] * 3,
        out_specs=(vmem, vmem, vmem),
        scratch_shapes=[
            pltpu.VMEM((chunks, group, depth_size, depth_rows, width), BF),
            pltpu.VMEM((chunks, group - 1, depth_size, depth_rows, width), BF),
            dma((chunks, bits)),
            dma((chunks, bits)),
            dma((chunks, depth_size)),
            dma((chunks, depth_size)),
            dma((chunks,)),
            pltpu.VMEM((2, all_rows, half), BF),
            pltpu.VMEM((2, all_rows, half), BF),
            pltpu.VMEM((2, depth_size - 1, rows, half), BF),
            dma((2,)),
            dma((2,)),
            dma((2, depth_size)),
            dma((2, depth_size)),
            dma((2,)),
            dma((2,)),
        ],
        compiler_params=pltpu.CompilerParams(
            collective_id=3, has_side_effects=True, vmem_limit_bytes=60 << 20
        ),
    )(out_part, back_part, grads)


def rotate(values, cosine, sine_table):
    half_rot = ROT // 2
    leading = values[..., :half_rot]
    trailing = values[..., half_rot:ROT]
    return jnp.concatenate(
        [
            leading * cosine - trailing * sine_table,
            trailing * cosine + leading * sine_table,
            values[..., ROT:],
        ],
        -1,
    )


def rope_tables(positions):
    freqs = 10000.0 ** (-(2.0 * jnp.arange(ROT // 2, dtype=F32)) / ROT)
    angles = positions.astype(F32)[:, None] * freqs[None, :]
    return (jnp.cos(angles), jnp.sin(angles))


def gelu_parts(values):
    gate = 0.5 * (1.0 + lax.erf(values * math.sqrt(0.5)))
    slope = gate + values * jnp.exp(-0.5 * values * values) * (1.0 / math.sqrt(2.0 * math.pi))
    return values * gate, slope


SMALL_ROWS = 96
VMEM_BYTES = 64 << 20


def slot_member(slot, bits):
    member = 0
    for stage in range(bits):
        member += ((slot >> stage) & 1) << (bits - 1 - stage)
    return member


def natural_blocks(depth_size, group):
    bits = group.bit_length() - 1
    return [
        depth * group + slot_member(slot, bits) for slot in range(group) for depth in range(depth_size)
    ]

ROW_TILE = 256
DROP = -1e30


def layout_of(depth_size, group, depth_rows, rows, width, ff_chunks):
    tokens = depth_size * rows
    half = width // 2
    landing = (group - 1) * depth_size * depth_rows
    heads = 3 + ff_chunks
    cols = 1 + ff_chunks
    return [
        ("wr", (heads, width, CHUNK), BF),
        ("wc", (cols, CHUNK, width), BF),
        ("gr", (heads, width, CHUNK), BF),
        ("gc", (cols, CHUNK, width), BF),
        ("lr", (heads, landing, CHUNK), BF),
        ("lc", (cols, CHUNK, landing), BF),
        ("x", (tokens, width), BF),
        ("dy", (tokens, width), BF),
        ("na", (tokens, width), BF),
        ("nm", (tokens, width), BF),
        ("nmt", (width, tokens), BF),
        ("kv", (group * tokens, 2 * HD), BF),
        ("q", (tokens, HD), BF),
        ("low", (tokens, 3 * HD), BF),
        ("al", (tokens, HD), BF),
        ("hg", (tokens, HD), BF),
        ("alt", (HD, tokens), BF),
        ("att", (HD, tokens), F32),
        ("dqt", (HD, tokens), F32),
        ("stat", (8, tokens), F32),
        ("tab", (group * tokens, 128), F32),
        ("kb", (8, HD), F32),
        ("hid", (ff_chunks, tokens, CHUNK), BF),
        ("ul", (ff_chunks, tokens, CHUNK), BF),
        ("tz", (2, 2, tokens // 2, half // 2), BF),
        ("te", (2, rows, half), BF),
        ("mean", (tokens, 1), F32),
        ("inv", (tokens, 1), F32),
        ("gv", (8, width), F32),
        ("biases", (8, HD), F32),
        ("places", (group * tokens // 128, 128), F32),
        ("ps", (group.bit_length(), SMALL_ROWS, 128), F32),
        ("pl", (group.bit_length() - 1, SMALL_ROWS, 128), F32),
        ("pz", (depth_size, SMALL_ROWS, 128), F32),
        ("px", (2, SMALL_ROWS, 128), F32),
    ]


def semaphores_of(depth_size, group, items):
    bits = group.bit_length() - 1
    return [
        ("z_s", (items, depth_size)),
        ("z_r", (items, depth_size)),
        ("z_l", (items,)),
        ("g_s", (items, bits)),
        ("g_r", (items, bits)),
        ("t_s", (2, 3)),
        ("t_r", (2, 3)),
        ("w_s", (2, 3)),
        ("w_r", (2, 3)),
        ("kv_s", (2, 2, bits)),
        ("kv_r", (2, 2, bits)),
        ("f_s", (items, bits)),
        ("f_r", (items, bits)),
        ("e_s", (items, depth_size)),
        ("e_r", (items, depth_size)),
        ("e_l", (items,)),
        ("o_s", (2, 6)),
        ("o_r", (2, 6)),
        ("p_s", (bits + depth_size,)),
        ("p_r", (bits + depth_size,)),
    ]


VECTORS = ("attn_gain", "attn_shift", "mlp_gain", "mlp_shift")
BIASES = ("b_query", "b_key", "b_value", "b_up")
INPUTS = ("blocks", "x_in", "dy_in", "freqs") + VECTORS + BIASES
INPUTS += ("w_query", "w_key", "w_value", "w_out", "w_up", "w_down")
OUTPUTS = ("fin", "g_query", "g_key", "g_value", "g_out", "g_up", "g_down")
OUTPUTS += ("norm_sums", "s_query", "s_key", "s_value", "s_up", "s_dy")


class Bag:
    pass


def fused_kernel(names, depth_size, group, *refs):
    m = Bag()
    for name, ref in zip(names, refs, strict=True):
        setattr(m, name, ref)
    at = Place(depth_size, group)
    at.greet(at.everyone())
    bits = at.bits
    rows, width = m.x_in.shape
    depth_rows = width // (depth_size * group)
    tokens = depth_size * rows
    half = width // 2
    ff_width = m.w_up.shape[1] // depth_size
    ff_chunks = ff_width // CHUNK
    block_count = width // depth_rows
    own_block = at.slot * depth_size + at.depth
    natural = natural_blocks(depth_size, group)
    sends, settled = [], []

    def blocks(first, count):
        return pl.ds(pl.multiple_of(first * depth_rows, depth_rows), count * depth_rows)

    def token_rows(depth):
        return pl.ds(pl.multiple_of(depth * rows, rows), rows)

    def peer(step):
        return lax.rem(at.depth + step, depth_size)

    my_cols = pl.ds(pl.multiple_of(at.tp * half, half), half)
    her_cols = pl.ds(pl.multiple_of((1 - at.tp) * half, half), half)

    units = [("r", 0), ("r", 1), ("r", 2), ("c", 0)]
    for i in range(ff_chunks):
        units += [("r", 3 + i), ("c", 1 + i)]
    row_pairs = [(m.w_query, m.g_query), (m.w_key, m.g_key), (m.w_value, m.g_value)]

    def outer(kind, a, depth, which):
        if kind == "r" and a < 3:
            return row_pairs[a][which].at[:, pl.ds(pl.multiple_of(depth * HD, HD), HD)]
        if kind == "r":
            first = pl.multiple_of(depth * ff_width + (a - 3) * CHUNK, CHUNK)
            return (m.w_up, m.g_up)[which].at[:, pl.ds(first, CHUNK)]
        if a == 0:
            return (m.w_out, m.g_out)[which].at[pl.ds(pl.multiple_of(depth * HD, HD), HD), :]
        first = pl.multiple_of(depth * ff_width + (a - 1) * CHUNK, CHUNK)
        return (m.w_down, m.g_down)[which].at[pl.ds(first, CHUNK), :]

    def part(pair, kind, a, first, count):
        if kind == "r":
            return pair[0].at[a, blocks(first, count), :]
        return pair[1].at[a, :, blocks(first, count)]

    weights, grads, landing = (m.wr, m.wc), (m.gr, m.gc), (m.lr, m.lc)

    def z_start(k):
        kind, a = units[k]
        into = part(weights, kind, a, own_block, 1)
        copies = [
            remote(outer(kind, a, peer(s), 0), into, m.z_s.at[k, s], m.z_r.at[k, s], at.along(s))
            for s in range(1, depth_size)
        ]
        copies.append(local(outer(kind, a, at.depth, 0), into, m.z_l.at[k]))
        return copies

    def z_wait(copies):
        received(copies[:-1])
        copies[-1].wait()

    def g_start(k, stage):
        kind, a = units[k]
        held = part(weights, kind, a, at.base(stage) * depth_size, 2**stage * depth_size)
        return [remote(held, held, m.g_s.at[k, stage], m.g_r.at[k, stage], at.across(stage))]

    def received(copies):
        for copy in copies:
            copy.wait_recv()
        sends.extend(copies)

    def settle(copies):
        for copy in copies:
            copy.wait_send()
        settled.extend(copies)

    def fold_start(k, stage):
        kind, a = units[k]
        size = 2**stage
        other = at.base(stage) + (1 - 2 * at.bit(stage)) * size
        return [
            remote(
                part(grads, kind, a, other * depth_size, size * depth_size),
                part(landing, kind, a, (size - 1) * depth_size, size * depth_size),
                m.f_s.at[k, stage],
                m.f_r.at[k, stage],
                at.across(stage),
            )
        ]

    def fold_finish(k, stage, copies):
        received(copies)
        kind, a = units[k]
        size = 2**stage
        own = at.base(stage) * depth_size

        def add(i, _):
            mine = blocks(own + i, 1)
            theirs = blocks((size - 1) * depth_size + i, 1)
            if kind == "r":
                total = m.gr[a, mine, :].astype(F32) + m.lr[a, theirs, :].astype(F32)
                m.gr[a, mine, :] = total.astype(BF)
            else:
                total = m.gc[a, :, mine].astype(F32) + m.lc[a, :, theirs].astype(F32)
                m.gc[a, :, mine] = total.astype(BF)
            return 0

        lax.fori_loop(0, size * depth_size, add, 0)

    def end_start(k):
        kind, a = units[k]
        into = outer(kind, a, at.depth, 1)
        copies = [
            remote(
                part(grads, kind, a, at.slot * depth_size + peer(s), 1),
                into,
                m.e_s.at[k, s],
                m.e_r.at[k, s],
                at.along(s),
            )
            for s in range(1, depth_size)
        ]
        copies.append(local(part(grads, kind, a, own_block, 1), into, m.e_l.at[k]))
        return copies

    near = {"ctx": at.ctx + (1 - 2 * (at.depth % 2)) * group}
    far = {"ctx": at.ctx + (2 - 4 * (at.depth // 2)) * group}
    near_depth = at.depth + 1 - 2 * (at.depth % 2)
    pair_first = at.depth // 2 * 2
    my_pair = pl.ds(pl.multiple_of(pair_first * rows, rows), 2 * rows)
    her_pair = pl.ds(pl.multiple_of((2 - pair_first) * rows, rows), 2 * rows)
    quarter = half // 2
    my_quarter = pl.ds(pl.multiple_of(at.tp * half + at.depth % 2 * quarter, quarter), quarter)
    her_quarter = pl.ds(pl.multiple_of(at.tp * half + (1 - at.depth % 2) * quarter, quarter), quarter)

    def token_step(i, buffer, step, copies):
        if copies:
            received(copies[-1:])
        brought = [
            None,
            (token_rows(near_depth), my_cols),
            (her_pair, my_quarter),
            (her_pair, her_quarter),
        ]
        given = [(token_rows(at.depth), my_cols), (my_pair, my_quarter), (her_pair, my_quarter)]
        if step < 3:
            piece = buffer.at[given[step][0], given[step][1]]
            there = far if step == 1 else near
            copies.append(remote(piece, piece, m.t_s.at[i, step], m.t_r.at[i, step], there))
        if step:
            piece = buffer.at[brought[step][0], brought[step][1]]
            swapped[i].append(
                remote(piece, piece, m.w_s.at[i, step - 1], m.w_r.at[i, step - 1], at.twin())
            )
        return copies

    def kv_start(h, stage):
        size = 2**stage * tokens
        rows_held = pl.ds(pl.multiple_of(at.base(stage) * tokens, tokens), size)
        held = m.kv.at[rows_held, slice(h * HD, (h + 1) * HD)]
        return remote(held, held, m.kv_s.at[0, h, stage], m.kv_r.at[0, h, stage], at.across(stage))

    spare = (m.lr.at[1 + ff_chunks], m.lr.at[2 + ff_chunks])

    def dkv_start(stage):
        size = 2**stage
        other = at.base(stage) + (1 - 2 * at.bit(stage)) * size
        given = pl.ds(pl.multiple_of(other * tokens, tokens), size * tokens)
        taken = pl.ds((size - 1) * tokens, size * tokens)
        return [
            remote(
                m.kv.at[given, slice(h * HD, (h + 1) * HD)],
                spare[h].at[taken, :],
                m.kv_s.at[1, h, stage],
                m.kv_r.at[1, h, stage],
                at.across(stage),
            )
            for h in range(2)
        ]

    def dkv_finish(stage, copies):
        received(copies)
        size = 2**stage
        own = at.base(stage) * tokens
        step = ROW_TILE

        def add(i, _):
            mine = pl.ds(pl.multiple_of(own + i * step, step), step)
            theirs = pl.ds(pl.multiple_of((size - 1) * tokens + i * step, step), step)
            for h in range(2):
                cols = slice(h * HD, (h + 1) * HD)
                total = m.kv[mine, cols].astype(F32) + spare[h][theirs, :].astype(F32)
                m.kv[mine, cols] = total.astype(BF)
            return 0

        lax.fori_loop(0, size * tokens // step, add, 0)

    lane = lax.broadcasted_iota(jnp.int32, (1, 128), 1)

    def place_rows():
        mine = token_rows(at.depth)
        for b in range(block_count):
            c = natural[b]
            into = slice(b * depth_rows, (b + 1) * depth_rows)
            out_of = slice(c * depth_rows, (c + 1) * depth_rows)
            m.x[mine, into] = m.x_in[:, out_of]
            m.dy[mine, into] = m.dy_in[:, out_of]

    def place_vectors():
        m.ps[0] = jnp.zeros_like(m.ps[0])
        for row, name in enumerate(VECTORS):
            for b in range(block_count):
                c = natural[b]
                m.gv[row : row + 1, b * depth_rows : (b + 1) * depth_rows] = getattr(m, name)[c : c + 1, :]
        per_head = HD // 128
        for a in range(3):
            for h in range(per_head):
                row = getattr(m, BIASES[a])[pl.ds(at.depth * per_head + h, 1), :]
                m.biases[a : a + 1, h * 128 : (h + 1) * 128] = row
        for i in range(ff_chunks):
            for h in range(per_head):
                row = m.b_up[pl.ds((at.depth * ff_chunks + i) * per_head + h, 1), :]
                m.biases[3 + i : 4 + i, h * 128 : (h + 1) * 128] = row
        block_rows = rows // 2
        for n in range(group * depth_size):
            c = natural[n]
            first = jnp.where(lane < block_rows, m.blocks[2 * c], m.blocks[2 * c + 1])
            m.places[n : n + 1, :] = (first * block_rows + lane % block_rows).astype(F32)

    def affine():
        step = 32

        def stats(i, _):
            here = pl.ds(pl.multiple_of(i * step, step), step)
            x = m.x[here, :].astype(F32)
            mean = jnp.mean(x, -1, keepdims=True)
            centered = x - mean
            m.mean[here, :] = mean
            m.inv[here, :] = lax.rsqrt(jnp.mean(centered * centered, -1, keepdims=True) + norm_epsilon)
            return 0

        lax.fori_loop(0, tokens // step, stats, 0)

        def body(i, _):
            here = token_rows(i)
            for n in range(width // 512):
                cols = slice(n * 512, (n + 1) * 512)
                normal = (m.x[here, cols].astype(F32) - m.mean[here, :]) * m.inv[here, :]
                m.na[here, cols] = (normal * m.gv[0:1, cols] + m.gv[1:2, cols]).astype(BF)
                mlp = normal * m.gv[2:3, cols] + m.gv[3:4, cols]
                m.nm[here, cols] = mlp.astype(BF)
                m.nmt[cols, here] = mlp.T.astype(BF)
            return 0

        lax.fori_loop(0, depth_size, body, 0)

    def place_column(n):
        return jnp.broadcast_to(m.places[pl.ds(n, 1), :], (128, 128)).T

    def make_tables():
        def body(n, _):
            angles = place_column(n) * m.freqs[0:1, :]
            here = pl.ds(pl.multiple_of(n * 128, 128), 128)
            m.tab[here, :] = jnp.cos(angles - jnp.where(lane < ROT, 0.0, math.pi / 2))
            return 0

        lax.fori_loop(0, group * tokens // 128, body, 0)

    def turned(value, here, sign):
        head = value[:, :128]
        left = pltpu.roll(head, 128 - ROT // 2, 1)
        right = pltpu.roll(head, ROT // 2, 1)
        table = m.tab[here, :]
        cosine = jnp.where(lane < ROT, table, 1.0)
        sine = sign * pltpu.roll(table, ROT, 1)
        crossed = jnp.where(lane < ROT // 2, -left, jnp.where(lane < ROT, right, 0.0))
        return head * cosine + crossed * sine

    def project(a):
        return mm(m.na[...], m.wr[a]) + m.biases[a : a + 1, :]

    kv_own = pl.ds(pl.multiple_of(at.slot * tokens, tokens), tokens)
    score_scale = 1.0 / math.sqrt(HD)

    def make_query():
        query = project(0)
        m.q[:, :128] = turned(query, kv_own, 1.0).astype(BF)
        m.q[:, 128:] = query[:, 128:].astype(BF)

    def make_keys():
        keys = project(1)
        m.kv[kv_own, :128] = turned(keys, kv_own, 1.0).astype(BF)
        m.kv[kv_own, 128:HD] = keys[:, 128:].astype(BF)

    def make_values():
        m.kv[kv_own, HD:] = project(2).astype(BF)

    def key_rows(j):
        return pl.ds(pl.multiple_of(j * tokens, tokens), tokens)

    def masked_scores(j):
        scores = mm_nt(m.kv[key_rows(j), :HD], m.q[...]) * score_scale
        count = tokens // 128
        column = jnp.concatenate([place_column(j * count + n)[:, :1] for n in range(count)], 0)
        row = jnp.concatenate([m.places[pl.ds(at.slot * count + n, 1), :] for n in range(count)], 1)
        return jnp.where(column <= row, scores, DROP)

    def attend(j):
        scores = masked_scores(j)
        if j == 0:
            old = jnp.full((1, tokens), -1e20, F32)
        else:
            old = m.stat[0:1, :]
        new = jnp.maximum(old, jnp.max(scores, 0, keepdims=True))
        raw = jnp.exp(scores - new)
        total = jnp.sum(raw, 0, keepdims=True)
        value = mm(m.kv[key_rows(j), HD:].T, raw.astype(BF))
        m.stat[0:1, :] = new
        if j:
            factor = jnp.exp(old - new)
            total = total + m.stat[1:2, :] * factor
            value = value + m.att[...] * factor
        m.stat[1:2, :] = total
        m.att[...] = value
        if j == group - 1:
            m.stat[2:3, :] = new + jnp.log(total)
            value = value / total
            m.att[...] = value
            m.alt[...] = value.astype(BF)
            m.al[...] = value.T.astype(BF)

    def head_grads():
        grad = mm_nt(m.dy[...], m.wc[0])
        low = grad.astype(BF)
        m.hg[...] = low
        m.stat[3:4, :] = jnp.sum(low.astype(F32).T * m.att[...], 0, keepdims=True)

    def attend_back(j):
        probs = jnp.exp(masked_scores(j) - m.stat[2:3, :])
        value_part = mm(probs.astype(BF), m.hg[...])
        prob_grad = mm_nt(m.kv[key_rows(j), HD:], m.hg[...])
        score_grad = (probs * (prob_grad - m.stat[3:4, :]) * score_scale).astype(BF)
        query_part = mm(m.kv[key_rows(j), :HD].T, score_grad)
        key_part = mm(score_grad, m.q[...])
        head_sum = jnp.sum(turned(key_part, key_rows(j), -1.0), 0, keepdims=True)
        rest_sum = jnp.sum(key_part[:, 128:], 0, keepdims=True)
        if j:
            query_part = query_part + m.dqt[...]
            head_sum = head_sum + m.kb[0:1, :128]
            rest_sum = rest_sum + m.kb[0:1, 128:]
        m.dqt[...] = query_part
        m.kb[0:1, :128] = head_sum
        m.kb[0:1, 128:] = rest_sum
        m.kv[key_rows(j), :HD] = key_part.astype(BF)
        m.kv[key_rows(j), HD:] = value_part.astype(BF)

    def small_store(first, row):
        for n in range(row.shape[1] // 128):
            m.ps[0, first + n : first + n + 1, :] = row[:, n * 128 : (n + 1) * 128]

    def attention_grads():
        query = m.dqt[...].T
        head = turned(query, kv_own, -1.0)
        keys = m.kv[kv_own, :HD].astype(F32)
        key_head = turned(keys, kv_own, -1.0)
        m.low[:, :128] = head.astype(BF)
        m.low[:, 128:HD] = query[:, 128:].astype(BF)
        m.low[:, HD : HD + 128] = key_head.astype(BF)
        m.low[:, HD + 128 : 2 * HD] = m.kv[kv_own, 128:HD]
        m.low[:, 2 * HD :] = m.kv[kv_own, HD:]
        small_store(64, jnp.sum(head, 0, keepdims=True))
        small_store(65, jnp.sum(query[:, 128:], 0, keepdims=True))
        small_store(66, m.kb[0:1, :])
        small_store(68, jnp.sum(m.kv[kv_own, HD:].astype(F32), 0, keepdims=True))

        def body(n, _):
            tile = pl.ds(pl.multiple_of(n * ROW_TILE, ROW_TILE), ROW_TILE)
            turned_in = m.na[:, tile].T
            for a in range(3):
                m.gr[a, tile, :] = mm(turned_in, m.low[:, a * HD : (a + 1) * HD]).astype(BF)
            return 0

        lax.fori_loop(0, width // ROW_TILE, body, 0)

    def out_grads():
        def body(n, _):
            tile = pl.ds(pl.multiple_of(n * 512, 512), 512)
            m.gc[0, :, tile] = mm(m.alt[...], m.dy[:, tile]).astype(BF)
            return 0

        lax.fori_loop(0, width // 512, body, 0)

    def feed_forward(i):
        activated, slope = gelu_parts(mm(m.nm[...], m.wr[3 + i]) + m.biases[3 + i : 4 + i, :])
        m.hid[i] = activated.astype(BF)
        up_grad = mm_nt(m.dy[...], m.wc[1 + i]) * slope
        small_store(70 + 2 * i, jnp.sum(up_grad, 0, keepdims=True))
        m.ul[i] = up_grad.astype(BF)
        turned_hidden = activated.T.astype(BF)

        def body(n, _):
            tile = pl.ds(pl.multiple_of(n * 512, 512), 512)
            m.gr[3 + i, tile, :] = mm(m.nmt[tile, :], m.ul[i]).astype(BF)
            m.gc[1 + i, :, tile] = mm(turned_hidden, m.dy[:, tile]).astype(BF)
            return 0

        lax.fori_loop(0, width // 512, body, 0)

    out, back = m.na, m.dy

    def tile_of(n):
        return pl.ds(pl.multiple_of(n * ROW_TILE, ROW_TILE), ROW_TILE)

    def small_add_rows(first, n, value):
        row = jnp.sum(value, 0, keepdims=True)
        for h in range(ROW_TILE // 128):
            m.ps[0, pl.ds(first + n * (ROW_TILE // 128) + h, 1), :] = row[:, h * 128 : (h + 1) * 128]

    def end_out(n):
        tile = tile_of(n)
        total = mm(m.al[...], m.wc[0, :, tile])
        for i in range(ff_chunks):
            total += mm(m.hid[i], m.wc[1 + i, :, tile])
        out[:, tile] = total.astype(BF)

    def end_back(n):
        tile = tile_of(n)
        attn_back = mm_nt(m.low[:, :HD], m.wr[0, tile, :])
        for a in (1, 2):
            attn_back += mm_nt(m.low[:, a * HD : (a + 1) * HD], m.wr[a, tile, :])
        mlp_back = mm_nt(m.ul[0], m.wr[3, tile, :])
        for i in range(1, ff_chunks):
            mlp_back += mm_nt(m.ul[i], m.wr[3 + i, tile, :])
        normal = (m.x[:, tile].astype(F32) - m.mean[...]) * m.inv[...]
        small_add_rows(0, n, attn_back * normal)
        small_add_rows(16, n, attn_back)
        small_add_rows(32, n, mlp_back * normal)
        small_add_rows(48, n, mlp_back)
        small_add_rows(78, n, m.dy[:, tile].astype(F32))
        back[:, tile] = (attn_back * m.gv[0:1, tile] + mlp_back * m.gv[2:3, tile]).astype(BF)

    def end_quarter(piece, which, n):
        count = quarter // ROW_TILE
        odd = at.depth % 2
        first = which * 2 + (odd if n else 1 - odd)

        def body(i, _):
            piece(first * count + i)
            return 0

        lax.fori_loop(0, count, body, 0)

    ends = (out, back)

    def quarter_of(which, n):
        odd = at.depth % 2
        return pl.ds(pl.multiple_of(which * half + (odd if n else 1 - odd) * quarter, quarter), quarter)

    def offer():
        pl.semaphore_signal(m.free, inc=1, device_id=at.twin(), device_id_type=MESH)

    def sum_start(i, n):
        if i == n == 0:
            pl.semaphore_wait(m.free, 1)
        return remote(
            ends[i].at[:, quarter_of(1 - at.tp, n)],
            m.nm.at[:, quarter_of(i, n)],
            m.o_s.at[i, n],
            m.o_r.at[i, n],
            at.twin(),
        )

    def sum_add(i, n):
        mine = ends[i]
        into, source = quarter_of(at.tp, n), quarter_of(i, n)

        def add(z, _):
            block = token_rows(z)
            total = mine[block, into].astype(F32) + m.nm[block, source].astype(F32)
            mine[block, into] = total.astype(BF)
            return 0

        lax.fori_loop(0, depth_size, add, 0)

    def sum_step(i, step, copy):
        received([copy])
        mine = ends[i]
        if step == 0:
            sum_add(i, 0)
            source, into, there = mine.at[her_pair, her_quarter], m.tz.at[i, 0], near
        elif step == 1:
            total = mine[her_pair, my_quarter].astype(F32) + m.tz[i, 0].astype(F32)
            mine[her_pair, my_quarter] = total.astype(BF)
            source, into, there = mine.at[her_pair, my_quarter], m.tz.at[i, 1], far
        elif step == 2:
            total = mine[my_pair, my_quarter].astype(F32) + m.tz[i, 1].astype(F32)
            mine[my_pair, my_quarter] = total.astype(BF)
            source, into, there = mine.at[token_rows(near_depth), my_cols], m.te.at[i], near
        else:
            total = mine[token_rows(at.depth), my_cols].astype(F32) + m.te[i].astype(F32)
            m.fin[i, :, my_cols] = total.astype(BF)
            source, into, there = m.fin.at[i, :, my_cols], m.fin.at[i, :, my_cols], at.twin()
        return remote(source, into, m.o_s.at[i, 2 + step], m.o_r.at[i, 2 + step], there)

    def small_group(stage):
        return remote(m.ps.at[stage], m.pl.at[stage], m.p_s.at[stage], m.p_r.at[stage], at.across(stage))

    def small_add(stage, copy):
        received([copy])
        m.ps[stage + 1] = m.ps[stage] + m.pl[stage]

    def small_depth():
        total = m.ps.at[bits]
        copies = [
            remote(total, m.pz.at[at.depth], m.p_s.at[bits + s], m.p_r.at[bits + s], at.along(s))
            for s in range(1, depth_size)
        ]
        m.pz[at.depth] = m.ps[bits]
        return copies

    def small_twin(copies):
        received(copies)
        value = m.pz[0]
        for z in range(1, depth_size):
            value = value + m.pz[z]
        m.px[0] = value
        return remote(m.px.at[0], m.px.at[1], m.p_s.at[bits], m.p_r.at[bits], at.twin())

    def small_finish(copy):
        received([copy])
        for v in range(4):
            for b in range(block_count):
                row = v * 16 + b
                into = v * 16 + natural[b]
                m.norm_sums[into : into + 1, :] = m.px[0, row : row + 1, :] + m.px[1, row : row + 1, :]
        for b in range(block_count):
            m.s_dy[natural[b] : natural[b] + 1, :] = m.ps[bits, 78 + b : 79 + b, :]
        for z in range(depth_size):
            m.s_query[2 * z : 2 * z + 2, :] = m.pz[z, 64:66, :]
            m.s_key[2 * z : 2 * z + 2, :] = m.pz[z, 66:68, :]
            m.s_value[2 * z : 2 * z + 2, :] = m.pz[z, 68:70, :]
            m.s_up[8 * z : 8 * z + 8, :] = m.pz[z, 70:78, :]

    live = {}
    swapped = {0: [], 1: []}
    buffers = (m.x, m.dy)

    def run(name, n):
        if name == "zs":
            live["z", n] = z_start(n)
        elif name == "zy":
            z_wait(live["z", n])
            live["g", n] = g_start(n, 0)
        elif name == "yc":
            received(live["g", n])
            live["g", n] = g_start(n, 1)
        elif name == "cw":
            received(live["g", n])
        elif name == "ta":
            live["t", n] = token_step(n, buffers[n], 0, [])
        elif name == "tb":
            token_step(n, buffers[n], 1, live["t", n])
        elif name == "tc":
            token_step(n, buffers[n], 2, live["t", n])
        elif name == "td":
            token_step(n, buffers[n], 3, live["t", n])
        elif name == "te":
            received(swapped[n])
        elif name == "norm":
            place_rows()
        elif name == "vec":
            place_vectors()
        elif name == "tab":
            make_tables()
        elif name == "aff":
            affine()
        elif name == "qq":
            make_query()
        elif name == "kk":
            make_keys()
        elif name == "go":
            out_grads()
        elif name == "val":
            make_values()
        elif name == "ky":
            live["k", n] = [kv_start(n, 0)]
        elif name == "kc":
            received(live["k", n])
            live["k", n].append(kv_start(n, 1))
        elif name == "kw":
            received(live["k", n][1:])
        elif name == "at":
            attend(n)
        elif name == "hg":
            head_grads()
        elif name == "bw":
            if n == 0:
                settle(live["k", 0] + live["k", 1])
            attend_back(n)
        elif name == "dc":
            live["d"] = dkv_start(1)
        elif name == "dy":
            dkv_finish(1, live["d"])
            live["d"] = dkv_start(0)
        elif name == "dw":
            dkv_finish(0, live["d"])
        elif name == "ag":
            attention_grads()
        elif name == "ff":
            feed_forward(n)
        elif name == "fc":
            live["f", n] = fold_start(n, 1)
        elif name == "fy":
            fold_finish(n, 1, live["f", n])
            live["f", n] = fold_start(n, 0)
        elif name == "fz":
            fold_finish(n, 0, live["f", n])
            live["e", n] = end_start(n)
        elif name == "of":
            offer()
        elif name == "eo":
            end_quarter(end_out, at.tp if n >= 2 else 1 - at.tp, n % 2)
        elif name == "eb":
            if n == 0:
                settle(live["t", 1] + swapped[1])
            end_quarter(end_back, at.tp if n >= 2 else 1 - at.tp, n % 2)
        elif name == "sx":
            live["sx", n] = sum_start(n // 2, n % 2)
        elif name == "sa":
            live["s", n] = sum_step(n, 0, live["sx", 2 * n])
        elif name == "sm":
            received([live["sx", 2 * n + 1]])
            sum_add(n, 1)
        elif name == "sb":
            live["s", n] = sum_step(n, 1, live["s", n])
        elif name == "sc":
            live["s", n] = sum_step(n, 2, live["s", n])
        elif name == "sd":
            live["s", n] = sum_step(n, 3, live["s", n])
        elif name == "sw":
            received([live["s", n]])
        elif name == "pa":
            live["p"] = small_group(0)
        elif name == "pb":
            small_add(0, live["p"])
            live["p"] = small_group(1)
        elif name == "pc":
            small_add(1, live["p"])
            live["p"] = small_depth()
        elif name == "pd":
            live["p"] = small_twin(live["p"])
        elif name == "pe":
            small_finish(live["p"])
        elif name == "ew":
            received(live["e", n][:-1])
            live["e", n][-1].wait()

    for entry in SCHEDULE:
        name = entry.rstrip("0123456789")
        run(name, int(entry[len(name) :] or 0))
    for copy in sends:
        if not any(copy is other for other in settled):
            copy.wait_send()


SCHEDULE = (
    "zs1", "vec", "zs6", "zs4", "zy1", "norm", "ta0", "zy6", "zs7", "zs5", "tb0", "zs2",
    "yc1", "ta1", "zs3", "zy4", "tab", "zy5", "zy7", "yc5", "tc0", "zs9", "cw1", "yc7",
    "zy2", "zs0", "zy3", "td0", "yc2", "cw2", "tb1", "zy9", "yc6", "te0", "zs8", "zy0",
    "aff", "kk", "ky0", "val", "ky1", "yc0", "yc4", "tc1", "yc3", "cw3", "zs11", "kc0",
    "zy8", "cw0", "cw4", "yc9", "td1", "zs10", "kc1", "qq", "zy11", "kw1", "cw7", "kw0",
    "cw6", "at0", "cw9", "at1", "at2", "yc8", "at3", "te1", "ff1", "fc6", "fc7", "zy10",
    "hg", "bw0", "cw8", "bw1", "bw2", "bw3", "dc", "cw5", "fy7", "go", "fc3", "yc10",
    "ff0", "dy", "fz7", "ff2", "yc11", "fc4", "cw10", "fy3", "cw11", "ff3", "dw", "of0",
    "fy6", "fc9", "ag", "eo0", "fz3", "sx0", "fc0", "eb0", "eb1", "fy9", "fc2", "fz6",
    "fy0", "fc8", "eb2", "sx2", "fc5", "eo2", "fy4", "fz9", "sx3", "fc10", "fz0", "fy5",
    "fz4", "fc11", "sa1", "fy11", "eb3", "pa", "fz5", "eo3", "sm1", "fc1", "pb", "eo1",
    "sb1", "sx1", "sa0", "fy8", "fy1", "fz11", "ew4", "fz1", "fy2", "ew9", "sm0", "ew5",
    "fy10", "sb0", "pc", "fz8", "sc1", "ew7", "sc0", "ew0", "ew11", "fz2", "ew3", "fz10",
    "sd1", "sd0", "pd", "pe", "sw0", "ew8", "sw1", "ew2", "ew10", "ew1", "ew6",
)


def fits(depth_size, group, depth_rows, rows, width, ff_chunks):
    sizes = layout_of(depth_size, group, depth_rows, rows, width, ff_chunks)
    total = sum(math.prod(shape) * jnp.dtype(kind).itemsize for _, shape, kind in sizes)
    shaped = group == depth_size == ff_chunks == 4 and depth_rows == rows == 128
    return shaped and total < VMEM_BYTES


def fused_shards(
    layer_input,
    block_order,
    attn_gain,
    attn_shift,
    mlp_gain,
    mlp_shift,
    w_query,
    b_query,
    w_key,
    b_key,
    w_value,
    b_value,
    w_out,
    b_out,
    w_up,
    b_up,
    w_down,
    b_down,
    out_grad,
):
    rows, width = layer_input.shape
    tp_size = lax.axis_size("tp")
    depth_size = HEADS // tp_size
    group = lax.axis_size("ctx") // depth_size
    depth_rows = width // (depth_size * group)
    ff_width = w_up.shape[1] // depth_size
    ff_chunks = ff_width // CHUNK
    tokens = depth_size * rows
    at = Place(depth_size, group)

    freqs = (10000.0 ** (-(2.0 * np.arange(ROT // 2, dtype=np.float32)) / ROT)).astype(np.float32)
    freqs = np.tile(freqs, (8, 128 // (ROT // 2)))

    def in_rows(vector):
        return vector.reshape(-1, 128)

    buffers = layout_of(depth_size, group, depth_rows, rows, width, ff_chunks)
    semaphores = semaphores_of(depth_size, group, 4 + 2 * ff_chunks)
    names = tuple(INPUTS) + tuple(OUTPUTS) + tuple(b[0] for b in buffers) + tuple(s[0] for s in semaphores) + ("free",)
    vmem = pl.BlockSpec(memory_space=pltpu.VMEM)
    hbm = pl.BlockSpec(memory_space=pl.ANY)
    shape = jax.ShapeDtypeStruct
    wide, thin = depth_size * HD, depth_size * ff_width
    results = pl.pallas_call(
        functools.partial(fused_kernel, names, depth_size, group),
        out_shape=(
            shape((2, rows, width), BF),
            shape((depth_rows, wide), BF),
            shape((depth_rows, wide), BF),
            shape((depth_rows, wide), BF),
            shape((wide, depth_rows), BF),
            shape((depth_rows, thin), BF),
            shape((thin, depth_rows), BF),
            shape((4 * width // 128, 128), F32),
            shape((wide // 128, 128), F32),
            shape((wide // 128, 128), F32),
            shape((wide // 128, 128), F32),
            shape((thin // 128, 128), F32),
            shape((width // 128, 128), F32),
        ),
        in_specs=[pl.BlockSpec(memory_space=pltpu.SMEM)] + [vmem] * 11 + [hbm] * 6,
        out_specs=(vmem,) + (hbm,) * 6 + (vmem,) * 6,
        scratch_shapes=[pltpu.VMEM(s, t) for _, s, t in buffers]
        + [pltpu.SemaphoreType.DMA(s) for _, s in semaphores]
        + [pltpu.SemaphoreType.REGULAR],
        compiler_params=pltpu.CompilerParams(
            collective_id=4, has_side_effects=True, vmem_limit_bytes=VMEM_BYTES
        ),
    )(
        block_order,
        layer_input,
        out_grad,
        freqs,
        *[in_rows(v) for v in (attn_gain, attn_shift, mlp_gain, mlp_shift)],
        *[in_rows(v) for v in (b_query, b_key, b_value, b_up)],
        w_query,
        w_key,
        w_value,
        w_out,
        w_up,
        w_down,
    )
    sums, *parts = results
    output, input_grad, *rest = close(
        depth_size, group, layer_input, out_grad, sums, in_rows(b_out), in_rows(b_down), parts
    )
    small = [vector.reshape(-1) for vector in rest[6:]]
    norms, (to_query, to_key, to_value, to_up, to_dy, again) = small[:4], small[4:]
    return (output, input_grad, *rest[:6], to_query, to_key, to_value, to_dy, to_up, again, *norms)


def close_kernel(depth_size, group, x_in, dy_in, sums, b_out, b_down, *refs):
    grads, (norm_sums, *small), results = refs[:6], refs[6:12], refs[12:]
    layer_output, input_grad, wide, norms, others = (
        results[0],
        results[1],
        results[2:8],
        results[8:12],
        results[12:],
    )
    for source, into in zip(grads, wide, strict=True):
        into[...] = source[...].astype(F32)
    for v, into in enumerate(norms):
        count = into.shape[0]
        into[...] = norm_sums[v * count : (v + 1) * count, :]
    for source, into in zip(small + small[-1:], others, strict=True):
        into[...] = source[...]
    x = x_in[...].astype(F32)
    width = x.shape[1]
    natural = natural_blocks(depth_size, group)
    size = width // len(natural)
    centered = x - jnp.mean(x, -1, keepdims=True)
    inverse = lax.rsqrt(jnp.mean(centered * centered, -1, keepdims=True) + norm_epsilon)
    normal = centered * inverse
    total = jnp.zeros((x.shape[0], 1), F32)
    against = jnp.zeros((x.shape[0], 1), F32)
    for b, c in enumerate(natural):
        out_of, into = slice(b * size, (b + 1) * size), slice(c * size, (c + 1) * size)
        bias = b_out[c : c + 1, :] + b_down[c : c + 1, :]
        layer_output[:, into] = (x[:, into] + sums[0, :, out_of].astype(F32) + bias).astype(BF)
        piece = sums[1, :, out_of].astype(F32)
        total += jnp.sum(piece, -1, keepdims=True)
        against += jnp.sum(piece * normal[:, into], -1, keepdims=True)
    total, against = total / width, against / width
    for b, c in enumerate(natural):
        out_of, into = slice(b * size, (b + 1) * size), slice(c * size, (c + 1) * size)
        piece = sums[1, :, out_of].astype(F32) - total - normal[:, into] * against
        input_grad[:, into] = dy_in[:, into].astype(F32) + inverse * piece


def close(depth_size, group, x_in, dy_in, sums, b_out, b_down, parts):
    rows, width = x_in.shape
    steps = rows // 64
    grads, small = parts[:6], parts[6:]
    norms = [jax.ShapeDtypeStruct((width // 128, 128), F32)] * 4
    copies = [jax.ShapeDtypeStruct(s.shape, F32) for s in small[1:] + small[-1:]]

    def by_rows(shape):
        block = shape[:-2] + (shape[-2] // steps, shape[-1])
        return pl.BlockSpec(block, lambda i: (0,) * (len(shape) - 2) + (i, 0))

    def all_of(shape):
        return pl.BlockSpec(shape, lambda i: (0,) * len(shape))

    return pl.pallas_call(
        functools.partial(close_kernel, depth_size, group),
        grid=(steps,),
        out_shape=[
            jax.ShapeDtypeStruct(x_in.shape, BF),
            jax.ShapeDtypeStruct(x_in.shape, F32),
            *[jax.ShapeDtypeStruct(g.shape, F32) for g in grads],
            *norms,
            *copies,
        ],
        in_specs=[by_rows(x_in.shape)] * 2
        + [by_rows(sums.shape), all_of(b_out.shape), all_of(b_down.shape)]
        + [by_rows(g.shape) for g in grads]
        + [all_of(s.shape) for s in small],
        out_specs=[by_rows(x_in.shape)] * 2
        + [by_rows(g.shape) for g in grads]
        + [all_of(s.shape) for s in norms + copies],
        compiler_params=pltpu.CompilerParams(vmem_limit_bytes=VMEM_BYTES),
    )(x_in, dy_in, sums, b_out, b_down, *grads, *small)


def shards(
    layer_input,
    block_order,
    attn_gain,
    attn_shift,
    mlp_gain,
    mlp_shift,
    w_query,
    b_query,
    w_key,
    b_key,
    w_value,
    b_value,
    w_out,
    b_out,
    w_up,
    b_up,
    w_down,
    b_down,
    out_grad,
):
    rows, width = layer_input.shape
    depth_size = HEADS // lax.axis_size("tp")
    group = lax.axis_size("ctx") // depth_size
    ff_chunks = w_up.shape[1] // depth_size // CHUNK
    whole = fits(depth_size, group, width // (depth_size * group), rows, width, ff_chunks)
    chosen = fused_shards if whole else staged_shards
    return chosen(
        layer_input, block_order, attn_gain, attn_shift, mlp_gain, mlp_shift, w_query, b_query, w_key, b_key, w_value, b_value, w_out, b_out, w_up, b_up, w_down, b_down, out_grad
    )


def staged_shards(
    layer_input,
    block_order,
    attn_gain,
    attn_shift,
    mlp_gain,
    mlp_shift,
    w_query,
    b_query,
    w_key,
    b_key,
    w_value,
    b_value,
    w_out,
    b_out,
    w_up,
    b_up,
    w_down,
    b_down,
    out_grad,
):
    rows, width = layer_input.shape
    ctx_size = lax.axis_size("ctx")
    tp_size = lax.axis_size("tp")
    depth_size = HEADS // tp_size
    group = ctx_size // depth_size
    bits = group.bit_length() - 1
    depth_rows = width // ctx_size
    hidden_width = w_up.shape[1] // depth_size
    ff_chunks = hidden_width // CHUNK
    at = Place(depth_size, group)
    block_rows = rows // 2

    def permuted(array):
        lead = array.shape[:-1]
        n = len(lead)
        split = array.reshape(lead + (depth_size,) + (2,) * bits + (depth_rows,))
        order = tuple(range(n)) + tuple(n + 1 + b for b in reversed(range(bits))) + (n, n + 1 + bits)
        return split.transpose(order).reshape(lead + (width,))

    def restored(array):
        lead = array.shape[:-1]
        n = len(lead)
        split = array.reshape(lead + (2,) * bits + (depth_size, depth_rows))
        order = tuple(range(n)) + (n + bits,) + tuple(n + b for b in reversed(range(bits))) + (n + bits + 1,)
        return split.transpose(order).reshape(lead + (width,))

    def slot_members():
        table = []
        for slot in range(group):
            member = 0
            for stage in range(bits):
                member += ((slot >> stage) & 1) << (bits - 1 - stage)
            table.append(member)
        return table

    blocks = block_order.reshape(depth_size, group, 2)
    order = jnp.stack([blocks[:, m] for m in slot_members()], 0)
    place = order[..., None] * block_rows + jnp.arange(block_rows, dtype=jnp.int32)
    key_place = place.reshape(group * depth_size * rows)
    token_total = depth_size * rows
    query_place = lax.dynamic_slice_in_dim(key_place, at.slot * token_total, token_total)
    cosine, sine_table = rope_tables(query_place)

    inputs32 = layer_input.astype(F32)
    centered = inputs32 - jnp.mean(inputs32, -1, keepdims=True)
    inverse = lax.rsqrt(jnp.mean(centered * centered, -1, keepdims=True) + norm_epsilon)
    normal32 = centered * inverse

    def halves(array):
        return permuted(array).reshape(rows, tp_size, width // tp_size).transpose(1, 0, 2)

    def by_head(weight):
        return weight.reshape(depth_rows, depth_size, HD).transpose(1, 0, 2)

    def by_chunk(weight):
        return weight.reshape(depth_rows, depth_size, ff_chunks, CHUNK).transpose(2, 1, 0, 3)

    weights = jnp.concatenate(
        [
            jnp.concatenate([by_head(w_query), by_head(w_key)], -1)[None],
            jnp.concatenate([by_head(w_value), by_head(w_out.T)], -1)[None],
            jnp.concatenate([by_chunk(w_up), by_chunk(w_down.T)], -1),
        ],
        0,
    )
    normal, grad, gathered = gather_all(
        depth_size, group, halves(normal32.astype(BF)), halves(out_grad), weights
    )
    full = gathered.reshape(2 + ff_chunks, width, 2 * HD)
    gain_a, shift_a, gain_m, shift_m = permuted(jnp.stack([attn_gain, attn_shift, mlp_gain, mlp_shift]))
    normal_tokens = normal.astype(F32)
    attn_in = (normal_tokens * gain_a + shift_a).astype(BF)
    mlp_in = (normal_tokens * gain_m + shift_m).astype(BF)

    def own_part(vector, size):
        return lax.dynamic_slice_in_dim(vector, at.depth * size, size)

    query_key = mm(attn_in, full[0])
    query = rotate(query_key[:, :HD] + own_part(b_query, HD), cosine, sine_table).astype(BF)
    keys = rotate(query_key[:, HD:] + own_part(b_key, HD), cosine, sine_table).astype(BF)
    values = (mm(attn_in, full[1, :, :HD]) + own_part(b_value, HD)).astype(BF)
    out_t = full[1, :, HD:]
    shared = share_group(depth_size, group, jnp.concatenate([keys, values], -1))
    shared = shared.reshape(group * token_total, 2 * HD)
    all_keys, all_values = shared[:, :HD], shared[:, HD:]
    score_scale = 1.0 / math.sqrt(HD)
    scores = mm_nt(query, all_keys) * score_scale
    allowed = key_place[None, :] <= query_place[:, None]
    scores = jnp.where(allowed, scores, -1e30)
    top = jnp.max(scores, -1, keepdims=True)
    raw = jnp.exp(scores - top)
    probs = raw / jnp.sum(raw, -1, keepdims=True)
    probs_low = probs.astype(BF)
    attended = mm(probs_low, all_values)
    attn_low = attended.astype(BF)

    head_grad = mm(grad, out_t).astype(BF)
    delta = jnp.sum(head_grad.astype(F32) * attended, -1, keepdims=True)
    value_part = mm_tn(probs_low, head_grad)
    score_grad = (probs * (mm_nt(head_grad, all_values) - delta) * score_scale).astype(BF)
    query_acc = mm(score_grad, all_keys)
    key_part = mm_tn(score_grad, query)
    parts = jnp.concatenate([key_part, value_part], -1).astype(BF)
    folded = fold_group(depth_size, group, parts.reshape(group, token_total, 2 * HD))
    own_grads = lax.dynamic_index_in_dim(folded, at.slot, 0, keepdims=False).astype(F32)
    query_lin = rotate(query_acc, cosine, -sine_table)
    key_lin = rotate(own_grads[:, :HD], cosine, -sine_table)
    value_lin = own_grads[:, HD:]
    query_low, key_low, value_low = query_lin.astype(BF), key_lin.astype(BF), value_lin.astype(BF)
    query_key_low = jnp.concatenate([query_low, key_low], -1)
    attn_back = mm_nt(query_key_low, full[0]) + mm_nt(value_low, full[1, :, :HD])
    grad_chunks = [
        mm_tn(attn_in, query_key_low).astype(BF),
        jnp.concatenate([mm_tn(attn_in, value_low), mm_tn(grad, attn_low)], -1).astype(BF),
    ]

    branches = mm_nt(attn_low, out_t)
    mlp_back = jnp.zeros((token_total, width), F32)
    bias_up = own_part(b_up, hidden_width).reshape(ff_chunks, CHUNK)
    up_sums = []
    for i in range(ff_chunks):
        up, down_t = full[2 + i, :, :CHUNK], full[2 + i, :, CHUNK:]
        activated, slope = gelu_parts(mm(mlp_in, up) + bias_up[i])
        hidden = activated.astype(BF)
        up_grad = mm(grad, down_t) * slope
        up_sums.append(jnp.sum(up_grad, 0))
        up_low = up_grad.astype(BF)
        branches = branches + mm_nt(hidden, down_t)
        mlp_back = mlp_back + mm_nt(up_low, up)
        grad_chunks.append(jnp.concatenate([mm_tn(mlp_in, up_low), mm_tn(grad, hidden)], -1).astype(BF))

    normal_tokens2 = normal.astype(F32)
    back = attn_back * gain_a + mlp_back * gain_m
    grads = jnp.stack(grad_chunks).reshape(2 + ff_chunks, group, depth_size, depth_rows, 2 * HD)
    norm_sums = restored(
        jnp.stack(
            [
                jnp.sum(attn_back * normal_tokens2, 0),
                jnp.sum(attn_back, 0),
                jnp.sum(mlp_back * normal_tokens2, 0),
                jnp.sum(mlp_back, 0),
            ]
        )
    )
    own_biases = jnp.concatenate(
        [jnp.sum(query_lin, 0), jnp.sum(key_lin, 0), jnp.sum(value_lin, 0)] + up_sums
    )
    spread = jnp.where(
        jnp.arange(depth_size, dtype=jnp.int32)[:, None] == at.depth, own_biases[None, :], 0.0
    )
    norm_sums = lax.psum(norm_sums, ("ctx", "tp"))
    grad32 = out_grad.astype(F32)
    spread, bias_grad = lax.psum((spread, jnp.sum(grad32, 0)), "ctx")

    out_sum, back_sum, grad_shares = reduce_all(
        depth_size, group, branches.astype(BF), back.astype(BF), grads
    )
    layer_output = (inputs32 + restored(out_sum).astype(F32) + b_out + b_down).astype(BF)
    back_total = restored(back_sum).astype(F32)
    input_grad = grad32 + inverse * (
        back_total
        - jnp.mean(back_total, -1, keepdims=True)
        - normal32 * jnp.mean(back_total * normal32, -1, keepdims=True)
    )

    def from_head(share):
        return share.transpose(1, 0, 2).reshape(depth_rows, depth_size * HD).astype(F32)

    def from_chunk(share):
        return share.transpose(2, 1, 0, 3).reshape(depth_rows, depth_size * hidden_width).astype(F32)

    return (
        layer_output,
        input_grad,
        from_head(grad_shares[0, :, :, :HD]),
        from_head(grad_shares[0, :, :, HD:]),
        from_head(grad_shares[1, :, :, :HD]),
        from_head(grad_shares[1, :, :, HD:]).T,
        from_chunk(grad_shares[2:, :, :, :CHUNK]),
        from_chunk(grad_shares[2:, :, :, CHUNK:]).T,
        spread[:, :HD].reshape(-1),
        spread[:, HD : 2 * HD].reshape(-1),
        spread[:, 2 * HD : 3 * HD].reshape(-1),
        bias_grad,
        spread[:, 3 * HD :].reshape(-1),
        bias_grad,
        norm_sums[0],
        norm_sums[1],
        norm_sums[2],
        norm_sums[3],
    )


def solution(mesh):
    in_specs = (
        P("ctx", None),
        P(),
        P(),
        P(),
        P(),
        P(),
        P("ctx", "tp"),
        P("tp"),
        P("ctx", "tp"),
        P("tp"),
        P("ctx", "tp"),
        P("tp"),
        P("tp", "ctx"),
        P(),
        P("ctx", "tp"),
        P("tp"),
        P("tp", "ctx"),
        P(),
        P("ctx", None),
    )
    out_specs = (
        P("ctx", None),
        P("ctx", None),
        P("ctx", "tp"),
        P("ctx", "tp"),
        P("ctx", "tp"),
        P("tp", "ctx"),
        P("ctx", "tp"),
        P("tp", "ctx"),
        P("tp"),
        P("tp"),
        P("tp"),
        P(),
        P("tp"),
        P(),
        P(),
        P(),
        P(),
        P(),
    )
    return jax.shard_map(shards, mesh=mesh, in_specs=in_specs, out_specs=out_specs, check_vma=False)
```

```python
import functools
import math

import jax
import jax.numpy as jnp
import numpy as np
from jax import lax
from jax.experimental import pallas as pl
from jax.experimental.pallas import tpu as pltpu
from jax.sharding import PartitionSpec as P

HEADS = 8
HD = 256
ROT = 64
CHUNK = 256

norm_epsilon = 1e-05
BF = jnp.bfloat16
F32 = jnp.float32
MESH = pl.DeviceIdType.MESH


def mm(a, b):
    return jnp.dot(a, b, preferred_element_type=F32)


def mm_tn(a, b):
    return lax.dot_general(a, b, (((0,), (0,)), ((), ())), preferred_element_type=F32)


def mm_nt(a, b):
    return lax.dot_general(a, b, (((1,), (1,)), ((), ())), preferred_element_type=F32)


class Place:
    def __init__(self, depth_size, group):
        self.depth_size = depth_size
        self.group = group
        self.bits = group.bit_length() - 1
        self.ctx = lax.axis_index("ctx")
        self.tp = lax.axis_index("tp")
        self.depth = self.ctx // group
        self.member = self.ctx % group
        slot = 0
        for stage in range(self.bits):
            slot = slot + self.bit(stage) * 2**stage
        self.slot = slot

    def bit(self, stage):
        return (self.member // 2 ** (self.bits - 1 - stage)) % 2

    def along(self, step):
        return {"ctx": lax.rem(self.depth + step, self.depth_size) * self.group + self.member}

    def across(self, stage):
        reach = 2 ** (self.bits - 1 - stage)
        return {"ctx": self.ctx + (1 - 2 * self.bit(stage)) * reach}

    def twin(self):
        return {"tp": 1 - self.tp}

    def base(self, stage):
        return (self.slot // 2**stage) * 2**stage

    def greet(self, devices):
        barrier = pltpu.get_barrier_semaphore()
        for device in devices:
            pl.semaphore_signal(barrier, inc=1, device_id=device, device_id_type=MESH)
        pl.semaphore_wait(barrier, len(devices))

    def everyone(self):
        return (
            [self.along(step) for step in range(1, self.depth_size)]
            + [self.across(stage) for stage in range(self.bits)]
            + [self.twin()]
        )


def remote(src, dst, send, recv, device):
    copy = pltpu.make_async_remote_copy(
        src_ref=src, dst_ref=dst, send_sem=send, recv_sem=recv, device_id=device, device_id_type=MESH
    )
    copy.start()
    return copy


def local(src, dst, sem):
    copy = pltpu.make_async_copy(src, dst, sem)
    copy.start()
    return copy


def gather_kernel(depth_size, group, x_in, dy_in, w_in, x_out, dy_out, w_out, tz_s, tz_r, tx_s, tx_r, t_l, z_s, z_r, z_l, g_s, g_r):
    at = Place(depth_size, group)
    at.greet(at.everyone())
    rows, half = x_in.shape[1:]
    sent = []
    mine = pl.ds(pl.multiple_of(at.depth * rows, rows), rows)
    my_cols = pl.ds(pl.multiple_of(at.tp * half, half), half)

    def token_start(i, src, dst):
        copies = [
            remote(src.at[at.tp], dst.at[mine, my_cols], tz_s.at[i, s], tz_r.at[i, s], at.along(s))
            for s in range(1, depth_size)
        ]
        copies.append(local(src.at[at.tp], dst.at[mine, my_cols], t_l.at[i]))
        return copies

    def token_swap(i, copies, dst):
        for copy in copies[:-1]:
            copy.wait_recv()
            sent.append(copy)
        copies[-1].wait()
        return remote(dst.at[:, my_cols], dst.at[:, my_cols], tx_s.at[i], tx_r.at[i], at.twin())

    chunks = w_in.shape[0]

    def z_start(k):
        copies = [
            remote(
                w_in.at[k, lax.rem(at.depth + s, depth_size)],
                w_out.at[k, at.slot, at.depth],
                z_s.at[k, s],
                z_r.at[k, s],
                at.along(s),
            )
            for s in range(1, depth_size)
        ]
        copies.append(local(w_in.at[k, at.depth], w_out.at[k, at.slot, at.depth], z_l.at[k]))
        return copies

    def z_wait(copies):
        for copy in copies[:-1]:
            copy.wait_recv()
            sent.append(copy)
        copies[-1].wait()

    def g_start(k, stage):
        held = pl.ds(at.base(stage), 2**stage)
        return remote(
            w_out.at[k, held], w_out.at[k, held], g_s.at[k, stage], g_r.at[k, stage], at.across(stage)
        )

    ahead = 2
    tokens = [token_start(0, x_in, x_out)]
    z_copies = {k: z_start(k) for k in range(min(ahead, chunks))}
    stages = {}
    swaps = []
    for step in range(chunks + at.bits):
        if step < chunks:
            z_wait(z_copies[step])
            stages[step] = [g_start(step, 0)]
            if step + ahead < chunks:
                z_copies[step + ahead] = z_start(step + ahead)
            if step == 0:
                swaps.append(token_swap(0, tokens[0], x_out))
                tokens.append(token_start(1, dy_in, dy_out))
            if step == 1:
                swaps.append(token_swap(1, tokens[1], dy_out))
        for stage in range(1, at.bits + 1):
            k = step - stage
            if 0 <= k < chunks:
                stages[k][stage - 1].wait_recv()
                if stage < at.bits:
                    stages[k].append(g_start(k, stage))
    for swap in swaps:
        swap.wait()
    for k in range(chunks):
        for copy in stages[k]:
            copy.wait_send()
    for copy in sent:
        copy.wait_send()


def gather_all(depth_size, group, x_halves, dy_halves, weights):
    tp, rows, half = x_halves.shape
    chunks, _, depth_rows, width = weights.shape
    bits = group.bit_length() - 1
    dma = pltpu.SemaphoreType.DMA
    hbm = pl.BlockSpec(memory_space=pl.ANY)
    tokens = jax.ShapeDtypeStruct((depth_size * rows, tp * half), BF)
    return pl.pallas_call(
        functools.partial(gather_kernel, depth_size, group),
        out_shape=(
            tokens,
            tokens,
            jax.ShapeDtypeStruct((chunks, group, depth_size, depth_rows, width), BF),
        ),
        in_specs=[hbm] * 3,
        out_specs=(hbm, hbm, hbm),
        scratch_shapes=[
            dma((2, depth_size)),
            dma((2, depth_size)),
            dma((2,)),
            dma((2,)),
            dma((2,)),
            dma((chunks, depth_size)),
            dma((chunks, depth_size)),
            dma((chunks,)),
            dma((chunks, bits)),
            dma((chunks, bits)),
        ],
        compiler_params=pltpu.CompilerParams(collective_id=0, has_side_effects=True),
    )(x_halves, dy_halves, weights)


def share_kernel(depth_size, group, kv_in, kv_out, send, recv, loc):
    at = Place(depth_size, group)
    at.greet([at.across(stage) for stage in range(at.bits)])
    local(kv_in, kv_out.at[at.slot], loc).wait()
    copies = []
    for stage in range(at.bits):
        held = pl.ds(at.base(stage), 2**stage)
        copy = remote(kv_out.at[held], kv_out.at[held], send.at[stage], recv.at[stage], at.across(stage))
        copy.wait_recv()
        copies.append(copy)
    for copy in copies:
        copy.wait_send()


def share_group(depth_size, group, kv):
    bits = group.bit_length() - 1
    dma = pltpu.SemaphoreType.DMA
    hbm = pl.BlockSpec(memory_space=pl.ANY)
    return pl.pallas_call(
        functools.partial(share_kernel, depth_size, group),
        out_shape=jax.ShapeDtypeStruct((group,) + kv.shape, BF),
        in_specs=[hbm],
        out_specs=hbm,
        scratch_shapes=[dma((bits,)), dma((bits,)), dma],
        compiler_params=pltpu.CompilerParams(collective_id=1, has_side_effects=True),
    )(kv)


def fold_kernel(depth_size, group, g_in, total, landing, send, recv):
    at = Place(depth_size, group)
    at.greet([at.across(stage) for stage in range(at.bits)])
    for stage in reversed(range(at.bits)):
        size = 2**stage
        own = at.base(stage)
        other = own + (1 - 2 * at.bit(stage)) * size
        source = g_in if stage == at.bits - 1 else total
        copy = remote(
            source.at[pl.ds(other, size)],
            landing.at[pl.ds(size - 1, size)],
            send.at[stage],
            recv.at[stage],
            at.across(stage),
        )
        copy.wait()

        def add(i, _):
            total[own + i] = (
                source[own + i].astype(F32) + landing[size - 1 + i].astype(F32)
            ).astype(BF)
            return 0

        lax.fori_loop(0, size, add, 0)


def fold_group(depth_size, group, grads):
    bits = group.bit_length() - 1
    dma = pltpu.SemaphoreType.DMA
    vmem = pl.BlockSpec(memory_space=pltpu.VMEM)
    return pl.pallas_call(
        functools.partial(fold_kernel, depth_size, group),
        out_shape=jax.ShapeDtypeStruct(grads.shape, BF),
        in_specs=[vmem],
        out_specs=vmem,
        scratch_shapes=[
            pltpu.VMEM((group - 1,) + grads.shape[1:], BF),
            dma((bits,)),
            dma((bits,)),
        ],
        compiler_params=pltpu.CompilerParams(
            collective_id=2, has_side_effects=True, vmem_limit_bytes=60 << 20
        ),
    )(grads)


def reduce_kernel(depth_size, group, out_in, back_in, g_in, out_sum, back_sum, g_out, total, landing, g_s, g_r, z_s, z_r, z_l, t_acc, t_swap, t_land, tx_s, tx_r, tz_s, tz_r, ty_s, ty_r):
    at = Place(depth_size, group)
    at.greet(at.everyone())
    chunks = g_in.shape[0]
    depth_rows = g_in.shape[3]
    rows = out_sum.shape[0]
    half = t_acc.shape[2]
    last = at.bits - 1
    sent = []

    def g_start(k, stage):
        size = 2**stage
        other = at.base(stage) + (1 - 2 * at.bit(stage)) * size
        source = g_in.at[k] if stage == last else total.at[k]
        return remote(
            source.at[pl.ds(other, size)],
            landing.at[k, pl.ds(size - 1, size)],
            g_s.at[k, stage],
            g_r.at[k, stage],
            at.across(stage),
        )

    def g_finish(k, stage, copy):
        copy.wait_recv()
        sent.append(copy)
        size = 2**stage
        own = at.base(stage)
        source = g_in.at[k] if stage == last else total.at[k]

        def add(i, _):
            j = i // depth_size
            z = i % depth_size
            total[k, own + j, z] = (
                source[own + j, z].astype(F32) + landing[k, size - 1 + j, z].astype(F32)
            ).astype(BF)
            return 0

        lax.fori_loop(0, size * depth_size, add, 0)

    def z_start(k):
        copies = [
            remote(
                total.at[k, at.slot, lax.rem(at.depth + s, depth_size)],
                g_out.at[k, at.depth],
                z_s.at[k, s],
                z_r.at[k, s],
                at.along(s),
            )
            for s in range(1, depth_size)
        ]
        copies.append(local(total.at[k, at.slot, at.depth], g_out.at[k, at.depth], z_l.at[k]))
        return copies

    my_cols = pl.ds(pl.multiple_of(at.tp * half, half), half)
    her_cols = pl.ds(pl.multiple_of((1 - at.tp) * half, half), half)

    def token_first(i, src):
        return remote(src.at[:, her_cols], t_swap.at[i], tx_s.at[i], tx_r.at[i], at.twin())

    def token_second(i, src, copy):
        copy.wait_recv()
        sent.append(copy)

        def add(z, _):
            block = pl.ds(pl.multiple_of(z * rows, rows), rows)
            t_acc[i, block, :] = (
                src[block, my_cols].astype(F32) + t_swap[i, block, :].astype(F32)
            ).astype(BF)
            return 0

        lax.fori_loop(0, depth_size, add, 0)
        copies = []
        for s in range(1, depth_size):
            there = lax.rem(at.depth + s, depth_size)
            block = pl.ds(pl.multiple_of(there * rows, rows), rows)
            copies.append(
                remote(
                    t_acc.at[i, block, :], t_land.at[i, s - 1], tz_s.at[i, s], tz_r.at[i, s], at.along(s)
                )
            )
        return copies

    def token_third(i, dst, copies):
        for copy in copies:
            copy.wait_recv()
            sent.append(copy)
        mine = pl.ds(pl.multiple_of(at.depth * rows, rows), rows)
        value = t_acc[i, mine, :].astype(F32)
        for s in range(1, depth_size):
            value = value + t_land[i, s - 1].astype(F32)
        dst[:, my_cols] = value.astype(BF)
        return remote(dst.at[:, my_cols], dst.at[:, my_cols], ty_s.at[i], ty_r.at[i], at.twin())

    firsts = [token_first(0, out_in), token_first(1, back_in)]
    copies_of = {k: [g_start(k, last)] for k in range(chunks)}
    z_copies = {}
    seconds = []
    thirds = []
    for step in range(chunks + at.bits):
        for back in range(at.bits):
            k = step - back
            stage = last - back
            if 0 <= k < chunks:
                g_finish(k, stage, copies_of[k][back])
                if stage > 0:
                    copies_of[k].append(g_start(k, stage - 1))
                else:
                    z_copies[k] = z_start(k)
        if step == 1:
            seconds.append(token_second(0, out_in, firsts[0]))
        if step == 2:
            seconds.append(token_second(1, back_in, firsts[1]))
        if step == 4:
            thirds.append(token_third(0, out_sum, seconds[0]))
        if step == 5:
            thirds.append(token_third(1, back_sum, seconds[1]))
    for k in range(chunks):
        for copy in z_copies[k][:-1]:
            copy.wait()
        z_copies[k][-1].wait()
    for copy in thirds:
        copy.wait()
    for copy in sent:
        copy.wait_send()


def reduce_all(depth_size, group, out_part, back_part, grads):
    chunks, _, _, depth_rows, width = grads.shape
    all_rows, columns = out_part.shape
    rows = all_rows // depth_size
    half = columns // 2
    bits = group.bit_length() - 1
    dma = pltpu.SemaphoreType.DMA
    vmem = pl.BlockSpec(memory_space=pltpu.VMEM)
    tokens = jax.ShapeDtypeStruct((rows, columns), BF)
    return pl.pallas_call(
        functools.partial(reduce_kernel, depth_size, group),
        out_shape=(tokens, tokens, jax.ShapeDtypeStruct((chunks, depth_size, depth_rows, width), BF)),
        in_specs=[vmem] * 3,
        out_specs=(vmem, vmem, vmem),
        scratch_shapes=[
            pltpu.VMEM((chunks, group, depth_size, depth_rows, width), BF),
            pltpu.VMEM((chunks, group - 1, depth_size, depth_rows, width), BF),
            dma((chunks, bits)),
            dma((chunks, bits)),
            dma((chunks, depth_size)),
            dma((chunks, depth_size)),
            dma((chunks,)),
            pltpu.VMEM((2, all_rows, half), BF),
            pltpu.VMEM((2, all_rows, half), BF),
            pltpu.VMEM((2, depth_size - 1, rows, half), BF),
            dma((2,)),
            dma((2,)),
            dma((2, depth_size)),
            dma((2, depth_size)),
            dma((2,)),
            dma((2,)),
        ],
        compiler_params=pltpu.CompilerParams(
            collective_id=3, has_side_effects=True, vmem_limit_bytes=60 << 20
        ),
    )(out_part, back_part, grads)


def rotate(values, cosine, sine_table):
    half_rot = ROT // 2
    leading = values[..., :half_rot]
    trailing = values[..., half_rot:ROT]
    return jnp.concatenate(
        [
            leading * cosine - trailing * sine_table,
            trailing * cosine + leading * sine_table,
            values[..., ROT:],
        ],
        -1,
    )


def rope_tables(positions):
    freqs = 10000.0 ** (-(2.0 * jnp.arange(ROT // 2, dtype=F32)) / ROT)
    angles = positions.astype(F32)[:, None] * freqs[None, :]
    return (jnp.cos(angles), jnp.sin(angles))


def gelu_parts(values):
    gate = 0.5 * (1.0 + lax.erf(values * math.sqrt(0.5)))
    slope = gate + values * jnp.exp(-0.5 * values * values) * (1.0 / math.sqrt(2.0 * math.pi))
    return values * gate, slope


SMALL_ROWS = 96
VMEM_BYTES = 64 << 20


def slot_member(slot, bits):
    member = 0
    for stage in range(bits):
        member += ((slot >> stage) & 1) << (bits - 1 - stage)
    return member


def natural_blocks(depth_size, group):
    bits = group.bit_length() - 1
    return [
        depth * group + slot_member(slot, bits) for slot in range(group) for depth in range(depth_size)
    ]

ROW_TILE = 256
DROP = -1e30


def layout_of(depth_size, group, depth_rows, rows, width, ff_chunks):
    tokens = depth_size * rows
    half = width // 2
    landing = (group - 1) * depth_size * depth_rows
    heads = 3 + ff_chunks
    cols = 1 + ff_chunks
    return [
        ("wr", (heads, width, CHUNK), BF),
        ("wc", (cols, CHUNK, width), BF),
        ("gr", (heads, width, CHUNK), BF),
        ("gc", (cols, CHUNK, width), BF),
        ("lr", (heads, landing, CHUNK), BF),
        ("lc", (cols, CHUNK, landing), BF),
        ("x", (tokens, width), BF),
        ("dy", (tokens, width), BF),
        ("na", (tokens, width), BF),
        ("nm", (tokens, width), BF),
        ("nmt", (width, tokens), BF),
        ("kv", (group * tokens, 2 * HD), BF),
        ("q", (tokens, HD), BF),
        ("low", (tokens, 3 * HD), BF),
        ("al", (tokens, HD), BF),
        ("hg", (tokens, HD), BF),
        ("alt", (HD, tokens), BF),
        ("att", (HD, tokens), F32),
        ("dqt", (HD, tokens), F32),
        ("stat", (8, tokens), F32),
        ("tab", (group * tokens, 128), F32),
        ("kb", (8, HD), F32),
        ("hid", (ff_chunks, tokens, CHUNK), BF),
        ("ul", (ff_chunks, tokens, CHUNK), BF),
        ("tz", (2, 2, tokens // 2, half // 2), BF),
        ("te", (2, rows, half), BF),
        ("mean", (tokens, 1), F32),
        ("inv", (tokens, 1), F32),
        ("gv", (8, width), F32),
        ("biases", (8, HD), F32),
        ("places", (group * tokens // 128, 128), F32),
        ("ps", (group.bit_length(), SMALL_ROWS, 128), F32),
        ("pl", (group.bit_length() - 1, SMALL_ROWS, 128), F32),
        ("pz", (depth_size, SMALL_ROWS, 128), F32),
        ("px", (2, SMALL_ROWS, 128), F32),
    ]


def semaphores_of(depth_size, group, items):
    bits = group.bit_length() - 1
    return [
        ("z_s", (items, depth_size)),
        ("z_r", (items, depth_size)),
        ("z_l", (items,)),
        ("g_s", (items, bits)),
        ("g_r", (items, bits)),
        ("t_s", (2, 3)),
        ("t_r", (2, 3)),
        ("w_s", (2, 3)),
        ("w_r", (2, 3)),
        ("kv_s", (2, 2, bits)),
        ("kv_r", (2, 2, bits)),
        ("f_s", (items, bits)),
        ("f_r", (items, bits)),
        ("e_s", (items, depth_size)),
        ("e_r", (items, depth_size)),
        ("e_l", (items,)),
        ("o_s", (2, 6)),
        ("o_r", (2, 6)),
        ("p_s", (bits + depth_size,)),
        ("p_r", (bits + depth_size,)),
    ]


VECTORS = ("attn_gain", "attn_shift", "mlp_gain", "mlp_shift")
BIASES = ("b_query", "b_key", "b_value", "b_up")
INPUTS = ("blocks", "x_in", "dy_in", "freqs") + VECTORS + BIASES
INPUTS += ("w_query", "w_key", "w_value", "w_out", "w_up", "w_down")
OUTPUTS = ("fin", "g_query", "g_key", "g_value", "g_out", "g_up", "g_down")
OUTPUTS += ("norm_sums", "s_query", "s_key", "s_value", "s_up", "s_dy")


class Bag:
    pass


def fused_kernel(names, depth_size, group, *refs):
    m = Bag()
    for name, ref in zip(names, refs, strict=True):
        setattr(m, name, ref)
    at = Place(depth_size, group)
    at.greet(at.everyone())
    bits = at.bits
    rows, width = m.x_in.shape
    depth_rows = width // (depth_size * group)
    tokens = depth_size * rows
    half = width // 2
    ff_width = m.w_up.shape[1] // depth_size
    ff_chunks = ff_width // CHUNK
    block_count = width // depth_rows
    own_block = at.slot * depth_size + at.depth
    natural = natural_blocks(depth_size, group)
    sends, settled = [], []

    def blocks(first, count):
        return pl.ds(pl.multiple_of(first * depth_rows, depth_rows), count * depth_rows)

    def token_rows(depth):
        return pl.ds(pl.multiple_of(depth * rows, rows), rows)

    def peer(step):
        return lax.rem(at.depth + step, depth_size)

    my_cols = pl.ds(pl.multiple_of(at.tp * half, half), half)
    her_cols = pl.ds(pl.multiple_of((1 - at.tp) * half, half), half)

    units = [("r", 0), ("r", 1), ("r", 2), ("c", 0)]
    for i in range(ff_chunks):
        units += [("r", 3 + i), ("c", 1 + i)]
    row_pairs = [(m.w_query, m.g_query), (m.w_key, m.g_key), (m.w_value, m.g_value)]

    def outer(kind, a, depth, which):
        if kind == "r" and a < 3:
            return row_pairs[a][which].at[:, pl.ds(pl.multiple_of(depth * HD, HD), HD)]
        if kind == "r":
            first = pl.multiple_of(depth * ff_width + (a - 3) * CHUNK, CHUNK)
            return (m.w_up, m.g_up)[which].at[:, pl.ds(first, CHUNK)]
        if a == 0:
            return (m.w_out, m.g_out)[which].at[pl.ds(pl.multiple_of(depth * HD, HD), HD), :]
        first = pl.multiple_of(depth * ff_width + (a - 1) * CHUNK, CHUNK)
        return (m.w_down, m.g_down)[which].at[pl.ds(first, CHUNK), :]

    def part(pair, kind, a, first, count):
        if kind == "r":
            return pair[0].at[a, blocks(first, count), :]
        return pair[1].at[a, :, blocks(first, count)]

    weights, grads, landing = (m.wr, m.wc), (m.gr, m.gc), (m.lr, m.lc)

    def z_start(k):
        kind, a = units[k]
        into = part(weights, kind, a, own_block, 1)
        copies = [
            remote(outer(kind, a, peer(s), 0), into, m.z_s.at[k, s], m.z_r.at[k, s], at.along(s))
            for s in range(1, depth_size)
        ]
        copies.append(local(outer(kind, a, at.depth, 0), into, m.z_l.at[k]))
        return copies

    def z_wait(copies):
        received(copies[:-1])
        copies[-1].wait()

    def g_start(k, stage):
        kind, a = units[k]
        held = part(weights, kind, a, at.base(stage) * depth_size, 2**stage * depth_size)
        return [remote(held, held, m.g_s.at[k, stage], m.g_r.at[k, stage], at.across(stage))]

    def received(copies):
        for copy in copies:
            copy.wait_recv()
        sends.extend(copies)

    def settle(copies):
        for copy in copies:
            copy.wait_send()
        settled.extend(copies)

    def fold_start(k, stage):
        kind, a = units[k]
        size = 2**stage
        other = at.base(stage) + (1 - 2 * at.bit(stage)) * size
        return [
            remote(
                part(grads, kind, a, other * depth_size, size * depth_size),
                part(landing, kind, a, (size - 1) * depth_size, size * depth_size),
                m.f_s.at[k, stage],
                m.f_r.at[k, stage],
                at.across(stage),
            )
        ]

    def fold_finish(k, stage, copies):
        received(copies)
        kind, a = units[k]
        size = 2**stage
        own = at.base(stage) * depth_size

        def add(i, _):
            mine = blocks(own + i, 1)
            theirs = blocks((size - 1) * depth_size + i, 1)
            if kind == "r":
                total = m.gr[a, mine, :].astype(F32) + m.lr[a, theirs, :].astype(F32)
                m.gr[a, mine, :] = total.astype(BF)
            else:
                total = m.gc[a, :, mine].astype(F32) + m.lc[a, :, theirs].astype(F32)
                m.gc[a, :, mine] = total.astype(BF)
            return 0

        lax.fori_loop(0, size * depth_size, add, 0)

    def end_start(k):
        kind, a = units[k]
        into = outer(kind, a, at.depth, 1)
        copies = [
            remote(
                part(grads, kind, a, at.slot * depth_size + peer(s), 1),
                into,
                m.e_s.at[k, s],
                m.e_r.at[k, s],
                at.along(s),
            )
            for s in range(1, depth_size)
        ]
        copies.append(local(part(grads, kind, a, own_block, 1), into, m.e_l.at[k]))
        return copies

    near = {"ctx": at.ctx + (1 - 2 * (at.depth % 2)) * group}
    far = {"ctx": at.ctx + (2 - 4 * (at.depth // 2)) * group}
    near_depth = at.depth + 1 - 2 * (at.depth % 2)
    pair_first = at.depth // 2 * 2
    my_pair = pl.ds(pl.multiple_of(pair_first * rows, rows), 2 * rows)
    her_pair = pl.ds(pl.multiple_of((2 - pair_first) * rows, rows), 2 * rows)
    quarter = half // 2
    my_quarter = pl.ds(pl.multiple_of(at.tp * half + at.depth % 2 * quarter, quarter), quarter)
    her_quarter = pl.ds(pl.multiple_of(at.tp * half + (1 - at.depth % 2) * quarter, quarter), quarter)

    def token_step(i, buffer, step, copies):
        if copies:
            received(copies[-1:])
        brought = [
            None,
            (token_rows(near_depth), my_cols),
            (her_pair, my_quarter),
            (her_pair, her_quarter),
        ]
        given = [(token_rows(at.depth), my_cols), (my_pair, my_quarter), (her_pair, my_quarter)]
        if step < 3:
            piece = buffer.at[given[step][0], given[step][1]]
            there = far if step == 1 else near
            copies.append(remote(piece, piece, m.t_s.at[i, step], m.t_r.at[i, step], there))
        if step:
            piece = buffer.at[brought[step][0], brought[step][1]]
            swapped[i].append(
                remote(piece, piece, m.w_s.at[i, step - 1], m.w_r.at[i, step - 1], at.twin())
            )
        return copies

    def kv_start(h, stage):
        size = 2**stage * tokens
        rows_held = pl.ds(pl.multiple_of(at.base(stage) * tokens, tokens), size)
        held = m.kv.at[rows_held, slice(h * HD, (h + 1) * HD)]
        return remote(held, held, m.kv_s.at[0, h, stage], m.kv_r.at[0, h, stage], at.across(stage))

    spare = (m.lr.at[1 + ff_chunks], m.lr.at[2 + ff_chunks])

    def dkv_start(stage):
        size = 2**stage
        other = at.base(stage) + (1 - 2 * at.bit(stage)) * size
        given = pl.ds(pl.multiple_of(other * tokens, tokens), size * tokens)
        taken = pl.ds((size - 1) * tokens, size * tokens)
        return [
            remote(
                m.kv.at[given, slice(h * HD, (h + 1) * HD)],
                spare[h].at[taken, :],
                m.kv_s.at[1, h, stage],
                m.kv_r.at[1, h, stage],
                at.across(stage),
            )
            for h in range(2)
        ]

    def dkv_finish(stage, copies):
        received(copies)
        size = 2**stage
        own = at.base(stage) * tokens
        step = ROW_TILE

        def add(i, _):
            mine = pl.ds(pl.multiple_of(own + i * step, step), step)
            theirs = pl.ds(pl.multiple_of((size - 1) * tokens + i * step, step), step)
            for h in range(2):
                cols = slice(h * HD, (h + 1) * HD)
                total = m.kv[mine, cols].astype(F32) + spare[h][theirs, :].astype(F32)
                m.kv[mine, cols] = total.astype(BF)
            return 0

        lax.fori_loop(0, size * tokens // step, add, 0)

    lane = lax.broadcasted_iota(jnp.int32, (1, 128), 1)

    def place_rows():
        mine = token_rows(at.depth)
        for b in range(block_count):
            c = natural[b]
            into = slice(b * depth_rows, (b + 1) * depth_rows)
            out_of = slice(c * depth_rows, (c + 1) * depth_rows)
            m.x[mine, into] = m.x_in[:, out_of]
            m.dy[mine, into] = m.dy_in[:, out_of]

    def place_vectors():
        m.ps[0] = jnp.zeros_like(m.ps[0])
        for row, name in enumerate(VECTORS):
            for b in range(block_count):
                c = natural[b]
                m.gv[row : row + 1, b * depth_rows : (b + 1) * depth_rows] = getattr(m, name)[c : c + 1, :]
        per_head = HD // 128
        for a in range(3):
            for h in range(per_head):
                row = getattr(m, BIASES[a])[pl.ds(at.depth * per_head + h, 1), :]
                m.biases[a : a + 1, h * 128 : (h + 1) * 128] = row
        for i in range(ff_chunks):
            for h in range(per_head):
                row = m.b_up[pl.ds((at.depth * ff_chunks + i) * per_head + h, 1), :]
                m.biases[3 + i : 4 + i, h * 128 : (h + 1) * 128] = row
        block_rows = rows // 2
        for n in range(group * depth_size):
            c = natural[n]
            first = jnp.where(lane < block_rows, m.blocks[2 * c], m.blocks[2 * c + 1])
            m.places[n : n + 1, :] = (first * block_rows + lane % block_rows).astype(F32)

    def affine():
        step = 32

        def stats(i, _):
            here = pl.ds(pl.multiple_of(i * step, step), step)
            x = m.x[here, :].astype(F32)
            mean = jnp.mean(x, -1, keepdims=True)
            centered = x - mean
            m.mean[here, :] = mean
            m.inv[here, :] = lax.rsqrt(jnp.mean(centered * centered, -1, keepdims=True) + norm_epsilon)
            return 0

        lax.fori_loop(0, tokens // step, stats, 0)

        def body(i, _):
            here = token_rows(i)
            for n in range(width // 512):
                cols = slice(n * 512, (n + 1) * 512)
                normal = (m.x[here, cols].astype(F32) - m.mean[here, :]) * m.inv[here, :]
                m.na[here, cols] = (normal * m.gv[0:1, cols] + m.gv[1:2, cols]).astype(BF)
                mlp = normal * m.gv[2:3, cols] + m.gv[3:4, cols]
                m.nm[here, cols] = mlp.astype(BF)
                m.nmt[cols, here] = mlp.T.astype(BF)
            return 0

        lax.fori_loop(0, depth_size, body, 0)

    def place_column(n):
        return jnp.broadcast_to(m.places[pl.ds(n, 1), :], (128, 128)).T

    def make_tables():
        def body(n, _):
            angles = place_column(n) * m.freqs[0:1, :]
            here = pl.ds(pl.multiple_of(n * 128, 128), 128)
            m.tab[here, :] = jnp.cos(angles - jnp.where(lane < ROT, 0.0, math.pi / 2))
            return 0

        lax.fori_loop(0, group * tokens // 128, body, 0)

    def turned(value, here, sign):
        head = value[:, :128]
        left = pltpu.roll(head, 128 - ROT // 2, 1)
        right = pltpu.roll(head, ROT // 2, 1)
        table = m.tab[here, :]
        cosine = jnp.where(lane < ROT, table, 1.0)
        sine = sign * pltpu.roll(table, ROT, 1)
        crossed = jnp.where(lane < ROT // 2, -left, jnp.where(lane < ROT, right, 0.0))
        return head * cosine + crossed * sine

    def project(a):
        return mm(m.na[...], m.wr[a]) + m.biases[a : a + 1, :]

    kv_own = pl.ds(pl.multiple_of(at.slot * tokens, tokens), tokens)
    score_scale = 1.0 / math.sqrt(HD)

    def make_query():
        query = project(0)
        m.q[:, :128] = turned(query, kv_own, 1.0).astype(BF)
        m.q[:, 128:] = query[:, 128:].astype(BF)

    def make_keys():
        keys = project(1)
        m.kv[kv_own, :128] = turned(keys, kv_own, 1.0).astype(BF)
        m.kv[kv_own, 128:HD] = keys[:, 128:].astype(BF)

    def make_values():
        m.kv[kv_own, HD:] = project(2).astype(BF)

    def key_rows(j):
        return pl.ds(pl.multiple_of(j * tokens, tokens), tokens)

    def masked_scores(j):
        scores = mm_nt(m.kv[key_rows(j), :HD], m.q[...]) * score_scale
        count = tokens // 128
        column = jnp.concatenate([place_column(j * count + n)[:, :1] for n in range(count)], 0)
        row = jnp.concatenate([m.places[pl.ds(at.slot * count + n, 1), :] for n in range(count)], 1)
        return jnp.where(column <= row, scores, DROP)

    def attend(j):
        scores = masked_scores(j)
        if j == 0:
            old = jnp.full((1, tokens), -1e20, F32)
        else:
            old = m.stat[0:1, :]
        new = jnp.maximum(old, jnp.max(scores, 0, keepdims=True))
        raw = jnp.exp(scores - new)
        total = jnp.sum(raw, 0, keepdims=True)
        value = mm(m.kv[key_rows(j), HD:].T, raw.astype(BF))
        m.stat[0:1, :] = new
        if j:
            factor = jnp.exp(old - new)
            total = total + m.stat[1:2, :] * factor
            value = value + m.att[...] * factor
        m.stat[1:2, :] = total
        m.att[...] = value
        if j == group - 1:
            m.stat[2:3, :] = new + jnp.log(total)
            value = value / total
            m.att[...] = value
            m.alt[...] = value.astype(BF)
            m.al[...] = value.T.astype(BF)

    def head_grads():
        grad = mm_nt(m.dy[...], m.wc[0])
        low = grad.astype(BF)
        m.hg[...] = low
        m.stat[3:4, :] = jnp.sum(low.astype(F32).T * m.att[...], 0, keepdims=True)

    def attend_back(j):
        probs = jnp.exp(masked_scores(j) - m.stat[2:3, :])
        value_part = mm(probs.astype(BF), m.hg[...])
        prob_grad = mm_nt(m.kv[key_rows(j), HD:], m.hg[...])
        score_grad = (probs * (prob_grad - m.stat[3:4, :]) * score_scale).astype(BF)
        query_part = mm(m.kv[key_rows(j), :HD].T, score_grad)
        key_part = mm(score_grad, m.q[...])
        head_sum = jnp.sum(turned(key_part, key_rows(j), -1.0), 0, keepdims=True)
        rest_sum = jnp.sum(key_part[:, 128:], 0, keepdims=True)
        if j:
            query_part = query_part + m.dqt[...]
            head_sum = head_sum + m.kb[0:1, :128]
            rest_sum = rest_sum + m.kb[0:1, 128:]
        m.dqt[...] = query_part
        m.kb[0:1, :128] = head_sum
        m.kb[0:1, 128:] = rest_sum
        m.kv[key_rows(j), :HD] = key_part.astype(BF)
        m.kv[key_rows(j), HD:] = value_part.astype(BF)

    def small_store(first, row):
        for n in range(row.shape[1] // 128):
            m.ps[0, first + n : first + n + 1, :] = row[:, n * 128 : (n + 1) * 128]

    def attention_grads():
        query = m.dqt[...].T
        head = turned(query, kv_own, -1.0)
        keys = m.kv[kv_own, :HD].astype(F32)
        key_head = turned(keys, kv_own, -1.0)
        m.low[:, :128] = head.astype(BF)
        m.low[:, 128:HD] = query[:, 128:].astype(BF)
        m.low[:, HD : HD + 128] = key_head.astype(BF)
        m.low[:, HD + 128 : 2 * HD] = m.kv[kv_own, 128:HD]
        m.low[:, 2 * HD :] = m.kv[kv_own, HD:]
        small_store(64, jnp.sum(head, 0, keepdims=True))
        small_store(65, jnp.sum(query[:, 128:], 0, keepdims=True))
        small_store(66, m.kb[0:1, :])
        small_store(68, jnp.sum(m.kv[kv_own, HD:].astype(F32), 0, keepdims=True))

        def body(n, _):
            tile = pl.ds(pl.multiple_of(n * ROW_TILE, ROW_TILE), ROW_TILE)
            turned_in = m.na[:, tile].T
            for a in range(3):
                m.gr[a, tile, :] = mm(turned_in, m.low[:, a * HD : (a + 1) * HD]).astype(BF)
            return 0

        lax.fori_loop(0, width // ROW_TILE, body, 0)

    def out_grads():
        def body(n, _):
            tile = pl.ds(pl.multiple_of(n * 512, 512), 512)
            m.gc[0, :, tile] = mm(m.alt[...], m.dy[:, tile]).astype(BF)
            return 0

        lax.fori_loop(0, width // 512, body, 0)

    def feed_forward(i):
        activated, slope = gelu_parts(mm(m.nm[...], m.wr[3 + i]) + m.biases[3 + i : 4 + i, :])
        m.hid[i] = activated.astype(BF)
        up_grad = mm_nt(m.dy[...], m.wc[1 + i]) * slope
        small_store(70 + 2 * i, jnp.sum(up_grad, 0, keepdims=True))
        m.ul[i] = up_grad.astype(BF)
        turned_hidden = activated.T.astype(BF)

        def body(n, _):
            tile = pl.ds(pl.multiple_of(n * 512, 512), 512)
            m.gr[3 + i, tile, :] = mm(m.nmt[tile, :], m.ul[i]).astype(BF)
            m.gc[1 + i, :, tile] = mm(turned_hidden, m.dy[:, tile]).astype(BF)
            return 0

        lax.fori_loop(0, width // 512, body, 0)

    out, back = m.na, m.dy

    def tile_of(n):
        return pl.ds(pl.multiple_of(n * ROW_TILE, ROW_TILE), ROW_TILE)

    def small_add_rows(first, n, value):
        row = jnp.sum(value, 0, keepdims=True)
        for h in range(ROW_TILE // 128):
            m.ps[0, pl.ds(first + n * (ROW_TILE // 128) + h, 1), :] = row[:, h * 128 : (h + 1) * 128]

    def end_out(n):
        tile = tile_of(n)
        total = mm(m.al[...], m.wc[0, :, tile])
        for i in range(ff_chunks):
            total += mm(m.hid[i], m.wc[1 + i, :, tile])
        out[:, tile] = total.astype(BF)

    def end_back(n):
        tile = tile_of(n)
        attn_back = mm_nt(m.low[:, :HD], m.wr[0, tile, :])
        for a in (1, 2):
            attn_back += mm_nt(m.low[:, a * HD : (a + 1) * HD], m.wr[a, tile, :])
        mlp_back = mm_nt(m.ul[0], m.wr[3, tile, :])
        for i in range(1, ff_chunks):
            mlp_back += mm_nt(m.ul[i], m.wr[3 + i, tile, :])
        normal = (m.x[:, tile].astype(F32) - m.mean[...]) * m.inv[...]
        small_add_rows(0, n, attn_back * normal)
        small_add_rows(16, n, attn_back)
        small_add_rows(32, n, mlp_back * normal)
        small_add_rows(48, n, mlp_back)
        small_add_rows(78, n, m.dy[:, tile].astype(F32))
        back[:, tile] = (attn_back * m.gv[0:1, tile] + mlp_back * m.gv[2:3, tile]).astype(BF)

    def end_quarter(piece, which, n):
        count = quarter // ROW_TILE
        odd = at.depth % 2
        first = which * 2 + (odd if n else 1 - odd)

        def body(i, _):
            piece(first * count + i)
            return 0

        lax.fori_loop(0, count, body, 0)

    ends = (out, back)

    def quarter_of(which, n):
        odd = at.depth % 2
        return pl.ds(pl.multiple_of(which * half + (odd if n else 1 - odd) * quarter, quarter), quarter)

    def offer():
        pl.semaphore_signal(m.free, inc=1, device_id=at.twin(), device_id_type=MESH)

    def sum_start(i, n):
        if i == n == 0:
            pl.semaphore_wait(m.free, 1)
        return remote(
            ends[i].at[:, quarter_of(1 - at.tp, n)],
            m.nm.at[:, quarter_of(i, n)],
            m.o_s.at[i, n],
            m.o_r.at[i, n],
            at.twin(),
        )

    def sum_add(i, n):
        mine = ends[i]
        into, source = quarter_of(at.tp, n), quarter_of(i, n)

        def add(z, _):
            block = token_rows(z)
            total = mine[block, into].astype(F32) + m.nm[block, source].astype(F32)
            mine[block, into] = total.astype(BF)
            return 0

        lax.fori_loop(0, depth_size, add, 0)

    def sum_step(i, step, copy):
        received([copy])
        mine = ends[i]
        if step == 0:
            sum_add(i, 0)
            source, into, there = mine.at[her_pair, her_quarter], m.tz.at[i, 0], near
        elif step == 1:
            total = mine[her_pair, my_quarter].astype(F32) + m.tz[i, 0].astype(F32)
            mine[her_pair, my_quarter] = total.astype(BF)
            source, into, there = mine.at[her_pair, my_quarter], m.tz.at[i, 1], far
        elif step == 2:
            total = mine[my_pair, my_quarter].astype(F32) + m.tz[i, 1].astype(F32)
            mine[my_pair, my_quarter] = total.astype(BF)
            source, into, there = mine.at[token_rows(near_depth), my_cols], m.te.at[i], near
        else:
            total = mine[token_rows(at.depth), my_cols].astype(F32) + m.te[i].astype(F32)
            m.fin[i, :, my_cols] = total.astype(BF)
            source, into, there = m.fin.at[i, :, my_cols], m.fin.at[i, :, my_cols], at.twin()
        return remote(source, into, m.o_s.at[i, 2 + step], m.o_r.at[i, 2 + step], there)

    def small_group(stage):
        return remote(m.ps.at[stage], m.pl.at[stage], m.p_s.at[stage], m.p_r.at[stage], at.across(stage))

    def small_add(stage, copy):
        received([copy])
        m.ps[stage + 1] = m.ps[stage] + m.pl[stage]

    def small_depth():
        total = m.ps.at[bits]
        copies = [
            remote(total, m.pz.at[at.depth], m.p_s.at[bits + s], m.p_r.at[bits + s], at.along(s))
            for s in range(1, depth_size)
        ]
        m.pz[at.depth] = m.ps[bits]
        return copies

    def small_twin(copies):
        received(copies)
        value = m.pz[0]
        for z in range(1, depth_size):
            value = value + m.pz[z]
        m.px[0] = value
        return remote(m.px.at[0], m.px.at[1], m.p_s.at[bits], m.p_r.at[bits], at.twin())

    def small_finish(copy):
        received([copy])
        for v in range(4):
            for b in range(block_count):
                row = v * 16 + b
                into = v * 16 + natural[b]
                m.norm_sums[into : into + 1, :] = m.px[0, row : row + 1, :] + m.px[1, row : row + 1, :]
        for b in range(block_count):
            m.s_dy[natural[b] : natural[b] + 1, :] = m.ps[bits, 78 + b : 79 + b, :]
        for z in range(depth_size):
            m.s_query[2 * z : 2 * z + 2, :] = m.pz[z, 64:66, :]
            m.s_key[2 * z : 2 * z + 2, :] = m.pz[z, 66:68, :]
            m.s_value[2 * z : 2 * z + 2, :] = m.pz[z, 68:70, :]
            m.s_up[8 * z : 8 * z + 8, :] = m.pz[z, 70:78, :]

    z_live, g_live, t_live, k_live, f_live, e_live, x_live, s_live, d_live, p_live = ({} for _ in range(10))
    swapped = {0: [], 1: []}
    buffers = (m.x, m.dy)

    def do_zs(n):
        z_live[n] = z_start(n)

    def do_zy(n):
        z_wait(z_live[n])
        g_live[n] = g_start(n, 0)

    def do_yc(n):
        received(g_live[n])
        g_live[n] = g_start(n, 1)

    def do_cw(n):
        received(g_live[n])

    def do_ta(n):
        t_live[n] = token_step(n, buffers[n], 0, [])

    def do_tb(n):
        token_step(n, buffers[n], 1, t_live[n])

    def do_tc(n):
        token_step(n, buffers[n], 2, t_live[n])

    def do_td(n):
        token_step(n, buffers[n], 3, t_live[n])

    def do_te(n):
        received(swapped[n])

    do_norm, do_vec, do_tab, do_aff = place_rows, place_vectors, make_tables, affine
    do_qq, do_kk, do_val, do_hg = make_query, make_keys, make_values, head_grads
    do_at, do_ag, do_go, do_ff, do_of = attend, attention_grads, out_grads, feed_forward, offer

    def do_ky(n):
        k_live[n] = [kv_start(n, 0)]

    def do_kc(n):
        received(k_live[n])
        k_live[n].append(kv_start(n, 1))

    def do_kw(n):
        received(k_live[n][1:])

    def do_bw(n):
        if n == 0:
            settle(k_live[0] + k_live[1])
        attend_back(n)

    def do_dc():
        d_live[1] = dkv_start(1)

    def do_dy():
        dkv_finish(1, d_live[1])
        d_live[0] = dkv_start(0)

    def do_dw():
        dkv_finish(0, d_live[0])

    def do_fc(n):
        f_live[n] = fold_start(n, 1)

    def do_fy(n):
        fold_finish(n, 1, f_live[n])
        f_live[n] = fold_start(n, 0)

    def do_fz(n):
        fold_finish(n, 0, f_live[n])
        e_live[n] = end_start(n)

    def do_ew(n):
        received(e_live[n][:-1])
        e_live[n][-1].wait()

    def do_eo(n):
        end_quarter(end_out, at.tp if n >= 2 else 1 - at.tp, n % 2)

    def do_eb(n):
        if n == 0:
            settle(t_live[1] + swapped[1])
        end_quarter(end_back, at.tp if n >= 2 else 1 - at.tp, n % 2)

    def do_sx(n):
        x_live[n] = sum_start(n // 2, n % 2)

    def do_sa(n):
        s_live[n] = sum_step(n, 0, x_live[2 * n])

    def do_sm(n):
        received([x_live[2 * n + 1]])
        sum_add(n, 1)

    def do_sb(n):
        s_live[n] = sum_step(n, 1, s_live[n])

    def do_sc(n):
        s_live[n] = sum_step(n, 2, s_live[n])

    def do_sd(n):
        s_live[n] = sum_step(n, 3, s_live[n])

    def do_sw(n):
        received([s_live[n]])

    def do_pa():
        p_live[0] = small_group(0)

    def do_pb():
        small_add(0, p_live[0])
        p_live[1] = small_group(1)

    def do_pc():
        small_add(1, p_live[1])
        p_live[2] = small_depth()

    def do_pd():
        p_live[3] = small_twin(p_live[2])

    def do_pe():
        small_finish(p_live[3])

    do_zs(1)
    do_vec()
    do_zs(6)
    do_zs(4)
    do_zy(1)
    do_norm()
    do_ta(0)
    do_zy(6)
    do_zs(7)
    do_zs(5)
    do_tb(0)
    do_zs(2)
    do_yc(1)
    do_ta(1)
    do_zs(3)
    do_zy(4)
    do_tab()
    do_zy(5)
    do_zy(7)
    do_yc(5)
    do_tc(0)
    do_zs(9)
    do_cw(1)
    do_yc(7)
    do_zy(2)
    do_zs(0)
    do_zy(3)
    do_td(0)
    do_yc(2)
    do_cw(2)
    do_tb(1)
    do_zy(9)
    do_yc(6)
    do_te(0)
    do_zs(8)
    do_zy(0)
    do_aff()
    do_kk()
    do_ky(0)
    do_val()
    do_ky(1)
    do_yc(0)
    do_yc(4)
    do_tc(1)
    do_yc(3)
    do_cw(3)
    do_zs(11)
    do_kc(0)
    do_zy(8)
    do_cw(0)
    do_cw(4)
    do_yc(9)
    do_td(1)
    do_zs(10)
    do_kc(1)
    do_qq()
    do_zy(11)
    do_kw(1)
    do_cw(7)
    do_kw(0)
    do_cw(6)
    do_at(0)
    do_cw(9)
    do_at(1)
    do_at(2)
    do_yc(8)
    do_at(3)
    do_te(1)
    do_ff(1)
    do_fc(6)
    do_fc(7)
    do_zy(10)
    do_hg()
    do_bw(0)
    do_cw(8)
    do_bw(1)
    do_bw(2)
    do_bw(3)
    do_dc()
    do_cw(5)
    do_fy(7)
    do_go()
    do_fc(3)
    do_yc(10)
    do_ff(0)
    do_dy()
    do_fz(7)
    do_ff(2)
    do_yc(11)
    do_fc(4)
    do_cw(10)
    do_fy(3)
    do_cw(11)
    do_ff(3)
    do_dw()
    do_of()
    do_fy(6)
    do_fc(9)
    do_ag()
    do_eo(0)
    do_fz(3)
    do_sx(0)
    do_fc(0)
    do_eb(0)
    do_eb(1)
    do_fy(9)
    do_fc(2)
    do_fz(6)
    do_fy(0)
    do_fc(8)
    do_eb(2)
    do_sx(2)
    do_fc(5)
    do_eo(2)
    do_fy(4)
    do_fz(9)
    do_sx(3)
    do_fc(10)
    do_fz(0)
    do_fy(5)
    do_fz(4)
    do_fc(11)
    do_sa(1)
    do_fy(11)
    do_eb(3)
    do_pa()
    do_fz(5)
    do_eo(3)
    do_sm(1)
    do_fc(1)
    do_pb()
    do_eo(1)
    do_sb(1)
    do_sx(1)
    do_sa(0)
    do_fy(8)
    do_fy(1)
    do_fz(11)
    do_ew(4)
    do_fz(1)
    do_fy(2)
    do_ew(9)
    do_sm(0)
    do_ew(5)
    do_fy(10)
    do_sb(0)
    do_pc()
    do_fz(8)
    do_sc(1)
    do_ew(7)
    do_sc(0)
    do_ew(0)
    do_ew(11)
    do_fz(2)
    do_ew(3)
    do_fz(10)
    do_sd(1)
    do_sd(0)
    do_pd()
    do_pe()
    do_sw(0)
    do_ew(8)
    do_sw(1)
    do_ew(2)
    do_ew(10)
    do_ew(1)
    do_ew(6)
    for copy in sends:
        if not any(copy is other for other in settled):
            copy.wait_send()


def fits(depth_size, group, depth_rows, rows, width, ff_chunks):
    sizes = layout_of(depth_size, group, depth_rows, rows, width, ff_chunks)
    total = sum(math.prod(shape) * jnp.dtype(kind).itemsize for _, shape, kind in sizes)
    shaped = group == depth_size == ff_chunks == 4 and depth_rows == rows == 128
    return shaped and total < VMEM_BYTES


def fused_shards(
    layer_input,
    block_order,
    attn_gain,
    attn_shift,
    mlp_gain,
    mlp_shift,
    w_query,
    b_query,
    w_key,
    b_key,
    w_value,
    b_value,
    w_out,
    b_out,
    w_up,
    b_up,
    w_down,
    b_down,
    out_grad,
):
    rows, width = layer_input.shape
    tp_size = lax.axis_size("tp")
    depth_size = HEADS // tp_size
    group = lax.axis_size("ctx") // depth_size
    depth_rows = width // (depth_size * group)
    ff_width = w_up.shape[1] // depth_size
    ff_chunks = ff_width // CHUNK
    tokens = depth_size * rows
    at = Place(depth_size, group)

    freqs = (10000.0 ** (-(2.0 * np.arange(ROT // 2, dtype=np.float32)) / ROT)).astype(np.float32)
    freqs = np.tile(freqs, (8, 128 // (ROT // 2)))

    def in_rows(vector):
        return vector.reshape(-1, 128)

    buffers = layout_of(depth_size, group, depth_rows, rows, width, ff_chunks)
    semaphores = semaphores_of(depth_size, group, 4 + 2 * ff_chunks)
    names = tuple(INPUTS) + tuple(OUTPUTS) + tuple(b[0] for b in buffers) + tuple(s[0] for s in semaphores) + ("free",)
    vmem = pl.BlockSpec(memory_space=pltpu.VMEM)
    hbm = pl.BlockSpec(memory_space=pl.ANY)
    shape = jax.ShapeDtypeStruct
    wide, thin = depth_size * HD, depth_size * ff_width
    results = pl.pallas_call(
        functools.partial(fused_kernel, names, depth_size, group),
        out_shape=(
            shape((2, rows, width), BF),
            shape((depth_rows, wide), BF),
            shape((depth_rows, wide), BF),
            shape((depth_rows, wide), BF),
            shape((wide, depth_rows), BF),
            shape((depth_rows, thin), BF),
            shape((thin, depth_rows), BF),
            shape((4 * width // 128, 128), F32),
            shape((wide // 128, 128), F32),
            shape((wide // 128, 128), F32),
            shape((wide // 128, 128), F32),
            shape((thin // 128, 128), F32),
            shape((width // 128, 128), F32),
        ),
        in_specs=[pl.BlockSpec(memory_space=pltpu.SMEM)] + [vmem] * 11 + [hbm] * 6,
        out_specs=(vmem,) + (hbm,) * 6 + (vmem,) * 6,
        scratch_shapes=[pltpu.VMEM(s, t) for _, s, t in buffers]
        + [pltpu.SemaphoreType.DMA(s) for _, s in semaphores]
        + [pltpu.SemaphoreType.REGULAR],
        compiler_params=pltpu.CompilerParams(
            collective_id=4, has_side_effects=True, vmem_limit_bytes=VMEM_BYTES
        ),
    )(
        block_order,
        layer_input,
        out_grad,
        freqs,
        *[in_rows(v) for v in (attn_gain, attn_shift, mlp_gain, mlp_shift)],
        *[in_rows(v) for v in (b_query, b_key, b_value, b_up)],
        w_query,
        w_key,
        w_value,
        w_out,
        w_up,
        w_down,
    )
    sums, *parts = results
    output, input_grad, *rest = close(
        depth_size, group, layer_input, out_grad, sums, in_rows(b_out), in_rows(b_down), parts
    )
    small = [vector.reshape(-1) for vector in rest[6:]]
    norms, (to_query, to_key, to_value, to_up, to_dy, again) = small[:4], small[4:]
    return (output, input_grad, *rest[:6], to_query, to_key, to_value, to_dy, to_up, again, *norms)


def close_kernel(depth_size, group, x_in, dy_in, sums, b_out, b_down, *refs):
    grads, (norm_sums, *small), results = refs[:6], refs[6:12], refs[12:]
    layer_output, input_grad, wide, norms, others = (
        results[0],
        results[1],
        results[2:8],
        results[8:12],
        results[12:],
    )
    for source, into in zip(grads, wide, strict=True):
        into[...] = source[...].astype(F32)
    for v, into in enumerate(norms):
        count = into.shape[0]
        into[...] = norm_sums[v * count : (v + 1) * count, :]
    for source, into in zip(small + small[-1:], others, strict=True):
        into[...] = source[...]
    x = x_in[...].astype(F32)
    width = x.shape[1]
    natural = natural_blocks(depth_size, group)
    size = width // len(natural)
    centered = x - jnp.mean(x, -1, keepdims=True)
    inverse = lax.rsqrt(jnp.mean(centered * centered, -1, keepdims=True) + norm_epsilon)
    normal = centered * inverse
    total = jnp.zeros((x.shape[0], 1), F32)
    against = jnp.zeros((x.shape[0], 1), F32)
    for b, c in enumerate(natural):
        out_of, into = slice(b * size, (b + 1) * size), slice(c * size, (c + 1) * size)
        bias = b_out[c : c + 1, :] + b_down[c : c + 1, :]
        layer_output[:, into] = (x[:, into] + sums[0, :, out_of].astype(F32) + bias).astype(BF)
        piece = sums[1, :, out_of].astype(F32)
        total += jnp.sum(piece, -1, keepdims=True)
        against += jnp.sum(piece * normal[:, into], -1, keepdims=True)
    total, against = total / width, against / width
    for b, c in enumerate(natural):
        out_of, into = slice(b * size, (b + 1) * size), slice(c * size, (c + 1) * size)
        piece = sums[1, :, out_of].astype(F32) - total - normal[:, into] * against
        input_grad[:, into] = dy_in[:, into].astype(F32) + inverse * piece


def close(depth_size, group, x_in, dy_in, sums, b_out, b_down, parts):
    rows, width = x_in.shape
    steps = rows // 64
    grads, small = parts[:6], parts[6:]
    norms = [jax.ShapeDtypeStruct((width // 128, 128), F32)] * 4
    copies = [jax.ShapeDtypeStruct(s.shape, F32) for s in small[1:] + small[-1:]]

    def by_rows(shape):
        block = shape[:-2] + (shape[-2] // steps, shape[-1])
        return pl.BlockSpec(block, lambda i: (0,) * (len(shape) - 2) + (i, 0))

    def all_of(shape):
        return pl.BlockSpec(shape, lambda i: (0,) * len(shape))

    return pl.pallas_call(
        functools.partial(close_kernel, depth_size, group),
        grid=(steps,),
        out_shape=[
            jax.ShapeDtypeStruct(x_in.shape, BF),
            jax.ShapeDtypeStruct(x_in.shape, F32),
            *[jax.ShapeDtypeStruct(g.shape, F32) for g in grads],
            *norms,
            *copies,
        ],
        in_specs=[by_rows(x_in.shape)] * 2
        + [by_rows(sums.shape), all_of(b_out.shape), all_of(b_down.shape)]
        + [by_rows(g.shape) for g in grads]
        + [all_of(s.shape) for s in small],
        out_specs=[by_rows(x_in.shape)] * 2
        + [by_rows(g.shape) for g in grads]
        + [all_of(s.shape) for s in norms + copies],
        compiler_params=pltpu.CompilerParams(vmem_limit_bytes=VMEM_BYTES),
    )(x_in, dy_in, sums, b_out, b_down, *grads, *small)


def shards(
    layer_input,
    block_order,
    attn_gain,
    attn_shift,
    mlp_gain,
    mlp_shift,
    w_query,
    b_query,
    w_key,
    b_key,
    w_value,
    b_value,
    w_out,
    b_out,
    w_up,
    b_up,
    w_down,
    b_down,
    out_grad,
):
    rows, width = layer_input.shape
    depth_size = HEADS // lax.axis_size("tp")
    group = lax.axis_size("ctx") // depth_size
    ff_chunks = w_up.shape[1] // depth_size // CHUNK
    whole = fits(depth_size, group, width // (depth_size * group), rows, width, ff_chunks)
    chosen = fused_shards if whole else staged_shards
    return chosen(
        layer_input, block_order, attn_gain, attn_shift, mlp_gain, mlp_shift, w_query, b_query, w_key, b_key, w_value, b_value, w_out, b_out, w_up, b_up, w_down, b_down, out_grad
    )


def staged_shards(
    layer_input,
    block_order,
    attn_gain,
    attn_shift,
    mlp_gain,
    mlp_shift,
    w_query,
    b_query,
    w_key,
    b_key,
    w_value,
    b_value,
    w_out,
    b_out,
    w_up,
    b_up,
    w_down,
    b_down,
    out_grad,
):
    rows, width = layer_input.shape
    ctx_size = lax.axis_size("ctx")
    tp_size = lax.axis_size("tp")
    depth_size = HEADS // tp_size
    group = ctx_size // depth_size
    bits = group.bit_length() - 1
    depth_rows = width // ctx_size
    hidden_width = w_up.shape[1] // depth_size
    ff_chunks = hidden_width // CHUNK
    at = Place(depth_size, group)
    block_rows = rows // 2

    def permuted(array):
        lead = array.shape[:-1]
        n = len(lead)
        split = array.reshape(lead + (depth_size,) + (2,) * bits + (depth_rows,))
        order = tuple(range(n)) + tuple(n + 1 + b for b in reversed(range(bits))) + (n, n + 1 + bits)
        return split.transpose(order).reshape(lead + (width,))

    def restored(array):
        lead = array.shape[:-1]
        n = len(lead)
        split = array.reshape(lead + (2,) * bits + (depth_size, depth_rows))
        order = tuple(range(n)) + (n + bits,) + tuple(n + b for b in reversed(range(bits))) + (n + bits + 1,)
        return split.transpose(order).reshape(lead + (width,))

    def slot_members():
        table = []
        for slot in range(group):
            member = 0
            for stage in range(bits):
                member += ((slot >> stage) & 1) << (bits - 1 - stage)
            table.append(member)
        return table

    blocks = block_order.reshape(depth_size, group, 2)
    order = jnp.stack([blocks[:, m] for m in slot_members()], 0)
    place = order[..., None] * block_rows + jnp.arange(block_rows, dtype=jnp.int32)
    key_place = place.reshape(group * depth_size * rows)
    token_total = depth_size * rows
    query_place = lax.dynamic_slice_in_dim(key_place, at.slot * token_total, token_total)
    cosine, sine_table = rope_tables(query_place)

    inputs32 = layer_input.astype(F32)
    centered = inputs32 - jnp.mean(inputs32, -1, keepdims=True)
    inverse = lax.rsqrt(jnp.mean(centered * centered, -1, keepdims=True) + norm_epsilon)
    normal32 = centered * inverse

    def halves(array):
        return permuted(array).reshape(rows, tp_size, width // tp_size).transpose(1, 0, 2)

    def by_head(weight):
        return weight.reshape(depth_rows, depth_size, HD).transpose(1, 0, 2)

    def by_chunk(weight):
        return weight.reshape(depth_rows, depth_size, ff_chunks, CHUNK).transpose(2, 1, 0, 3)

    weights = jnp.concatenate(
        [
            jnp.concatenate([by_head(w_query), by_head(w_key)], -1)[None],
            jnp.concatenate([by_head(w_value), by_head(w_out.T)], -1)[None],
            jnp.concatenate([by_chunk(w_up), by_chunk(w_down.T)], -1),
        ],
        0,
    )
    normal, grad, gathered = gather_all(
        depth_size, group, halves(normal32.astype(BF)), halves(out_grad), weights
    )
    full = gathered.reshape(2 + ff_chunks, width, 2 * HD)
    gain_a, shift_a, gain_m, shift_m = permuted(jnp.stack([attn_gain, attn_shift, mlp_gain, mlp_shift]))
    normal_tokens = normal.astype(F32)
    attn_in = (normal_tokens * gain_a + shift_a).astype(BF)
    mlp_in = (normal_tokens * gain_m + shift_m).astype(BF)

    def own_part(vector, size):
        return lax.dynamic_slice_in_dim(vector, at.depth * size, size)

    query_key = mm(attn_in, full[0])
    query = rotate(query_key[:, :HD] + own_part(b_query, HD), cosine, sine_table).astype(BF)
    keys = rotate(query_key[:, HD:] + own_part(b_key, HD), cosine, sine_table).astype(BF)
    values = (mm(attn_in, full[1, :, :HD]) + own_part(b_value, HD)).astype(BF)
    out_t = full[1, :, HD:]
    shared = share_group(depth_size, group, jnp.concatenate([keys, values], -1))
    shared = shared.reshape(group * token_total, 2 * HD)
    all_keys, all_values = shared[:, :HD], shared[:, HD:]
    score_scale = 1.0 / math.sqrt(HD)
    scores = mm_nt(query, all_keys) * score_scale
    allowed = key_place[None, :] <= query_place[:, None]
    scores = jnp.where(allowed, scores, -1e30)
    top = jnp.max(scores, -1, keepdims=True)
    raw = jnp.exp(scores - top)
    probs = raw / jnp.sum(raw, -1, keepdims=True)
    probs_low = probs.astype(BF)
    attended = mm(probs_low, all_values)
    attn_low = attended.astype(BF)

    head_grad = mm(grad, out_t).astype(BF)
    delta = jnp.sum(head_grad.astype(F32) * attended, -1, keepdims=True)
    value_part = mm_tn(probs_low, head_grad)
    score_grad = (probs * (mm_nt(head_grad, all_values) - delta) * score_scale).astype(BF)
    query_acc = mm(score_grad, all_keys)
    key_part = mm_tn(score_grad, query)
    parts = jnp.concatenate([key_part, value_part], -1).astype(BF)
    folded = fold_group(depth_size, group, parts.reshape(group, token_total, 2 * HD))
    own_grads = lax.dynamic_index_in_dim(folded, at.slot, 0, keepdims=False).astype(F32)
    query_lin = rotate(query_acc, cosine, -sine_table)
    key_lin = rotate(own_grads[:, :HD], cosine, -sine_table)
    value_lin = own_grads[:, HD:]
    query_low, key_low, value_low = query_lin.astype(BF), key_lin.astype(BF), value_lin.astype(BF)
    query_key_low = jnp.concatenate([query_low, key_low], -1)
    attn_back = mm_nt(query_key_low, full[0]) + mm_nt(value_low, full[1, :, :HD])
    grad_chunks = [
        mm_tn(attn_in, query_key_low).astype(BF),
        jnp.concatenate([mm_tn(attn_in, value_low), mm_tn(grad, attn_low)], -1).astype(BF),
    ]

    branches = mm_nt(attn_low, out_t)
    mlp_back = jnp.zeros((token_total, width), F32)
    bias_up = own_part(b_up, hidden_width).reshape(ff_chunks, CHUNK)
    up_sums = []
    for i in range(ff_chunks):
        up, down_t = full[2 + i, :, :CHUNK], full[2 + i, :, CHUNK:]
        activated, slope = gelu_parts(mm(mlp_in, up) + bias_up[i])
        hidden = activated.astype(BF)
        up_grad = mm(grad, down_t) * slope
        up_sums.append(jnp.sum(up_grad, 0))
        up_low = up_grad.astype(BF)
        branches = branches + mm_nt(hidden, down_t)
        mlp_back = mlp_back + mm_nt(up_low, up)
        grad_chunks.append(jnp.concatenate([mm_tn(mlp_in, up_low), mm_tn(grad, hidden)], -1).astype(BF))

    normal_tokens2 = normal.astype(F32)
    back = attn_back * gain_a + mlp_back * gain_m
    grads = jnp.stack(grad_chunks).reshape(2 + ff_chunks, group, depth_size, depth_rows, 2 * HD)
    norm_sums = restored(
        jnp.stack(
            [
                jnp.sum(attn_back * normal_tokens2, 0),
                jnp.sum(attn_back, 0),
                jnp.sum(mlp_back * normal_tokens2, 0),
                jnp.sum(mlp_back, 0),
            ]
        )
    )
    own_biases = jnp.concatenate(
        [jnp.sum(query_lin, 0), jnp.sum(key_lin, 0), jnp.sum(value_lin, 0)] + up_sums
    )
    spread = jnp.where(
        jnp.arange(depth_size, dtype=jnp.int32)[:, None] == at.depth, own_biases[None, :], 0.0
    )
    norm_sums = lax.psum(norm_sums, ("ctx", "tp"))
    grad32 = out_grad.astype(F32)
    spread, bias_grad = lax.psum((spread, jnp.sum(grad32, 0)), "ctx")

    out_sum, back_sum, grad_shares = reduce_all(
        depth_size, group, branches.astype(BF), back.astype(BF), grads
    )
    layer_output = (inputs32 + restored(out_sum).astype(F32) + b_out + b_down).astype(BF)
    back_total = restored(back_sum).astype(F32)
    input_grad = grad32 + inverse * (
        back_total
        - jnp.mean(back_total, -1, keepdims=True)
        - normal32 * jnp.mean(back_total * normal32, -1, keepdims=True)
    )

    def from_head(share):
        return share.transpose(1, 0, 2).reshape(depth_rows, depth_size * HD).astype(F32)

    def from_chunk(share):
        return share.transpose(2, 1, 0, 3).reshape(depth_rows, depth_size * hidden_width).astype(F32)

    return (
        layer_output,
        input_grad,
        from_head(grad_shares[0, :, :, :HD]),
        from_head(grad_shares[0, :, :, HD:]),
        from_head(grad_shares[1, :, :, :HD]),
        from_head(grad_shares[1, :, :, HD:]).T,
        from_chunk(grad_shares[2:, :, :, :CHUNK]),
        from_chunk(grad_shares[2:, :, :, CHUNK:]).T,
        spread[:, :HD].reshape(-1),
        spread[:, HD : 2 * HD].reshape(-1),
        spread[:, 2 * HD : 3 * HD].reshape(-1),
        bias_grad,
        spread[:, 3 * HD :].reshape(-1),
        bias_grad,
        norm_sums[0],
        norm_sums[1],
        norm_sums[2],
        norm_sums[3],
    )


def solution(mesh):
    in_specs = (
        P("ctx", None),
        P(),
        P(),
        P(),
        P(),
        P(),
        P("ctx", "tp"),
        P("tp"),
        P("ctx", "tp"),
        P("tp"),
        P("ctx", "tp"),
        P("tp"),
        P("tp", "ctx"),
        P(),
        P("ctx", "tp"),
        P("tp"),
        P("tp", "ctx"),
        P(),
        P("ctx", None),
    )
    out_specs = (
        P("ctx", None),
        P("ctx", None),
        P("ctx", "tp"),
        P("ctx", "tp"),
        P("ctx", "tp"),
        P("tp", "ctx"),
        P("ctx", "tp"),
        P("tp", "ctx"),
        P("tp"),
        P("tp"),
        P("tp"),
        P(),
        P("tp"),
        P(),
        P(),
        P(),
        P(),
        P(),
    )
    return jax.shard_map(shards, mesh=mesh, in_specs=in_specs, out_specs=out_specs, check_vma=False)
```

```python
import functools
import math

import jax
import jax.numpy as jnp
import numpy as np
from jax import lax
from jax.experimental import pallas as pl
from jax.experimental.pallas import tpu as pltpu
from jax.sharding import PartitionSpec as P

HEADS = 8
HD = 256
ROT = 64
CHUNK = 256

norm_epsilon = 1e-05
BF = jnp.bfloat16
F32 = jnp.float32
MESH = pl.DeviceIdType.MESH


def mm(a, b):
    return jnp.dot(a, b, preferred_element_type=F32)


def mm_tn(a, b):
    return lax.dot_general(a, b, (((0,), (0,)), ((), ())), preferred_element_type=F32)


def mm_nt(a, b):
    return lax.dot_general(a, b, (((1,), (1,)), ((), ())), preferred_element_type=F32)


class Place:
    def __init__(self, depth_size, group):
        self.depth_size = depth_size
        self.group = group
        self.bits = group.bit_length() - 1
        self.ctx = lax.axis_index("ctx")
        self.tp = lax.axis_index("tp")
        self.depth = self.ctx // group
        self.member = self.ctx % group
        slot = 0
        for stage in range(self.bits):
            slot = slot + self.bit(stage) * 2**stage
        self.slot = slot

    def bit(self, stage):
        return (self.member // 2 ** (self.bits - 1 - stage)) % 2

    def along(self, step):
        return {"ctx": lax.rem(self.depth + step, self.depth_size) * self.group + self.member}

    def across(self, stage):
        reach = 2 ** (self.bits - 1 - stage)
        return {"ctx": self.ctx + (1 - 2 * self.bit(stage)) * reach}

    def twin(self):
        return {"tp": 1 - self.tp}

    def base(self, stage):
        return (self.slot // 2**stage) * 2**stage

    def greet(self, devices):
        barrier = pltpu.get_barrier_semaphore()
        for device in devices:
            pl.semaphore_signal(barrier, inc=1, device_id=device, device_id_type=MESH)
        pl.semaphore_wait(barrier, len(devices))

    def everyone(self):
        return (
            [self.along(step) for step in range(1, self.depth_size)]
            + [self.across(stage) for stage in range(self.bits)]
            + [self.twin()]
        )


def remote(src, dst, send, recv, device):
    copy = pltpu.make_async_remote_copy(
        src_ref=src, dst_ref=dst, send_sem=send, recv_sem=recv, device_id=device, device_id_type=MESH
    )
    copy.start()
    return copy


def local(src, dst, sem):
    copy = pltpu.make_async_copy(src, dst, sem)
    copy.start()
    return copy


def gather_kernel(depth_size, group, x_in, dy_in, w_in, x_out, dy_out, w_out, tz_s, tz_r, tx_s, tx_r, t_l, z_s, z_r, z_l, g_s, g_r):
    at = Place(depth_size, group)
    at.greet(at.everyone())
    rows, half = x_in.shape[1:]
    sent = []
    mine = pl.ds(pl.multiple_of(at.depth * rows, rows), rows)
    my_cols = pl.ds(pl.multiple_of(at.tp * half, half), half)

    def token_start(i, src, dst):
        copies = [
            remote(src.at[at.tp], dst.at[mine, my_cols], tz_s.at[i, s], tz_r.at[i, s], at.along(s))
            for s in range(1, depth_size)
        ]
        copies.append(local(src.at[at.tp], dst.at[mine, my_cols], t_l.at[i]))
        return copies

    def token_swap(i, copies, dst):
        for copy in copies[:-1]:
            copy.wait_recv()
            sent.append(copy)
        copies[-1].wait()
        return remote(dst.at[:, my_cols], dst.at[:, my_cols], tx_s.at[i], tx_r.at[i], at.twin())

    chunks = w_in.shape[0]

    def z_start(k):
        copies = [
            remote(
                w_in.at[k, lax.rem(at.depth + s, depth_size)],
                w_out.at[k, at.slot, at.depth],
                z_s.at[k, s],
                z_r.at[k, s],
                at.along(s),
            )
            for s in range(1, depth_size)
        ]
        copies.append(local(w_in.at[k, at.depth], w_out.at[k, at.slot, at.depth], z_l.at[k]))
        return copies

    def z_wait(copies):
        for copy in copies[:-1]:
            copy.wait_recv()
            sent.append(copy)
        copies[-1].wait()

    def g_start(k, stage):
        held = pl.ds(at.base(stage), 2**stage)
        return remote(
            w_out.at[k, held], w_out.at[k, held], g_s.at[k, stage], g_r.at[k, stage], at.across(stage)
        )

    ahead = 2
    tokens = [token_start(0, x_in, x_out)]
    z_copies = {k: z_start(k) for k in range(min(ahead, chunks))}
    stages = {}
    swaps = []
    for step in range(chunks + at.bits):
        if step < chunks:
            z_wait(z_copies[step])
            stages[step] = [g_start(step, 0)]
            if step + ahead < chunks:
                z_copies[step + ahead] = z_start(step + ahead)
            if step == 0:
                swaps.append(token_swap(0, tokens[0], x_out))
                tokens.append(token_start(1, dy_in, dy_out))
            if step == 1:
                swaps.append(token_swap(1, tokens[1], dy_out))
        for stage in range(1, at.bits + 1):
            k = step - stage
            if 0 <= k < chunks:
                stages[k][stage - 1].wait_recv()
                if stage < at.bits:
                    stages[k].append(g_start(k, stage))
    for swap in swaps:
        swap.wait()
    for k in range(chunks):
        for copy in stages[k]:
            copy.wait_send()
    for copy in sent:
        copy.wait_send()


def gather_all(depth_size, group, x_halves, dy_halves, weights):
    tp, rows, half = x_halves.shape
    chunks, _, depth_rows, width = weights.shape
    bits = group.bit_length() - 1
    dma = pltpu.SemaphoreType.DMA
    hbm = pl.BlockSpec(memory_space=pl.ANY)
    tokens = jax.ShapeDtypeStruct((depth_size * rows, tp * half), BF)
    return pl.pallas_call(
        functools.partial(gather_kernel, depth_size, group),
        out_shape=(
            tokens,
            tokens,
            jax.ShapeDtypeStruct((chunks, group, depth_size, depth_rows, width), BF),
        ),
        in_specs=[hbm] * 3,
        out_specs=(hbm, hbm, hbm),
        scratch_shapes=[
            dma((2, depth_size)),
            dma((2, depth_size)),
            dma((2,)),
            dma((2,)),
            dma((2,)),
            dma((chunks, depth_size)),
            dma((chunks, depth_size)),
            dma((chunks,)),
            dma((chunks, bits)),
            dma((chunks, bits)),
        ],
        compiler_params=pltpu.CompilerParams(collective_id=0, has_side_effects=True),
    )(x_halves, dy_halves, weights)


def share_kernel(depth_size, group, kv_in, kv_out, send, recv, loc):
    at = Place(depth_size, group)
    at.greet([at.across(stage) for stage in range(at.bits)])
    local(kv_in, kv_out.at[at.slot], loc).wait()
    copies = []
    for stage in range(at.bits):
        held = pl.ds(at.base(stage), 2**stage)
        copy = remote(kv_out.at[held], kv_out.at[held], send.at[stage], recv.at[stage], at.across(stage))
        copy.wait_recv()
        copies.append(copy)
    for copy in copies:
        copy.wait_send()


def share_group(depth_size, group, kv):
    bits = group.bit_length() - 1
    dma = pltpu.SemaphoreType.DMA
    hbm = pl.BlockSpec(memory_space=pl.ANY)
    return pl.pallas_call(
        functools.partial(share_kernel, depth_size, group),
        out_shape=jax.ShapeDtypeStruct((group,) + kv.shape, BF),
        in_specs=[hbm],
        out_specs=hbm,
        scratch_shapes=[dma((bits,)), dma((bits,)), dma],
        compiler_params=pltpu.CompilerParams(collective_id=1, has_side_effects=True),
    )(kv)


def fold_kernel(depth_size, group, g_in, total, landing, send, recv):
    at = Place(depth_size, group)
    at.greet([at.across(stage) for stage in range(at.bits)])
    for stage in reversed(range(at.bits)):
        size = 2**stage
        own = at.base(stage)
        other = own + (1 - 2 * at.bit(stage)) * size
        source = g_in if stage == at.bits - 1 else total
        copy = remote(
            source.at[pl.ds(other, size)],
            landing.at[pl.ds(size - 1, size)],
            send.at[stage],
            recv.at[stage],
            at.across(stage),
        )
        copy.wait()

        def add(i, _):
            total[own + i] = (
                source[own + i].astype(F32) + landing[size - 1 + i].astype(F32)
            ).astype(BF)
            return 0

        lax.fori_loop(0, size, add, 0)


def fold_group(depth_size, group, grads):
    bits = group.bit_length() - 1
    dma = pltpu.SemaphoreType.DMA
    vmem = pl.BlockSpec(memory_space=pltpu.VMEM)
    return pl.pallas_call(
        functools.partial(fold_kernel, depth_size, group),
        out_shape=jax.ShapeDtypeStruct(grads.shape, BF),
        in_specs=[vmem],
        out_specs=vmem,
        scratch_shapes=[
            pltpu.VMEM((group - 1,) + grads.shape[1:], BF),
            dma((bits,)),
            dma((bits,)),
        ],
        compiler_params=pltpu.CompilerParams(
            collective_id=2, has_side_effects=True, vmem_limit_bytes=60 << 20
        ),
    )(grads)


def reduce_kernel(depth_size, group, out_in, back_in, g_in, out_sum, back_sum, g_out, total, landing, g_s, g_r, z_s, z_r, z_l, t_acc, t_swap, t_land, tx_s, tx_r, tz_s, tz_r, ty_s, ty_r):
    at = Place(depth_size, group)
    at.greet(at.everyone())
    chunks = g_in.shape[0]
    depth_rows = g_in.shape[3]
    rows = out_sum.shape[0]
    half = t_acc.shape[2]
    last = at.bits - 1
    sent = []

    def g_start(k, stage):
        size = 2**stage
        other = at.base(stage) + (1 - 2 * at.bit(stage)) * size
        source = g_in.at[k] if stage == last else total.at[k]
        return remote(
            source.at[pl.ds(other, size)],
            landing.at[k, pl.ds(size - 1, size)],
            g_s.at[k, stage],
            g_r.at[k, stage],
            at.across(stage),
        )

    def g_finish(k, stage, copy):
        copy.wait_recv()
        sent.append(copy)
        size = 2**stage
        own = at.base(stage)
        source = g_in.at[k] if stage == last else total.at[k]

        def add(i, _):
            j = i // depth_size
            z = i % depth_size
            total[k, own + j, z] = (
                source[own + j, z].astype(F32) + landing[k, size - 1 + j, z].astype(F32)
            ).astype(BF)
            return 0

        lax.fori_loop(0, size * depth_size, add, 0)

    def z_start(k):
        copies = [
            remote(
                total.at[k, at.slot, lax.rem(at.depth + s, depth_size)],
                g_out.at[k, at.depth],
                z_s.at[k, s],
                z_r.at[k, s],
                at.along(s),
            )
            for s in range(1, depth_size)
        ]
        copies.append(local(total.at[k, at.slot, at.depth], g_out.at[k, at.depth], z_l.at[k]))
        return copies

    my_cols = pl.ds(pl.multiple_of(at.tp * half, half), half)
    her_cols = pl.ds(pl.multiple_of((1 - at.tp) * half, half), half)

    def token_first(i, src):
        return remote(src.at[:, her_cols], t_swap.at[i], tx_s.at[i], tx_r.at[i], at.twin())

    def token_second(i, src, copy):
        copy.wait_recv()
        sent.append(copy)

        def add(z, _):
            block = pl.ds(pl.multiple_of(z * rows, rows), rows)
            t_acc[i, block, :] = (
                src[block, my_cols].astype(F32) + t_swap[i, block, :].astype(F32)
            ).astype(BF)
            return 0

        lax.fori_loop(0, depth_size, add, 0)
        copies = []
        for s in range(1, depth_size):
            there = lax.rem(at.depth + s, depth_size)
            block = pl.ds(pl.multiple_of(there * rows, rows), rows)
            copies.append(
                remote(
                    t_acc.at[i, block, :], t_land.at[i, s - 1], tz_s.at[i, s], tz_r.at[i, s], at.along(s)
                )
            )
        return copies

    def token_third(i, dst, copies):
        for copy in copies:
            copy.wait_recv()
            sent.append(copy)
        mine = pl.ds(pl.multiple_of(at.depth * rows, rows), rows)
        value = t_acc[i, mine, :].astype(F32)
        for s in range(1, depth_size):
            value = value + t_land[i, s - 1].astype(F32)
        dst[:, my_cols] = value.astype(BF)
        return remote(dst.at[:, my_cols], dst.at[:, my_cols], ty_s.at[i], ty_r.at[i], at.twin())

    firsts = [token_first(0, out_in), token_first(1, back_in)]
    copies_of = {k: [g_start(k, last)] for k in range(chunks)}
    z_copies = {}
    seconds = []
    thirds = []
    for step in range(chunks + at.bits):
        for back in range(at.bits):
            k = step - back
            stage = last - back
            if 0 <= k < chunks:
                g_finish(k, stage, copies_of[k][back])
                if stage > 0:
                    copies_of[k].append(g_start(k, stage - 1))
                else:
                    z_copies[k] = z_start(k)
        if step == 1:
            seconds.append(token_second(0, out_in, firsts[0]))
        if step == 2:
            seconds.append(token_second(1, back_in, firsts[1]))
        if step == 4:
            thirds.append(token_third(0, out_sum, seconds[0]))
        if step == 5:
            thirds.append(token_third(1, back_sum, seconds[1]))
    for k in range(chunks):
        for copy in z_copies[k][:-1]:
            copy.wait()
        z_copies[k][-1].wait()
    for copy in thirds:
        copy.wait()
    for copy in sent:
        copy.wait_send()


def reduce_all(depth_size, group, out_part, back_part, grads):
    chunks, _, _, depth_rows, width = grads.shape
    all_rows, columns = out_part.shape
    rows = all_rows // depth_size
    half = columns // 2
    bits = group.bit_length() - 1
    dma = pltpu.SemaphoreType.DMA
    vmem = pl.BlockSpec(memory_space=pltpu.VMEM)
    tokens = jax.ShapeDtypeStruct((rows, columns), BF)
    return pl.pallas_call(
        functools.partial(reduce_kernel, depth_size, group),
        out_shape=(tokens, tokens, jax.ShapeDtypeStruct((chunks, depth_size, depth_rows, width), BF)),
        in_specs=[vmem] * 3,
        out_specs=(vmem, vmem, vmem),
        scratch_shapes=[
            pltpu.VMEM((chunks, group, depth_size, depth_rows, width), BF),
            pltpu.VMEM((chunks, group - 1, depth_size, depth_rows, width), BF),
            dma((chunks, bits)),
            dma((chunks, bits)),
            dma((chunks, depth_size)),
            dma((chunks, depth_size)),
            dma((chunks,)),
            pltpu.VMEM((2, all_rows, half), BF),
            pltpu.VMEM((2, all_rows, half), BF),
            pltpu.VMEM((2, depth_size - 1, rows, half), BF),
            dma((2,)),
            dma((2,)),
            dma((2, depth_size)),
            dma((2, depth_size)),
            dma((2,)),
            dma((2,)),
        ],
        compiler_params=pltpu.CompilerParams(
            collective_id=3, has_side_effects=True, vmem_limit_bytes=60 << 20
        ),
    )(out_part, back_part, grads)


def rotate(values, cosine, sine_table):
    half_rot = ROT // 2
    leading = values[..., :half_rot]
    trailing = values[..., half_rot:ROT]
    return jnp.concatenate(
        [
            leading * cosine - trailing * sine_table,
            trailing * cosine + leading * sine_table,
            values[..., ROT:],
        ],
        -1,
    )


def rope_tables(positions):
    freqs = 10000.0 ** (-(2.0 * jnp.arange(ROT // 2, dtype=F32)) / ROT)
    angles = positions.astype(F32)[:, None] * freqs[None, :]
    return (jnp.cos(angles), jnp.sin(angles))


def gelu_parts(values):
    gate = 0.5 * (1.0 + lax.erf(values * math.sqrt(0.5)))
    slope = gate + values * jnp.exp(-0.5 * values * values) * (1.0 / math.sqrt(2.0 * math.pi))
    return values * gate, slope


SMALL_ROWS = 96
LATE = (3, 7,)
LATE_ROWS = 1
LATE_COLS = 2
VMEM_BYTES = 64 << 20


def slot_member(slot, bits):
    member = 0
    for stage in range(bits):
        member += ((slot >> stage) & 1) << (bits - 1 - stage)
    return member


def natural_blocks(depth_size, group):
    bits = group.bit_length() - 1
    return [
        depth * group + slot_member(slot, bits) for slot in range(group) for depth in range(depth_size)
    ]

ROW_TILE = 256
DROP = -1e30


def layout_of(depth_size, group, depth_rows, rows, width, ff_chunks):
    tokens = depth_size * rows
    half = width // 2
    landing = (group - 1) * depth_size * depth_rows
    heads = 3 + ff_chunks
    cols = 1 + ff_chunks
    return [
        ("wr", (heads, width, CHUNK), BF),
        ("wc", (cols, CHUNK, width), BF),
        ("gr", (heads, width, CHUNK), BF),
        ("gc", (cols, CHUNK, width), BF),
        ("lr", (heads, landing, CHUNK), BF),
        ("lc", (cols, CHUNK, landing), BF),
        ("x", (tokens, width), BF),
        ("dy", (tokens, width), BF),
        ("na", (tokens, width), BF),
        ("nm", (tokens, width), BF),
        ("nmt", (width, tokens), BF),
        ("kv", (group * tokens, 2 * HD), BF),
        ("q", (tokens, HD), BF),
        ("low", (tokens, 3 * HD), BF),
        ("al", (tokens, HD), BF),
        ("hg", (tokens, HD), BF),
        ("alt", (HD, tokens), BF),
        ("att", (HD, tokens), F32),
        ("dqt", (HD, tokens), F32),
        ("stat", (8, tokens), F32),
        ("tab", (group * tokens, 128), F32),
        ("kb", (8, HD), F32),
        ("hid", (ff_chunks, tokens, CHUNK), BF),
        ("ul", (ff_chunks, tokens, CHUNK), BF),
        ("tz", (2, 2, tokens // 2, half // 2), BF),
        ("te", (2, rows, half), BF),
        ("mean", (tokens, 1), F32),
        ("inv", (tokens, 1), F32),
        ("gv", (8, width), F32),
        ("biases", (8, HD), F32),
        ("places", (group * tokens // 128, 128), F32),
        ("ps", (group.bit_length(), SMALL_ROWS, 128), F32),
        ("pl", (group.bit_length() - 1, SMALL_ROWS, 128), F32),
        ("pz", (depth_size, SMALL_ROWS, 128), F32),
        ("px", (2, SMALL_ROWS, 128), F32),
        ("dr", (LATE_ROWS, 2, depth_size * depth_rows, CHUNK), BF),
        ("dc", (LATE_COLS, 2, CHUNK, depth_size * depth_rows), BF),
    ]


def semaphores_of(depth_size, group, items):
    bits = group.bit_length() - 1
    return [
        ("z_s", (items, depth_size)),
        ("z_r", (items, depth_size)),
        ("z_l", (items,)),
        ("g_s", (items, bits)),
        ("g_r", (items, bits)),
        ("t_s", (2, 3)),
        ("t_r", (2, 3)),
        ("w_s", (2, 3)),
        ("w_r", (2, 3)),
        ("kv_s", (2, 2, bits)),
        ("kv_r", (2, 2, bits)),
        ("f_s", (items, bits)),
        ("f_r", (items, bits)),
        ("e_s", (items, depth_size)),
        ("e_r", (items, depth_size)),
        ("e_l", (items,)),
        ("d_s", (LATE_ROWS + LATE_COLS, 2, depth_size)),
        ("d_r", (LATE_ROWS + LATE_COLS, 2, depth_size)),
        ("d_l", (LATE_ROWS + LATE_COLS, depth_size)),
        ("o_s", (2, 6)),
        ("o_r", (2, 6)),
        ("p_s", (bits + depth_size,)),
        ("p_r", (bits + depth_size,)),
    ]


VECTORS = ("attn_gain", "attn_shift", "mlp_gain", "mlp_shift")
BIASES = ("b_query", "b_key", "b_value", "b_up")
INPUTS = ("blocks", "x_in", "dy_in", "freqs") + VECTORS + BIASES
INPUTS += ("w_query", "w_key", "w_value", "w_out", "w_up", "w_down")
OUTPUTS = ("fin", "g_query", "g_key", "g_value", "g_out", "g_up", "g_down")
OUTPUTS += ("norm_sums", "s_query", "s_key", "s_value", "s_up", "s_dy")


class Bag:
    pass


def fused_kernel(names, depth_size, group, *refs):
    m = Bag()
    for name, ref in zip(names, refs, strict=True):
        setattr(m, name, ref)
    at = Place(depth_size, group)
    at.greet(at.everyone())
    bits = at.bits
    rows, width = m.x_in.shape
    depth_rows = width // (depth_size * group)
    tokens = depth_size * rows
    half = width // 2
    ff_width = m.w_up.shape[1] // depth_size
    ff_chunks = ff_width // CHUNK
    block_count = width // depth_rows
    own_block = at.slot * depth_size + at.depth
    natural = natural_blocks(depth_size, group)
    sends, settled = [], []

    def blocks(first, count):
        return pl.ds(pl.multiple_of(first * depth_rows, depth_rows), count * depth_rows)

    def token_rows(depth):
        return pl.ds(pl.multiple_of(depth * rows, rows), rows)

    def peer(step):
        return lax.rem(at.depth + step, depth_size)

    my_cols = pl.ds(pl.multiple_of(at.tp * half, half), half)
    her_cols = pl.ds(pl.multiple_of((1 - at.tp) * half, half), half)

    units = [("r", 0), ("r", 1), ("r", 2), ("c", 0)]
    for i in range(ff_chunks):
        units += [("r", 3 + i), ("c", 1 + i)]
    row_pairs = [(m.w_query, m.g_query), (m.w_key, m.g_key), (m.w_value, m.g_value)]

    def outer(kind, a, depth, which):
        if kind == "r" and a < 3:
            return row_pairs[a][which].at[:, pl.ds(pl.multiple_of(depth * HD, HD), HD)]
        if kind == "r":
            first = pl.multiple_of(depth * ff_width + (a - 3) * CHUNK, CHUNK)
            return (m.w_up, m.g_up)[which].at[:, pl.ds(first, CHUNK)]
        if a == 0:
            return (m.w_out, m.g_out)[which].at[pl.ds(pl.multiple_of(depth * HD, HD), HD), :]
        first = pl.multiple_of(depth * ff_width + (a - 1) * CHUNK, CHUNK)
        return (m.w_down, m.g_down)[which].at[pl.ds(first, CHUNK), :]

    def part(pair, kind, a, first, count):
        if kind == "r":
            return pair[0].at[a, blocks(first, count), :]
        return pair[1].at[a, :, blocks(first, count)]

    weights, grads, landing = (m.wr, m.wc), (m.gr, m.gc), (m.lr, m.lc)

    def z_start(k):
        kind, a = units[k]
        into = part(weights, kind, a, own_block, 1)
        copies = [
            remote(outer(kind, a, peer(s), 0), into, m.z_s.at[k, s], m.z_r.at[k, s], at.along(s))
            for s in range(1, depth_size)
        ]
        copies.append(local(outer(kind, a, at.depth, 0), into, m.z_l.at[k]))
        return copies

    def z_wait(copies):
        received(copies[:-1])
        copies[-1].wait()

    def g_start(k, stage):
        kind, a = units[k]
        held = part(weights, kind, a, at.base(stage) * depth_size, 2**stage * depth_size)
        return [remote(held, held, m.g_s.at[k, stage], m.g_r.at[k, stage], at.across(stage))]

    def received(copies):
        for copy in copies:
            copy.wait_recv()
        sends.extend(copies)

    def settle(copies):
        for copy in copies:
            copy.wait_send()
        settled.extend(copies)

    def fold_start(k, stage):
        kind, a = units[k]
        size = 2**stage
        other = at.base(stage) + (1 - 2 * at.bit(stage)) * size
        return [
            remote(
                part(grads, kind, a, other * depth_size, size * depth_size),
                part(landing, kind, a, (size - 1) * depth_size, size * depth_size),
                m.f_s.at[k, stage],
                m.f_r.at[k, stage],
                at.across(stage),
            )
        ]

    def fold_add(k, stage, copies):
        received(copies)
        kind, a = units[k]
        size = 2**stage
        own = at.base(stage) * depth_size

        def add(i, _):
            mine = blocks(own + i, 1)
            theirs = blocks((size - 1) * depth_size + i, 1)
            if kind == "r":
                total = m.gr[a, mine, :].astype(F32) + m.lr[a, theirs, :].astype(F32)
                m.gr[a, mine, :] = total.astype(BF)
            else:
                total = m.gc[a, :, mine].astype(F32) + m.lc[a, :, theirs].astype(F32)
                m.gc[a, :, mine] = total.astype(BF)
            return 0

        lax.fori_loop(0, size * depth_size, add, 0)

    def end_start(k):
        kind, a = units[k]
        into = outer(kind, a, at.depth, 1)
        copies = [
            remote(
                part(grads, kind, a, at.slot * depth_size + peer(s), 1),
                into,
                m.e_s.at[k, s],
                m.e_r.at[k, s],
                at.along(s),
            )
            for s in range(1, depth_size)
        ]
        copies.append(local(part(grads, kind, a, own_block, 1), into, m.e_l.at[k]))
        return copies

    late = {k: n for n, k in enumerate(LATE)}
    other_slot = at.base(1) + 1 - at.bit(0)

    def depth_buffer(k, h, first, count):
        kind, a = units[k]
        same = [j for j in LATE if units[j][0] == kind].index(k)
        if kind == "r":
            return m.dr.at[same, h, blocks(first, count), :]
        return m.dc.at[same, h, :, blocks(first, count)]

    def depth_first_start(k, copies):
        fold_add(k, 1, copies)
        kind, a = units[k]
        n = late[k]
        copies = []
        for h, slot in enumerate((at.slot, other_slot)):
            for s in range(1, depth_size):
                copies.append(
                    remote(
                        part(grads, kind, a, slot * depth_size + peer(s), 1),
                        depth_buffer(k, h, at.depth, 1),
                        m.d_s.at[n, h, s],
                        m.d_r.at[n, h, s],
                        at.along(s),
                    )
                )
            own = part(grads, kind, a, slot * depth_size + at.depth, 1)
            depth_buffer(k, h, at.depth, 1)[...] = own[...]
        return copies

    def depth_first_fold(k, copies):
        received(copies)
        kind, a = units[k]
        return [
            remote(
                depth_buffer(k, 1, 0, depth_size),
                part(landing, kind, a, 0, depth_size),
                m.f_s.at[k, 0],
                m.f_r.at[k, 0],
                at.across(0),
            )
        ]

    def depth_first_end(k, copies):
        received(copies)
        kind, a = units[k]
        ends = []
        for z in range(depth_size):
            mine = depth_buffer(k, 0, z, 1)
            theirs = part(landing, kind, a, z, 1)
            mine[...] = (mine[...].astype(F32) + theirs[...].astype(F32)).astype(BF)
            ends.append(local(mine, outer(kind, a, z, 1), m.d_l.at[late[k], z]))
        return ends

    near = {"ctx": at.ctx + (1 - 2 * (at.depth % 2)) * group}
    far = {"ctx": at.ctx + (2 - 4 * (at.depth // 2)) * group}
    near_depth = at.depth + 1 - 2 * (at.depth % 2)
    pair_first = at.depth // 2 * 2
    my_pair = pl.ds(pl.multiple_of(pair_first * rows, rows), 2 * rows)
    her_pair = pl.ds(pl.multiple_of((2 - pair_first) * rows, rows), 2 * rows)
    quarter = half // 2
    my_quarter = pl.ds(pl.multiple_of(at.tp * half + at.depth % 2 * quarter, quarter), quarter)
    her_quarter = pl.ds(pl.multiple_of(at.tp * half + (1 - at.depth % 2) * quarter, quarter), quarter)

    def token_step(i, buffer, step, copies):
        if copies:
            received(copies[-1:])
        brought = [
            None,
            (token_rows(near_depth), my_cols),
            (her_pair, my_quarter),
            (her_pair, her_quarter),
        ]
        given = [(token_rows(at.depth), my_cols), (my_pair, my_quarter), (her_pair, my_quarter)]
        if step < 3:
            piece = buffer.at[given[step][0], given[step][1]]
            there = far if step == 1 else near
            copies.append(remote(piece, piece, m.t_s.at[i, step], m.t_r.at[i, step], there))
        if step:
            piece = buffer.at[brought[step][0], brought[step][1]]
            swapped[i].append(
                remote(piece, piece, m.w_s.at[i, step - 1], m.w_r.at[i, step - 1], at.twin())
            )
        return copies

    def kv_start(h, stage):
        size = 2**stage * tokens
        rows_held = pl.ds(pl.multiple_of(at.base(stage) * tokens, tokens), size)
        held = m.kv.at[rows_held, slice(h * HD, (h + 1) * HD)]
        return remote(held, held, m.kv_s.at[0, h, stage], m.kv_r.at[0, h, stage], at.across(stage))

    spare = (m.lr.at[1 + ff_chunks], m.lr.at[2 + ff_chunks])

    def dkv_start(stage):
        size = 2**stage
        other = at.base(stage) + (1 - 2 * at.bit(stage)) * size
        given = pl.ds(pl.multiple_of(other * tokens, tokens), size * tokens)
        taken = pl.ds((size - 1) * tokens, size * tokens)
        return [
            remote(
                m.kv.at[given, slice(h * HD, (h + 1) * HD)],
                spare[h].at[taken, :],
                m.kv_s.at[1, h, stage],
                m.kv_r.at[1, h, stage],
                at.across(stage),
            )
            for h in range(2)
        ]

    def dkv_finish(stage, copies):
        received(copies)
        size = 2**stage
        own = at.base(stage) * tokens
        step = ROW_TILE

        def add(i, _):
            mine = pl.ds(pl.multiple_of(own + i * step, step), step)
            theirs = pl.ds(pl.multiple_of((size - 1) * tokens + i * step, step), step)
            for h in range(2):
                cols = slice(h * HD, (h + 1) * HD)
                total = m.kv[mine, cols].astype(F32) + spare[h][theirs, :].astype(F32)
                m.kv[mine, cols] = total.astype(BF)
            return 0

        lax.fori_loop(0, size * tokens // step, add, 0)

    lane = lax.broadcasted_iota(jnp.int32, (1, 128), 1)

    def place_rows():
        mine = token_rows(at.depth)
        for b in range(block_count):
            c = natural[b]
            into = slice(b * depth_rows, (b + 1) * depth_rows)
            out_of = slice(c * depth_rows, (c + 1) * depth_rows)
            m.x[mine, into] = m.x_in[:, out_of]
            m.dy[mine, into] = m.dy_in[:, out_of]

    def place_vectors():
        m.ps[0] = jnp.zeros_like(m.ps[0])
        for row, name in enumerate(VECTORS):
            for b in range(block_count):
                c = natural[b]
                m.gv[row : row + 1, b * depth_rows : (b + 1) * depth_rows] = getattr(m, name)[c : c + 1, :]
        per_head = HD // 128
        for a in range(3):
            for h in range(per_head):
                row = getattr(m, BIASES[a])[pl.ds(at.depth * per_head + h, 1), :]
                m.biases[a : a + 1, h * 128 : (h + 1) * 128] = row
        for i in range(ff_chunks):
            for h in range(per_head):
                row = m.b_up[pl.ds((at.depth * ff_chunks + i) * per_head + h, 1), :]
                m.biases[3 + i : 4 + i, h * 128 : (h + 1) * 128] = row
        block_rows = rows // 2
        for n in range(group * depth_size):
            c = natural[n]
            first = jnp.where(lane < block_rows, m.blocks[2 * c], m.blocks[2 * c + 1])
            m.places[n : n + 1, :] = (first * block_rows + lane % block_rows).astype(F32)

    def affine():
        step = 32

        def stats(i, _):
            here = pl.ds(pl.multiple_of(i * step, step), step)
            x = m.x[here, :].astype(F32)
            mean = jnp.mean(x, -1, keepdims=True)
            centered = x - mean
            m.mean[here, :] = mean
            m.inv[here, :] = lax.rsqrt(jnp.mean(centered * centered, -1, keepdims=True) + norm_epsilon)
            return 0

        lax.fori_loop(0, tokens // step, stats, 0)

        def body(i, _):
            here = token_rows(i)
            for n in range(width // 512):
                cols = slice(n * 512, (n + 1) * 512)
                normal = (m.x[here, cols].astype(F32) - m.mean[here, :]) * m.inv[here, :]
                m.na[here, cols] = (normal * m.gv[0:1, cols] + m.gv[1:2, cols]).astype(BF)
                mlp = normal * m.gv[2:3, cols] + m.gv[3:4, cols]
                m.nm[here, cols] = mlp.astype(BF)
                m.nmt[cols, here] = mlp.T.astype(BF)
            return 0

        lax.fori_loop(0, depth_size, body, 0)

    def place_column(n):
        return jnp.broadcast_to(m.places[pl.ds(n, 1), :], (128, 128)).T

    def make_tables():
        def body(n, _):
            angles = place_column(n) * m.freqs[0:1, :]
            here = pl.ds(pl.multiple_of(n * 128, 128), 128)
            m.tab[here, :] = jnp.cos(angles - jnp.where(lane < ROT, 0.0, math.pi / 2))
            return 0

        lax.fori_loop(0, group * tokens // 128, body, 0)

    def turned(value, here, sign):
        head = value[:, :128]
        left = pltpu.roll(head, 128 - ROT // 2, 1)
        right = pltpu.roll(head, ROT // 2, 1)
        table = m.tab[here, :]
        cosine = jnp.where(lane < ROT, table, 1.0)
        sine = sign * pltpu.roll(table, ROT, 1)
        crossed = jnp.where(lane < ROT // 2, -left, jnp.where(lane < ROT, right, 0.0))
        return head * cosine + crossed * sine

    def project(a):
        return mm(m.na[...], m.wr[a]) + m.biases[a : a + 1, :]

    kv_own = pl.ds(pl.multiple_of(at.slot * tokens, tokens), tokens)
    score_scale = 1.0 / math.sqrt(HD)

    def make_query():
        query = project(0)
        m.q[:, :128] = turned(query, kv_own, 1.0).astype(BF)
        m.q[:, 128:] = query[:, 128:].astype(BF)

    def make_keys():
        keys = project(1)
        m.kv[kv_own, :128] = turned(keys, kv_own, 1.0).astype(BF)
        m.kv[kv_own, 128:HD] = keys[:, 128:].astype(BF)

    def make_values():
        m.kv[kv_own, HD:] = project(2).astype(BF)

    def key_rows(j):
        return pl.ds(pl.multiple_of(j * tokens, tokens), tokens)

    def masked_scores(j):
        scores = mm_nt(m.kv[key_rows(j), :HD], m.q[...]) * score_scale
        count = tokens // 128
        column = jnp.concatenate([place_column(j * count + n)[:, :1] for n in range(count)], 0)
        row = jnp.concatenate([m.places[pl.ds(at.slot * count + n, 1), :] for n in range(count)], 1)
        return jnp.where(column <= row, scores, DROP)

    def attend(j):
        scores = masked_scores(j)
        if j == 0:
            old = jnp.full((1, tokens), -1e20, F32)
        else:
            old = m.stat[0:1, :]
        new = jnp.maximum(old, jnp.max(scores, 0, keepdims=True))
        raw = jnp.exp(scores - new)
        total = jnp.sum(raw, 0, keepdims=True)
        value = mm(m.kv[key_rows(j), HD:].T, raw.astype(BF))
        m.stat[0:1, :] = new
        if j:
            factor = jnp.exp(old - new)
            total = total + m.stat[1:2, :] * factor
            value = value + m.att[...] * factor
        m.stat[1:2, :] = total
        m.att[...] = value
        if j == group - 1:
            m.stat[2:3, :] = new + jnp.log(total)
            value = value / total
            m.att[...] = value
            m.alt[...] = value.astype(BF)
            m.al[...] = value.T.astype(BF)

    def head_grads():
        grad = mm_nt(m.dy[...], m.wc[0])
        low = grad.astype(BF)
        m.hg[...] = low
        m.stat[3:4, :] = jnp.sum(low.astype(F32).T * m.att[...], 0, keepdims=True)

    def attend_back(j):
        probs = jnp.exp(masked_scores(j) - m.stat[2:3, :])
        value_part = mm(probs.astype(BF), m.hg[...])
        prob_grad = mm_nt(m.kv[key_rows(j), HD:], m.hg[...])
        score_grad = (probs * (prob_grad - m.stat[3:4, :]) * score_scale).astype(BF)
        query_part = mm(m.kv[key_rows(j), :HD].T, score_grad)
        key_part = mm(score_grad, m.q[...])
        head_sum = jnp.sum(turned(key_part, key_rows(j), -1.0), 0, keepdims=True)
        rest_sum = jnp.sum(key_part[:, 128:], 0, keepdims=True)
        if j:
            query_part = query_part + m.dqt[...]
            head_sum = head_sum + m.kb[0:1, :128]
            rest_sum = rest_sum + m.kb[0:1, 128:]
        m.dqt[...] = query_part
        m.kb[0:1, :128] = head_sum
        m.kb[0:1, 128:] = rest_sum
        m.kv[key_rows(j), :HD] = key_part.astype(BF)
        m.kv[key_rows(j), HD:] = value_part.astype(BF)

    def small_store(first, row):
        for n in range(row.shape[1] // 128):
            m.ps[0, first + n : first + n + 1, :] = row[:, n * 128 : (n + 1) * 128]

    def attention_grads():
        query = m.dqt[...].T
        head = turned(query, kv_own, -1.0)
        keys = m.kv[kv_own, :HD].astype(F32)
        key_head = turned(keys, kv_own, -1.0)
        m.low[:, :128] = head.astype(BF)
        m.low[:, 128:HD] = query[:, 128:].astype(BF)
        m.low[:, HD : HD + 128] = key_head.astype(BF)
        m.low[:, HD + 128 : 2 * HD] = m.kv[kv_own, 128:HD]
        m.low[:, 2 * HD :] = m.kv[kv_own, HD:]
        small_store(64, jnp.sum(head, 0, keepdims=True))
        small_store(65, jnp.sum(query[:, 128:], 0, keepdims=True))
        small_store(66, m.kb[0:1, :])
        small_store(68, jnp.sum(m.kv[kv_own, HD:].astype(F32), 0, keepdims=True))

        def body(n, _):
            tile = pl.ds(pl.multiple_of(n * ROW_TILE, ROW_TILE), ROW_TILE)
            turned_in = m.na[:, tile].T
            for a in range(3):
                m.gr[a, tile, :] = mm(turned_in, m.low[:, a * HD : (a + 1) * HD]).astype(BF)
            return 0

        lax.fori_loop(0, width // ROW_TILE, body, 0)

    def out_grads():
        def body(n, _):
            tile = pl.ds(pl.multiple_of(n * 512, 512), 512)
            m.gc[0, :, tile] = mm(m.alt[...], m.dy[:, tile]).astype(BF)
            return 0

        lax.fori_loop(0, width // 512, body, 0)

    def feed_forward(i):
        activated, slope = gelu_parts(mm(m.nm[...], m.wr[3 + i]) + m.biases[3 + i : 4 + i, :])
        m.hid[i] = activated.astype(BF)
        up_grad = mm_nt(m.dy[...], m.wc[1 + i]) * slope
        small_store(70 + 2 * i, jnp.sum(up_grad, 0, keepdims=True))
        m.ul[i] = up_grad.astype(BF)
        turned_hidden = activated.T.astype(BF)

        def body(n, _):
            tile = pl.ds(pl.multiple_of(n * 512, 512), 512)
            m.gr[3 + i, tile, :] = mm(m.nmt[tile, :], m.ul[i]).astype(BF)
            m.gc[1 + i, :, tile] = mm(turned_hidden, m.dy[:, tile]).astype(BF)
            return 0

        lax.fori_loop(0, width // 512, body, 0)

    out, back = m.na, m.dy

    def tile_of(n):
        return pl.ds(pl.multiple_of(n * ROW_TILE, ROW_TILE), ROW_TILE)

    def small_add_rows(first, n, value):
        row = jnp.sum(value, 0, keepdims=True)
        for h in range(ROW_TILE // 128):
            m.ps[0, pl.ds(first + n * (ROW_TILE // 128) + h, 1), :] = row[:, h * 128 : (h + 1) * 128]

    def end_out(n):
        tile = tile_of(n)
        total = mm(m.al[...], m.wc[0, :, tile])
        for i in range(ff_chunks):
            total += mm(m.hid[i], m.wc[1 + i, :, tile])
        out[:, tile] = total.astype(BF)

    def end_back(n):
        tile = tile_of(n)
        attn_back = mm_nt(m.low[:, :HD], m.wr[0, tile, :])
        for a in (1, 2):
            attn_back += mm_nt(m.low[:, a * HD : (a + 1) * HD], m.wr[a, tile, :])
        mlp_back = mm_nt(m.ul[0], m.wr[3, tile, :])
        for i in range(1, ff_chunks):
            mlp_back += mm_nt(m.ul[i], m.wr[3 + i, tile, :])
        normal = (m.x[:, tile].astype(F32) - m.mean[...]) * m.inv[...]
        small_add_rows(0, n, attn_back * normal)
        small_add_rows(16, n, attn_back)
        small_add_rows(32, n, mlp_back * normal)
        small_add_rows(48, n, mlp_back)
        small_add_rows(78, n, m.dy[:, tile].astype(F32))
        back[:, tile] = (attn_back * m.gv[0:1, tile] + mlp_back * m.gv[2:3, tile]).astype(BF)

    def end_quarter(piece, which, n):
        count = quarter // ROW_TILE
        odd = at.depth % 2
        first = which * 2 + (odd if n else 1 - odd)

        def body(i, _):
            piece(first * count + i)
            return 0

        lax.fori_loop(0, count, body, 0)

    ends = (out, back)

    def quarter_of(which, n):
        odd = at.depth % 2
        return pl.ds(pl.multiple_of(which * half + (odd if n else 1 - odd) * quarter, quarter), quarter)

    def offer():
        pl.semaphore_signal(m.free, inc=1, device_id=at.twin(), device_id_type=MESH)

    def sum_start(i, n):
        if i == n == 0:
            pl.semaphore_wait(m.free, 1)
        return remote(
            ends[i].at[:, quarter_of(1 - at.tp, n)],
            m.nm.at[:, quarter_of(i, n)],
            m.o_s.at[i, n],
            m.o_r.at[i, n],
            at.twin(),
        )

    def sum_add(i, n):
        mine = ends[i]
        into, source = quarter_of(at.tp, n), quarter_of(i, n)

        def add(z, _):
            block = token_rows(z)
            total = mine[block, into].astype(F32) + m.nm[block, source].astype(F32)
            mine[block, into] = total.astype(BF)
            return 0

        lax.fori_loop(0, depth_size, add, 0)

    def sum_step(i, step, copy):
        received([copy])
        mine = ends[i]
        if step == 0:
            sum_add(i, 0)
            source, into, there = mine.at[her_pair, her_quarter], m.tz.at[i, 0], near
        elif step == 1:
            total = mine[her_pair, my_quarter].astype(F32) + m.tz[i, 0].astype(F32)
            mine[her_pair, my_quarter] = total.astype(BF)
            source, into, there = mine.at[her_pair, my_quarter], m.tz.at[i, 1], far
        elif step == 2:
            total = mine[my_pair, my_quarter].astype(F32) + m.tz[i, 1].astype(F32)
            mine[my_pair, my_quarter] = total.astype(BF)
            source, into, there = mine.at[token_rows(near_depth), my_cols], m.te.at[i], near
        else:
            total = mine[token_rows(at.depth), my_cols].astype(F32) + m.te[i].astype(F32)
            m.fin[i, :, my_cols] = total.astype(BF)
            source, into, there = m.fin.at[i, :, my_cols], m.fin.at[i, :, my_cols], at.twin()
        return remote(source, into, m.o_s.at[i, 2 + step], m.o_r.at[i, 2 + step], there)

    def small_group(stage):
        return remote(m.ps.at[stage], m.pl.at[stage], m.p_s.at[stage], m.p_r.at[stage], at.across(stage))

    def small_add(stage, copy):
        received([copy])
        m.ps[stage + 1] = m.ps[stage] + m.pl[stage]

    def small_depth():
        total = m.ps.at[bits]
        copies = [
            remote(total, m.pz.at[at.depth], m.p_s.at[bits + s], m.p_r.at[bits + s], at.along(s))
            for s in range(1, depth_size)
        ]
        m.pz[at.depth] = m.ps[bits]
        return copies

    def small_twin(copies):
        received(copies)
        value = m.pz[0]
        for z in range(1, depth_size):
            value = value + m.pz[z]
        m.px[0] = value
        return remote(m.px.at[0], m.px.at[1], m.p_s.at[bits], m.p_r.at[bits], at.twin())

    def small_finish(copy):
        received([copy])
        for v in range(4):
            for b in range(block_count):
                row = v * 16 + b
                into = v * 16 + natural[b]
                m.norm_sums[into : into + 1, :] = m.px[0, row : row + 1, :] + m.px[1, row : row + 1, :]
        for b in range(block_count):
            m.s_dy[natural[b] : natural[b] + 1, :] = m.ps[bits, 78 + b : 79 + b, :]
        for z in range(depth_size):
            m.s_query[2 * z : 2 * z + 2, :] = m.pz[z, 64:66, :]
            m.s_key[2 * z : 2 * z + 2, :] = m.pz[z, 66:68, :]
            m.s_value[2 * z : 2 * z + 2, :] = m.pz[z, 68:70, :]
            m.s_up[8 * z : 8 * z + 8, :] = m.pz[z, 70:78, :]

    z_live, g_live, t_live, k_live, f_live, e_live, x_live, s_live, d_live, p_live = ({} for _ in range(10))
    swapped = {0: [], 1: []}
    buffers = (m.x, m.dy)

    def do_zs(n):
        z_live[n] = z_start(n)

    def do_zy(n):
        z_wait(z_live[n])
        g_live[n] = g_start(n, 0)

    def do_yc(n):
        received(g_live[n])
        g_live[n] = g_start(n, 1)

    def do_cw(n):
        received(g_live[n])

    def do_ta(n):
        t_live[n] = token_step(n, buffers[n], 0, [])

    def do_tb(n):
        token_step(n, buffers[n], 1, t_live[n])

    def do_tc(n):
        token_step(n, buffers[n], 2, t_live[n])

    def do_td(n):
        token_step(n, buffers[n], 3, t_live[n])

    def do_te(n):
        received(swapped[n])

    do_norm, do_vec, do_tab, do_aff = place_rows, place_vectors, make_tables, affine
    do_qq, do_kk, do_val, do_hg = make_query, make_keys, make_values, head_grads
    do_at, do_ag, do_go, do_ff, do_of = attend, attention_grads, out_grads, feed_forward, offer

    def do_ky(n):
        k_live[n] = [kv_start(n, 0)]

    def do_kc(n):
        received(k_live[n])
        k_live[n].append(kv_start(n, 1))

    def do_kw(n):
        received(k_live[n][1:])

    def do_bw(n):
        if n == 0:
            settle(k_live[0] + k_live[1])
        attend_back(n)

    def do_dc():
        d_live[1] = dkv_start(1)

    def do_dy():
        dkv_finish(1, d_live[1])
        d_live[0] = dkv_start(0)

    def do_dw():
        dkv_finish(0, d_live[0])

    def do_fc(n):
        f_live[n] = fold_start(n, 1)

    def do_fy(n):
        fold_add(n, 1, f_live[n])
        f_live[n] = fold_start(n, 0)

    def do_fz(n):
        fold_add(n, 0, f_live[n])
        e_live[n] = end_start(n)

    def do_fq(n):
        f_live[n] = depth_first_start(n, f_live[n])

    def do_fr(n):
        f_live[n] = depth_first_fold(n, f_live[n])

    def do_fs(n):
        e_live[n] = depth_first_end(n, f_live[n])

    def do_ew(n):
        here = depth_size if n in late else 1
        received(e_live[n][:-here])
        for copy in e_live[n][-here:]:
            copy.wait()

    def do_eo(n):
        end_quarter(end_out, at.tp if n >= 2 else 1 - at.tp, n % 2)

    def do_eb(n):
        if n == 0:
            settle(t_live[1] + swapped[1])
        end_quarter(end_back, at.tp if n >= 2 else 1 - at.tp, n % 2)

    def do_sx(n):
        x_live[n] = sum_start(n // 2, n % 2)

    def do_sa(n):
        s_live[n] = sum_step(n, 0, x_live[2 * n])

    def do_sm(n):
        received([x_live[2 * n + 1]])
        sum_add(n, 1)

    def do_sb(n):
        s_live[n] = sum_step(n, 1, s_live[n])

    def do_sc(n):
        s_live[n] = sum_step(n, 2, s_live[n])

    def do_sd(n):
        s_live[n] = sum_step(n, 3, s_live[n])

    def do_sw(n):
        received([s_live[n]])

    def do_pa():
        p_live[0] = small_group(0)

    def do_pb():
        small_add(0, p_live[0])
        p_live[1] = small_group(1)

    def do_pc():
        small_add(1, p_live[1])
        p_live[2] = small_depth()

    def do_pd():
        p_live[3] = small_twin(p_live[2])

    def do_pe():
        small_finish(p_live[3])

    do_zs(1)
    do_zs(2)
    do_norm()
    do_zs(10)
    do_zy(1)
    do_ta(0)
    do_vec()
    do_zy(2)
    do_zs(4)
    do_tb(0)
    do_ta(1)
    do_zy(10)
    do_yc(2)
    do_tab()
    do_zy(4)
    do_zs(3)
    do_tc(0)
    do_cw(2)
    do_zs(0)
    do_zy(3)
    do_zs(9)
    do_td(0)
    do_tb(1)
    do_yc(10)
    do_yc(1)
    do_zy(0)
    do_zs(11)
    do_yc(4)
    do_te(0)
    do_zs(8)
    do_zy(9)
    do_zs(6)
    do_aff()
    do_yc(3)
    do_val()
    do_ky(1)
    do_cw(1)
    do_kk()
    do_tc(1)
    do_ky(0)
    do_zs(7)
    do_yc(0)
    do_cw(0)
    do_kc(1)
    do_zy(11)
    do_kc(0)
    do_zy(8)
    do_qq()
    do_kw(0)
    do_td(1)
    do_yc(9)
    do_kw(1)
    do_at(0)
    do_at(1)
    do_at(2)
    do_cw(3)
    do_zs(5)
    do_zy(6)
    do_yc(11)
    do_cw(4)
    do_at(3)
    do_yc(8)
    do_te(1)
    do_go()
    do_fc(3)
    do_hg()
    do_cw(10)
    do_bw(0)
    do_zy(7)
    do_bw(1)
    do_cw(8)
    do_cw(11)
    do_bw(2)
    do_bw(3)
    do_dc()
    do_zy(5)
    do_ff(3)
    do_yc(6)
    do_cw(9)
    do_fq(3)
    do_ff(2)
    do_fc(9)
    do_cw(6)
    do_yc(7)
    do_dy()
    do_yc(5)
    do_cw(7)
    do_ff(1)
    do_fc(7)
    do_cw(5)
    do_ff(0)
    do_fc(5)
    do_of()
    do_fc(6)
    do_fy(9)
    do_fq(7)
    do_fy(5)
    do_dw()
    do_ag()
    do_fc(0)
    do_eo(0)
    do_sx(0)
    do_fc(4)
    do_eo(1)
    do_fz(9)
    do_sx(1)
    do_eb(0)
    do_fy(0)
    do_eb(1)
    do_eo(2)
    do_eb(3)
    do_fc(1)
    do_fz(5)
    do_eb(2)
    do_pa()
    do_ew(9)
    do_fc(11)
    do_pb()
    do_fc(2)
    do_fy(1)
    do_fc(10)
    do_fy(4)
    do_sx(2)
    do_fz(0)
    do_pc()
    do_fy(10)
    do_eo(3)
    do_sa(0)
    do_fz(1)
    do_fz(4)
    do_sm(0)
    do_pd()
    do_fy(11)
    do_fc(8)
    do_sx(3)
    do_ew(0)
    do_fr(7)
    do_sb(0)
    do_sa(1)
    do_fz(11)
    do_fy(2)
    do_ew(1)
    do_sm(1)
    do_sb(1)
    do_fs(7)
    do_fy(8)
    do_ew(5)
    do_fr(3)
    do_pe()
    do_sc(0)
    do_fy(6)
    do_fz(8)
    do_fz(10)
    do_sc(1)
    do_fz(6)
    do_sd(0)
    do_fs(3)
    do_fz(2)
    do_ew(10)
    do_ew(11)
    do_ew(4)
    do_ew(8)
    do_sd(1)
    do_ew(2)
    do_sw(0)
    do_ew(6)
    do_ew(7)
    do_sw(1)
    do_ew(3)
    for copy in sends:
        if not any(copy is other for other in settled):
            copy.wait_send()


def fits(depth_size, group, depth_rows, rows, width, ff_chunks):
    sizes = layout_of(depth_size, group, depth_rows, rows, width, ff_chunks)
    total = sum(math.prod(shape) * jnp.dtype(kind).itemsize for _, shape, kind in sizes)
    shaped = group == depth_size == ff_chunks == 4 and depth_rows == rows == 128
    return shaped and total < VMEM_BYTES


def fused_shards(
    layer_input,
    block_order,
    attn_gain,
    attn_shift,
    mlp_gain,
    mlp_shift,
    w_query,
    b_query,
    w_key,
    b_key,
    w_value,
    b_value,
    w_out,
    b_out,
    w_up,
    b_up,
    w_down,
    b_down,
    out_grad,
):
    rows, width = layer_input.shape
    tp_size = lax.axis_size("tp")
    depth_size = HEADS // tp_size
    group = lax.axis_size("ctx") // depth_size
    depth_rows = width // (depth_size * group)
    ff_width = w_up.shape[1] // depth_size
    ff_chunks = ff_width // CHUNK
    tokens = depth_size * rows
    at = Place(depth_size, group)

    freqs = (10000.0 ** (-(2.0 * np.arange(ROT // 2, dtype=np.float32)) / ROT)).astype(np.float32)
    freqs = np.tile(freqs, (8, 128 // (ROT // 2)))

    def in_rows(vector):
        return vector.reshape(-1, 128)

    buffers = layout_of(depth_size, group, depth_rows, rows, width, ff_chunks)
    semaphores = semaphores_of(depth_size, group, 4 + 2 * ff_chunks)
    names = tuple(INPUTS) + tuple(OUTPUTS) + tuple(b[0] for b in buffers) + tuple(s[0] for s in semaphores) + ("free",)
    vmem = pl.BlockSpec(memory_space=pltpu.VMEM)
    hbm = pl.BlockSpec(memory_space=pl.ANY)
    shape = jax.ShapeDtypeStruct
    wide, thin = depth_size * HD, depth_size * ff_width
    results = pl.pallas_call(
        functools.partial(fused_kernel, names, depth_size, group),
        out_shape=(
            shape((2, rows, width), BF),
            shape((depth_rows, wide), BF),
            shape((depth_rows, wide), BF),
            shape((depth_rows, wide), BF),
            shape((wide, depth_rows), BF),
            shape((depth_rows, thin), BF),
            shape((thin, depth_rows), BF),
            shape((4 * width // 128, 128), F32),
            shape((wide // 128, 128), F32),
            shape((wide // 128, 128), F32),
            shape((wide // 128, 128), F32),
            shape((thin // 128, 128), F32),
            shape((width // 128, 128), F32),
        ),
        in_specs=[pl.BlockSpec(memory_space=pltpu.SMEM)] + [vmem] * 11 + [hbm] * 6,
        out_specs=(vmem,) + (hbm,) * 6 + (vmem,) * 6,
        scratch_shapes=[pltpu.VMEM(s, t) for _, s, t in buffers]
        + [pltpu.SemaphoreType.DMA(s) for _, s in semaphores]
        + [pltpu.SemaphoreType.REGULAR],
        compiler_params=pltpu.CompilerParams(
            collective_id=4, has_side_effects=True, vmem_limit_bytes=VMEM_BYTES
        ),
    )(
        block_order,
        layer_input,
        out_grad,
        freqs,
        *[in_rows(v) for v in (attn_gain, attn_shift, mlp_gain, mlp_shift)],
        *[in_rows(v) for v in (b_query, b_key, b_value, b_up)],
        w_query,
        w_key,
        w_value,
        w_out,
        w_up,
        w_down,
    )
    sums, *parts = results
    output, input_grad, *rest = close(
        depth_size, group, layer_input, out_grad, sums, in_rows(b_out), in_rows(b_down), parts
    )
    small = [vector.reshape(-1) for vector in rest[6:]]
    norms, (to_query, to_key, to_value, to_up, to_dy, again) = small[:4], small[4:]
    return (output, input_grad, *rest[:6], to_query, to_key, to_value, to_dy, to_up, again, *norms)


def close_kernel(depth_size, group, x_in, dy_in, sums, b_out, b_down, *refs):
    grads, (norm_sums, *small), results = refs[:6], refs[6:12], refs[12:]
    layer_output, input_grad, wide, norms, others = (
        results[0],
        results[1],
        results[2:8],
        results[8:12],
        results[12:],
    )
    for source, into in zip(grads, wide, strict=True):
        into[...] = source[...].astype(F32)
    for v, into in enumerate(norms):
        count = into.shape[0]
        into[...] = norm_sums[v * count : (v + 1) * count, :]
    for source, into in zip(small + small[-1:], others, strict=True):
        into[...] = source[...]
    x = x_in[...].astype(F32)
    width = x.shape[1]
    natural = natural_blocks(depth_size, group)
    size = width // len(natural)
    centered = x - jnp.mean(x, -1, keepdims=True)
    inverse = lax.rsqrt(jnp.mean(centered * centered, -1, keepdims=True) + norm_epsilon)
    normal = centered * inverse
    total = jnp.zeros((x.shape[0], 1), F32)
    against = jnp.zeros((x.shape[0], 1), F32)
    for b, c in enumerate(natural):
        out_of, into = slice(b * size, (b + 1) * size), slice(c * size, (c + 1) * size)
        bias = b_out[c : c + 1, :] + b_down[c : c + 1, :]
        layer_output[:, into] = (x[:, into] + sums[0, :, out_of].astype(F32) + bias).astype(BF)
        piece = sums[1, :, out_of].astype(F32)
        total += jnp.sum(piece, -1, keepdims=True)
        against += jnp.sum(piece * normal[:, into], -1, keepdims=True)
    total, against = total / width, against / width
    for b, c in enumerate(natural):
        out_of, into = slice(b * size, (b + 1) * size), slice(c * size, (c + 1) * size)
        piece = sums[1, :, out_of].astype(F32) - total - normal[:, into] * against
        input_grad[:, into] = dy_in[:, into].astype(F32) + inverse * piece


def close(depth_size, group, x_in, dy_in, sums, b_out, b_down, parts):
    rows, width = x_in.shape
    steps = rows // 64
    grads, small = parts[:6], parts[6:]
    norms = [jax.ShapeDtypeStruct((width // 128, 128), F32)] * 4
    copies = [jax.ShapeDtypeStruct(s.shape, F32) for s in small[1:] + small[-1:]]

    def by_rows(shape):
        block = shape[:-2] + (shape[-2] // steps, shape[-1])
        return pl.BlockSpec(block, lambda i: (0,) * (len(shape) - 2) + (i, 0))

    def all_of(shape):
        return pl.BlockSpec(shape, lambda i: (0,) * len(shape))

    return pl.pallas_call(
        functools.partial(close_kernel, depth_size, group),
        grid=(steps,),
        out_shape=[
            jax.ShapeDtypeStruct(x_in.shape, BF),
            jax.ShapeDtypeStruct(x_in.shape, F32),
            *[jax.ShapeDtypeStruct(g.shape, F32) for g in grads],
            *norms,
            *copies,
        ],
        in_specs=[by_rows(x_in.shape)] * 2
        + [by_rows(sums.shape), all_of(b_out.shape), all_of(b_down.shape)]
        + [by_rows(g.shape) for g in grads]
        + [all_of(s.shape) for s in small],
        out_specs=[by_rows(x_in.shape)] * 2
        + [by_rows(g.shape) for g in grads]
        + [all_of(s.shape) for s in norms + copies],
        compiler_params=pltpu.CompilerParams(vmem_limit_bytes=VMEM_BYTES),
    )(x_in, dy_in, sums, b_out, b_down, *grads, *small)


def shards(
    layer_input,
    block_order,
    attn_gain,
    attn_shift,
    mlp_gain,
    mlp_shift,
    w_query,
    b_query,
    w_key,
    b_key,
    w_value,
    b_value,
    w_out,
    b_out,
    w_up,
    b_up,
    w_down,
    b_down,
    out_grad,
):
    rows, width = layer_input.shape
    depth_size = HEADS // lax.axis_size("tp")
    group = lax.axis_size("ctx") // depth_size
    ff_chunks = w_up.shape[1] // depth_size // CHUNK
    whole = fits(depth_size, group, width // (depth_size * group), rows, width, ff_chunks)
    chosen = fused_shards if whole else staged_shards
    return chosen(
        layer_input, block_order, attn_gain, attn_shift, mlp_gain, mlp_shift, w_query, b_query, w_key, b_key, w_value, b_value, w_out, b_out, w_up, b_up, w_down, b_down, out_grad
    )


def staged_shards(
    layer_input,
    block_order,
    attn_gain,
    attn_shift,
    mlp_gain,
    mlp_shift,
    w_query,
    b_query,
    w_key,
    b_key,
    w_value,
    b_value,
    w_out,
    b_out,
    w_up,
    b_up,
    w_down,
    b_down,
    out_grad,
):
    rows, width = layer_input.shape
    ctx_size = lax.axis_size("ctx")
    tp_size = lax.axis_size("tp")
    depth_size = HEADS // tp_size
    group = ctx_size // depth_size
    bits = group.bit_length() - 1
    depth_rows = width // ctx_size
    hidden_width = w_up.shape[1] // depth_size
    ff_chunks = hidden_width // CHUNK
    at = Place(depth_size, group)
    block_rows = rows // 2

    def permuted(array):
        lead = array.shape[:-1]
        n = len(lead)
        split = array.reshape(lead + (depth_size,) + (2,) * bits + (depth_rows,))
        order = tuple(range(n)) + tuple(n + 1 + b for b in reversed(range(bits))) + (n, n + 1 + bits)
        return split.transpose(order).reshape(lead + (width,))

    def restored(array):
        lead = array.shape[:-1]
        n = len(lead)
        split = array.reshape(lead + (2,) * bits + (depth_size, depth_rows))
        order = tuple(range(n)) + (n + bits,) + tuple(n + b for b in reversed(range(bits))) + (n + bits + 1,)
        return split.transpose(order).reshape(lead + (width,))

    def slot_members():
        table = []
        for slot in range(group):
            member = 0
            for stage in range(bits):
                member += ((slot >> stage) & 1) << (bits - 1 - stage)
            table.append(member)
        return table

    blocks = block_order.reshape(depth_size, group, 2)
    order = jnp.stack([blocks[:, m] for m in slot_members()], 0)
    place = order[..., None] * block_rows + jnp.arange(block_rows, dtype=jnp.int32)
    key_place = place.reshape(group * depth_size * rows)
    token_total = depth_size * rows
    query_place = lax.dynamic_slice_in_dim(key_place, at.slot * token_total, token_total)
    cosine, sine_table = rope_tables(query_place)

    inputs32 = layer_input.astype(F32)
    centered = inputs32 - jnp.mean(inputs32, -1, keepdims=True)
    inverse = lax.rsqrt(jnp.mean(centered * centered, -1, keepdims=True) + norm_epsilon)
    normal32 = centered * inverse

    def halves(array):
        return permuted(array).reshape(rows, tp_size, width // tp_size).transpose(1, 0, 2)

    def by_head(weight):
        return weight.reshape(depth_rows, depth_size, HD).transpose(1, 0, 2)

    def by_chunk(weight):
        return weight.reshape(depth_rows, depth_size, ff_chunks, CHUNK).transpose(2, 1, 0, 3)

    weights = jnp.concatenate(
        [
            jnp.concatenate([by_head(w_query), by_head(w_key)], -1)[None],
            jnp.concatenate([by_head(w_value), by_head(w_out.T)], -1)[None],
            jnp.concatenate([by_chunk(w_up), by_chunk(w_down.T)], -1),
        ],
        0,
    )
    normal, grad, gathered = gather_all(
        depth_size, group, halves(normal32.astype(BF)), halves(out_grad), weights
    )
    full = gathered.reshape(2 + ff_chunks, width, 2 * HD)
    gain_a, shift_a, gain_m, shift_m = permuted(jnp.stack([attn_gain, attn_shift, mlp_gain, mlp_shift]))
    normal_tokens = normal.astype(F32)
    attn_in = (normal_tokens * gain_a + shift_a).astype(BF)
    mlp_in = (normal_tokens * gain_m + shift_m).astype(BF)

    def own_part(vector, size):
        return lax.dynamic_slice_in_dim(vector, at.depth * size, size)

    query_key = mm(attn_in, full[0])
    query = rotate(query_key[:, :HD] + own_part(b_query, HD), cosine, sine_table).astype(BF)
    keys = rotate(query_key[:, HD:] + own_part(b_key, HD), cosine, sine_table).astype(BF)
    values = (mm(attn_in, full[1, :, :HD]) + own_part(b_value, HD)).astype(BF)
    out_t = full[1, :, HD:]
    shared = share_group(depth_size, group, jnp.concatenate([keys, values], -1))
    shared = shared.reshape(group * token_total, 2 * HD)
    all_keys, all_values = shared[:, :HD], shared[:, HD:]
    score_scale = 1.0 / math.sqrt(HD)
    scores = mm_nt(query, all_keys) * score_scale
    allowed = key_place[None, :] <= query_place[:, None]
    scores = jnp.where(allowed, scores, -1e30)
    top = jnp.max(scores, -1, keepdims=True)
    raw = jnp.exp(scores - top)
    probs = raw / jnp.sum(raw, -1, keepdims=True)
    probs_low = probs.astype(BF)
    attended = mm(probs_low, all_values)
    attn_low = attended.astype(BF)

    head_grad = mm(grad, out_t).astype(BF)
    delta = jnp.sum(head_grad.astype(F32) * attended, -1, keepdims=True)
    value_part = mm_tn(probs_low, head_grad)
    score_grad = (probs * (mm_nt(head_grad, all_values) - delta) * score_scale).astype(BF)
    query_acc = mm(score_grad, all_keys)
    key_part = mm_tn(score_grad, query)
    parts = jnp.concatenate([key_part, value_part], -1).astype(BF)
    folded = fold_group(depth_size, group, parts.reshape(group, token_total, 2 * HD))
    own_grads = lax.dynamic_index_in_dim(folded, at.slot, 0, keepdims=False).astype(F32)
    query_lin = rotate(query_acc, cosine, -sine_table)
    key_lin = rotate(own_grads[:, :HD], cosine, -sine_table)
    value_lin = own_grads[:, HD:]
    query_low, key_low, value_low = query_lin.astype(BF), key_lin.astype(BF), value_lin.astype(BF)
    query_key_low = jnp.concatenate([query_low, key_low], -1)
    attn_back = mm_nt(query_key_low, full[0]) + mm_nt(value_low, full[1, :, :HD])
    grad_chunks = [
        mm_tn(attn_in, query_key_low).astype(BF),
        jnp.concatenate([mm_tn(attn_in, value_low), mm_tn(grad, attn_low)], -1).astype(BF),
    ]

    branches = mm_nt(attn_low, out_t)
    mlp_back = jnp.zeros((token_total, width), F32)
    bias_up = own_part(b_up, hidden_width).reshape(ff_chunks, CHUNK)
    up_sums = []
    for i in range(ff_chunks):
        up, down_t = full[2 + i, :, :CHUNK], full[2 + i, :, CHUNK:]
        activated, slope = gelu_parts(mm(mlp_in, up) + bias_up[i])
        hidden = activated.astype(BF)
        up_grad = mm(grad, down_t) * slope
        up_sums.append(jnp.sum(up_grad, 0))
        up_low = up_grad.astype(BF)
        branches = branches + mm_nt(hidden, down_t)
        mlp_back = mlp_back + mm_nt(up_low, up)
        grad_chunks.append(jnp.concatenate([mm_tn(mlp_in, up_low), mm_tn(grad, hidden)], -1).astype(BF))

    normal_tokens2 = normal.astype(F32)
    back = attn_back * gain_a + mlp_back * gain_m
    grads = jnp.stack(grad_chunks).reshape(2 + ff_chunks, group, depth_size, depth_rows, 2 * HD)
    norm_sums = restored(
        jnp.stack(
            [
                jnp.sum(attn_back * normal_tokens2, 0),
                jnp.sum(attn_back, 0),
                jnp.sum(mlp_back * normal_tokens2, 0),
                jnp.sum(mlp_back, 0),
            ]
        )
    )
    own_biases = jnp.concatenate(
        [jnp.sum(query_lin, 0), jnp.sum(key_lin, 0), jnp.sum(value_lin, 0)] + up_sums
    )
    spread = jnp.where(
        jnp.arange(depth_size, dtype=jnp.int32)[:, None] == at.depth, own_biases[None, :], 0.0
    )
    norm_sums = lax.psum(norm_sums, ("ctx", "tp"))
    grad32 = out_grad.astype(F32)
    spread, bias_grad = lax.psum((spread, jnp.sum(grad32, 0)), "ctx")

    out_sum, back_sum, grad_shares = reduce_all(
        depth_size, group, branches.astype(BF), back.astype(BF), grads
    )
    layer_output = (inputs32 + restored(out_sum).astype(F32) + b_out + b_down).astype(BF)
    back_total = restored(back_sum).astype(F32)
    input_grad = grad32 + inverse * (
        back_total
        - jnp.mean(back_total, -1, keepdims=True)
        - normal32 * jnp.mean(back_total * normal32, -1, keepdims=True)
    )

    def from_head(share):
        return share.transpose(1, 0, 2).reshape(depth_rows, depth_size * HD).astype(F32)

    def from_chunk(share):
        return share.transpose(2, 1, 0, 3).reshape(depth_rows, depth_size * hidden_width).astype(F32)

    return (
        layer_output,
        input_grad,
        from_head(grad_shares[0, :, :, :HD]),
        from_head(grad_shares[0, :, :, HD:]),
        from_head(grad_shares[1, :, :, :HD]),
        from_head(grad_shares[1, :, :, HD:]).T,
        from_chunk(grad_shares[2:, :, :, :CHUNK]),
        from_chunk(grad_shares[2:, :, :, CHUNK:]).T,
        spread[:, :HD].reshape(-1),
        spread[:, HD : 2 * HD].reshape(-1),
        spread[:, 2 * HD : 3 * HD].reshape(-1),
        bias_grad,
        spread[:, 3 * HD :].reshape(-1),
        bias_grad,
        norm_sums[0],
        norm_sums[1],
        norm_sums[2],
        norm_sums[3],
    )


def solution(mesh):
    in_specs = (
        P("ctx", None),
        P(),
        P(),
        P(),
        P(),
        P(),
        P("ctx", "tp"),
        P("tp"),
        P("ctx", "tp"),
        P("tp"),
        P("ctx", "tp"),
        P("tp"),
        P("tp", "ctx"),
        P(),
        P("ctx", "tp"),
        P("tp"),
        P("tp", "ctx"),
        P(),
        P("ctx", None),
    )
    out_specs = (
        P("ctx", None),
        P("ctx", None),
        P("ctx", "tp"),
        P("ctx", "tp"),
        P("ctx", "tp"),
        P("tp", "ctx"),
        P("ctx", "tp"),
        P("tp", "ctx"),
        P("tp"),
        P("tp"),
        P("tp"),
        P(),
        P("tp"),
        P(),
        P(),
        P(),
        P(),
        P(),
    )
    return jax.shard_map(shards, mesh=mesh, in_specs=in_specs, out_specs=out_specs, check_vma=False)
```

```python
import functools
import math

import jax
import jax.numpy as jnp
import numpy as np
from jax import lax
from jax.experimental import pallas as pl
from jax.experimental.pallas import tpu as pltpu
from jax.sharding import PartitionSpec as P

HEADS = 8
HD = 256
ROT = 64
CHUNK = 256

norm_epsilon = 1e-05
BF = jnp.bfloat16
F32 = jnp.float32
MESH = pl.DeviceIdType.MESH


def mm(a, b):
    return jnp.dot(a, b, preferred_element_type=F32)


def mm_tn(a, b):
    return lax.dot_general(a, b, (((0,), (0,)), ((), ())), preferred_element_type=F32)


def mm_nt(a, b):
    return lax.dot_general(a, b, (((1,), (1,)), ((), ())), preferred_element_type=F32)


class Place:
    def __init__(self, depth_size, group):
        self.depth_size = depth_size
        self.group = group
        self.bits = group.bit_length() - 1
        self.ctx = lax.axis_index("ctx")
        self.tp = lax.axis_index("tp")
        self.depth = self.ctx // group
        self.member = self.ctx % group
        slot = 0
        for stage in range(self.bits):
            slot = slot + self.bit(stage) * 2**stage
        self.slot = slot

    def bit(self, stage):
        return (self.member // 2 ** (self.bits - 1 - stage)) % 2

    def along(self, step):
        return {"ctx": lax.rem(self.depth + step, self.depth_size) * self.group + self.member}

    def across(self, stage):
        reach = 2 ** (self.bits - 1 - stage)
        return {"ctx": self.ctx + (1 - 2 * self.bit(stage)) * reach}

    def twin(self):
        return {"tp": 1 - self.tp}

    def base(self, stage):
        return (self.slot // 2**stage) * 2**stage

    def greet(self, devices):
        barrier = pltpu.get_barrier_semaphore()
        for device in devices:
            pl.semaphore_signal(barrier, inc=1, device_id=device, device_id_type=MESH)
        pl.semaphore_wait(barrier, len(devices))

    def everyone(self):
        return (
            [self.along(step) for step in range(1, self.depth_size)]
            + [self.across(stage) for stage in range(self.bits)]
            + [self.twin()]
        )


def remote(src, dst, send, recv, device):
    copy = pltpu.make_async_remote_copy(
        src_ref=src, dst_ref=dst, send_sem=send, recv_sem=recv, device_id=device, device_id_type=MESH
    )
    copy.start()
    return copy


def local(src, dst, sem):
    copy = pltpu.make_async_copy(src, dst, sem)
    copy.start()
    return copy


def gather_kernel(depth_size, group, x_in, dy_in, w_in, x_out, dy_out, w_out, tz_s, tz_r, tx_s, tx_r, t_l, z_s, z_r, z_l, g_s, g_r):
    at = Place(depth_size, group)
    at.greet(at.everyone())
    rows, half = x_in.shape[1:]
    sent = []
    mine = pl.ds(pl.multiple_of(at.depth * rows, rows), rows)
    my_cols = pl.ds(pl.multiple_of(at.tp * half, half), half)

    def token_start(i, src, dst):
        copies = [
            remote(src.at[at.tp], dst.at[mine, my_cols], tz_s.at[i, s], tz_r.at[i, s], at.along(s))
            for s in range(1, depth_size)
        ]
        copies.append(local(src.at[at.tp], dst.at[mine, my_cols], t_l.at[i]))
        return copies

    def token_swap(i, copies, dst):
        for copy in copies[:-1]:
            copy.wait_recv()
            sent.append(copy)
        copies[-1].wait()
        return remote(dst.at[:, my_cols], dst.at[:, my_cols], tx_s.at[i], tx_r.at[i], at.twin())

    chunks = w_in.shape[0]

    def z_start(k):
        copies = [
            remote(
                w_in.at[k, lax.rem(at.depth + s, depth_size)],
                w_out.at[k, at.slot, at.depth],
                z_s.at[k, s],
                z_r.at[k, s],
                at.along(s),
            )
            for s in range(1, depth_size)
        ]
        copies.append(local(w_in.at[k, at.depth], w_out.at[k, at.slot, at.depth], z_l.at[k]))
        return copies

    def z_wait(copies):
        for copy in copies[:-1]:
            copy.wait_recv()
            sent.append(copy)
        copies[-1].wait()

    def g_start(k, stage):
        held = pl.ds(at.base(stage), 2**stage)
        return remote(
            w_out.at[k, held], w_out.at[k, held], g_s.at[k, stage], g_r.at[k, stage], at.across(stage)
        )

    ahead = 2
    tokens = [token_start(0, x_in, x_out)]
    z_copies = {k: z_start(k) for k in range(min(ahead, chunks))}
    stages = {}
    swaps = []
    for step in range(chunks + at.bits):
        if step < chunks:
            z_wait(z_copies[step])
            stages[step] = [g_start(step, 0)]
            if step + ahead < chunks:
                z_copies[step + ahead] = z_start(step + ahead)
            if step == 0:
                swaps.append(token_swap(0, tokens[0], x_out))
                tokens.append(token_start(1, dy_in, dy_out))
            if step == 1:
                swaps.append(token_swap(1, tokens[1], dy_out))
        for stage in range(1, at.bits + 1):
            k = step - stage
            if 0 <= k < chunks:
                stages[k][stage - 1].wait_recv()
                if stage < at.bits:
                    stages[k].append(g_start(k, stage))
    for swap in swaps:
        swap.wait()
    for k in range(chunks):
        for copy in stages[k]:
            copy.wait_send()
    for copy in sent:
        copy.wait_send()


def gather_all(depth_size, group, x_halves, dy_halves, weights):
    tp, rows, half = x_halves.shape
    chunks, _, depth_rows, width = weights.shape
    bits = group.bit_length() - 1
    dma = pltpu.SemaphoreType.DMA
    hbm = pl.BlockSpec(memory_space=pl.ANY)
    tokens = jax.ShapeDtypeStruct((depth_size * rows, tp * half), BF)
    return pl.pallas_call(
        functools.partial(gather_kernel, depth_size, group),
        out_shape=(
            tokens,
            tokens,
            jax.ShapeDtypeStruct((chunks, group, depth_size, depth_rows, width), BF),
        ),
        in_specs=[hbm] * 3,
        out_specs=(hbm, hbm, hbm),
        scratch_shapes=[
            dma((2, depth_size)),
            dma((2, depth_size)),
            dma((2,)),
            dma((2,)),
            dma((2,)),
            dma((chunks, depth_size)),
            dma((chunks, depth_size)),
            dma((chunks,)),
            dma((chunks, bits)),
            dma((chunks, bits)),
        ],
        compiler_params=pltpu.CompilerParams(collective_id=0, has_side_effects=True),
    )(x_halves, dy_halves, weights)


def share_kernel(depth_size, group, kv_in, kv_out, send, recv, loc):
    at = Place(depth_size, group)
    at.greet([at.across(stage) for stage in range(at.bits)])
    local(kv_in, kv_out.at[at.slot], loc).wait()
    copies = []
    for stage in range(at.bits):
        held = pl.ds(at.base(stage), 2**stage)
        copy = remote(kv_out.at[held], kv_out.at[held], send.at[stage], recv.at[stage], at.across(stage))
        copy.wait_recv()
        copies.append(copy)
    for copy in copies:
        copy.wait_send()


def share_group(depth_size, group, kv):
    bits = group.bit_length() - 1
    dma = pltpu.SemaphoreType.DMA
    hbm = pl.BlockSpec(memory_space=pl.ANY)
    return pl.pallas_call(
        functools.partial(share_kernel, depth_size, group),
        out_shape=jax.ShapeDtypeStruct((group,) + kv.shape, BF),
        in_specs=[hbm],
        out_specs=hbm,
        scratch_shapes=[dma((bits,)), dma((bits,)), dma],
        compiler_params=pltpu.CompilerParams(collective_id=1, has_side_effects=True),
    )(kv)


def fold_kernel(depth_size, group, g_in, total, landing, send, recv):
    at = Place(depth_size, group)
    at.greet([at.across(stage) for stage in range(at.bits)])
    for stage in reversed(range(at.bits)):
        size = 2**stage
        own = at.base(stage)
        other = own + (1 - 2 * at.bit(stage)) * size
        source = g_in if stage == at.bits - 1 else total
        copy = remote(
            source.at[pl.ds(other, size)],
            landing.at[pl.ds(size - 1, size)],
            send.at[stage],
            recv.at[stage],
            at.across(stage),
        )
        copy.wait()

        def add(i, _):
            total[own + i] = (
                source[own + i].astype(F32) + landing[size - 1 + i].astype(F32)
            ).astype(BF)
            return 0

        lax.fori_loop(0, size, add, 0)


def fold_group(depth_size, group, grads):
    bits = group.bit_length() - 1
    dma = pltpu.SemaphoreType.DMA
    vmem = pl.BlockSpec(memory_space=pltpu.VMEM)
    return pl.pallas_call(
        functools.partial(fold_kernel, depth_size, group),
        out_shape=jax.ShapeDtypeStruct(grads.shape, BF),
        in_specs=[vmem],
        out_specs=vmem,
        scratch_shapes=[
            pltpu.VMEM((group - 1,) + grads.shape[1:], BF),
            dma((bits,)),
            dma((bits,)),
        ],
        compiler_params=pltpu.CompilerParams(
            collective_id=2, has_side_effects=True, vmem_limit_bytes=60 << 20
        ),
    )(grads)


def reduce_kernel(depth_size, group, out_in, back_in, g_in, out_sum, back_sum, g_out, total, landing, g_s, g_r, z_s, z_r, z_l, t_acc, t_swap, t_land, tx_s, tx_r, tz_s, tz_r, ty_s, ty_r):
    at = Place(depth_size, group)
    at.greet(at.everyone())
    chunks = g_in.shape[0]
    depth_rows = g_in.shape[3]
    rows = out_sum.shape[0]
    half = t_acc.shape[2]
    last = at.bits - 1
    sent = []

    def g_start(k, stage):
        size = 2**stage
        other = at.base(stage) + (1 - 2 * at.bit(stage)) * size
        source = g_in.at[k] if stage == last else total.at[k]
        return remote(
            source.at[pl.ds(other, size)],
            landing.at[k, pl.ds(size - 1, size)],
            g_s.at[k, stage],
            g_r.at[k, stage],
            at.across(stage),
        )

    def g_finish(k, stage, copy):
        copy.wait_recv()
        sent.append(copy)
        size = 2**stage
        own = at.base(stage)
        source = g_in.at[k] if stage == last else total.at[k]

        def add(i, _):
            j = i // depth_size
            z = i % depth_size
            total[k, own + j, z] = (
                source[own + j, z].astype(F32) + landing[k, size - 1 + j, z].astype(F32)
            ).astype(BF)
            return 0

        lax.fori_loop(0, size * depth_size, add, 0)

    def z_start(k):
        copies = [
            remote(
                total.at[k, at.slot, lax.rem(at.depth + s, depth_size)],
                g_out.at[k, at.depth],
                z_s.at[k, s],
                z_r.at[k, s],
                at.along(s),
            )
            for s in range(1, depth_size)
        ]
        copies.append(local(total.at[k, at.slot, at.depth], g_out.at[k, at.depth], z_l.at[k]))
        return copies

    my_cols = pl.ds(pl.multiple_of(at.tp * half, half), half)
    her_cols = pl.ds(pl.multiple_of((1 - at.tp) * half, half), half)

    def token_first(i, src):
        return remote(src.at[:, her_cols], t_swap.at[i], tx_s.at[i], tx_r.at[i], at.twin())

    def token_second(i, src, copy):
        copy.wait_recv()
        sent.append(copy)

        def add(z, _):
            block = pl.ds(pl.multiple_of(z * rows, rows), rows)
            t_acc[i, block, :] = (
                src[block, my_cols].astype(F32) + t_swap[i, block, :].astype(F32)
            ).astype(BF)
            return 0

        lax.fori_loop(0, depth_size, add, 0)
        copies = []
        for s in range(1, depth_size):
            there = lax.rem(at.depth + s, depth_size)
            block = pl.ds(pl.multiple_of(there * rows, rows), rows)
            copies.append(
                remote(
                    t_acc.at[i, block, :], t_land.at[i, s - 1], tz_s.at[i, s], tz_r.at[i, s], at.along(s)
                )
            )
        return copies

    def token_third(i, dst, copies):
        for copy in copies:
            copy.wait_recv()
            sent.append(copy)
        mine = pl.ds(pl.multiple_of(at.depth * rows, rows), rows)
        value = t_acc[i, mine, :].astype(F32)
        for s in range(1, depth_size):
            value = value + t_land[i, s - 1].astype(F32)
        dst[:, my_cols] = value.astype(BF)
        return remote(dst.at[:, my_cols], dst.at[:, my_cols], ty_s.at[i], ty_r.at[i], at.twin())

    firsts = [token_first(0, out_in), token_first(1, back_in)]
    copies_of = {k: [g_start(k, last)] for k in range(chunks)}
    z_copies = {}
    seconds = []
    thirds = []
    for step in range(chunks + at.bits):
        for back in range(at.bits):
            k = step - back
            stage = last - back
            if 0 <= k < chunks:
                g_finish(k, stage, copies_of[k][back])
                if stage > 0:
                    copies_of[k].append(g_start(k, stage - 1))
                else:
                    z_copies[k] = z_start(k)
        if step == 1:
            seconds.append(token_second(0, out_in, firsts[0]))
        if step == 2:
            seconds.append(token_second(1, back_in, firsts[1]))
        if step == 4:
            thirds.append(token_third(0, out_sum, seconds[0]))
        if step == 5:
            thirds.append(token_third(1, back_sum, seconds[1]))
    for k in range(chunks):
        for copy in z_copies[k][:-1]:
            copy.wait()
        z_copies[k][-1].wait()
    for copy in thirds:
        copy.wait()
    for copy in sent:
        copy.wait_send()


def reduce_all(depth_size, group, out_part, back_part, grads):
    chunks, _, _, depth_rows, width = grads.shape
    all_rows, columns = out_part.shape
    rows = all_rows // depth_size
    half = columns // 2
    bits = group.bit_length() - 1
    dma = pltpu.SemaphoreType.DMA
    vmem = pl.BlockSpec(memory_space=pltpu.VMEM)
    tokens = jax.ShapeDtypeStruct((rows, columns), BF)
    return pl.pallas_call(
        functools.partial(reduce_kernel, depth_size, group),
        out_shape=(tokens, tokens, jax.ShapeDtypeStruct((chunks, depth_size, depth_rows, width), BF)),
        in_specs=[vmem] * 3,
        out_specs=(vmem, vmem, vmem),
        scratch_shapes=[
            pltpu.VMEM((chunks, group, depth_size, depth_rows, width), BF),
            pltpu.VMEM((chunks, group - 1, depth_size, depth_rows, width), BF),
            dma((chunks, bits)),
            dma((chunks, bits)),
            dma((chunks, depth_size)),
            dma((chunks, depth_size)),
            dma((chunks,)),
            pltpu.VMEM((2, all_rows, half), BF),
            pltpu.VMEM((2, all_rows, half), BF),
            pltpu.VMEM((2, depth_size - 1, rows, half), BF),
            dma((2,)),
            dma((2,)),
            dma((2, depth_size)),
            dma((2, depth_size)),
            dma((2,)),
            dma((2,)),
        ],
        compiler_params=pltpu.CompilerParams(
            collective_id=3, has_side_effects=True, vmem_limit_bytes=60 << 20
        ),
    )(out_part, back_part, grads)


def rotate(values, cosine, sine_table):
    half_rot = ROT // 2
    leading = values[..., :half_rot]
    trailing = values[..., half_rot:ROT]
    return jnp.concatenate(
        [
            leading * cosine - trailing * sine_table,
            trailing * cosine + leading * sine_table,
            values[..., ROT:],
        ],
        -1,
    )


def rope_tables(positions):
    freqs = 10000.0 ** (-(2.0 * jnp.arange(ROT // 2, dtype=F32)) / ROT)
    angles = positions.astype(F32)[:, None] * freqs[None, :]
    return (jnp.cos(angles), jnp.sin(angles))


def gelu_parts(values):
    gate = 0.5 * (1.0 + lax.erf(values * math.sqrt(0.5)))
    slope = gate + values * jnp.exp(-0.5 * values * values) * (1.0 / math.sqrt(2.0 * math.pi))
    return values * gate, slope


SMALL_ROWS = 96
SMALL_SENT = 80
LATE = (3, 7,)
LATE_ROWS = 1
LATE_COLS = 2
VMEM_BYTES = 64 << 20


def slot_member(slot, bits):
    member = 0
    for stage in range(bits):
        member += ((slot >> stage) & 1) << (bits - 1 - stage)
    return member


def natural_blocks(depth_size, group):
    bits = group.bit_length() - 1
    return [
        depth * group + slot_member(slot, bits) for slot in range(group) for depth in range(depth_size)
    ]

ROW_TILE = 256
DROP = -1e30


def layout_of(depth_size, group, depth_rows, rows, width, ff_chunks):
    tokens = depth_size * rows
    half = width // 2
    landing = (group - 1) * depth_size * depth_rows
    heads = 3 + ff_chunks
    cols = 1 + ff_chunks
    return [
        ("wr", (heads, width, CHUNK), BF),
        ("wc", (cols, CHUNK, width), BF),
        ("gr", (heads, width, CHUNK), BF),
        ("gc", (cols, CHUNK, width), BF),
        ("lr", (heads, landing, CHUNK), BF),
        ("lc", (cols, CHUNK, landing), BF),
        ("x", (tokens, width), BF),
        ("dy", (tokens, width), BF),
        ("na", (tokens, width), BF),
        ("nm", (tokens, width), BF),
        ("nmt", (width, tokens), BF),
        ("kv", (group * tokens, 2 * HD), BF),
        ("q", (tokens, HD), BF),
        ("low", (tokens, 3 * HD), BF),
        ("al", (tokens, HD), BF),
        ("hg", (tokens, HD), BF),
        ("alt", (HD, tokens), BF),
        ("att", (HD, tokens), F32),
        ("dqt", (HD, tokens), F32),
        ("stat", (8, tokens), F32),
        ("tab", (group * tokens, 128), F32),
        ("kb", (8, HD), F32),
        ("hid", (ff_chunks, tokens, CHUNK), BF),
        ("ul", (ff_chunks, tokens, CHUNK), BF),
        ("tz", (2, 2, tokens // 2, half // 2), BF),
        ("te", (2, rows, half), BF),
        ("mean", (tokens, 1), F32),
        ("inv", (tokens, 1), F32),
        ("xl", (2, rows, width), BF),
        ("gv", (8, width), F32),
        ("biases", (8, HD), F32),
        ("places", (group * tokens // 128, 128), F32),
        ("ps", (group.bit_length(), SMALL_ROWS, 128), F32),
        ("pl", (group.bit_length() - 1, SMALL_ROWS, 128), F32),
        ("pz", (depth_size, SMALL_SENT, 128), F32),
        ("px", (2, SMALL_SENT, 128), F32),
        ("dr", (LATE_ROWS, 2, depth_size * depth_rows, CHUNK), BF),
        ("dc", (LATE_COLS, 2, CHUNK, depth_size * depth_rows), BF),
    ]


def semaphores_of(depth_size, group, items):
    bits = group.bit_length() - 1
    return [
        ("z_s", (items, depth_size)),
        ("z_r", (items, depth_size)),
        ("z_l", (items,)),
        ("g_s", (items, bits)),
        ("g_r", (items, bits)),
        ("t_s", (2, 3)),
        ("t_r", (2, 3)),
        ("w_s", (2, 3)),
        ("w_r", (2, 3)),
        ("kv_s", (2, 2, bits)),
        ("kv_r", (2, 2, bits)),
        ("f_s", (items, bits)),
        ("f_r", (items, bits)),
        ("e_s", (items, depth_size)),
        ("e_r", (items, depth_size)),
        ("e_l", (items,)),
        ("x_l", (2,)),
        ("d_s", (LATE_ROWS + LATE_COLS, 2, depth_size)),
        ("d_r", (LATE_ROWS + LATE_COLS, 2, depth_size)),
        ("d_l", (LATE_ROWS + LATE_COLS, depth_size)),
        ("o_s", (2, 6)),
        ("o_r", (2, 6)),
        ("p_s", (bits + depth_size,)),
        ("p_r", (bits + depth_size,)),
    ]


VECTORS = ("attn_gain", "attn_shift", "mlp_gain", "mlp_shift")
BIASES = ("b_query", "b_key", "b_value", "b_up")
INPUTS = ("blocks", "x_in", "dy_in", "freqs") + VECTORS + BIASES
INPUTS += ("w_query", "w_key", "w_value", "w_out", "w_up", "w_down")
OUTPUTS = ("fin", "g_query", "g_key", "g_value", "g_out", "g_up", "g_down")
OUTPUTS += ("norm_sums", "s_query", "s_key", "s_value", "s_up", "s_dy")


class Bag:
    pass


def fused_kernel(names, depth_size, group, *refs):
    m = Bag()
    for name, ref in zip(names, refs, strict=True):
        setattr(m, name, ref)
    at = Place(depth_size, group)
    loads = [local(source, m.xl.at[i], m.x_l.at[i]) for i, source in enumerate((m.x_in, m.dy_in))]
    at.greet(at.everyone())
    bits = at.bits
    rows, width = m.x_in.shape
    depth_rows = width // (depth_size * group)
    tokens = depth_size * rows
    half = width // 2
    ff_width = m.w_up.shape[1] // depth_size
    ff_chunks = ff_width // CHUNK
    block_count = width // depth_rows
    own_block = at.slot * depth_size + at.depth
    natural = natural_blocks(depth_size, group)
    sends, settled = [], []

    def blocks(first, count):
        return pl.ds(pl.multiple_of(first * depth_rows, depth_rows), count * depth_rows)

    def token_rows(depth):
        return pl.ds(pl.multiple_of(depth * rows, rows), rows)

    def peer(step):
        return lax.rem(at.depth + step, depth_size)

    my_cols = pl.ds(pl.multiple_of(at.tp * half, half), half)
    her_cols = pl.ds(pl.multiple_of((1 - at.tp) * half, half), half)

    units = [("r", 0), ("r", 1), ("r", 2), ("c", 0)]
    for i in range(ff_chunks):
        units += [("r", 3 + i), ("c", 1 + i)]
    row_pairs = [(m.w_query, m.g_query), (m.w_key, m.g_key), (m.w_value, m.g_value)]

    def outer(kind, a, depth, which):
        if kind == "r" and a < 3:
            return row_pairs[a][which].at[:, pl.ds(pl.multiple_of(depth * HD, HD), HD)]
        if kind == "r":
            first = pl.multiple_of(depth * ff_width + (a - 3) * CHUNK, CHUNK)
            return (m.w_up, m.g_up)[which].at[:, pl.ds(first, CHUNK)]
        if a == 0:
            return (m.w_out, m.g_out)[which].at[pl.ds(pl.multiple_of(depth * HD, HD), HD), :]
        first = pl.multiple_of(depth * ff_width + (a - 1) * CHUNK, CHUNK)
        return (m.w_down, m.g_down)[which].at[pl.ds(first, CHUNK), :]

    def part(pair, kind, a, first, count):
        if kind == "r":
            return pair[0].at[a, blocks(first, count), :]
        return pair[1].at[a, :, blocks(first, count)]

    weights, grads, landing = (m.wr, m.wc), (m.gr, m.gc), (m.lr, m.lc)

    def z_start(k):
        kind, a = units[k]
        into = part(weights, kind, a, own_block, 1)
        copies = [
            remote(outer(kind, a, peer(s), 0), into, m.z_s.at[k, s], m.z_r.at[k, s], at.along(s))
            for s in range(1, depth_size)
        ]
        copies.append(local(outer(kind, a, at.depth, 0), into, m.z_l.at[k]))
        return copies

    def z_wait(copies):
        received(copies[:-1])
        copies[-1].wait()

    def g_start(k, stage):
        kind, a = units[k]
        held = part(weights, kind, a, at.base(stage) * depth_size, 2**stage * depth_size)
        return [remote(held, held, m.g_s.at[k, stage], m.g_r.at[k, stage], at.across(stage))]

    def received(copies):
        for copy in copies:
            copy.wait_recv()
        sends.extend(copies)

    def settle(copies):
        for copy in copies:
            copy.wait_send()
        settled.extend(copies)

    def fold_start(k, stage):
        kind, a = units[k]
        size = 2**stage
        other = at.base(stage) + (1 - 2 * at.bit(stage)) * size
        return [
            remote(
                part(grads, kind, a, other * depth_size, size * depth_size),
                part(landing, kind, a, (size - 1) * depth_size, size * depth_size),
                m.f_s.at[k, stage],
                m.f_r.at[k, stage],
                at.across(stage),
            )
        ]

    def fold_add(k, stage, copies):
        received(copies)
        kind, a = units[k]
        size = 2**stage
        own = at.base(stage) * depth_size

        def add(i, _):
            mine = blocks(own + i, 1)
            theirs = blocks((size - 1) * depth_size + i, 1)
            if kind == "r":
                total = m.gr[a, mine, :].astype(F32) + m.lr[a, theirs, :].astype(F32)
                m.gr[a, mine, :] = total.astype(BF)
            else:
                total = m.gc[a, :, mine].astype(F32) + m.lc[a, :, theirs].astype(F32)
                m.gc[a, :, mine] = total.astype(BF)
            return 0

        lax.fori_loop(0, size * depth_size, add, 0)

    def end_start(k):
        kind, a = units[k]
        into = outer(kind, a, at.depth, 1)
        copies = [
            remote(
                part(grads, kind, a, at.slot * depth_size + peer(s), 1),
                into,
                m.e_s.at[k, s],
                m.e_r.at[k, s],
                at.along(s),
            )
            for s in range(1, depth_size)
        ]
        copies.append(local(part(grads, kind, a, own_block, 1), into, m.e_l.at[k]))
        return copies

    late = {k: n for n, k in enumerate(LATE)}
    other_slot = at.base(1) + 1 - at.bit(0)

    def depth_buffer(k, h, first, count):
        kind, a = units[k]
        same = [j for j in LATE if units[j][0] == kind].index(k)
        if kind == "r":
            return m.dr.at[same, h, blocks(first, count), :]
        return m.dc.at[same, h, :, blocks(first, count)]

    def depth_first_start(k, copies):
        fold_add(k, 1, copies)
        kind, a = units[k]
        n = late[k]
        copies = []
        for h, slot in enumerate((at.slot, other_slot)):
            for s in range(1, depth_size):
                copies.append(
                    remote(
                        part(grads, kind, a, slot * depth_size + peer(s), 1),
                        depth_buffer(k, h, at.depth, 1),
                        m.d_s.at[n, h, s],
                        m.d_r.at[n, h, s],
                        at.along(s),
                    )
                )
            own = part(grads, kind, a, slot * depth_size + at.depth, 1)
            depth_buffer(k, h, at.depth, 1)[...] = own[...]
        return copies

    def depth_first_fold(k, copies):
        received(copies)
        kind, a = units[k]
        return [
            remote(
                depth_buffer(k, 1, 0, depth_size),
                part(landing, kind, a, 0, depth_size),
                m.f_s.at[k, 0],
                m.f_r.at[k, 0],
                at.across(0),
            )
        ]

    def depth_first_end(k, copies):
        received(copies)
        kind, a = units[k]
        ends = []
        for z in range(depth_size):
            mine = depth_buffer(k, 0, z, 1)
            theirs = part(landing, kind, a, z, 1)
            mine[...] = (mine[...].astype(F32) + theirs[...].astype(F32)).astype(BF)
            ends.append(local(mine, outer(kind, a, z, 1), m.d_l.at[late[k], z]))
        return ends

    near = {"ctx": at.ctx + (1 - 2 * (at.depth % 2)) * group}
    far = {"ctx": at.ctx + (2 - 4 * (at.depth // 2)) * group}
    near_depth = at.depth + 1 - 2 * (at.depth % 2)
    pair_first = at.depth // 2 * 2
    my_pair = pl.ds(pl.multiple_of(pair_first * rows, rows), 2 * rows)
    her_pair = pl.ds(pl.multiple_of((2 - pair_first) * rows, rows), 2 * rows)
    quarter = half // 2
    my_quarter = pl.ds(pl.multiple_of(at.tp * half + at.depth % 2 * quarter, quarter), quarter)
    her_quarter = pl.ds(pl.multiple_of(at.tp * half + (1 - at.depth % 2) * quarter, quarter), quarter)

    def token_step(i, buffer, step, copies):
        if copies:
            received(copies[-1:])
        brought = [
            None,
            (token_rows(near_depth), my_cols),
            (her_pair, my_quarter),
            (her_pair, her_quarter),
        ]
        given = [(token_rows(at.depth), my_cols), (my_pair, my_quarter), (her_pair, my_quarter)]
        if step < 3:
            piece = buffer.at[given[step][0], given[step][1]]
            there = far if step == 1 else near
            copies.append(remote(piece, piece, m.t_s.at[i, step], m.t_r.at[i, step], there))
        if step:
            piece = buffer.at[brought[step][0], brought[step][1]]
            swapped[i].append(
                remote(piece, piece, m.w_s.at[i, step - 1], m.w_r.at[i, step - 1], at.twin())
            )
        return copies

    def kv_start(h, stage):
        size = 2**stage * tokens
        rows_held = pl.ds(pl.multiple_of(at.base(stage) * tokens, tokens), size)
        held = m.kv.at[rows_held, slice(h * HD, (h + 1) * HD)]
        return remote(held, held, m.kv_s.at[0, h, stage], m.kv_r.at[0, h, stage], at.across(stage))

    spare = (m.lr.at[1 + ff_chunks], m.lr.at[2 + ff_chunks])

    def dkv_start(stage):
        size = 2**stage
        other = at.base(stage) + (1 - 2 * at.bit(stage)) * size
        given = pl.ds(pl.multiple_of(other * tokens, tokens), size * tokens)
        taken = pl.ds((size - 1) * tokens, size * tokens)
        return [
            remote(
                m.kv.at[given, slice(h * HD, (h + 1) * HD)],
                spare[h].at[taken, :],
                m.kv_s.at[1, h, stage],
                m.kv_r.at[1, h, stage],
                at.across(stage),
            )
            for h in range(2)
        ]

    def dkv_finish(stage, copies):
        received(copies)
        size = 2**stage
        own = at.base(stage) * tokens
        step = ROW_TILE

        def add(i, _):
            mine = pl.ds(pl.multiple_of(own + i * step, step), step)
            theirs = pl.ds(pl.multiple_of((size - 1) * tokens + i * step, step), step)
            for h in range(2):
                cols = slice(h * HD, (h + 1) * HD)
                total = m.kv[mine, cols].astype(F32) + spare[h][theirs, :].astype(F32)
                m.kv[mine, cols] = total.astype(BF)
            return 0

        lax.fori_loop(0, size * tokens // step, add, 0)

    lane = lax.broadcasted_iota(jnp.int32, (1, 128), 1)

    def place_rows():
        mine = token_rows(at.depth)
        for copy in loads:
            copy.wait()
        for b in range(block_count):
            c = natural[b]
            into = slice(b * depth_rows, (b + 1) * depth_rows)
            out_of = slice(c * depth_rows, (c + 1) * depth_rows)
            m.x[mine, into] = m.xl[0, :, out_of]
            m.dy[mine, into] = m.xl[1, :, out_of]

    def place_vectors():
        m.ps[0] = jnp.zeros_like(m.ps[0])
        for row, name in enumerate(VECTORS):
            for b in range(block_count):
                c = natural[b]
                m.gv[row : row + 1, b * depth_rows : (b + 1) * depth_rows] = getattr(m, name)[c : c + 1, :]
        per_head = HD // 128
        for a in range(3):
            for h in range(per_head):
                row = getattr(m, BIASES[a])[pl.ds(at.depth * per_head + h, 1), :]
                m.biases[a : a + 1, h * 128 : (h + 1) * 128] = row
        for i in range(ff_chunks):
            for h in range(per_head):
                row = m.b_up[pl.ds((at.depth * ff_chunks + i) * per_head + h, 1), :]
                m.biases[3 + i : 4 + i, h * 128 : (h + 1) * 128] = row
        block_rows = rows // 2
        for n in range(group * depth_size):
            c = natural[n]
            first = jnp.where(lane < block_rows, m.blocks[2 * c], m.blocks[2 * c + 1])
            m.places[n : n + 1, :] = (first * block_rows + lane % block_rows).astype(F32)

    def affine():
        step = 32

        def stats(i, _):
            here = pl.ds(pl.multiple_of(i * step, step), step)
            x = m.x[here, :].astype(F32)
            mean = jnp.mean(x, -1, keepdims=True)
            centered = x - mean
            m.mean[here, :] = mean
            m.inv[here, :] = lax.rsqrt(jnp.mean(centered * centered, -1, keepdims=True) + norm_epsilon)
            return 0

        lax.fori_loop(0, tokens // step, stats, 0)

        def body(i, _):
            here = token_rows(i)
            for n in range(width // 512):
                cols = slice(n * 512, (n + 1) * 512)
                normal = (m.x[here, cols].astype(F32) - m.mean[here, :]) * m.inv[here, :]
                m.na[here, cols] = (normal * m.gv[0:1, cols] + m.gv[1:2, cols]).astype(BF)
                mlp = normal * m.gv[2:3, cols] + m.gv[3:4, cols]
                m.nm[here, cols] = mlp.astype(BF)
                m.nmt[cols, here] = mlp.T.astype(BF)
            return 0

        lax.fori_loop(0, depth_size, body, 0)

    def place_column(n):
        return jnp.broadcast_to(m.places[pl.ds(n, 1), :], (128, 128)).T

    def make_tables():
        def body(n, _):
            angles = place_column(n) * m.freqs[0:1, :]
            here = pl.ds(pl.multiple_of(n * 128, 128), 128)
            m.tab[here, :] = jnp.cos(angles - jnp.where(lane < ROT, 0.0, math.pi / 2))
            return 0

        lax.fori_loop(0, group * tokens // 128, body, 0)

    def turned(value, here, sign):
        head = value[:, :128]
        left = pltpu.roll(head, 128 - ROT // 2, 1)
        right = pltpu.roll(head, ROT // 2, 1)
        table = m.tab[here, :]
        cosine = jnp.where(lane < ROT, table, 1.0)
        sine = sign * pltpu.roll(table, ROT, 1)
        crossed = jnp.where(lane < ROT // 2, -left, jnp.where(lane < ROT, right, 0.0))
        return head * cosine + crossed * sine

    def project(a):
        return mm(m.na[...], m.wr[a]) + m.biases[a : a + 1, :]

    kv_own = pl.ds(pl.multiple_of(at.slot * tokens, tokens), tokens)
    score_scale = 1.0 / math.sqrt(HD)

    def make_query():
        query = project(0)
        m.q[:, :128] = turned(query, kv_own, 1.0).astype(BF)
        m.q[:, 128:] = query[:, 128:].astype(BF)

    def make_keys():
        keys = project(1)
        m.kv[kv_own, :128] = turned(keys, kv_own, 1.0).astype(BF)
        m.kv[kv_own, 128:HD] = keys[:, 128:].astype(BF)

    def make_values():
        m.kv[kv_own, HD:] = project(2).astype(BF)

    def key_rows(j):
        return pl.ds(pl.multiple_of(j * tokens, tokens), tokens)

    def masked_scores(j):
        scores = mm_nt(m.kv[key_rows(j), :HD], m.q[...]) * score_scale
        count = tokens // 128
        column = jnp.concatenate([place_column(j * count + n)[:, :1] for n in range(count)], 0)
        row = jnp.concatenate([m.places[pl.ds(at.slot * count + n, 1), :] for n in range(count)], 1)
        return jnp.where(column <= row, scores, DROP)

    def attend(j):
        scores = masked_scores(j)
        if j == 0:
            old = jnp.full((1, tokens), -1e20, F32)
        else:
            old = m.stat[0:1, :]
        new = jnp.maximum(old, jnp.max(scores, 0, keepdims=True))
        raw = jnp.exp(scores - new)
        total = jnp.sum(raw, 0, keepdims=True)
        value = mm(m.kv[key_rows(j), HD:].T, raw.astype(BF))
        m.stat[0:1, :] = new
        if j:
            factor = jnp.exp(old - new)
            total = total + m.stat[1:2, :] * factor
            value = value + m.att[...] * factor
        m.stat[1:2, :] = total
        m.att[...] = value
        if j == group - 1:
            m.stat[2:3, :] = new + jnp.log(total)
            value = value / total
            m.att[...] = value
            m.alt[...] = value.astype(BF)
            m.al[...] = value.T.astype(BF)

    def head_grads():
        grad = mm_nt(m.dy[...], m.wc[0])
        low = grad.astype(BF)
        m.hg[...] = low
        m.stat[3:4, :] = jnp.sum(low.astype(F32).T * m.att[...], 0, keepdims=True)

    def attend_back(j):
        probs = jnp.exp(masked_scores(j) - m.stat[2:3, :])
        value_part = mm(probs.astype(BF), m.hg[...])
        prob_grad = mm_nt(m.kv[key_rows(j), HD:], m.hg[...])
        score_grad = (probs * (prob_grad - m.stat[3:4, :]) * score_scale).astype(BF)
        query_part = mm(m.kv[key_rows(j), :HD].T, score_grad)
        key_part = mm(score_grad, m.q[...])
        head_sum = jnp.sum(turned(key_part, key_rows(j), -1.0), 0, keepdims=True)
        rest_sum = jnp.sum(key_part[:, 128:], 0, keepdims=True)
        if j:
            query_part = query_part + m.dqt[...]
            head_sum = head_sum + m.kb[0:1, :128]
            rest_sum = rest_sum + m.kb[0:1, 128:]
        m.dqt[...] = query_part
        m.kb[0:1, :128] = head_sum
        m.kb[0:1, 128:] = rest_sum
        m.kv[key_rows(j), :HD] = key_part.astype(BF)
        m.kv[key_rows(j), HD:] = value_part.astype(BF)

    def small_store(first, row):
        for n in range(row.shape[1] // 128):
            m.ps[0, first + n : first + n + 1, :] = row[:, n * 128 : (n + 1) * 128]

    def attention_grads():
        query = m.dqt[...].T
        head = turned(query, kv_own, -1.0)
        keys = m.kv[kv_own, :HD].astype(F32)
        key_head = turned(keys, kv_own, -1.0)
        m.low[:, :128] = head.astype(BF)
        m.low[:, 128:HD] = query[:, 128:].astype(BF)
        m.low[:, HD : HD + 128] = key_head.astype(BF)
        m.low[:, HD + 128 : 2 * HD] = m.kv[kv_own, 128:HD]
        m.low[:, 2 * HD :] = m.kv[kv_own, HD:]
        small_store(64, jnp.sum(head, 0, keepdims=True))
        small_store(65, jnp.sum(query[:, 128:], 0, keepdims=True))
        small_store(66, m.kb[0:1, :])
        small_store(68, jnp.sum(m.kv[kv_own, HD:].astype(F32), 0, keepdims=True))

        def body(n, _):
            tile = pl.ds(pl.multiple_of(n * ROW_TILE, ROW_TILE), ROW_TILE)
            turned_in = m.na[:, tile].T
            for a in range(3):
                m.gr[a, tile, :] = mm(turned_in, m.low[:, a * HD : (a + 1) * HD]).astype(BF)
            return 0

        lax.fori_loop(0, width // ROW_TILE, body, 0)

    def out_grads():
        def body(n, _):
            tile = pl.ds(pl.multiple_of(n * 512, 512), 512)
            m.gc[0, :, tile] = mm(m.alt[...], m.dy[:, tile]).astype(BF)
            return 0

        lax.fori_loop(0, width // 512, body, 0)

    def feed_forward(i):
        activated, slope = gelu_parts(mm(m.nm[...], m.wr[3 + i]) + m.biases[3 + i : 4 + i, :])
        m.hid[i] = activated.astype(BF)
        up_grad = mm_nt(m.dy[...], m.wc[1 + i]) * slope
        small_store(70 + 2 * i, jnp.sum(up_grad, 0, keepdims=True))
        m.ul[i] = up_grad.astype(BF)
        turned_hidden = activated.T.astype(BF)

        def body(n, _):
            tile = pl.ds(pl.multiple_of(n * 512, 512), 512)
            m.gr[3 + i, tile, :] = mm(m.nmt[tile, :], m.ul[i]).astype(BF)
            m.gc[1 + i, :, tile] = mm(turned_hidden, m.dy[:, tile]).astype(BF)
            return 0

        lax.fori_loop(0, width // 512, body, 0)

    out, back = m.na, m.dy

    def tile_of(n):
        return pl.ds(pl.multiple_of(n * ROW_TILE, ROW_TILE), ROW_TILE)

    def small_add_rows(first, n, value):
        row = jnp.sum(value, 0, keepdims=True)
        for h in range(ROW_TILE // 128):
            m.ps[0, pl.ds(first + n * (ROW_TILE // 128) + h, 1), :] = row[:, h * 128 : (h + 1) * 128]

    def end_out(n):
        tile = tile_of(n)
        total = mm(m.al[...], m.wc[0, :, tile])
        for i in range(ff_chunks):
            total += mm(m.hid[i], m.wc[1 + i, :, tile])
        out[:, tile] = total.astype(BF)

    def end_back(n):
        tile = tile_of(n)
        attn_back = mm_nt(m.low[:, :HD], m.wr[0, tile, :])
        for a in (1, 2):
            attn_back += mm_nt(m.low[:, a * HD : (a + 1) * HD], m.wr[a, tile, :])
        mlp_back = mm_nt(m.ul[0], m.wr[3, tile, :])
        for i in range(1, ff_chunks):
            mlp_back += mm_nt(m.ul[i], m.wr[3 + i, tile, :])
        normal = (m.x[:, tile].astype(F32) - m.mean[...]) * m.inv[...]
        small_add_rows(0, n, attn_back * normal)
        small_add_rows(16, n, attn_back)
        small_add_rows(32, n, mlp_back * normal)
        small_add_rows(48, n, mlp_back)
        small_add_rows(78, n, m.dy[:, tile].astype(F32))
        back[:, tile] = (attn_back * m.gv[0:1, tile] + mlp_back * m.gv[2:3, tile]).astype(BF)

    def end_quarter(piece, which, n):
        count = quarter // ROW_TILE
        odd = at.depth % 2
        first = which * 2 + (odd if n else 1 - odd)

        def body(i, _):
            piece(first * count + i)
            return 0

        lax.fori_loop(0, count, body, 0)

    ends = (out, back)

    def quarter_of(which, n):
        odd = at.depth % 2
        return pl.ds(pl.multiple_of(which * half + (odd if n else 1 - odd) * quarter, quarter), quarter)

    def offer():
        pl.semaphore_signal(m.free, inc=1, device_id=at.twin(), device_id_type=MESH)

    def sum_start(i, n):
        if i == n == 0:
            pl.semaphore_wait(m.free, 1)
        return remote(
            ends[i].at[:, quarter_of(1 - at.tp, n)],
            m.nm.at[:, quarter_of(i, n)],
            m.o_s.at[i, n],
            m.o_r.at[i, n],
            at.twin(),
        )

    def sum_add(i, n):
        mine = ends[i]
        into, source = quarter_of(at.tp, n), quarter_of(i, n)

        def add(z, _):
            block = token_rows(z)
            total = mine[block, into].astype(F32) + m.nm[block, source].astype(F32)
            mine[block, into] = total.astype(BF)
            return 0

        lax.fori_loop(0, depth_size, add, 0)

    def sum_step(i, step, copy):
        received([copy])
        mine = ends[i]
        if step == 0:
            sum_add(i, 0)
            source, into, there = mine.at[her_pair, her_quarter], m.tz.at[i, 0], near
        elif step == 1:
            total = mine[her_pair, my_quarter].astype(F32) + m.tz[i, 0].astype(F32)
            mine[her_pair, my_quarter] = total.astype(BF)
            source, into, there = mine.at[her_pair, my_quarter], m.tz.at[i, 1], far
        elif step == 2:
            total = mine[my_pair, my_quarter].astype(F32) + m.tz[i, 1].astype(F32)
            mine[my_pair, my_quarter] = total.astype(BF)
            source, into, there = mine.at[token_rows(near_depth), my_cols], m.te.at[i], near
        else:
            total = mine[token_rows(at.depth), my_cols].astype(F32) + m.te[i].astype(F32)
            m.fin[i, :, my_cols] = total.astype(BF)
            source, into, there = m.fin.at[i, :, my_cols], m.fin.at[i, :, my_cols], at.twin()
        return remote(source, into, m.o_s.at[i, 2 + step], m.o_r.at[i, 2 + step], there)

    def small_group(stage):
        return remote(m.ps.at[stage], m.pl.at[stage], m.p_s.at[stage], m.p_r.at[stage], at.across(stage))

    def small_add(stage, copy):
        received([copy])
        m.ps[stage + 1] = m.ps[stage] + m.pl[stage]

    def small_depth():
        total = m.ps.at[bits, 0:SMALL_SENT, :]
        copies = [
            remote(total, m.pz.at[at.depth], m.p_s.at[bits + s], m.p_r.at[bits + s], at.along(s))
            for s in range(1, depth_size)
        ]
        m.pz[at.depth] = m.ps[bits, 0:SMALL_SENT, :]
        return copies

    def small_twin(copies):
        received(copies)
        value = m.pz[0]
        for z in range(1, depth_size):
            value = value + m.pz[z]
        m.px[0] = value
        return remote(m.px.at[0], m.px.at[1], m.p_s.at[bits], m.p_r.at[bits], at.twin())

    def small_finish(copy):
        received([copy])
        for v in range(4):
            for b in range(block_count):
                row = v * 16 + b
                into = v * 16 + natural[b]
                m.norm_sums[into : into + 1, :] = m.px[0, row : row + 1, :] + m.px[1, row : row + 1, :]
        for b in range(block_count):
            m.s_dy[natural[b] : natural[b] + 1, :] = m.ps[bits, 78 + b : 79 + b, :]
        for z in range(depth_size):
            m.s_query[2 * z : 2 * z + 2, :] = m.pz[z, 64:66, :]
            m.s_key[2 * z : 2 * z + 2, :] = m.pz[z, 66:68, :]
            m.s_value[2 * z : 2 * z + 2, :] = m.pz[z, 68:70, :]
            m.s_up[8 * z : 8 * z + 8, :] = m.pz[z, 70:78, :]

    z_live, g_live, t_live, k_live, f_live, e_live, x_live, s_live, d_live, p_live = ({} for _ in range(10))
    swapped = {0: [], 1: []}
    buffers = (m.x, m.dy)

    def do_zs(n):
        z_live[n] = z_start(n)

    def do_zy(n):
        z_wait(z_live[n])
        g_live[n] = g_start(n, 0)

    def do_yc(n):
        received(g_live[n])
        g_live[n] = g_start(n, 1)

    def do_cw(n):
        received(g_live[n])

    def do_ta(n):
        t_live[n] = token_step(n, buffers[n], 0, [])

    def do_tb(n):
        token_step(n, buffers[n], 1, t_live[n])

    def do_tc(n):
        token_step(n, buffers[n], 2, t_live[n])

    def do_td(n):
        token_step(n, buffers[n], 3, t_live[n])

    def do_te(n):
        received(swapped[n])

    do_norm, do_vec, do_tab, do_aff = place_rows, place_vectors, make_tables, affine
    do_qq, do_kk, do_val, do_hg = make_query, make_keys, make_values, head_grads
    do_at, do_ag, do_go, do_ff, do_of = attend, attention_grads, out_grads, feed_forward, offer

    def do_ky(n):
        k_live[n] = [kv_start(n, 0)]

    def do_kc(n):
        received(k_live[n])
        k_live[n].append(kv_start(n, 1))

    def do_kw(n):
        received(k_live[n][1:])

    def do_bw(n):
        if n == 0:
            settle(k_live[0] + k_live[1])
        attend_back(n)

    def do_dc():
        d_live[1] = dkv_start(1)

    def do_dy():
        dkv_finish(1, d_live[1])
        d_live[0] = dkv_start(0)

    def do_dw():
        dkv_finish(0, d_live[0])

    def do_fc(n):
        f_live[n] = fold_start(n, 1)

    def do_fy(n):
        fold_add(n, 1, f_live[n])
        f_live[n] = fold_start(n, 0)

    def do_fz(n):
        fold_add(n, 0, f_live[n])
        e_live[n] = end_start(n)

    def do_fq(n):
        f_live[n] = depth_first_start(n, f_live[n])

    def do_fr(n):
        f_live[n] = depth_first_fold(n, f_live[n])

    def do_fs(n):
        e_live[n] = depth_first_end(n, f_live[n])

    def do_ew(n):
        here = depth_size if n in late else 1
        received(e_live[n][:-here])
        for copy in e_live[n][-here:]:
            copy.wait()

    def do_eo(n):
        end_quarter(end_out, at.tp if n >= 2 else 1 - at.tp, n % 2)

    def do_eb(n):
        if n == 0:
            settle(t_live[1] + swapped[1])
        end_quarter(end_back, at.tp if n >= 2 else 1 - at.tp, n % 2)

    def do_sx(n):
        x_live[n] = sum_start(n // 2, n % 2)

    def do_sa(n):
        s_live[n] = sum_step(n, 0, x_live[2 * n])

    def do_sm(n):
        received([x_live[2 * n + 1]])
        sum_add(n, 1)

    def do_sb(n):
        s_live[n] = sum_step(n, 1, s_live[n])

    def do_sc(n):
        s_live[n] = sum_step(n, 2, s_live[n])

    def do_sd(n):
        s_live[n] = sum_step(n, 3, s_live[n])

    def do_sw(n):
        received([s_live[n]])

    def do_pa():
        p_live[0] = small_group(0)

    def do_pb():
        small_add(0, p_live[0])
        p_live[1] = small_group(1)

    def do_pc():
        small_add(1, p_live[1])
        p_live[2] = small_depth()

    def do_pd():
        p_live[3] = small_twin(p_live[2])

    def do_pe():
        small_finish(p_live[3])

    do_zs(1)
    do_zs(2)
    do_norm()
    do_zs(10)
    do_zy(1)
    do_ta(0)
    do_vec()
    do_zy(2)
    do_zs(4)
    do_tb(0)
    do_ta(1)
    do_zy(10)
    do_yc(2)
    do_tab()
    do_zy(4)
    do_zs(3)
    do_tc(0)
    do_cw(2)
    do_zs(0)
    do_zy(3)
    do_zs(9)
    do_td(0)
    do_tb(1)
    do_yc(10)
    do_yc(1)
    do_zy(0)
    do_zs(11)
    do_yc(4)
    do_te(0)
    do_zs(8)
    do_zy(9)
    do_zs(6)
    do_aff()
    do_yc(3)
    do_val()
    do_ky(1)
    do_cw(1)
    do_kk()
    do_tc(1)
    do_ky(0)
    do_zs(7)
    do_yc(0)
    do_cw(0)
    do_kc(1)
    do_zy(11)
    do_kc(0)
    do_zy(8)
    do_qq()
    do_kw(0)
    do_td(1)
    do_yc(9)
    do_kw(1)
    do_at(0)
    do_at(1)
    do_at(2)
    do_cw(3)
    do_zs(5)
    do_zy(6)
    do_yc(11)
    do_cw(4)
    do_at(3)
    do_yc(8)
    do_te(1)
    do_go()
    do_fc(3)
    do_hg()
    do_cw(10)
    do_bw(0)
    do_zy(7)
    do_bw(1)
    do_cw(8)
    do_cw(11)
    do_bw(2)
    do_bw(3)
    do_dc()
    do_zy(5)
    do_ff(3)
    do_yc(6)
    do_cw(9)
    do_fq(3)
    do_ff(2)
    do_fc(9)
    do_cw(6)
    do_yc(7)
    do_dy()
    do_yc(5)
    do_cw(7)
    do_ff(1)
    do_fc(7)
    do_cw(5)
    do_ff(0)
    do_fc(5)
    do_of()
    do_fc(6)
    do_fy(9)
    do_fq(7)
    do_fy(5)
    do_dw()
    do_ag()
    do_fc(0)
    do_eo(0)
    do_sx(0)
    do_fc(4)
    do_eo(1)
    do_fz(9)
    do_sx(1)
    do_eb(0)
    do_fy(0)
    do_eb(1)
    do_eo(2)
    do_eb(3)
    do_fc(1)
    do_fz(5)
    do_eb(2)
    do_pa()
    do_ew(9)
    do_fc(11)
    do_pb()
    do_fc(2)
    do_fy(1)
    do_fc(10)
    do_fy(4)
    do_sx(2)
    do_fz(0)
    do_pc()
    do_fy(10)
    do_eo(3)
    do_sa(0)
    do_fz(1)
    do_fz(4)
    do_sm(0)
    do_pd()
    do_fy(11)
    do_fc(8)
    do_sx(3)
    do_ew(0)
    do_fr(7)
    do_sb(0)
    do_sa(1)
    do_fz(11)
    do_fy(2)
    do_ew(1)
    do_sm(1)
    do_sb(1)
    do_fs(7)
    do_fy(8)
    do_ew(5)
    do_fr(3)
    do_pe()
    do_sc(0)
    do_fy(6)
    do_fz(8)
    do_fz(10)
    do_sc(1)
    do_fz(6)
    do_sd(0)
    do_fs(3)
    do_fz(2)
    do_ew(10)
    do_ew(11)
    do_ew(4)
    do_ew(8)
    do_sd(1)
    do_ew(2)
    do_sw(0)
    do_ew(6)
    do_ew(7)
    do_sw(1)
    do_ew(3)
    for copy in sends:
        if not any(copy is other for other in settled):
            copy.wait_send()


def fits(depth_size, group, depth_rows, rows, width, ff_chunks):
    sizes = layout_of(depth_size, group, depth_rows, rows, width, ff_chunks)
    total = sum(math.prod(shape) * jnp.dtype(kind).itemsize for _, shape, kind in sizes)
    shaped = group == depth_size == ff_chunks == 4 and depth_rows == rows == 128
    return shaped and total < VMEM_BYTES


def fused_shards(
    layer_input,
    block_order,
    attn_gain,
    attn_shift,
    mlp_gain,
    mlp_shift,
    w_query,
    b_query,
    w_key,
    b_key,
    w_value,
    b_value,
    w_out,
    b_out,
    w_up,
    b_up,
    w_down,
    b_down,
    out_grad,
):
    rows, width = layer_input.shape
    tp_size = lax.axis_size("tp")
    depth_size = HEADS // tp_size
    group = lax.axis_size("ctx") // depth_size
    depth_rows = width // (depth_size * group)
    ff_width = w_up.shape[1] // depth_size
    ff_chunks = ff_width // CHUNK
    tokens = depth_size * rows
    at = Place(depth_size, group)

    freqs = (10000.0 ** (-(2.0 * np.arange(ROT // 2, dtype=np.float32)) / ROT)).astype(np.float32)
    freqs = np.tile(freqs, (8, 128 // (ROT // 2)))

    def in_rows(vector):
        return vector.reshape(-1, 128)

    buffers = layout_of(depth_size, group, depth_rows, rows, width, ff_chunks)
    semaphores = semaphores_of(depth_size, group, 4 + 2 * ff_chunks)
    names = tuple(INPUTS) + tuple(OUTPUTS) + tuple(b[0] for b in buffers) + tuple(s[0] for s in semaphores) + ("free",)
    vmem = pl.BlockSpec(memory_space=pltpu.VMEM)
    hbm = pl.BlockSpec(memory_space=pl.ANY)
    shape = jax.ShapeDtypeStruct
    wide, thin = depth_size * HD, depth_size * ff_width
    results = pl.pallas_call(
        functools.partial(fused_kernel, names, depth_size, group),
        out_shape=(
            shape((2, rows, width), BF),
            shape((depth_rows, wide), BF),
            shape((depth_rows, wide), BF),
            shape((depth_rows, wide), BF),
            shape((wide, depth_rows), BF),
            shape((depth_rows, thin), BF),
            shape((thin, depth_rows), BF),
            shape((4 * width // 128, 128), F32),
            shape((wide // 128, 128), F32),
            shape((wide // 128, 128), F32),
            shape((wide // 128, 128), F32),
            shape((thin // 128, 128), F32),
            shape((width // 128, 128), F32),
        ),
        in_specs=[pl.BlockSpec(memory_space=pltpu.SMEM)] + [hbm] * 2 + [vmem] * 9 + [hbm] * 6,
        out_specs=(vmem,) + (hbm,) * 6 + (vmem,) * 6,
        scratch_shapes=[pltpu.VMEM(s, t) for _, s, t in buffers]
        + [pltpu.SemaphoreType.DMA(s) for _, s in semaphores]
        + [pltpu.SemaphoreType.REGULAR],
        compiler_params=pltpu.CompilerParams(
            collective_id=4, has_side_effects=True, vmem_limit_bytes=VMEM_BYTES
        ),
    )(
        block_order,
        layer_input,
        out_grad,
        freqs,
        *[in_rows(v) for v in (attn_gain, attn_shift, mlp_gain, mlp_shift)],
        *[in_rows(v) for v in (b_query, b_key, b_value, b_up)],
        w_query,
        w_key,
        w_value,
        w_out,
        w_up,
        w_down,
    )
    sums, *parts = results
    output, input_grad, *rest = close(
        depth_size, group, layer_input, out_grad, sums, in_rows(b_out), in_rows(b_down), parts
    )
    small = [vector.reshape(-1) for vector in rest[6:]]
    norms, (to_query, to_key, to_value, to_up, to_dy, again) = small[:4], small[4:]
    return (output, input_grad, *rest[:6], to_query, to_key, to_value, to_dy, to_up, again, *norms)


def close_kernel(depth_size, group, x_in, dy_in, sums, b_out, b_down, *refs):
    grads, (norm_sums, *small), results = refs[:6], refs[6:12], refs[12:]
    layer_output, input_grad, wide, norms, others = (
        results[0],
        results[1],
        results[2:8],
        results[8:12],
        results[12:],
    )
    for source, into in zip(grads, wide, strict=True):
        into[...] = source[...].astype(F32)
    for v, into in enumerate(norms):
        count = into.shape[0]
        into[...] = norm_sums[v * count : (v + 1) * count, :]
    for source, into in zip(small + small[-1:], others, strict=True):
        into[...] = source[...]
    x = x_in[...].astype(F32)
    width = x.shape[1]
    natural = natural_blocks(depth_size, group)
    size = width // len(natural)
    centered = x - jnp.mean(x, -1, keepdims=True)
    inverse = lax.rsqrt(jnp.mean(centered * centered, -1, keepdims=True) + norm_epsilon)
    normal = centered * inverse
    total = jnp.zeros((x.shape[0], 1), F32)
    against = jnp.zeros((x.shape[0], 1), F32)
    for b, c in enumerate(natural):
        out_of, into = slice(b * size, (b + 1) * size), slice(c * size, (c + 1) * size)
        bias = b_out[c : c + 1, :] + b_down[c : c + 1, :]
        layer_output[:, into] = (x[:, into] + sums[0, :, out_of].astype(F32) + bias).astype(BF)
        piece = sums[1, :, out_of].astype(F32)
        total += jnp.sum(piece, -1, keepdims=True)
        against += jnp.sum(piece * normal[:, into], -1, keepdims=True)
    total, against = total / width, against / width
    for b, c in enumerate(natural):
        out_of, into = slice(b * size, (b + 1) * size), slice(c * size, (c + 1) * size)
        piece = sums[1, :, out_of].astype(F32) - total - normal[:, into] * against
        input_grad[:, into] = dy_in[:, into].astype(F32) + inverse * piece


def close(depth_size, group, x_in, dy_in, sums, b_out, b_down, parts):
    rows, width = x_in.shape
    steps = rows // 64
    grads, small = parts[:6], parts[6:]
    norms = [jax.ShapeDtypeStruct((width // 128, 128), F32)] * 4
    copies = [jax.ShapeDtypeStruct(s.shape, F32) for s in small[1:] + small[-1:]]

    def by_rows(shape):
        block = shape[:-2] + (shape[-2] // steps, shape[-1])
        return pl.BlockSpec(block, lambda i: (0,) * (len(shape) - 2) + (i, 0))

    def all_of(shape):
        return pl.BlockSpec(shape, lambda i: (0,) * len(shape))

    return pl.pallas_call(
        functools.partial(close_kernel, depth_size, group),
        grid=(steps,),
        out_shape=[
            jax.ShapeDtypeStruct(x_in.shape, BF),
            jax.ShapeDtypeStruct(x_in.shape, F32),
            *[jax.ShapeDtypeStruct(g.shape, F32) for g in grads],
            *norms,
            *copies,
        ],
        in_specs=[by_rows(x_in.shape)] * 2
        + [by_rows(sums.shape), all_of(b_out.shape), all_of(b_down.shape)]
        + [by_rows(g.shape) for g in grads]
        + [all_of(s.shape) for s in small],
        out_specs=[by_rows(x_in.shape)] * 2
        + [by_rows(g.shape) for g in grads]
        + [all_of(s.shape) for s in norms + copies],
        compiler_params=pltpu.CompilerParams(vmem_limit_bytes=VMEM_BYTES),
    )(x_in, dy_in, sums, b_out, b_down, *grads, *small)


def shards(
    layer_input,
    block_order,
    attn_gain,
    attn_shift,
    mlp_gain,
    mlp_shift,
    w_query,
    b_query,
    w_key,
    b_key,
    w_value,
    b_value,
    w_out,
    b_out,
    w_up,
    b_up,
    w_down,
    b_down,
    out_grad,
):
    rows, width = layer_input.shape
    depth_size = HEADS // lax.axis_size("tp")
    group = lax.axis_size("ctx") // depth_size
    ff_chunks = w_up.shape[1] // depth_size // CHUNK
    whole = fits(depth_size, group, width // (depth_size * group), rows, width, ff_chunks)
    chosen = fused_shards if whole else staged_shards
    return chosen(
        layer_input, block_order, attn_gain, attn_shift, mlp_gain, mlp_shift, w_query, b_query, w_key, b_key, w_value, b_value, w_out, b_out, w_up, b_up, w_down, b_down, out_grad
    )


def staged_shards(
    layer_input,
    block_order,
    attn_gain,
    attn_shift,
    mlp_gain,
    mlp_shift,
    w_query,
    b_query,
    w_key,
    b_key,
    w_value,
    b_value,
    w_out,
    b_out,
    w_up,
    b_up,
    w_down,
    b_down,
    out_grad,
):
    rows, width = layer_input.shape
    ctx_size = lax.axis_size("ctx")
    tp_size = lax.axis_size("tp")
    depth_size = HEADS // tp_size
    group = ctx_size // depth_size
    bits = group.bit_length() - 1
    depth_rows = width // ctx_size
    hidden_width = w_up.shape[1] // depth_size
    ff_chunks = hidden_width // CHUNK
    at = Place(depth_size, group)
    block_rows = rows // 2

    def permuted(array):
        lead = array.shape[:-1]
        n = len(lead)
        split = array.reshape(lead + (depth_size,) + (2,) * bits + (depth_rows,))
        order = tuple(range(n)) + tuple(n + 1 + b for b in reversed(range(bits))) + (n, n + 1 + bits)
        return split.transpose(order).reshape(lead + (width,))

    def restored(array):
        lead = array.shape[:-1]
        n = len(lead)
        split = array.reshape(lead + (2,) * bits + (depth_size, depth_rows))
        order = tuple(range(n)) + (n + bits,) + tuple(n + b for b in reversed(range(bits))) + (n + bits + 1,)
        return split.transpose(order).reshape(lead + (width,))

    def slot_members():
        table = []
        for slot in range(group):
            member = 0
            for stage in range(bits):
                member += ((slot >> stage) & 1) << (bits - 1 - stage)
            table.append(member)
        return table

    blocks = block_order.reshape(depth_size, group, 2)
    order = jnp.stack([blocks[:, m] for m in slot_members()], 0)
    place = order[..., None] * block_rows + jnp.arange(block_rows, dtype=jnp.int32)
    key_place = place.reshape(group * depth_size * rows)
    token_total = depth_size * rows
    query_place = lax.dynamic_slice_in_dim(key_place, at.slot * token_total, token_total)
    cosine, sine_table = rope_tables(query_place)

    inputs32 = layer_input.astype(F32)
    centered = inputs32 - jnp.mean(inputs32, -1, keepdims=True)
    inverse = lax.rsqrt(jnp.mean(centered * centered, -1, keepdims=True) + norm_epsilon)
    normal32 = centered * inverse

    def halves(array):
        return permuted(array).reshape(rows, tp_size, width // tp_size).transpose(1, 0, 2)

    def by_head(weight):
        return weight.reshape(depth_rows, depth_size, HD).transpose(1, 0, 2)

    def by_chunk(weight):
        return weight.reshape(depth_rows, depth_size, ff_chunks, CHUNK).transpose(2, 1, 0, 3)

    weights = jnp.concatenate(
        [
            jnp.concatenate([by_head(w_query), by_head(w_key)], -1)[None],
            jnp.concatenate([by_head(w_value), by_head(w_out.T)], -1)[None],
            jnp.concatenate([by_chunk(w_up), by_chunk(w_down.T)], -1),
        ],
        0,
    )
    normal, grad, gathered = gather_all(
        depth_size, group, halves(normal32.astype(BF)), halves(out_grad), weights
    )
    full = gathered.reshape(2 + ff_chunks, width, 2 * HD)
    gain_a, shift_a, gain_m, shift_m = permuted(jnp.stack([attn_gain, attn_shift, mlp_gain, mlp_shift]))
    normal_tokens = normal.astype(F32)
    attn_in = (normal_tokens * gain_a + shift_a).astype(BF)
    mlp_in = (normal_tokens * gain_m + shift_m).astype(BF)

    def own_part(vector, size):
        return lax.dynamic_slice_in_dim(vector, at.depth * size, size)

    query_key = mm(attn_in, full[0])
    query = rotate(query_key[:, :HD] + own_part(b_query, HD), cosine, sine_table).astype(BF)
    keys = rotate(query_key[:, HD:] + own_part(b_key, HD), cosine, sine_table).astype(BF)
    values = (mm(attn_in, full[1, :, :HD]) + own_part(b_value, HD)).astype(BF)
    out_t = full[1, :, HD:]
    shared = share_group(depth_size, group, jnp.concatenate([keys, values], -1))
    shared = shared.reshape(group * token_total, 2 * HD)
    all_keys, all_values = shared[:, :HD], shared[:, HD:]
    score_scale = 1.0 / math.sqrt(HD)
    scores = mm_nt(query, all_keys) * score_scale
    allowed = key_place[None, :] <= query_place[:, None]
    scores = jnp.where(allowed, scores, -1e30)
    top = jnp.max(scores, -1, keepdims=True)
    raw = jnp.exp(scores - top)
    probs = raw / jnp.sum(raw, -1, keepdims=True)
    probs_low = probs.astype(BF)
    attended = mm(probs_low, all_values)
    attn_low = attended.astype(BF)

    head_grad = mm(grad, out_t).astype(BF)
    delta = jnp.sum(head_grad.astype(F32) * attended, -1, keepdims=True)
    value_part = mm_tn(probs_low, head_grad)
    score_grad = (probs * (mm_nt(head_grad, all_values) - delta) * score_scale).astype(BF)
    query_acc = mm(score_grad, all_keys)
    key_part = mm_tn(score_grad, query)
    parts = jnp.concatenate([key_part, value_part], -1).astype(BF)
    folded = fold_group(depth_size, group, parts.reshape(group, token_total, 2 * HD))
    own_grads = lax.dynamic_index_in_dim(folded, at.slot, 0, keepdims=False).astype(F32)
    query_lin = rotate(query_acc, cosine, -sine_table)
    key_lin = rotate(own_grads[:, :HD], cosine, -sine_table)
    value_lin = own_grads[:, HD:]
    query_low, key_low, value_low = query_lin.astype(BF), key_lin.astype(BF), value_lin.astype(BF)
    query_key_low = jnp.concatenate([query_low, key_low], -1)
    attn_back = mm_nt(query_key_low, full[0]) + mm_nt(value_low, full[1, :, :HD])
    grad_chunks = [
        mm_tn(attn_in, query_key_low).astype(BF),
        jnp.concatenate([mm_tn(attn_in, value_low), mm_tn(grad, attn_low)], -1).astype(BF),
    ]

    branches = mm_nt(attn_low, out_t)
    mlp_back = jnp.zeros((token_total, width), F32)
    bias_up = own_part(b_up, hidden_width).reshape(ff_chunks, CHUNK)
    up_sums = []
    for i in range(ff_chunks):
        up, down_t = full[2 + i, :, :CHUNK], full[2 + i, :, CHUNK:]
        activated, slope = gelu_parts(mm(mlp_in, up) + bias_up[i])
        hidden = activated.astype(BF)
        up_grad = mm(grad, down_t) * slope
        up_sums.append(jnp.sum(up_grad, 0))
        up_low = up_grad.astype(BF)
        branches = branches + mm_nt(hidden, down_t)
        mlp_back = mlp_back + mm_nt(up_low, up)
        grad_chunks.append(jnp.concatenate([mm_tn(mlp_in, up_low), mm_tn(grad, hidden)], -1).astype(BF))

    normal_tokens2 = normal.astype(F32)
    back = attn_back * gain_a + mlp_back * gain_m
    grads = jnp.stack(grad_chunks).reshape(2 + ff_chunks, group, depth_size, depth_rows, 2 * HD)
    norm_sums = restored(
        jnp.stack(
            [
                jnp.sum(attn_back * normal_tokens2, 0),
                jnp.sum(attn_back, 0),
                jnp.sum(mlp_back * normal_tokens2, 0),
                jnp.sum(mlp_back, 0),
            ]
        )
    )
    own_biases = jnp.concatenate(
        [jnp.sum(query_lin, 0), jnp.sum(key_lin, 0), jnp.sum(value_lin, 0)] + up_sums
    )
    spread = jnp.where(
        jnp.arange(depth_size, dtype=jnp.int32)[:, None] == at.depth, own_biases[None, :], 0.0
    )
    norm_sums = lax.psum(norm_sums, ("ctx", "tp"))
    grad32 = out_grad.astype(F32)
    spread, bias_grad = lax.psum((spread, jnp.sum(grad32, 0)), "ctx")

    out_sum, back_sum, grad_shares = reduce_all(
        depth_size, group, branches.astype(BF), back.astype(BF), grads
    )
    layer_output = (inputs32 + restored(out_sum).astype(F32) + b_out + b_down).astype(BF)
    back_total = restored(back_sum).astype(F32)
    input_grad = grad32 + inverse * (
        back_total
        - jnp.mean(back_total, -1, keepdims=True)
        - normal32 * jnp.mean(back_total * normal32, -1, keepdims=True)
    )

    def from_head(share):
        return share.transpose(1, 0, 2).reshape(depth_rows, depth_size * HD).astype(F32)

    def from_chunk(share):
        return share.transpose(2, 1, 0, 3).reshape(depth_rows, depth_size * hidden_width).astype(F32)

    return (
        layer_output,
        input_grad,
        from_head(grad_shares[0, :, :, :HD]),
        from_head(grad_shares[0, :, :, HD:]),
        from_head(grad_shares[1, :, :, :HD]),
        from_head(grad_shares[1, :, :, HD:]).T,
        from_chunk(grad_shares[2:, :, :, :CHUNK]),
        from_chunk(grad_shares[2:, :, :, CHUNK:]).T,
        spread[:, :HD].reshape(-1),
        spread[:, HD : 2 * HD].reshape(-1),
        spread[:, 2 * HD : 3 * HD].reshape(-1),
        bias_grad,
        spread[:, 3 * HD :].reshape(-1),
        bias_grad,
        norm_sums[0],
        norm_sums[1],
        norm_sums[2],
        norm_sums[3],
    )


def solution(mesh):
    in_specs = (
        P("ctx", None),
        P(),
        P(),
        P(),
        P(),
        P(),
        P("ctx", "tp"),
        P("tp"),
        P("ctx", "tp"),
        P("tp"),
        P("ctx", "tp"),
        P("tp"),
        P("tp", "ctx"),
        P(),
        P("ctx", "tp"),
        P("tp"),
        P("tp", "ctx"),
        P(),
        P("ctx", None),
    )
    out_specs = (
        P("ctx", None),
        P("ctx", None),
        P("ctx", "tp"),
        P("ctx", "tp"),
        P("ctx", "tp"),
        P("tp", "ctx"),
        P("ctx", "tp"),
        P("tp", "ctx"),
        P("tp"),
        P("tp"),
        P("tp"),
        P(),
        P("tp"),
        P(),
        P(),
        P(),
        P(),
        P(),
    )
    return jax.shard_map(shards, mesh=mesh, in_specs=in_specs, out_specs=out_specs, check_vma=False)
```

```python
import functools
import math

import jax
import jax.numpy as jnp
import numpy as np
from jax import lax
from jax.experimental import pallas as pl
from jax.experimental.pallas import tpu as pltpu
from jax.sharding import PartitionSpec as P

HEADS = 8
HD = 256
ROT = 64
CHUNK = 256

norm_epsilon = 1e-05
BF = jnp.bfloat16
F32 = jnp.float32
MESH = pl.DeviceIdType.MESH


def mm(a, b):
    return jnp.dot(a, b, preferred_element_type=F32)


def mm_tn(a, b):
    return lax.dot_general(a, b, (((0,), (0,)), ((), ())), preferred_element_type=F32)


def mm_nt(a, b):
    return lax.dot_general(a, b, (((1,), (1,)), ((), ())), preferred_element_type=F32)


class Place:
    def __init__(self, depth_size, group):
        self.depth_size = depth_size
        self.group = group
        self.bits = group.bit_length() - 1
        self.ctx = lax.axis_index("ctx")
        self.tp = lax.axis_index("tp")
        self.depth = self.ctx // group
        self.member = self.ctx % group
        slot = 0
        for stage in range(self.bits):
            slot = slot + self.bit(stage) * 2**stage
        self.slot = slot

    def bit(self, stage):
        return (self.member // 2 ** (self.bits - 1 - stage)) % 2

    def along(self, step):
        return {"ctx": lax.rem(self.depth + step, self.depth_size) * self.group + self.member}

    def across(self, stage):
        reach = 2 ** (self.bits - 1 - stage)
        return {"ctx": self.ctx + (1 - 2 * self.bit(stage)) * reach}

    def twin(self):
        return {"tp": 1 - self.tp}

    def base(self, stage):
        return (self.slot // 2**stage) * 2**stage

    def greet(self, devices):
        barrier = pltpu.get_barrier_semaphore()
        for device in devices:
            pl.semaphore_signal(barrier, inc=1, device_id=device, device_id_type=MESH)
        pl.semaphore_wait(barrier, len(devices))

    def everyone(self):
        return (
            [self.along(step) for step in range(1, self.depth_size)]
            + [self.across(stage) for stage in range(self.bits)]
            + [self.twin()]
        )


def remote(src, dst, send, recv, device):
    copy = pltpu.make_async_remote_copy(
        src_ref=src, dst_ref=dst, send_sem=send, recv_sem=recv, device_id=device, device_id_type=MESH
    )
    copy.start()
    return copy


def local(src, dst, sem):
    copy = pltpu.make_async_copy(src, dst, sem)
    copy.start()
    return copy


def gather_kernel(depth_size, group, x_in, dy_in, w_in, x_out, dy_out, w_out, tz_s, tz_r, tx_s, tx_r, t_l, z_s, z_r, z_l, g_s, g_r):
    at = Place(depth_size, group)
    at.greet(at.everyone())
    rows, half = x_in.shape[1:]
    sent = []
    mine = pl.ds(pl.multiple_of(at.depth * rows, rows), rows)
    my_cols = pl.ds(pl.multiple_of(at.tp * half, half), half)

    def token_start(i, src, dst):
        copies = [
            remote(src.at[at.tp], dst.at[mine, my_cols], tz_s.at[i, s], tz_r.at[i, s], at.along(s))
            for s in range(1, depth_size)
        ]
        copies.append(local(src.at[at.tp], dst.at[mine, my_cols], t_l.at[i]))
        return copies

    def token_swap(i, copies, dst):
        for copy in copies[:-1]:
            copy.wait_recv()
            sent.append(copy)
        copies[-1].wait()
        return remote(dst.at[:, my_cols], dst.at[:, my_cols], tx_s.at[i], tx_r.at[i], at.twin())

    chunks = w_in.shape[0]

    def z_start(k):
        copies = [
            remote(
                w_in.at[k, lax.rem(at.depth + s, depth_size)],
                w_out.at[k, at.slot, at.depth],
                z_s.at[k, s],
                z_r.at[k, s],
                at.along(s),
            )
            for s in range(1, depth_size)
        ]
        copies.append(local(w_in.at[k, at.depth], w_out.at[k, at.slot, at.depth], z_l.at[k]))
        return copies

    def z_wait(copies):
        for copy in copies[:-1]:
            copy.wait_recv()
            sent.append(copy)
        copies[-1].wait()

    def g_start(k, stage):
        held = pl.ds(at.base(stage), 2**stage)
        return remote(
            w_out.at[k, held], w_out.at[k, held], g_s.at[k, stage], g_r.at[k, stage], at.across(stage)
        )

    ahead = 2
    tokens = [token_start(0, x_in, x_out)]
    z_copies = {k: z_start(k) for k in range(min(ahead, chunks))}
    stages = {}
    swaps = []
    for step in range(chunks + at.bits):
        if step < chunks:
            z_wait(z_copies[step])
            stages[step] = [g_start(step, 0)]
            if step + ahead < chunks:
                z_copies[step + ahead] = z_start(step + ahead)
            if step == 0:
                swaps.append(token_swap(0, tokens[0], x_out))
                tokens.append(token_start(1, dy_in, dy_out))
            if step == 1:
                swaps.append(token_swap(1, tokens[1], dy_out))
        for stage in range(1, at.bits + 1):
            k = step - stage
            if 0 <= k < chunks:
                stages[k][stage - 1].wait_recv()
                if stage < at.bits:
                    stages[k].append(g_start(k, stage))
    for swap in swaps:
        swap.wait()
    for k in range(chunks):
        for copy in stages[k]:
            copy.wait_send()
    for copy in sent:
        copy.wait_send()


def gather_all(depth_size, group, x_halves, dy_halves, weights):
    tp, rows, half = x_halves.shape
    chunks, _, depth_rows, width = weights.shape
    bits = group.bit_length() - 1
    dma = pltpu.SemaphoreType.DMA
    hbm = pl.BlockSpec(memory_space=pl.ANY)
    tokens = jax.ShapeDtypeStruct((depth_size * rows, tp * half), BF)
    return pl.pallas_call(
        functools.partial(gather_kernel, depth_size, group),
        out_shape=(
            tokens,
            tokens,
            jax.ShapeDtypeStruct((chunks, group, depth_size, depth_rows, width), BF),
        ),
        in_specs=[hbm] * 3,
        out_specs=(hbm, hbm, hbm),
        scratch_shapes=[
            dma((2, depth_size)),
            dma((2, depth_size)),
            dma((2,)),
            dma((2,)),
            dma((2,)),
            dma((chunks, depth_size)),
            dma((chunks, depth_size)),
            dma((chunks,)),
            dma((chunks, bits)),
            dma((chunks, bits)),
        ],
        compiler_params=pltpu.CompilerParams(collective_id=0, has_side_effects=True),
    )(x_halves, dy_halves, weights)


def share_kernel(depth_size, group, kv_in, kv_out, send, recv, loc):
    at = Place(depth_size, group)
    at.greet([at.across(stage) for stage in range(at.bits)])
    local(kv_in, kv_out.at[at.slot], loc).wait()
    copies = []
    for stage in range(at.bits):
        held = pl.ds(at.base(stage), 2**stage)
        copy = remote(kv_out.at[held], kv_out.at[held], send.at[stage], recv.at[stage], at.across(stage))
        copy.wait_recv()
        copies.append(copy)
    for copy in copies:
        copy.wait_send()


def share_group(depth_size, group, kv):
    bits = group.bit_length() - 1
    dma = pltpu.SemaphoreType.DMA
    hbm = pl.BlockSpec(memory_space=pl.ANY)
    return pl.pallas_call(
        functools.partial(share_kernel, depth_size, group),
        out_shape=jax.ShapeDtypeStruct((group,) + kv.shape, BF),
        in_specs=[hbm],
        out_specs=hbm,
        scratch_shapes=[dma((bits,)), dma((bits,)), dma],
        compiler_params=pltpu.CompilerParams(collective_id=1, has_side_effects=True),
    )(kv)


def fold_kernel(depth_size, group, g_in, total, landing, send, recv):
    at = Place(depth_size, group)
    at.greet([at.across(stage) for stage in range(at.bits)])
    for stage in reversed(range(at.bits)):
        size = 2**stage
        own = at.base(stage)
        other = own + (1 - 2 * at.bit(stage)) * size
        source = g_in if stage == at.bits - 1 else total
        copy = remote(
            source.at[pl.ds(other, size)],
            landing.at[pl.ds(size - 1, size)],
            send.at[stage],
            recv.at[stage],
            at.across(stage),
        )
        copy.wait()

        def add(i, _):
            total[own + i] = (
                source[own + i].astype(F32) + landing[size - 1 + i].astype(F32)
            ).astype(BF)
            return 0

        lax.fori_loop(0, size, add, 0)


def fold_group(depth_size, group, grads):
    bits = group.bit_length() - 1
    dma = pltpu.SemaphoreType.DMA
    vmem = pl.BlockSpec(memory_space=pltpu.VMEM)
    return pl.pallas_call(
        functools.partial(fold_kernel, depth_size, group),
        out_shape=jax.ShapeDtypeStruct(grads.shape, BF),
        in_specs=[vmem],
        out_specs=vmem,
        scratch_shapes=[
            pltpu.VMEM((group - 1,) + grads.shape[1:], BF),
            dma((bits,)),
            dma((bits,)),
        ],
        compiler_params=pltpu.CompilerParams(
            collective_id=2, has_side_effects=True, vmem_limit_bytes=60 << 20
        ),
    )(grads)


def reduce_kernel(depth_size, group, out_in, back_in, g_in, out_sum, back_sum, g_out, total, landing, g_s, g_r, z_s, z_r, z_l, t_acc, t_swap, t_land, tx_s, tx_r, tz_s, tz_r, ty_s, ty_r):
    at = Place(depth_size, group)
    at.greet(at.everyone())
    chunks = g_in.shape[0]
    depth_rows = g_in.shape[3]
    rows = out_sum.shape[0]
    half = t_acc.shape[2]
    last = at.bits - 1
    sent = []

    def g_start(k, stage):
        size = 2**stage
        other = at.base(stage) + (1 - 2 * at.bit(stage)) * size
        source = g_in.at[k] if stage == last else total.at[k]
        return remote(
            source.at[pl.ds(other, size)],
            landing.at[k, pl.ds(size - 1, size)],
            g_s.at[k, stage],
            g_r.at[k, stage],
            at.across(stage),
        )

    def g_finish(k, stage, copy):
        copy.wait_recv()
        sent.append(copy)
        size = 2**stage
        own = at.base(stage)
        source = g_in.at[k] if stage == last else total.at[k]

        def add(i, _):
            j = i // depth_size
            z = i % depth_size
            total[k, own + j, z] = (
                source[own + j, z].astype(F32) + landing[k, size - 1 + j, z].astype(F32)
            ).astype(BF)
            return 0

        lax.fori_loop(0, size * depth_size, add, 0)

    def z_start(k):
        copies = [
            remote(
                total.at[k, at.slot, lax.rem(at.depth + s, depth_size)],
                g_out.at[k, at.depth],
                z_s.at[k, s],
                z_r.at[k, s],
                at.along(s),
            )
            for s in range(1, depth_size)
        ]
        copies.append(local(total.at[k, at.slot, at.depth], g_out.at[k, at.depth], z_l.at[k]))
        return copies

    my_cols = pl.ds(pl.multiple_of(at.tp * half, half), half)
    her_cols = pl.ds(pl.multiple_of((1 - at.tp) * half, half), half)

    def token_first(i, src):
        return remote(src.at[:, her_cols], t_swap.at[i], tx_s.at[i], tx_r.at[i], at.twin())

    def token_second(i, src, copy):
        copy.wait_recv()
        sent.append(copy)

        def add(z, _):
            block = pl.ds(pl.multiple_of(z * rows, rows), rows)
            t_acc[i, block, :] = (
                src[block, my_cols].astype(F32) + t_swap[i, block, :].astype(F32)
            ).astype(BF)
            return 0

        lax.fori_loop(0, depth_size, add, 0)
        copies = []
        for s in range(1, depth_size):
            there = lax.rem(at.depth + s, depth_size)
            block = pl.ds(pl.multiple_of(there * rows, rows), rows)
            copies.append(
                remote(
                    t_acc.at[i, block, :], t_land.at[i, s - 1], tz_s.at[i, s], tz_r.at[i, s], at.along(s)
                )
            )
        return copies

    def token_third(i, dst, copies):
        for copy in copies:
            copy.wait_recv()
            sent.append(copy)
        mine = pl.ds(pl.multiple_of(at.depth * rows, rows), rows)
        value = t_acc[i, mine, :].astype(F32)
        for s in range(1, depth_size):
            value = value + t_land[i, s - 1].astype(F32)
        dst[:, my_cols] = value.astype(BF)
        return remote(dst.at[:, my_cols], dst.at[:, my_cols], ty_s.at[i], ty_r.at[i], at.twin())

    firsts = [token_first(0, out_in), token_first(1, back_in)]
    copies_of = {k: [g_start(k, last)] for k in range(chunks)}
    z_copies = {}
    seconds = []
    thirds = []
    for step in range(chunks + at.bits):
        for back in range(at.bits):
            k = step - back
            stage = last - back
            if 0 <= k < chunks:
                g_finish(k, stage, copies_of[k][back])
                if stage > 0:
                    copies_of[k].append(g_start(k, stage - 1))
                else:
                    z_copies[k] = z_start(k)
        if step == 1:
            seconds.append(token_second(0, out_in, firsts[0]))
        if step == 2:
            seconds.append(token_second(1, back_in, firsts[1]))
        if step == 4:
            thirds.append(token_third(0, out_sum, seconds[0]))
        if step == 5:
            thirds.append(token_third(1, back_sum, seconds[1]))
    for k in range(chunks):
        for copy in z_copies[k][:-1]:
            copy.wait()
        z_copies[k][-1].wait()
    for copy in thirds:
        copy.wait()
    for copy in sent:
        copy.wait_send()


def reduce_all(depth_size, group, out_part, back_part, grads):
    chunks, _, _, depth_rows, width = grads.shape
    all_rows, columns = out_part.shape
    rows = all_rows // depth_size
    half = columns // 2
    bits = group.bit_length() - 1
    dma = pltpu.SemaphoreType.DMA
    vmem = pl.BlockSpec(memory_space=pltpu.VMEM)
    tokens = jax.ShapeDtypeStruct((rows, columns), BF)
    return pl.pallas_call(
        functools.partial(reduce_kernel, depth_size, group),
        out_shape=(tokens, tokens, jax.ShapeDtypeStruct((chunks, depth_size, depth_rows, width), BF)),
        in_specs=[vmem] * 3,
        out_specs=(vmem, vmem, vmem),
        scratch_shapes=[
            pltpu.VMEM((chunks, group, depth_size, depth_rows, width), BF),
            pltpu.VMEM((chunks, group - 1, depth_size, depth_rows, width), BF),
            dma((chunks, bits)),
            dma((chunks, bits)),
            dma((chunks, depth_size)),
            dma((chunks, depth_size)),
            dma((chunks,)),
            pltpu.VMEM((2, all_rows, half), BF),
            pltpu.VMEM((2, all_rows, half), BF),
            pltpu.VMEM((2, depth_size - 1, rows, half), BF),
            dma((2,)),
            dma((2,)),
            dma((2, depth_size)),
            dma((2, depth_size)),
            dma((2,)),
            dma((2,)),
        ],
        compiler_params=pltpu.CompilerParams(
            collective_id=3, has_side_effects=True, vmem_limit_bytes=60 << 20
        ),
    )(out_part, back_part, grads)


def rotate(values, cosine, sine_table):
    half_rot = ROT // 2
    leading = values[..., :half_rot]
    trailing = values[..., half_rot:ROT]
    return jnp.concatenate(
        [
            leading * cosine - trailing * sine_table,
            trailing * cosine + leading * sine_table,
            values[..., ROT:],
        ],
        -1,
    )


def rope_tables(positions):
    freqs = 10000.0 ** (-(2.0 * jnp.arange(ROT // 2, dtype=F32)) / ROT)
    angles = positions.astype(F32)[:, None] * freqs[None, :]
    return (jnp.cos(angles), jnp.sin(angles))


def gelu_parts(values):
    gate = 0.5 * (1.0 + lax.erf(values * math.sqrt(0.5)))
    slope = gate + values * jnp.exp(-0.5 * values * values) * (1.0 / math.sqrt(2.0 * math.pi))
    return values * gate, slope


SMALL_ROWS = 96
SMALL_SENT = 80
LATE = (3, 7,)
LATE_ROWS = 1
LATE_COLS = 2
VMEM_BYTES = 64 << 20


def slot_member(slot, bits):
    member = 0
    for stage in range(bits):
        member += ((slot >> stage) & 1) << (bits - 1 - stage)
    return member


def natural_blocks(depth_size, group):
    bits = group.bit_length() - 1
    return [
        depth * group + slot_member(slot, bits) for slot in range(group) for depth in range(depth_size)
    ]

ROW_TILE = 256
DROP = -1e30


def layout_of(depth_size, group, depth_rows, rows, width, ff_chunks):
    tokens = depth_size * rows
    half = width // 2
    landing = (group - 1) * depth_size * depth_rows
    heads = 3 + ff_chunks
    cols = 1 + ff_chunks
    return [
        ("wr", (heads, width, CHUNK), BF),
        ("wc", (cols, CHUNK, width), BF),
        ("gr", (heads, width, CHUNK), BF),
        ("gc", (cols, CHUNK, width), BF),
        ("lr", (heads, landing, CHUNK), BF),
        ("lc", (cols, CHUNK, landing), BF),
        ("x", (tokens, width), BF),
        ("dy", (tokens, width), BF),
        ("na", (tokens, width), BF),
        ("nm", (tokens, width), BF),
        ("nmt", (width, tokens), BF),
        ("kv", (group * tokens, 2 * HD), BF),
        ("q", (tokens, HD), BF),
        ("low", (tokens, 3 * HD), BF),
        ("al", (tokens, HD), BF),
        ("hg", (tokens, HD), BF),
        ("alt", (HD, tokens), BF),
        ("att", (HD, tokens), F32),
        ("dqt", (HD, tokens), F32),
        ("stat", (8, tokens), F32),
        ("tab", (group * tokens, 128), F32),
        ("kb", (8, HD), F32),
        ("hid", (ff_chunks, tokens, CHUNK), BF),
        ("ul", (ff_chunks, tokens, CHUNK), BF),
        ("tz", (2, 2, tokens // 2, half // 2), BF),
        ("te", (2, rows, half), BF),
        ("mean", (tokens, 1), F32),
        ("inv", (tokens, 1), F32),
        ("xl", (2, rows, width), BF),
        ("gv", (8, width), F32),
        ("biases", (8, HD), F32),
        ("places", (group * tokens // 128, 128), F32),
        ("ps", (group.bit_length(), SMALL_ROWS, 128), F32),
        ("pl", (group.bit_length() - 1, SMALL_ROWS, 128), F32),
        ("pz", (depth_size, SMALL_SENT, 128), F32),
        ("px", (2, SMALL_SENT, 128), F32),
        ("dr", (LATE_ROWS, 2, depth_size * depth_rows, CHUNK), BF),
        ("dc", (LATE_COLS, 2, CHUNK, depth_size * depth_rows), BF),
    ]


def semaphores_of(depth_size, group, items):
    bits = group.bit_length() - 1
    return [
        ("z_s", (items, depth_size)),
        ("z_r", (items, depth_size)),
        ("z_l", (items,)),
        ("g_s", (items, bits)),
        ("g_r", (items, bits)),
        ("t_s", (2, 3)),
        ("t_r", (2, 3)),
        ("w_s", (2, 3)),
        ("w_r", (2, 3)),
        ("kv_s", (2, 2, bits)),
        ("kv_r", (2, 2, bits)),
        ("f_s", (items, bits)),
        ("f_r", (items, bits)),
        ("e_s", (items, depth_size)),
        ("e_r", (items, depth_size)),
        ("e_l", (items,)),
        ("x_l", (2,)),
        ("d_s", (LATE_ROWS + LATE_COLS, 2, depth_size)),
        ("d_r", (LATE_ROWS + LATE_COLS, 2, depth_size)),
        ("d_l", (LATE_ROWS + LATE_COLS, depth_size)),
        ("o_s", (2, 6)),
        ("o_r", (2, 6)),
        ("p_s", (bits + depth_size,)),
        ("p_r", (bits + depth_size,)),
    ]


VECTORS = ("attn_gain", "attn_shift", "mlp_gain", "mlp_shift")
BIASES = ("b_query", "b_key", "b_value", "b_up")
INPUTS = ("blocks", "x_in", "dy_in", "freqs") + VECTORS + BIASES
INPUTS += ("w_query", "w_key", "w_value", "w_out", "w_up", "w_down")
OUTPUTS = ("fin", "g_query", "g_key", "g_value", "g_out", "g_up", "g_down")
OUTPUTS += ("norm_sums", "s_query", "s_key", "s_value", "s_up", "s_dy")


class Bag:
    pass


def fused_kernel(names, depth_size, group, *refs):
    m = Bag()
    for name, ref in zip(names, refs, strict=True):
        setattr(m, name, ref)
    at = Place(depth_size, group)
    loads = [local(source, m.xl.at[i], m.x_l.at[i]) for i, source in enumerate((m.x_in, m.dy_in))]
    at.greet(at.everyone())
    bits = at.bits
    rows, width = m.x_in.shape
    depth_rows = width // (depth_size * group)
    tokens = depth_size * rows
    half = width // 2
    ff_width = m.w_up.shape[1] // depth_size
    ff_chunks = ff_width // CHUNK
    block_count = width // depth_rows
    own_block = at.slot * depth_size + at.depth
    natural = natural_blocks(depth_size, group)
    sends, settled = [], []

    def blocks(first, count):
        return pl.ds(pl.multiple_of(first * depth_rows, depth_rows), count * depth_rows)

    def token_rows(depth):
        return pl.ds(pl.multiple_of(depth * rows, rows), rows)

    def peer(step):
        return lax.rem(at.depth + step, depth_size)

    my_cols = pl.ds(pl.multiple_of(at.tp * half, half), half)
    her_cols = pl.ds(pl.multiple_of((1 - at.tp) * half, half), half)

    units = [("r", 0), ("r", 1), ("r", 2), ("c", 0)]
    for i in range(ff_chunks):
        units += [("r", 3 + i), ("c", 1 + i)]
    row_pairs = [(m.w_query, m.g_query), (m.w_key, m.g_key), (m.w_value, m.g_value)]

    def outer(kind, a, depth, which):
        if kind == "r" and a < 3:
            return row_pairs[a][which].at[:, pl.ds(pl.multiple_of(depth * HD, HD), HD)]
        if kind == "r":
            first = pl.multiple_of(depth * ff_width + (a - 3) * CHUNK, CHUNK)
            return (m.w_up, m.g_up)[which].at[:, pl.ds(first, CHUNK)]
        if a == 0:
            return (m.w_out, m.g_out)[which].at[pl.ds(pl.multiple_of(depth * HD, HD), HD), :]
        first = pl.multiple_of(depth * ff_width + (a - 1) * CHUNK, CHUNK)
        return (m.w_down, m.g_down)[which].at[pl.ds(first, CHUNK), :]

    def part(pair, kind, a, first, count):
        if kind == "r":
            return pair[0].at[a, blocks(first, count), :]
        return pair[1].at[a, :, blocks(first, count)]

    weights, grads, landing = (m.wr, m.wc), (m.gr, m.gc), (m.lr, m.lc)

    def z_start(k):
        kind, a = units[k]
        into = part(weights, kind, a, own_block, 1)
        copies = [
            remote(outer(kind, a, peer(s), 0), into, m.z_s.at[k, s], m.z_r.at[k, s], at.along(s))
            for s in range(1, depth_size)
        ]
        copies.append(local(outer(kind, a, at.depth, 0), into, m.z_l.at[k]))
        return copies

    def z_wait(copies):
        received(copies[:-1])
        copies[-1].wait()

    def g_start(k, stage):
        kind, a = units[k]
        held = part(weights, kind, a, at.base(stage) * depth_size, 2**stage * depth_size)
        return [remote(held, held, m.g_s.at[k, stage], m.g_r.at[k, stage], at.across(stage))]

    def received(copies):
        for copy in copies:
            copy.wait_recv()
        sends.extend(copies)

    def settle(copies):
        for copy in copies:
            copy.wait_send()
        settled.extend(copies)

    def fold_start(k, stage):
        kind, a = units[k]
        size = 2**stage
        other = at.base(stage) + (1 - 2 * at.bit(stage)) * size
        return [
            remote(
                part(grads, kind, a, other * depth_size, size * depth_size),
                part(landing, kind, a, (size - 1) * depth_size, size * depth_size),
                m.f_s.at[k, stage],
                m.f_r.at[k, stage],
                at.across(stage),
            )
        ]

    def fold_add(k, stage, copies):
        received(copies)
        kind, a = units[k]
        size = 2**stage
        own = at.base(stage) * depth_size

        def add(i, _):
            mine = blocks(own + i, 1)
            theirs = blocks((size - 1) * depth_size + i, 1)
            if kind == "r":
                total = m.gr[a, mine, :].astype(F32) + m.lr[a, theirs, :].astype(F32)
                m.gr[a, mine, :] = total.astype(BF)
            else:
                total = m.gc[a, :, mine].astype(F32) + m.lc[a, :, theirs].astype(F32)
                m.gc[a, :, mine] = total.astype(BF)
            return 0

        lax.fori_loop(0, size * depth_size, add, 0)

    def end_start(k):
        kind, a = units[k]
        into = outer(kind, a, at.depth, 1)
        copies = [
            remote(
                part(grads, kind, a, at.slot * depth_size + peer(s), 1),
                into,
                m.e_s.at[k, s],
                m.e_r.at[k, s],
                at.along(s),
            )
            for s in range(1, depth_size)
        ]
        copies.append(local(part(grads, kind, a, own_block, 1), into, m.e_l.at[k]))
        return copies

    late = {k: n for n, k in enumerate(LATE)}
    other_slot = at.base(1) + 1 - at.bit(0)

    def depth_buffer(k, h, first, count):
        kind, a = units[k]
        same = [j for j in LATE if units[j][0] == kind].index(k)
        if kind == "r":
            return m.dr.at[same, h, blocks(first, count), :]
        return m.dc.at[same, h, :, blocks(first, count)]

    def depth_first_start(k, copies):
        fold_add(k, 1, copies)
        kind, a = units[k]
        n = late[k]
        copies = []
        for h, slot in enumerate((at.slot, other_slot)):
            for s in range(1, depth_size):
                copies.append(
                    remote(
                        part(grads, kind, a, slot * depth_size + peer(s), 1),
                        depth_buffer(k, h, at.depth, 1),
                        m.d_s.at[n, h, s],
                        m.d_r.at[n, h, s],
                        at.along(s),
                    )
                )
            own = part(grads, kind, a, slot * depth_size + at.depth, 1)
            depth_buffer(k, h, at.depth, 1)[...] = own[...]
        return copies

    def depth_first_fold(k, copies):
        received(copies)
        kind, a = units[k]
        return [
            remote(
                depth_buffer(k, 1, 0, depth_size),
                part(landing, kind, a, 0, depth_size),
                m.f_s.at[k, 0],
                m.f_r.at[k, 0],
                at.across(0),
            )
        ]

    def depth_first_end(k, copies):
        received(copies)
        kind, a = units[k]
        ends = []
        for z in range(depth_size):
            mine = depth_buffer(k, 0, z, 1)
            theirs = part(landing, kind, a, z, 1)
            mine[...] = (mine[...].astype(F32) + theirs[...].astype(F32)).astype(BF)
            ends.append(local(mine, outer(kind, a, z, 1), m.d_l.at[late[k], z]))
        return ends

    near = {"ctx": at.ctx + (1 - 2 * (at.depth % 2)) * group}
    far = {"ctx": at.ctx + (2 - 4 * (at.depth // 2)) * group}
    near_depth = at.depth + 1 - 2 * (at.depth % 2)
    pair_first = at.depth // 2 * 2
    my_pair = pl.ds(pl.multiple_of(pair_first * rows, rows), 2 * rows)
    her_pair = pl.ds(pl.multiple_of((2 - pair_first) * rows, rows), 2 * rows)
    quarter = half // 2
    my_quarter = pl.ds(pl.multiple_of(at.tp * half + at.depth % 2 * quarter, quarter), quarter)
    her_quarter = pl.ds(pl.multiple_of(at.tp * half + (1 - at.depth % 2) * quarter, quarter), quarter)

    def token_step(i, buffer, step, copies):
        if copies:
            received(copies[-1:])
        brought = [
            None,
            (token_rows(near_depth), my_cols),
            (her_pair, my_quarter),
            (her_pair, her_quarter),
        ]
        given = [(token_rows(at.depth), my_cols), (my_pair, my_quarter), (her_pair, my_quarter)]
        if step < 3:
            piece = buffer.at[given[step][0], given[step][1]]
            there = far if step == 1 else near
            copies.append(remote(piece, piece, m.t_s.at[i, step], m.t_r.at[i, step], there))
        if step:
            piece = buffer.at[brought[step][0], brought[step][1]]
            swapped[i].append(
                remote(piece, piece, m.w_s.at[i, step - 1], m.w_r.at[i, step - 1], at.twin())
            )
        return copies

    def kv_start(h, stage):
        size = 2**stage * tokens
        rows_held = pl.ds(pl.multiple_of(at.base(stage) * tokens, tokens), size)
        held = m.kv.at[rows_held, slice(h * HD, (h + 1) * HD)]
        return remote(held, held, m.kv_s.at[0, h, stage], m.kv_r.at[0, h, stage], at.across(stage))

    spare = (m.lr.at[1 + ff_chunks], m.lr.at[2 + ff_chunks])

    def dkv_start(stage):
        size = 2**stage
        other = at.base(stage) + (1 - 2 * at.bit(stage)) * size
        given = pl.ds(pl.multiple_of(other * tokens, tokens), size * tokens)
        taken = pl.ds((size - 1) * tokens, size * tokens)
        return [
            remote(
                m.kv.at[given, slice(h * HD, (h + 1) * HD)],
                spare[h].at[taken, :],
                m.kv_s.at[1, h, stage],
                m.kv_r.at[1, h, stage],
                at.across(stage),
            )
            for h in range(2)
        ]

    def dkv_finish(stage, copies):
        received(copies)
        size = 2**stage
        own = at.base(stage) * tokens
        step = ROW_TILE

        def add(i, _):
            mine = pl.ds(pl.multiple_of(own + i * step, step), step)
            theirs = pl.ds(pl.multiple_of((size - 1) * tokens + i * step, step), step)
            for h in range(2):
                cols = slice(h * HD, (h + 1) * HD)
                total = m.kv[mine, cols].astype(F32) + spare[h][theirs, :].astype(F32)
                m.kv[mine, cols] = total.astype(BF)
            return 0

        lax.fori_loop(0, size * tokens // step, add, 0)

    lane = lax.broadcasted_iota(jnp.int32, (1, 128), 1)

    def place_rows():
        mine = token_rows(at.depth)
        for copy in loads:
            copy.wait()
        for b in range(block_count):
            c = natural[b]
            into = slice(b * depth_rows, (b + 1) * depth_rows)
            out_of = slice(c * depth_rows, (c + 1) * depth_rows)
            m.x[mine, into] = m.xl[0, :, out_of]
            m.dy[mine, into] = m.xl[1, :, out_of]

    def place_vectors():
        m.ps[0] = jnp.zeros_like(m.ps[0])
        for row, name in enumerate(VECTORS):
            for b in range(block_count):
                c = natural[b]
                m.gv[row : row + 1, b * depth_rows : (b + 1) * depth_rows] = getattr(m, name)[c : c + 1, :]
        per_head = HD // 128
        for a in range(3):
            for h in range(per_head):
                row = getattr(m, BIASES[a])[pl.ds(at.depth * per_head + h, 1), :]
                m.biases[a : a + 1, h * 128 : (h + 1) * 128] = row
        for i in range(ff_chunks):
            for h in range(per_head):
                row = m.b_up[pl.ds((at.depth * ff_chunks + i) * per_head + h, 1), :]
                m.biases[3 + i : 4 + i, h * 128 : (h + 1) * 128] = row
        block_rows = rows // 2
        for n in range(group * depth_size):
            c = natural[n]
            first = jnp.where(lane < block_rows, m.blocks[2 * c], m.blocks[2 * c + 1])
            m.places[n : n + 1, :] = (first * block_rows + lane % block_rows).astype(F32)

    def affine():
        step = 32

        def stats(i, _):
            here = pl.ds(pl.multiple_of(i * step, step), step)
            x = m.x[here, :].astype(F32)
            mean = jnp.mean(x, -1, keepdims=True)
            centered = x - mean
            m.mean[here, :] = mean
            m.inv[here, :] = lax.rsqrt(jnp.mean(centered * centered, -1, keepdims=True) + norm_epsilon)
            return 0

        lax.fori_loop(0, tokens // step, stats, 0)

        def body(i, _):
            here = token_rows(i)
            for n in range(width // 512):
                cols = slice(n * 512, (n + 1) * 512)
                normal = (m.x[here, cols].astype(F32) - m.mean[here, :]) * m.inv[here, :]
                m.na[here, cols] = (normal * m.gv[0:1, cols] + m.gv[1:2, cols]).astype(BF)
                mlp = normal * m.gv[2:3, cols] + m.gv[3:4, cols]
                m.nm[here, cols] = mlp.astype(BF)
                m.nmt[cols, here] = mlp.T.astype(BF)
            return 0

        lax.fori_loop(0, depth_size, body, 0)

    def place_column(n):
        return jnp.broadcast_to(m.places[pl.ds(n, 1), :], (128, 128)).T

    def make_tables():
        def body(n, _):
            angles = place_column(n) * m.freqs[0:1, :]
            here = pl.ds(pl.multiple_of(n * 128, 128), 128)
            m.tab[here, :] = jnp.cos(angles - jnp.where(lane < ROT, 0.0, math.pi / 2))
            return 0

        lax.fori_loop(0, group * tokens // 128, body, 0)

    def turned(value, here, sign):
        head = value[:, :128]
        left = pltpu.roll(head, 128 - ROT // 2, 1)
        right = pltpu.roll(head, ROT // 2, 1)
        table = m.tab[here, :]
        cosine = jnp.where(lane < ROT, table, 1.0)
        sine = sign * pltpu.roll(table, ROT, 1)
        crossed = jnp.where(lane < ROT // 2, -left, jnp.where(lane < ROT, right, 0.0))
        return head * cosine + crossed * sine

    def project(a):
        return mm(m.na[...], m.wr[a]) + m.biases[a : a + 1, :]

    kv_own = pl.ds(pl.multiple_of(at.slot * tokens, tokens), tokens)
    score_scale = 1.0 / math.sqrt(HD)

    def make_query():
        query = project(0)
        m.q[:, :128] = turned(query, kv_own, 1.0).astype(BF)
        m.q[:, 128:] = query[:, 128:].astype(BF)

    def make_keys():
        keys = project(1)
        m.kv[kv_own, :128] = turned(keys, kv_own, 1.0).astype(BF)
        m.kv[kv_own, 128:HD] = keys[:, 128:].astype(BF)

    def make_values():
        m.kv[kv_own, HD:] = project(2).astype(BF)

    def key_rows(j):
        return pl.ds(pl.multiple_of(j * tokens, tokens), tokens)

    def masked_scores(j):
        scores = mm_nt(m.kv[key_rows(j), :HD], m.q[...]) * score_scale
        count = tokens // 128
        column = jnp.concatenate([place_column(j * count + n)[:, :1] for n in range(count)], 0)
        row = jnp.concatenate([m.places[pl.ds(at.slot * count + n, 1), :] for n in range(count)], 1)
        return jnp.where(column <= row, scores, DROP)

    def attend(j):
        scores = masked_scores(j)
        if j == 0:
            old = jnp.full((1, tokens), -1e20, F32)
        else:
            old = m.stat[0:1, :]
        new = jnp.maximum(old, jnp.max(scores, 0, keepdims=True))
        raw = jnp.exp(scores - new)
        total = jnp.sum(raw, 0, keepdims=True)
        value = mm(m.kv[key_rows(j), HD:].T, raw.astype(BF))
        m.stat[0:1, :] = new
        if j:
            factor = jnp.exp(old - new)
            total = total + m.stat[1:2, :] * factor
            value = value + m.att[...] * factor
        m.stat[1:2, :] = total
        m.att[...] = value
        if j == group - 1:
            m.stat[2:3, :] = new + jnp.log(total)
            value = value / total
            m.att[...] = value
            m.alt[...] = value.astype(BF)
            m.al[...] = value.T.astype(BF)

    def head_grads():
        grad = mm_nt(m.dy[...], m.wc[0])
        low = grad.astype(BF)
        m.hg[...] = low
        m.stat[3:4, :] = jnp.sum(low.astype(F32).T * m.att[...], 0, keepdims=True)

    def attend_back(j):
        probs = jnp.exp(masked_scores(j) - m.stat[2:3, :])
        value_part = mm(probs.astype(BF), m.hg[...])
        prob_grad = mm_nt(m.kv[key_rows(j), HD:], m.hg[...])
        score_grad = (probs * (prob_grad - m.stat[3:4, :]) * score_scale).astype(BF)
        query_part = mm(m.kv[key_rows(j), :HD].T, score_grad)
        key_part = mm(score_grad, m.q[...])
        head_sum = jnp.sum(turned(key_part, key_rows(j), -1.0), 0, keepdims=True)
        rest_sum = jnp.sum(key_part[:, 128:], 0, keepdims=True)
        if j:
            query_part = query_part + m.dqt[...]
            head_sum = head_sum + m.kb[0:1, :128]
            rest_sum = rest_sum + m.kb[0:1, 128:]
        m.dqt[...] = query_part
        m.kb[0:1, :128] = head_sum
        m.kb[0:1, 128:] = rest_sum
        m.kv[key_rows(j), :HD] = key_part.astype(BF)
        m.kv[key_rows(j), HD:] = value_part.astype(BF)

    def small_store(first, row):
        for n in range(row.shape[1] // 128):
            m.ps[0, first + n : first + n + 1, :] = row[:, n * 128 : (n + 1) * 128]

    def attention_grads():
        query = m.dqt[...].T
        head = turned(query, kv_own, -1.0)
        keys = m.kv[kv_own, :HD].astype(F32)
        key_head = turned(keys, kv_own, -1.0)
        m.low[:, :128] = head.astype(BF)
        m.low[:, 128:HD] = query[:, 128:].astype(BF)
        m.low[:, HD : HD + 128] = key_head.astype(BF)
        m.low[:, HD + 128 : 2 * HD] = m.kv[kv_own, 128:HD]
        m.low[:, 2 * HD :] = m.kv[kv_own, HD:]
        small_store(64, jnp.sum(head, 0, keepdims=True))
        small_store(65, jnp.sum(query[:, 128:], 0, keepdims=True))
        small_store(66, m.kb[0:1, :])
        small_store(68, jnp.sum(m.kv[kv_own, HD:].astype(F32), 0, keepdims=True))

        def body(n, _):
            tile = pl.ds(pl.multiple_of(n * ROW_TILE, ROW_TILE), ROW_TILE)
            turned_in = m.na[:, tile].T
            for a in range(3):
                m.gr[a, tile, :] = mm(turned_in, m.low[:, a * HD : (a + 1) * HD]).astype(BF)
            return 0

        lax.fori_loop(0, width // ROW_TILE, body, 0)

    def out_grads():
        def body(n, _):
            tile = pl.ds(pl.multiple_of(n * 512, 512), 512)
            m.gc[0, :, tile] = mm(m.alt[...], m.dy[:, tile]).astype(BF)
            return 0

        lax.fori_loop(0, width // 512, body, 0)

    def feed_forward(i):
        activated, slope = gelu_parts(mm(m.nm[...], m.wr[3 + i]) + m.biases[3 + i : 4 + i, :])
        m.hid[i] = activated.astype(BF)
        up_grad = mm_nt(m.dy[...], m.wc[1 + i]) * slope
        small_store(70 + 2 * i, jnp.sum(up_grad, 0, keepdims=True))
        m.ul[i] = up_grad.astype(BF)
        turned_hidden = activated.T.astype(BF)

        def body(n, _):
            tile = pl.ds(pl.multiple_of(n * 512, 512), 512)
            m.gr[3 + i, tile, :] = mm(m.nmt[tile, :], m.ul[i]).astype(BF)
            m.gc[1 + i, :, tile] = mm(turned_hidden, m.dy[:, tile]).astype(BF)
            return 0

        lax.fori_loop(0, width // 512, body, 0)

    out, back = m.na, m.dy

    def tile_of(n):
        return pl.ds(pl.multiple_of(n * ROW_TILE, ROW_TILE), ROW_TILE)

    def small_add_rows(first, n, value):
        row = jnp.sum(value, 0, keepdims=True)
        for h in range(ROW_TILE // 128):
            m.ps[0, pl.ds(first + n * (ROW_TILE // 128) + h, 1), :] = row[:, h * 128 : (h + 1) * 128]

    def end_out(n):
        tile = tile_of(n)
        total = mm(m.al[...], m.wc[0, :, tile])
        for i in range(ff_chunks):
            total += mm(m.hid[i], m.wc[1 + i, :, tile])
        out[:, tile] = total.astype(BF)

    def end_back(n):
        tile = tile_of(n)
        attn_back = mm_nt(m.low[:, :HD], m.wr[0, tile, :])
        for a in (1, 2):
            attn_back += mm_nt(m.low[:, a * HD : (a + 1) * HD], m.wr[a, tile, :])
        mlp_back = mm_nt(m.ul[0], m.wr[3, tile, :])
        for i in range(1, ff_chunks):
            mlp_back += mm_nt(m.ul[i], m.wr[3 + i, tile, :])
        normal = (m.x[:, tile].astype(F32) - m.mean[...]) * m.inv[...]
        small_add_rows(0, n, attn_back * normal)
        small_add_rows(16, n, attn_back)
        small_add_rows(32, n, mlp_back * normal)
        small_add_rows(48, n, mlp_back)
        small_add_rows(78, n, m.dy[:, tile].astype(F32))
        back[:, tile] = (attn_back * m.gv[0:1, tile] + mlp_back * m.gv[2:3, tile]).astype(BF)

    def end_quarter(piece, which, n):
        count = quarter // ROW_TILE
        odd = at.depth % 2
        first = which * 2 + (odd if n else 1 - odd)

        def body(i, _):
            piece(first * count + i)
            return 0

        lax.fori_loop(0, count, body, 0)

    ends = (out, back)

    def quarter_of(which, n):
        odd = at.depth % 2
        return pl.ds(pl.multiple_of(which * half + (odd if n else 1 - odd) * quarter, quarter), quarter)

    def offer():
        pl.semaphore_signal(m.free, inc=1, device_id=at.twin(), device_id_type=MESH)

    def sum_start(i, n):
        if i == n == 0:
            pl.semaphore_wait(m.free, 1)
        return remote(
            ends[i].at[:, quarter_of(1 - at.tp, n)],
            m.nm.at[:, quarter_of(i, n)],
            m.o_s.at[i, n],
            m.o_r.at[i, n],
            at.twin(),
        )

    def sum_add(i, n):
        mine = ends[i]
        into, source = quarter_of(at.tp, n), quarter_of(i, n)

        def add(z, _):
            block = token_rows(z)
            total = mine[block, into].astype(F32) + m.nm[block, source].astype(F32)
            mine[block, into] = total.astype(BF)
            return 0

        lax.fori_loop(0, depth_size, add, 0)

    def sum_step(i, step, copy):
        received([copy])
        mine = ends[i]
        if step == 0:
            sum_add(i, 0)
            source, into, there = mine.at[her_pair, her_quarter], m.tz.at[i, 0], near
        elif step == 1:
            total = mine[her_pair, my_quarter].astype(F32) + m.tz[i, 0].astype(F32)
            mine[her_pair, my_quarter] = total.astype(BF)
            source, into, there = mine.at[her_pair, my_quarter], m.tz.at[i, 1], far
        elif step == 2:
            total = mine[my_pair, my_quarter].astype(F32) + m.tz[i, 1].astype(F32)
            mine[my_pair, my_quarter] = total.astype(BF)
            source, into, there = mine.at[token_rows(near_depth), my_cols], m.te.at[i], near
        else:
            total = mine[token_rows(at.depth), my_cols].astype(F32) + m.te[i].astype(F32)
            m.fin[i, :, my_cols] = total.astype(BF)
            source, into, there = m.fin.at[i, :, my_cols], m.fin.at[i, :, my_cols], at.twin()
        return remote(source, into, m.o_s.at[i, 2 + step], m.o_r.at[i, 2 + step], there)

    def small_group(stage):
        return remote(m.ps.at[stage], m.pl.at[stage], m.p_s.at[stage], m.p_r.at[stage], at.across(stage))

    def small_add(stage, copy):
        received([copy])
        m.ps[stage + 1] = m.ps[stage] + m.pl[stage]

    def small_depth():
        total = m.ps.at[bits, 0:SMALL_SENT, :]
        copies = [
            remote(total, m.pz.at[at.depth], m.p_s.at[bits + s], m.p_r.at[bits + s], at.along(s))
            for s in range(1, depth_size)
        ]
        m.pz[at.depth] = m.ps[bits, 0:SMALL_SENT, :]
        return copies

    def small_twin(copies):
        received(copies)
        value = m.pz[0]
        for z in range(1, depth_size):
            value = value + m.pz[z]
        m.px[0] = value
        return remote(m.px.at[0], m.px.at[1], m.p_s.at[bits], m.p_r.at[bits], at.twin())

    def small_finish(copy):
        received([copy])
        for v in range(4):
            for b in range(block_count):
                row = v * 16 + b
                into = v * 16 + natural[b]
                m.norm_sums[into : into + 1, :] = m.px[0, row : row + 1, :] + m.px[1, row : row + 1, :]
        for b in range(block_count):
            m.s_dy[natural[b] : natural[b] + 1, :] = m.ps[bits, 78 + b : 79 + b, :]
        for z in range(depth_size):
            m.s_query[2 * z : 2 * z + 2, :] = m.pz[z, 64:66, :]
            m.s_key[2 * z : 2 * z + 2, :] = m.pz[z, 66:68, :]
            m.s_value[2 * z : 2 * z + 2, :] = m.pz[z, 68:70, :]
            m.s_up[8 * z : 8 * z + 8, :] = m.pz[z, 70:78, :]

    z_live, g_live, t_live, k_live, f_live, e_live, x_live, s_live, d_live, p_live = ({} for _ in range(10))
    swapped = {0: [], 1: []}
    buffers = (m.x, m.dy)

    def do_zs(n):
        z_live[n] = z_start(n)

    def do_zy(n):
        z_wait(z_live[n])
        g_live[n] = g_start(n, 0)

    def do_yc(n):
        received(g_live[n])
        g_live[n] = g_start(n, 1)

    def do_cw(n):
        received(g_live[n])

    def do_ta(n):
        t_live[n] = token_step(n, buffers[n], 0, [])

    def do_tb(n):
        token_step(n, buffers[n], 1, t_live[n])

    def do_tc(n):
        token_step(n, buffers[n], 2, t_live[n])

    def do_td(n):
        token_step(n, buffers[n], 3, t_live[n])

    def do_te(n):
        received(swapped[n])

    do_norm, do_vec, do_tab, do_aff = place_rows, place_vectors, make_tables, affine
    do_qq, do_kk, do_val, do_hg = make_query, make_keys, make_values, head_grads
    do_at, do_ag, do_go, do_ff, do_of = attend, attention_grads, out_grads, feed_forward, offer

    def do_ky(n):
        k_live[n] = [kv_start(n, 0)]

    def do_kc(n):
        received(k_live[n])
        k_live[n].append(kv_start(n, 1))

    def do_kw(n):
        received(k_live[n][1:])

    def do_bw(n):
        if n == 0:
            settle(k_live[0] + k_live[1])
        attend_back(n)

    def do_dc():
        d_live[1] = dkv_start(1)

    def do_dy():
        dkv_finish(1, d_live[1])
        d_live[0] = dkv_start(0)

    def do_dw():
        dkv_finish(0, d_live[0])

    def do_fc(n):
        f_live[n] = fold_start(n, 1)

    def do_fy(n):
        fold_add(n, 1, f_live[n])
        f_live[n] = fold_start(n, 0)

    def do_fz(n):
        fold_add(n, 0, f_live[n])
        e_live[n] = end_start(n)

    def do_fq(n):
        f_live[n] = depth_first_start(n, f_live[n])

    def do_fr(n):
        f_live[n] = depth_first_fold(n, f_live[n])

    def do_fs(n):
        e_live[n] = depth_first_end(n, f_live[n])

    def do_ew(n):
        here = depth_size if n in late else 1
        received(e_live[n][:-here])
        for copy in e_live[n][-here:]:
            copy.wait()

    def do_eo(n):
        end_quarter(end_out, at.tp if n >= 2 else 1 - at.tp, n % 2)

    def do_eb(n):
        if n == 0:
            settle(t_live[1] + swapped[1])
        end_quarter(end_back, at.tp if n >= 2 else 1 - at.tp, n % 2)

    def do_sx(n):
        x_live[n] = sum_start(n // 2, n % 2)

    def do_sa(n):
        s_live[n] = sum_step(n, 0, x_live[2 * n])

    def do_sm(n):
        received([x_live[2 * n + 1]])
        sum_add(n, 1)

    def do_sb(n):
        s_live[n] = sum_step(n, 1, s_live[n])

    def do_sc(n):
        s_live[n] = sum_step(n, 2, s_live[n])

    def do_sd(n):
        s_live[n] = sum_step(n, 3, s_live[n])

    def do_sw(n):
        received([s_live[n]])

    def do_pa():
        p_live[0] = small_group(0)

    def do_pb():
        small_add(0, p_live[0])
        p_live[1] = small_group(1)

    def do_pc():
        small_add(1, p_live[1])
        p_live[2] = small_depth()

    def do_pd():
        p_live[3] = small_twin(p_live[2])

    def do_pe():
        small_finish(p_live[3])

    do_zs(1)
    do_zs(2)
    do_norm()
    do_zs(10)
    do_ta(0)
    do_zy(1)
    do_zy(2)
    do_zs(4)
    do_vec()
    do_tb(0)
    do_ta(1)
    do_zy(10)
    do_yc(2)
    do_tab()
    do_zy(4)
    do_zs(3)
    do_tc(0)
    do_zs(0)
    do_zy(3)
    do_zs(9)
    do_td(0)
    do_cw(2)
    do_tb(1)
    do_yc(10)
    do_yc(1)
    do_zy(0)
    do_zs(11)
    do_yc(4)
    do_te(0)
    do_zs(8)
    do_zy(9)
    do_zs(6)
    do_aff()
    do_yc(3)
    do_val()
    do_ky(1)
    do_cw(1)
    do_kk()
    do_tc(1)
    do_ky(0)
    do_zs(7)
    do_yc(0)
    do_cw(0)
    do_kc(1)
    do_qq()
    do_zy(11)
    do_kc(0)
    do_zy(8)
    do_kw(0)
    do_td(1)
    do_yc(9)
    do_kw(1)
    do_at(0)
    do_at(1)
    do_at(2)
    do_cw(3)
    do_zs(5)
    do_zy(6)
    do_yc(11)
    do_cw(4)
    do_at(3)
    do_yc(8)
    do_te(1)
    do_go()
    do_fc(3)
    do_hg()
    do_bw(0)
    do_cw(10)
    do_zy(7)
    do_bw(1)
    do_cw(8)
    do_cw(11)
    do_bw(2)
    do_bw(3)
    do_dc()
    do_zy(5)
    do_ff(3)
    do_yc(6)
    do_fq(3)
    do_cw(9)
    do_ff(2)
    do_fc(9)
    do_cw(6)
    do_yc(7)
    do_dy()
    do_yc(5)
    do_cw(7)
    do_ff(1)
    do_fc(7)
    do_cw(5)
    do_ff(0)
    do_fc(5)
    do_of()
    do_fc(6)
    do_fy(9)
    do_fq(7)
    do_fy(5)
    do_dw()
    do_ag()
    do_fc(0)
    do_eo(0)
    do_sx(0)
    do_fc(4)
    do_eo(1)
    do_sx(1)
    do_fz(9)
    do_eo(2)
    do_eb(0)
    do_fy(0)
    do_eb(1)
    do_eb(3)
    do_fc(1)
    do_fz(5)
    do_eb(2)
    do_pa()
    do_ew(9)
    do_fc(11)
    do_pb()
    do_fc(2)
    do_fy(1)
    do_fc(10)
    do_fy(4)
    do_sx(2)
    do_fz(0)
    do_pc()
    do_fy(10)
    do_eo(3)
    do_sa(0)
    do_fz(1)
    do_fz(4)
    do_sm(0)
    do_pd()
    do_fy(11)
    do_fc(8)
    do_sx(3)
    do_ew(0)
    do_fr(7)
    do_sb(0)
    do_sa(1)
    do_fz(11)
    do_fy(2)
    do_ew(1)
    do_sm(1)
    do_sb(1)
    do_fy(8)
    do_ew(5)
    do_fr(3)
    do_fs(7)
    do_pe()
    do_sc(0)
    do_fy(6)
    do_fz(8)
    do_fz(10)
    do_sc(1)
    do_sd(0)
    do_fs(3)
    do_fz(2)
    do_ew(4)
    do_ew(10)
    do_fz(6)
    do_ew(11)
    do_ew(8)
    do_sd(1)
    do_ew(2)
    do_sw(0)
    do_ew(6)
    do_ew(7)
    do_sw(1)
    do_ew(3)
    for copy in sends:
        if not any(copy is other for other in settled):
            copy.wait_send()


def fits(depth_size, group, depth_rows, rows, width, ff_chunks):
    sizes = layout_of(depth_size, group, depth_rows, rows, width, ff_chunks)
    total = sum(math.prod(shape) * jnp.dtype(kind).itemsize for _, shape, kind in sizes)
    shaped = group == depth_size == ff_chunks == 4 and depth_rows == rows == 128
    return shaped and total < VMEM_BYTES


def fused_shards(
    layer_input,
    block_order,
    attn_gain,
    attn_shift,
    mlp_gain,
    mlp_shift,
    w_query,
    b_query,
    w_key,
    b_key,
    w_value,
    b_value,
    w_out,
    b_out,
    w_up,
    b_up,
    w_down,
    b_down,
    out_grad,
):
    rows, width = layer_input.shape
    tp_size = lax.axis_size("tp")
    depth_size = HEADS // tp_size
    group = lax.axis_size("ctx") // depth_size
    depth_rows = width // (depth_size * group)
    ff_width = w_up.shape[1] // depth_size
    ff_chunks = ff_width // CHUNK
    tokens = depth_size * rows
    at = Place(depth_size, group)

    freqs = (10000.0 ** (-(2.0 * np.arange(ROT // 2, dtype=np.float32)) / ROT)).astype(np.float32)
    freqs = np.tile(freqs, (8, 128 // (ROT // 2)))

    def in_rows(vector):
        return vector.reshape(-1, 128)

    buffers = layout_of(depth_size, group, depth_rows, rows, width, ff_chunks)
    semaphores = semaphores_of(depth_size, group, 4 + 2 * ff_chunks)
    names = tuple(INPUTS) + tuple(OUTPUTS) + tuple(b[0] for b in buffers) + tuple(s[0] for s in semaphores) + ("free",)
    vmem = pl.BlockSpec(memory_space=pltpu.VMEM)
    hbm = pl.BlockSpec(memory_space=pl.ANY)
    shape = jax.ShapeDtypeStruct
    wide, thin = depth_size * HD, depth_size * ff_width
    results = pl.pallas_call(
        functools.partial(fused_kernel, names, depth_size, group),
        out_shape=(
            shape((2, rows, width), BF),
            shape((depth_rows, wide), BF),
            shape((depth_rows, wide), BF),
            shape((depth_rows, wide), BF),
            shape((wide, depth_rows), BF),
            shape((depth_rows, thin), BF),
            shape((thin, depth_rows), BF),
            shape((4 * width // 128, 128), F32),
            shape((wide // 128, 128), F32),
            shape((wide // 128, 128), F32),
            shape((wide // 128, 128), F32),
            shape((thin // 128, 128), F32),
            shape((width // 128, 128), F32),
        ),
        in_specs=[pl.BlockSpec(memory_space=pltpu.SMEM)] + [hbm] * 2 + [vmem] * 9 + [hbm] * 6,
        out_specs=(vmem,) + (hbm,) * 6 + (vmem,) * 6,
        scratch_shapes=[pltpu.VMEM(s, t) for _, s, t in buffers]
        + [pltpu.SemaphoreType.DMA(s) for _, s in semaphores]
        + [pltpu.SemaphoreType.REGULAR],
        compiler_params=pltpu.CompilerParams(
            collective_id=4, has_side_effects=True, vmem_limit_bytes=VMEM_BYTES
        ),
    )(
        block_order,
        layer_input,
        out_grad,
        freqs,
        *[in_rows(v) for v in (attn_gain, attn_shift, mlp_gain, mlp_shift)],
        *[in_rows(v) for v in (b_query, b_key, b_value, b_up)],
        w_query,
        w_key,
        w_value,
        w_out,
        w_up,
        w_down,
    )
    sums, *parts = results
    output, input_grad, *rest = close(
        depth_size, group, layer_input, out_grad, sums, in_rows(b_out), in_rows(b_down), parts
    )
    small = [vector.reshape(-1) for vector in rest[6:]]
    norms, (to_query, to_key, to_value, to_up, to_dy, again) = small[:4], small[4:]
    return (output, input_grad, *rest[:6], to_query, to_key, to_value, to_dy, to_up, again, *norms)


def close_kernel(depth_size, group, x_in, dy_in, sums, b_out, b_down, *refs):
    grads, (norm_sums, *small), results = refs[:6], refs[6:12], refs[12:]
    layer_output, input_grad, wide, norms, others = (
        results[0],
        results[1],
        results[2:8],
        results[8:12],
        results[12:],
    )
    for source, into in zip(grads, wide, strict=True):
        into[...] = source[...].astype(F32)
    for v, into in enumerate(norms):
        count = into.shape[0]
        into[...] = norm_sums[v * count : (v + 1) * count, :]
    for source, into in zip(small + small[-1:], others, strict=True):
        into[...] = source[...]
    x = x_in[...].astype(F32)
    width = x.shape[1]
    natural = natural_blocks(depth_size, group)
    size = width // len(natural)
    centered = x - jnp.mean(x, -1, keepdims=True)
    inverse = lax.rsqrt(jnp.mean(centered * centered, -1, keepdims=True) + norm_epsilon)
    normal = centered * inverse
    total = jnp.zeros((x.shape[0], 1), F32)
    against = jnp.zeros((x.shape[0], 1), F32)
    for b, c in enumerate(natural):
        out_of, into = slice(b * size, (b + 1) * size), slice(c * size, (c + 1) * size)
        bias = b_out[c : c + 1, :] + b_down[c : c + 1, :]
        layer_output[:, into] = (x[:, into] + sums[0, :, out_of].astype(F32) + bias).astype(BF)
        piece = sums[1, :, out_of].astype(F32)
        total += jnp.sum(piece, -1, keepdims=True)
        against += jnp.sum(piece * normal[:, into], -1, keepdims=True)
    total, against = total / width, against / width
    for b, c in enumerate(natural):
        out_of, into = slice(b * size, (b + 1) * size), slice(c * size, (c + 1) * size)
        piece = sums[1, :, out_of].astype(F32) - total - normal[:, into] * against
        input_grad[:, into] = dy_in[:, into].astype(F32) + inverse * piece


def close(depth_size, group, x_in, dy_in, sums, b_out, b_down, parts):
    rows, width = x_in.shape
    steps = rows // 64
    grads, small = parts[:6], parts[6:]
    norms = [jax.ShapeDtypeStruct((width // 128, 128), F32)] * 4
    copies = [jax.ShapeDtypeStruct(s.shape, F32) for s in small[1:] + small[-1:]]

    def by_rows(shape):
        block = shape[:-2] + (shape[-2] // steps, shape[-1])
        return pl.BlockSpec(block, lambda i: (0,) * (len(shape) - 2) + (i, 0))

    def all_of(shape):
        return pl.BlockSpec(shape, lambda i: (0,) * len(shape))

    return pl.pallas_call(
        functools.partial(close_kernel, depth_size, group),
        grid=(steps,),
        out_shape=[
            jax.ShapeDtypeStruct(x_in.shape, BF),
            jax.ShapeDtypeStruct(x_in.shape, F32),
            *[jax.ShapeDtypeStruct(g.shape, F32) for g in grads],
            *norms,
            *copies,
        ],
        in_specs=[by_rows(x_in.shape)] * 2
        + [by_rows(sums.shape), all_of(b_out.shape), all_of(b_down.shape)]
        + [by_rows(g.shape) for g in grads]
        + [all_of(s.shape) for s in small],
        out_specs=[by_rows(x_in.shape)] * 2
        + [by_rows(g.shape) for g in grads]
        + [all_of(s.shape) for s in norms + copies],
        compiler_params=pltpu.CompilerParams(vmem_limit_bytes=VMEM_BYTES),
    )(x_in, dy_in, sums, b_out, b_down, *grads, *small)


def shards(
    layer_input,
    block_order,
    attn_gain,
    attn_shift,
    mlp_gain,
    mlp_shift,
    w_query,
    b_query,
    w_key,
    b_key,
    w_value,
    b_value,
    w_out,
    b_out,
    w_up,
    b_up,
    w_down,
    b_down,
    out_grad,
):
    rows, width = layer_input.shape
    depth_size = HEADS // lax.axis_size("tp")
    group = lax.axis_size("ctx") // depth_size
    ff_chunks = w_up.shape[1] // depth_size // CHUNK
    whole = fits(depth_size, group, width // (depth_size * group), rows, width, ff_chunks)
    chosen = fused_shards if whole else staged_shards
    return chosen(
        layer_input, block_order, attn_gain, attn_shift, mlp_gain, mlp_shift, w_query, b_query, w_key, b_key, w_value, b_value, w_out, b_out, w_up, b_up, w_down, b_down, out_grad
    )


def staged_shards(
    layer_input,
    block_order,
    attn_gain,
    attn_shift,
    mlp_gain,
    mlp_shift,
    w_query,
    b_query,
    w_key,
    b_key,
    w_value,
    b_value,
    w_out,
    b_out,
    w_up,
    b_up,
    w_down,
    b_down,
    out_grad,
):
    rows, width = layer_input.shape
    ctx_size = lax.axis_size("ctx")
    tp_size = lax.axis_size("tp")
    depth_size = HEADS // tp_size
    group = ctx_size // depth_size
    bits = group.bit_length() - 1
    depth_rows = width // ctx_size
    hidden_width = w_up.shape[1] // depth_size
    ff_chunks = hidden_width // CHUNK
    at = Place(depth_size, group)
    block_rows = rows // 2

    def permuted(array):
        lead = array.shape[:-1]
        n = len(lead)
        split = array.reshape(lead + (depth_size,) + (2,) * bits + (depth_rows,))
        order = tuple(range(n)) + tuple(n + 1 + b for b in reversed(range(bits))) + (n, n + 1 + bits)
        return split.transpose(order).reshape(lead + (width,))

    def restored(array):
        lead = array.shape[:-1]
        n = len(lead)
        split = array.reshape(lead + (2,) * bits + (depth_size, depth_rows))
        order = tuple(range(n)) + (n + bits,) + tuple(n + b for b in reversed(range(bits))) + (n + bits + 1,)
        return split.transpose(order).reshape(lead + (width,))

    def slot_members():
        table = []
        for slot in range(group):
            member = 0
            for stage in range(bits):
                member += ((slot >> stage) & 1) << (bits - 1 - stage)
            table.append(member)
        return table

    blocks = block_order.reshape(depth_size, group, 2)
    order = jnp.stack([blocks[:, m] for m in slot_members()], 0)
    place = order[..., None] * block_rows + jnp.arange(block_rows, dtype=jnp.int32)
    key_place = place.reshape(group * depth_size * rows)
    token_total = depth_size * rows
    query_place = lax.dynamic_slice_in_dim(key_place, at.slot * token_total, token_total)
    cosine, sine_table = rope_tables(query_place)

    inputs32 = layer_input.astype(F32)
    centered = inputs32 - jnp.mean(inputs32, -1, keepdims=True)
    inverse = lax.rsqrt(jnp.mean(centered * centered, -1, keepdims=True) + norm_epsilon)
    normal32 = centered * inverse

    def halves(array):
        return permuted(array).reshape(rows, tp_size, width // tp_size).transpose(1, 0, 2)

    def by_head(weight):
        return weight.reshape(depth_rows, depth_size, HD).transpose(1, 0, 2)

    def by_chunk(weight):
        return weight.reshape(depth_rows, depth_size, ff_chunks, CHUNK).transpose(2, 1, 0, 3)

    weights = jnp.concatenate(
        [
            jnp.concatenate([by_head(w_query), by_head(w_key)], -1)[None],
            jnp.concatenate([by_head(w_value), by_head(w_out.T)], -1)[None],
            jnp.concatenate([by_chunk(w_up), by_chunk(w_down.T)], -1),
        ],
        0,
    )
    normal, grad, gathered = gather_all(
        depth_size, group, halves(normal32.astype(BF)), halves(out_grad), weights
    )
    full = gathered.reshape(2 + ff_chunks, width, 2 * HD)
    gain_a, shift_a, gain_m, shift_m = permuted(jnp.stack([attn_gain, attn_shift, mlp_gain, mlp_shift]))
    normal_tokens = normal.astype(F32)
    attn_in = (normal_tokens * gain_a + shift_a).astype(BF)
    mlp_in = (normal_tokens * gain_m + shift_m).astype(BF)

    def own_part(vector, size):
        return lax.dynamic_slice_in_dim(vector, at.depth * size, size)

    query_key = mm(attn_in, full[0])
    query = rotate(query_key[:, :HD] + own_part(b_query, HD), cosine, sine_table).astype(BF)
    keys = rotate(query_key[:, HD:] + own_part(b_key, HD), cosine, sine_table).astype(BF)
    values = (mm(attn_in, full[1, :, :HD]) + own_part(b_value, HD)).astype(BF)
    out_t = full[1, :, HD:]
    shared = share_group(depth_size, group, jnp.concatenate([keys, values], -1))
    shared = shared.reshape(group * token_total, 2 * HD)
    all_keys, all_values = shared[:, :HD], shared[:, HD:]
    score_scale = 1.0 / math.sqrt(HD)
    scores = mm_nt(query, all_keys) * score_scale
    allowed = key_place[None, :] <= query_place[:, None]
    scores = jnp.where(allowed, scores, -1e30)
    top = jnp.max(scores, -1, keepdims=True)
    raw = jnp.exp(scores - top)
    probs = raw / jnp.sum(raw, -1, keepdims=True)
    probs_low = probs.astype(BF)
    attended = mm(probs_low, all_values)
    attn_low = attended.astype(BF)

    head_grad = mm(grad, out_t).astype(BF)
    delta = jnp.sum(head_grad.astype(F32) * attended, -1, keepdims=True)
    value_part = mm_tn(probs_low, head_grad)
    score_grad = (probs * (mm_nt(head_grad, all_values) - delta) * score_scale).astype(BF)
    query_acc = mm(score_grad, all_keys)
    key_part = mm_tn(score_grad, query)
    parts = jnp.concatenate([key_part, value_part], -1).astype(BF)
    folded = fold_group(depth_size, group, parts.reshape(group, token_total, 2 * HD))
    own_grads = lax.dynamic_index_in_dim(folded, at.slot, 0, keepdims=False).astype(F32)
    query_lin = rotate(query_acc, cosine, -sine_table)
    key_lin = rotate(own_grads[:, :HD], cosine, -sine_table)
    value_lin = own_grads[:, HD:]
    query_low, key_low, value_low = query_lin.astype(BF), key_lin.astype(BF), value_lin.astype(BF)
    query_key_low = jnp.concatenate([query_low, key_low], -1)
    attn_back = mm_nt(query_key_low, full[0]) + mm_nt(value_low, full[1, :, :HD])
    grad_chunks = [
        mm_tn(attn_in, query_key_low).astype(BF),
        jnp.concatenate([mm_tn(attn_in, value_low), mm_tn(grad, attn_low)], -1).astype(BF),
    ]

    branches = mm_nt(attn_low, out_t)
    mlp_back = jnp.zeros((token_total, width), F32)
    bias_up = own_part(b_up, hidden_width).reshape(ff_chunks, CHUNK)
    up_sums = []
    for i in range(ff_chunks):
        up, down_t = full[2 + i, :, :CHUNK], full[2 + i, :, CHUNK:]
        activated, slope = gelu_parts(mm(mlp_in, up) + bias_up[i])
        hidden = activated.astype(BF)
        up_grad = mm(grad, down_t) * slope
        up_sums.append(jnp.sum(up_grad, 0))
        up_low = up_grad.astype(BF)
        branches = branches + mm_nt(hidden, down_t)
        mlp_back = mlp_back + mm_nt(up_low, up)
        grad_chunks.append(jnp.concatenate([mm_tn(mlp_in, up_low), mm_tn(grad, hidden)], -1).astype(BF))

    normal_tokens2 = normal.astype(F32)
    back = attn_back * gain_a + mlp_back * gain_m
    grads = jnp.stack(grad_chunks).reshape(2 + ff_chunks, group, depth_size, depth_rows, 2 * HD)
    norm_sums = restored(
        jnp.stack(
            [
                jnp.sum(attn_back * normal_tokens2, 0),
                jnp.sum(attn_back, 0),
                jnp.sum(mlp_back * normal_tokens2, 0),
                jnp.sum(mlp_back, 0),
            ]
        )
    )
    own_biases = jnp.concatenate(
        [jnp.sum(query_lin, 0), jnp.sum(key_lin, 0), jnp.sum(value_lin, 0)] + up_sums
    )
    spread = jnp.where(
        jnp.arange(depth_size, dtype=jnp.int32)[:, None] == at.depth, own_biases[None, :], 0.0
    )
    norm_sums = lax.psum(norm_sums, ("ctx", "tp"))
    grad32 = out_grad.astype(F32)
    spread, bias_grad = lax.psum((spread, jnp.sum(grad32, 0)), "ctx")

    out_sum, back_sum, grad_shares = reduce_all(
        depth_size, group, branches.astype(BF), back.astype(BF), grads
    )
    layer_output = (inputs32 + restored(out_sum).astype(F32) + b_out + b_down).astype(BF)
    back_total = restored(back_sum).astype(F32)
    input_grad = grad32 + inverse * (
        back_total
        - jnp.mean(back_total, -1, keepdims=True)
        - normal32 * jnp.mean(back_total * normal32, -1, keepdims=True)
    )

    def from_head(share):
        return share.transpose(1, 0, 2).reshape(depth_rows, depth_size * HD).astype(F32)

    def from_chunk(share):
        return share.transpose(2, 1, 0, 3).reshape(depth_rows, depth_size * hidden_width).astype(F32)

    return (
        layer_output,
        input_grad,
        from_head(grad_shares[0, :, :, :HD]),
        from_head(grad_shares[0, :, :, HD:]),
        from_head(grad_shares[1, :, :, :HD]),
        from_head(grad_shares[1, :, :, HD:]).T,
        from_chunk(grad_shares[2:, :, :, :CHUNK]),
        from_chunk(grad_shares[2:, :, :, CHUNK:]).T,
        spread[:, :HD].reshape(-1),
        spread[:, HD : 2 * HD].reshape(-1),
        spread[:, 2 * HD : 3 * HD].reshape(-1),
        bias_grad,
        spread[:, 3 * HD :].reshape(-1),
        bias_grad,
        norm_sums[0],
        norm_sums[1],
        norm_sums[2],
        norm_sums[3],
    )


def solution(mesh):
    in_specs = (
        P("ctx", None),
        P(),
        P(),
        P(),
        P(),
        P(),
        P("ctx", "tp"),
        P("tp"),
        P("ctx", "tp"),
        P("tp"),
        P("ctx", "tp"),
        P("tp"),
        P("tp", "ctx"),
        P(),
        P("ctx", "tp"),
        P("tp"),
        P("tp", "ctx"),
        P(),
        P("ctx", None),
    )
    out_specs = (
        P("ctx", None),
        P("ctx", None),
        P("ctx", "tp"),
        P("ctx", "tp"),
        P("ctx", "tp"),
        P("tp", "ctx"),
        P("ctx", "tp"),
        P("tp", "ctx"),
        P("tp"),
        P("tp"),
        P("tp"),
        P(),
        P("tp"),
        P(),
        P(),
        P(),
        P(),
        P(),
    )
    return jax.shard_map(shards, mesh=mesh, in_specs=in_specs, out_specs=out_specs, check_vma=False)
```

```python
import functools
import math

import jax
import jax.numpy as jnp
import numpy as np
from jax import lax
from jax.experimental import pallas as pl
from jax.experimental.pallas import tpu as pltpu
from jax.sharding import PartitionSpec as P

HEADS = 8
HD = 256
ROT = 64
CHUNK = 256

norm_epsilon = 1e-05
BF = jnp.bfloat16
F32 = jnp.float32
MESH = pl.DeviceIdType.MESH


def mm(a, b):
    return jnp.dot(a, b, preferred_element_type=F32)


def mm_tn(a, b):
    return lax.dot_general(a, b, (((0,), (0,)), ((), ())), preferred_element_type=F32)


def mm_nt(a, b):
    return lax.dot_general(a, b, (((1,), (1,)), ((), ())), preferred_element_type=F32)


class Place:
    def __init__(self, depth_size, group):
        self.depth_size = depth_size
        self.group = group
        self.bits = group.bit_length() - 1
        self.ctx = lax.axis_index("ctx")
        self.tp = lax.axis_index("tp")
        self.depth = self.ctx // group
        self.member = self.ctx % group
        slot = 0
        for stage in range(self.bits):
            slot = slot + self.bit(stage) * 2**stage
        self.slot = slot

    def bit(self, stage):
        return (self.member // 2 ** (self.bits - 1 - stage)) % 2

    def along(self, step):
        return {"ctx": lax.rem(self.depth + step, self.depth_size) * self.group + self.member}

    def across(self, stage):
        reach = 2 ** (self.bits - 1 - stage)
        return {"ctx": self.ctx + (1 - 2 * self.bit(stage)) * reach}

    def twin(self):
        return {"tp": 1 - self.tp}

    def base(self, stage):
        return (self.slot // 2**stage) * 2**stage

    def greet(self, devices):
        barrier = pltpu.get_barrier_semaphore()
        for device in devices:
            pl.semaphore_signal(barrier, inc=1, device_id=device, device_id_type=MESH)
        pl.semaphore_wait(barrier, len(devices))

    def everyone(self):
        return (
            [self.along(step) for step in range(1, self.depth_size)]
            + [self.across(stage) for stage in range(self.bits)]
            + [self.twin()]
        )


def remote(src, dst, send, recv, device):
    copy = pltpu.make_async_remote_copy(
        src_ref=src, dst_ref=dst, send_sem=send, recv_sem=recv, device_id=device, device_id_type=MESH
    )
    copy.start()
    return copy


def local(src, dst, sem):
    copy = pltpu.make_async_copy(src, dst, sem)
    copy.start()
    return copy


def gather_kernel(depth_size, group, x_in, dy_in, w_in, x_out, dy_out, w_out, tz_s, tz_r, tx_s, tx_r, t_l, z_s, z_r, z_l, g_s, g_r):
    at = Place(depth_size, group)
    at.greet(at.everyone())
    rows, half = x_in.shape[1:]
    sent = []
    mine = pl.ds(pl.multiple_of(at.depth * rows, rows), rows)
    my_cols = pl.ds(pl.multiple_of(at.tp * half, half), half)

    def token_start(i, src, dst):
        copies = [
            remote(src.at[at.tp], dst.at[mine, my_cols], tz_s.at[i, s], tz_r.at[i, s], at.along(s))
            for s in range(1, depth_size)
        ]
        copies.append(local(src.at[at.tp], dst.at[mine, my_cols], t_l.at[i]))
        return copies

    def token_swap(i, copies, dst):
        for copy in copies[:-1]:
            copy.wait_recv()
            sent.append(copy)
        copies[-1].wait()
        return remote(dst.at[:, my_cols], dst.at[:, my_cols], tx_s.at[i], tx_r.at[i], at.twin())

    chunks = w_in.shape[0]

    def z_start(k):
        copies = [
            remote(
                w_in.at[k, lax.rem(at.depth + s, depth_size)],
                w_out.at[k, at.slot, at.depth],
                z_s.at[k, s],
                z_r.at[k, s],
                at.along(s),
            )
            for s in range(1, depth_size)
        ]
        copies.append(local(w_in.at[k, at.depth], w_out.at[k, at.slot, at.depth], z_l.at[k]))
        return copies

    def z_wait(copies):
        for copy in copies[:-1]:
            copy.wait_recv()
            sent.append(copy)
        copies[-1].wait()

    def g_start(k, stage):
        held = pl.ds(at.base(stage), 2**stage)
        return remote(
            w_out.at[k, held], w_out.at[k, held], g_s.at[k, stage], g_r.at[k, stage], at.across(stage)
        )

    ahead = 2
    tokens = [token_start(0, x_in, x_out)]
    z_copies = {k: z_start(k) for k in range(min(ahead, chunks))}
    stages = {}
    swaps = []
    for step in range(chunks + at.bits):
        if step < chunks:
            z_wait(z_copies[step])
            stages[step] = [g_start(step, 0)]
            if step + ahead < chunks:
                z_copies[step + ahead] = z_start(step + ahead)
            if step == 0:
                swaps.append(token_swap(0, tokens[0], x_out))
                tokens.append(token_start(1, dy_in, dy_out))
            if step == 1:
                swaps.append(token_swap(1, tokens[1], dy_out))
        for stage in range(1, at.bits + 1):
            k = step - stage
            if 0 <= k < chunks:
                stages[k][stage - 1].wait_recv()
                if stage < at.bits:
                    stages[k].append(g_start(k, stage))
    for swap in swaps:
        swap.wait()
    for k in range(chunks):
        for copy in stages[k]:
            copy.wait_send()
    for copy in sent:
        copy.wait_send()


def gather_all(depth_size, group, x_halves, dy_halves, weights):
    tp, rows, half = x_halves.shape
    chunks, _, depth_rows, width = weights.shape
    bits = group.bit_length() - 1
    dma = pltpu.SemaphoreType.DMA
    hbm = pl.BlockSpec(memory_space=pl.ANY)
    tokens = jax.ShapeDtypeStruct((depth_size * rows, tp * half), BF)
    return pl.pallas_call(
        functools.partial(gather_kernel, depth_size, group),
        out_shape=(
            tokens,
            tokens,
            jax.ShapeDtypeStruct((chunks, group, depth_size, depth_rows, width), BF),
        ),
        in_specs=[hbm] * 3,
        out_specs=(hbm, hbm, hbm),
        scratch_shapes=[
            dma((2, depth_size)),
            dma((2, depth_size)),
            dma((2,)),
            dma((2,)),
            dma((2,)),
            dma((chunks, depth_size)),
            dma((chunks, depth_size)),
            dma((chunks,)),
            dma((chunks, bits)),
            dma((chunks, bits)),
        ],
        compiler_params=pltpu.CompilerParams(collective_id=0, has_side_effects=True),
    )(x_halves, dy_halves, weights)


def share_kernel(depth_size, group, kv_in, kv_out, send, recv, loc):
    at = Place(depth_size, group)
    at.greet([at.across(stage) for stage in range(at.bits)])
    local(kv_in, kv_out.at[at.slot], loc).wait()
    copies = []
    for stage in range(at.bits):
        held = pl.ds(at.base(stage), 2**stage)
        copy = remote(kv_out.at[held], kv_out.at[held], send.at[stage], recv.at[stage], at.across(stage))
        copy.wait_recv()
        copies.append(copy)
    for copy in copies:
        copy.wait_send()


def share_group(depth_size, group, kv):
    bits = group.bit_length() - 1
    dma = pltpu.SemaphoreType.DMA
    hbm = pl.BlockSpec(memory_space=pl.ANY)
    return pl.pallas_call(
        functools.partial(share_kernel, depth_size, group),
        out_shape=jax.ShapeDtypeStruct((group,) + kv.shape, BF),
        in_specs=[hbm],
        out_specs=hbm,
        scratch_shapes=[dma((bits,)), dma((bits,)), dma],
        compiler_params=pltpu.CompilerParams(collective_id=1, has_side_effects=True),
    )(kv)


def fold_kernel(depth_size, group, g_in, total, landing, send, recv):
    at = Place(depth_size, group)
    at.greet([at.across(stage) for stage in range(at.bits)])
    for stage in reversed(range(at.bits)):
        size = 2**stage
        own = at.base(stage)
        other = own + (1 - 2 * at.bit(stage)) * size
        source = g_in if stage == at.bits - 1 else total
        copy = remote(
            source.at[pl.ds(other, size)],
            landing.at[pl.ds(size - 1, size)],
            send.at[stage],
            recv.at[stage],
            at.across(stage),
        )
        copy.wait()

        def add(i, _):
            total[own + i] = (
                source[own + i].astype(F32) + landing[size - 1 + i].astype(F32)
            ).astype(BF)
            return 0

        lax.fori_loop(0, size, add, 0)


def fold_group(depth_size, group, grads):
    bits = group.bit_length() - 1
    dma = pltpu.SemaphoreType.DMA
    vmem = pl.BlockSpec(memory_space=pltpu.VMEM)
    return pl.pallas_call(
        functools.partial(fold_kernel, depth_size, group),
        out_shape=jax.ShapeDtypeStruct(grads.shape, BF),
        in_specs=[vmem],
        out_specs=vmem,
        scratch_shapes=[
            pltpu.VMEM((group - 1,) + grads.shape[1:], BF),
            dma((bits,)),
            dma((bits,)),
        ],
        compiler_params=pltpu.CompilerParams(
            collective_id=2, has_side_effects=True, vmem_limit_bytes=60 << 20
        ),
    )(grads)


def reduce_kernel(depth_size, group, out_in, back_in, g_in, out_sum, back_sum, g_out, total, landing, g_s, g_r, z_s, z_r, z_l, t_acc, t_swap, t_land, tx_s, tx_r, tz_s, tz_r, ty_s, ty_r):
    at = Place(depth_size, group)
    at.greet(at.everyone())
    chunks = g_in.shape[0]
    depth_rows = g_in.shape[3]
    rows = out_sum.shape[0]
    half = t_acc.shape[2]
    last = at.bits - 1
    sent = []

    def g_start(k, stage):
        size = 2**stage
        other = at.base(stage) + (1 - 2 * at.bit(stage)) * size
        source = g_in.at[k] if stage == last else total.at[k]
        return remote(
            source.at[pl.ds(other, size)],
            landing.at[k, pl.ds(size - 1, size)],
            g_s.at[k, stage],
            g_r.at[k, stage],
            at.across(stage),
        )

    def g_finish(k, stage, copy):
        copy.wait_recv()
        sent.append(copy)
        size = 2**stage
        own = at.base(stage)
        source = g_in.at[k] if stage == last else total.at[k]

        def add(i, _):
            j = i // depth_size
            z = i % depth_size
            total[k, own + j, z] = (
                source[own + j, z].astype(F32) + landing[k, size - 1 + j, z].astype(F32)
            ).astype(BF)
            return 0

        lax.fori_loop(0, size * depth_size, add, 0)

    def z_start(k):
        copies = [
            remote(
                total.at[k, at.slot, lax.rem(at.depth + s, depth_size)],
                g_out.at[k, at.depth],
                z_s.at[k, s],
                z_r.at[k, s],
                at.along(s),
            )
            for s in range(1, depth_size)
        ]
        copies.append(local(total.at[k, at.slot, at.depth], g_out.at[k, at.depth], z_l.at[k]))
        return copies

    my_cols = pl.ds(pl.multiple_of(at.tp * half, half), half)
    her_cols = pl.ds(pl.multiple_of((1 - at.tp) * half, half), half)

    def token_first(i, src):
        return remote(src.at[:, her_cols], t_swap.at[i], tx_s.at[i], tx_r.at[i], at.twin())

    def token_second(i, src, copy):
        copy.wait_recv()
        sent.append(copy)

        def add(z, _):
            block = pl.ds(pl.multiple_of(z * rows, rows), rows)
            t_acc[i, block, :] = (
                src[block, my_cols].astype(F32) + t_swap[i, block, :].astype(F32)
            ).astype(BF)
            return 0

        lax.fori_loop(0, depth_size, add, 0)
        copies = []
        for s in range(1, depth_size):
            there = lax.rem(at.depth + s, depth_size)
            block = pl.ds(pl.multiple_of(there * rows, rows), rows)
            copies.append(
                remote(
                    t_acc.at[i, block, :], t_land.at[i, s - 1], tz_s.at[i, s], tz_r.at[i, s], at.along(s)
                )
            )
        return copies

    def token_third(i, dst, copies):
        for copy in copies:
            copy.wait_recv()
            sent.append(copy)
        mine = pl.ds(pl.multiple_of(at.depth * rows, rows), rows)
        value = t_acc[i, mine, :].astype(F32)
        for s in range(1, depth_size):
            value = value + t_land[i, s - 1].astype(F32)
        dst[:, my_cols] = value.astype(BF)
        return remote(dst.at[:, my_cols], dst.at[:, my_cols], ty_s.at[i], ty_r.at[i], at.twin())

    firsts = [token_first(0, out_in), token_first(1, back_in)]
    copies_of = {k: [g_start(k, last)] for k in range(chunks)}
    z_copies = {}
    seconds = []
    thirds = []
    for step in range(chunks + at.bits):
        for back in range(at.bits):
            k = step - back
            stage = last - back
            if 0 <= k < chunks:
                g_finish(k, stage, copies_of[k][back])
                if stage > 0:
                    copies_of[k].append(g_start(k, stage - 1))
                else:
                    z_copies[k] = z_start(k)
        if step == 1:
            seconds.append(token_second(0, out_in, firsts[0]))
        if step == 2:
            seconds.append(token_second(1, back_in, firsts[1]))
        if step == 4:
            thirds.append(token_third(0, out_sum, seconds[0]))
        if step == 5:
            thirds.append(token_third(1, back_sum, seconds[1]))
    for k in range(chunks):
        for copy in z_copies[k][:-1]:
            copy.wait()
        z_copies[k][-1].wait()
    for copy in thirds:
        copy.wait()
    for copy in sent:
        copy.wait_send()


def reduce_all(depth_size, group, out_part, back_part, grads):
    chunks, _, _, depth_rows, width = grads.shape
    all_rows, columns = out_part.shape
    rows = all_rows // depth_size
    half = columns // 2
    bits = group.bit_length() - 1
    dma = pltpu.SemaphoreType.DMA
    vmem = pl.BlockSpec(memory_space=pltpu.VMEM)
    tokens = jax.ShapeDtypeStruct((rows, columns), BF)
    return pl.pallas_call(
        functools.partial(reduce_kernel, depth_size, group),
        out_shape=(tokens, tokens, jax.ShapeDtypeStruct((chunks, depth_size, depth_rows, width), BF)),
        in_specs=[vmem] * 3,
        out_specs=(vmem, vmem, vmem),
        scratch_shapes=[
            pltpu.VMEM((chunks, group, depth_size, depth_rows, width), BF),
            pltpu.VMEM((chunks, group - 1, depth_size, depth_rows, width), BF),
            dma((chunks, bits)),
            dma((chunks, bits)),
            dma((chunks, depth_size)),
            dma((chunks, depth_size)),
            dma((chunks,)),
            pltpu.VMEM((2, all_rows, half), BF),
            pltpu.VMEM((2, all_rows, half), BF),
            pltpu.VMEM((2, depth_size - 1, rows, half), BF),
            dma((2,)),
            dma((2,)),
            dma((2, depth_size)),
            dma((2, depth_size)),
            dma((2,)),
            dma((2,)),
        ],
        compiler_params=pltpu.CompilerParams(
            collective_id=3, has_side_effects=True, vmem_limit_bytes=60 << 20
        ),
    )(out_part, back_part, grads)


def rotate(values, cosine, sine_table):
    half_rot = ROT // 2
    leading = values[..., :half_rot]
    trailing = values[..., half_rot:ROT]
    return jnp.concatenate(
        [
            leading * cosine - trailing * sine_table,
            trailing * cosine + leading * sine_table,
            values[..., ROT:],
        ],
        -1,
    )


def rope_tables(positions):
    freqs = 10000.0 ** (-(2.0 * jnp.arange(ROT // 2, dtype=F32)) / ROT)
    angles = positions.astype(F32)[:, None] * freqs[None, :]
    return (jnp.cos(angles), jnp.sin(angles))


def gelu_parts(values):
    gate = 0.5 * (1.0 + lax.erf(values * math.sqrt(0.5)))
    slope = gate + values * jnp.exp(-0.5 * values * values) * (1.0 / math.sqrt(2.0 * math.pi))
    return values * gate, slope


SMALL_ROWS = 96
SMALL_SENT = 80
LATE = (3, 7,)
LATE_ROWS = 1
LATE_COLS = 2
VMEM_BYTES = 64 << 20


def slot_member(slot, bits):
    member = 0
    for stage in range(bits):
        member += ((slot >> stage) & 1) << (bits - 1 - stage)
    return member


def natural_blocks(depth_size, group):
    bits = group.bit_length() - 1
    return [
        depth * group + slot_member(slot, bits) for slot in range(group) for depth in range(depth_size)
    ]

ROW_TILE = 256
DROP = -1e30


def layout_of(depth_size, group, depth_rows, rows, width, ff_chunks):
    tokens = depth_size * rows
    half = width // 2
    landing = (group - 1) * depth_size * depth_rows
    heads = 3 + ff_chunks
    cols = 1 + ff_chunks
    return [
        ("wr", (heads, width, CHUNK), BF),
        ("wc", (cols, CHUNK, width), BF),
        ("gr", (heads, width, CHUNK), BF),
        ("gc", (cols, CHUNK, width), BF),
        ("lr", (heads, landing, CHUNK), BF),
        ("lc", (cols, CHUNK, landing), BF),
        ("x", (tokens, width), BF),
        ("dy", (tokens, width), BF),
        ("na", (tokens, width), BF),
        ("nm", (tokens, width), BF),
        ("nmt", (width, tokens), BF),
        ("kv", (group * tokens, 2 * HD), BF),
        ("q", (tokens, HD), BF),
        ("low", (tokens, 3 * HD), BF),
        ("al", (tokens, HD), BF),
        ("hg", (tokens, HD), BF),
        ("alt", (HD, tokens), BF),
        ("att", (HD, tokens), F32),
        ("dqt", (HD, tokens), F32),
        ("stat", (8, tokens), F32),
        ("tab", (group * tokens, 128), F32),
        ("kb", (8, HD), F32),
        ("hid", (ff_chunks, tokens, CHUNK), BF),
        ("ul", (ff_chunks, tokens, CHUNK), BF),
        ("tz", (2, 2, tokens // 2, half // 2), BF),
        ("te", (2, rows, half), BF),
        ("mean", (tokens, 1), F32),
        ("inv", (tokens, 1), F32),
        ("xl", (2, rows, width), BF),
        ("gv", (8, width), F32),
        ("biases", (8, HD), F32),
        ("places", (group * tokens // 128, 128), F32),
        ("ps", (group.bit_length(), SMALL_ROWS, 128), F32),
        ("pl", (group.bit_length() - 1, SMALL_ROWS, 128), F32),
        ("pz", (depth_size, SMALL_SENT, 128), F32),
        ("px", (2, SMALL_SENT, 128), F32),
        ("dr", (LATE_ROWS, 2, depth_size * depth_rows, CHUNK), BF),
        ("dc", (LATE_COLS, 2, CHUNK, depth_size * depth_rows), BF),
    ]


def semaphores_of(depth_size, group, items):
    bits = group.bit_length() - 1
    return [
        ("z_s", (items, depth_size)),
        ("z_r", (items, depth_size)),
        ("z_l", (items,)),
        ("g_s", (items, bits)),
        ("g_r", (items, bits)),
        ("t_s", (2, 3)),
        ("t_r", (2, 3)),
        ("w_s", (2, 3)),
        ("w_r", (2, 3)),
        ("kv_s", (2, 2, bits)),
        ("kv_r", (2, 2, bits)),
        ("f_s", (items, bits)),
        ("f_r", (items, bits)),
        ("e_s", (items, depth_size)),
        ("e_r", (items, depth_size)),
        ("e_l", (items,)),
        ("x_l", (2,)),
        ("d_s", (LATE_ROWS + LATE_COLS, 2, depth_size)),
        ("d_r", (LATE_ROWS + LATE_COLS, 2, depth_size)),
        ("d_l", (LATE_ROWS + LATE_COLS, depth_size)),
        ("o_s", (2, 6)),
        ("o_r", (2, 6)),
        ("p_s", (bits + depth_size,)),
        ("p_r", (bits + depth_size,)),
    ]


VECTORS = ("attn_gain", "attn_shift", "mlp_gain", "mlp_shift")
BIASES = ("b_query", "b_key", "b_value", "b_up")
INPUTS = ("blocks", "x_in", "dy_in", "freqs") + VECTORS + BIASES
INPUTS += ("w_query", "w_key", "w_value", "w_out", "w_up", "w_down")
OUTPUTS = ("fin", "g_query", "g_key", "g_value", "g_out", "g_up", "g_down")
OUTPUTS += ("norm_sums", "s_query", "s_key", "s_value", "s_up", "s_dy")


class Bag:
    pass


def fused_kernel(names, depth_size, group, *refs):
    m = Bag()
    for name, ref in zip(names, refs, strict=True):
        setattr(m, name, ref)
    at = Place(depth_size, group)
    loads = [local(source, m.xl.at[i], m.x_l.at[i]) for i, source in enumerate((m.x_in, m.dy_in))]
    at.greet(at.everyone())
    bits = at.bits
    rows, width = m.x_in.shape
    depth_rows = width // (depth_size * group)
    tokens = depth_size * rows
    half = width // 2
    ff_width = m.w_up.shape[1] // depth_size
    ff_chunks = ff_width // CHUNK
    block_count = width // depth_rows
    own_block = at.slot * depth_size + at.depth
    natural = natural_blocks(depth_size, group)
    sends, settled = [], []

    def blocks(first, count):
        return pl.ds(pl.multiple_of(first * depth_rows, depth_rows), count * depth_rows)

    def token_rows(depth):
        return pl.ds(pl.multiple_of(depth * rows, rows), rows)

    def peer(step):
        return lax.rem(at.depth + step, depth_size)

    my_cols = pl.ds(pl.multiple_of(at.tp * half, half), half)
    her_cols = pl.ds(pl.multiple_of((1 - at.tp) * half, half), half)

    units = [("r", 0), ("r", 1), ("r", 2), ("c", 0)]
    for i in range(ff_chunks):
        units += [("r", 3 + i), ("c", 1 + i)]
    row_pairs = [(m.w_query, m.g_query), (m.w_key, m.g_key), (m.w_value, m.g_value)]

    def outer(kind, a, depth, which):
        if kind == "r" and a < 3:
            return row_pairs[a][which].at[:, pl.ds(pl.multiple_of(depth * HD, HD), HD)]
        if kind == "r":
            first = pl.multiple_of(depth * ff_width + (a - 3) * CHUNK, CHUNK)
            return (m.w_up, m.g_up)[which].at[:, pl.ds(first, CHUNK)]
        if a == 0:
            return (m.w_out, m.g_out)[which].at[pl.ds(pl.multiple_of(depth * HD, HD), HD), :]
        first = pl.multiple_of(depth * ff_width + (a - 1) * CHUNK, CHUNK)
        return (m.w_down, m.g_down)[which].at[pl.ds(first, CHUNK), :]

    def part(pair, kind, a, first, count):
        if kind == "r":
            return pair[0].at[a, blocks(first, count), :]
        return pair[1].at[a, :, blocks(first, count)]

    weights, grads, landing = (m.wr, m.wc), (m.gr, m.gc), (m.lr, m.lc)

    def z_start(k):
        kind, a = units[k]
        into = part(weights, kind, a, own_block, 1)
        copies = [
            remote(outer(kind, a, peer(s), 0), into, m.z_s.at[k, s], m.z_r.at[k, s], at.along(s))
            for s in range(1, depth_size)
        ]
        copies.append(local(outer(kind, a, at.depth, 0), into, m.z_l.at[k]))
        return copies

    def z_wait(copies):
        received(copies[:-1])
        copies[-1].wait()

    def g_start(k, stage):
        kind, a = units[k]
        held = part(weights, kind, a, at.base(stage) * depth_size, 2**stage * depth_size)
        return [remote(held, held, m.g_s.at[k, stage], m.g_r.at[k, stage], at.across(stage))]

    def received(copies):
        for copy in copies:
            copy.wait_recv()
        sends.extend(copies)

    def settle(copies):
        for copy in copies:
            copy.wait_send()
        settled.extend(copies)

    def fold_start(k, stage):
        kind, a = units[k]
        size = 2**stage
        other = at.base(stage) + (1 - 2 * at.bit(stage)) * size
        return [
            remote(
                part(grads, kind, a, other * depth_size, size * depth_size),
                part(landing, kind, a, (size - 1) * depth_size, size * depth_size),
                m.f_s.at[k, stage],
                m.f_r.at[k, stage],
                at.across(stage),
            )
        ]

    def fold_add(k, stage, copies):
        received(copies)
        kind, a = units[k]
        size = 2**stage
        own = at.base(stage) * depth_size

        def add(i, _):
            mine = blocks(own + i, 1)
            theirs = blocks((size - 1) * depth_size + i, 1)
            if kind == "r":
                total = m.gr[a, mine, :].astype(F32) + m.lr[a, theirs, :].astype(F32)
                m.gr[a, mine, :] = total.astype(BF)
            else:
                total = m.gc[a, :, mine].astype(F32) + m.lc[a, :, theirs].astype(F32)
                m.gc[a, :, mine] = total.astype(BF)
            return 0

        lax.fori_loop(0, size * depth_size, add, 0)

    def end_start(k):
        kind, a = units[k]
        into = outer(kind, a, at.depth, 1)
        copies = [
            remote(
                part(grads, kind, a, at.slot * depth_size + peer(s), 1),
                into,
                m.e_s.at[k, s],
                m.e_r.at[k, s],
                at.along(s),
            )
            for s in range(1, depth_size)
        ]
        copies.append(local(part(grads, kind, a, own_block, 1), into, m.e_l.at[k]))
        return copies

    late = {k: n for n, k in enumerate(LATE)}
    other_slot = at.base(1) + 1 - at.bit(0)

    def depth_buffer(k, h, first, count):
        kind, a = units[k]
        same = [j for j in LATE if units[j][0] == kind].index(k)
        if kind == "r":
            return m.dr.at[same, h, blocks(first, count), :]
        return m.dc.at[same, h, :, blocks(first, count)]

    def depth_first_start(k, copies):
        fold_add(k, 1, copies)
        kind, a = units[k]
        n = late[k]
        copies = []
        for h, slot in enumerate((at.slot, other_slot)):
            for s in range(1, depth_size):
                copies.append(
                    remote(
                        part(grads, kind, a, slot * depth_size + peer(s), 1),
                        depth_buffer(k, h, at.depth, 1),
                        m.d_s.at[n, h, s],
                        m.d_r.at[n, h, s],
                        at.along(s),
                    )
                )
            own = part(grads, kind, a, slot * depth_size + at.depth, 1)
            depth_buffer(k, h, at.depth, 1)[...] = own[...]
        return copies

    def depth_first_fold(k, copies):
        received(copies)
        kind, a = units[k]
        return [
            remote(
                depth_buffer(k, 1, 0, depth_size),
                part(landing, kind, a, 0, depth_size),
                m.f_s.at[k, 0],
                m.f_r.at[k, 0],
                at.across(0),
            )
        ]

    def depth_first_end(k, copies):
        received(copies)
        kind, a = units[k]
        ends = []
        for z in range(depth_size):
            mine = depth_buffer(k, 0, z, 1)
            theirs = part(landing, kind, a, z, 1)
            mine[...] = (mine[...].astype(F32) + theirs[...].astype(F32)).astype(BF)
            ends.append(local(mine, outer(kind, a, z, 1), m.d_l.at[late[k], z]))
        return ends

    near = {"ctx": at.ctx + (1 - 2 * (at.depth % 2)) * group}
    far = {"ctx": at.ctx + (2 - 4 * (at.depth // 2)) * group}
    near_depth = at.depth + 1 - 2 * (at.depth % 2)
    pair_first = at.depth // 2 * 2
    my_pair = pl.ds(pl.multiple_of(pair_first * rows, rows), 2 * rows)
    her_pair = pl.ds(pl.multiple_of((2 - pair_first) * rows, rows), 2 * rows)
    quarter = half // 2
    my_quarter = pl.ds(pl.multiple_of(at.tp * half + at.depth % 2 * quarter, quarter), quarter)
    her_quarter = pl.ds(pl.multiple_of(at.tp * half + (1 - at.depth % 2) * quarter, quarter), quarter)

    def token_step(i, buffer, step, copies):
        if copies:
            received(copies[-1:])
        brought = [
            None,
            (token_rows(near_depth), my_cols),
            (her_pair, my_quarter),
            (her_pair, her_quarter),
        ]
        given = [(token_rows(at.depth), my_cols), (my_pair, my_quarter), (her_pair, my_quarter)]
        if step < 3:
            piece = buffer.at[given[step][0], given[step][1]]
            there = far if step == 1 else near
            copies.append(remote(piece, piece, m.t_s.at[i, step], m.t_r.at[i, step], there))
        if step:
            piece = buffer.at[brought[step][0], brought[step][1]]
            swapped[i].append(
                remote(piece, piece, m.w_s.at[i, step - 1], m.w_r.at[i, step - 1], at.twin())
            )
        return copies

    def kv_start(h, stage):
        size = 2**stage * tokens
        rows_held = pl.ds(pl.multiple_of(at.base(stage) * tokens, tokens), size)
        held = m.kv.at[rows_held, slice(h * HD, (h + 1) * HD)]
        return remote(held, held, m.kv_s.at[0, h, stage], m.kv_r.at[0, h, stage], at.across(stage))

    spare = (m.lr.at[1 + ff_chunks], m.lr.at[2 + ff_chunks])

    def dkv_start(stage):
        size = 2**stage
        other = at.base(stage) + (1 - 2 * at.bit(stage)) * size
        given = pl.ds(pl.multiple_of(other * tokens, tokens), size * tokens)
        taken = pl.ds((size - 1) * tokens, size * tokens)
        return [
            remote(
                m.kv.at[given, slice(h * HD, (h + 1) * HD)],
                spare[h].at[taken, :],
                m.kv_s.at[1, h, stage],
                m.kv_r.at[1, h, stage],
                at.across(stage),
            )
            for h in range(2)
        ]

    def dkv_finish(stage, copies):
        received(copies)
        size = 2**stage
        own = at.base(stage) * tokens
        step = ROW_TILE

        def add(i, _):
            mine = pl.ds(pl.multiple_of(own + i * step, step), step)
            theirs = pl.ds(pl.multiple_of((size - 1) * tokens + i * step, step), step)
            for h in range(2):
                cols = slice(h * HD, (h + 1) * HD)
                total = m.kv[mine, cols].astype(F32) + spare[h][theirs, :].astype(F32)
                m.kv[mine, cols] = total.astype(BF)
            return 0

        lax.fori_loop(0, size * tokens // step, add, 0)

    lane = lax.broadcasted_iota(jnp.int32, (1, 128), 1)

    def place_rows():
        mine = token_rows(at.depth)
        for copy in loads:
            copy.wait()
        for b in range(block_count):
            c = natural[b]
            into = slice(b * depth_rows, (b + 1) * depth_rows)
            out_of = slice(c * depth_rows, (c + 1) * depth_rows)
            m.x[mine, into] = m.xl[0, :, out_of]
            m.dy[mine, into] = m.xl[1, :, out_of]

    def place_vectors():
        m.ps[0] = jnp.zeros_like(m.ps[0])
        for row, name in enumerate(VECTORS):
            for b in range(block_count):
                c = natural[b]
                m.gv[row : row + 1, b * depth_rows : (b + 1) * depth_rows] = getattr(m, name)[c : c + 1, :]
        per_head = HD // 128
        for a in range(3):
            for h in range(per_head):
                row = getattr(m, BIASES[a])[pl.ds(at.depth * per_head + h, 1), :]
                m.biases[a : a + 1, h * 128 : (h + 1) * 128] = row
        for i in range(ff_chunks):
            for h in range(per_head):
                row = m.b_up[pl.ds((at.depth * ff_chunks + i) * per_head + h, 1), :]
                m.biases[3 + i : 4 + i, h * 128 : (h + 1) * 128] = row
        block_rows = rows // 2
        for n in range(group * depth_size):
            c = natural[n]
            first = jnp.where(lane < block_rows, m.blocks[2 * c], m.blocks[2 * c + 1])
            m.places[n : n + 1, :] = (first * block_rows + lane % block_rows).astype(F32)

    def affine():
        step = 32

        def stats(i, _):
            here = pl.ds(pl.multiple_of(i * step, step), step)
            x = m.x[here, :].astype(F32)
            mean = jnp.mean(x, -1, keepdims=True)
            centered = x - mean
            m.mean[here, :] = mean
            m.inv[here, :] = lax.rsqrt(jnp.mean(centered * centered, -1, keepdims=True) + norm_epsilon)
            return 0

        lax.fori_loop(0, tokens // step, stats, 0)

        def body(i, _):
            here = token_rows(i)
            for n in range(width // 512):
                cols = slice(n * 512, (n + 1) * 512)
                normal = (m.x[here, cols].astype(F32) - m.mean[here, :]) * m.inv[here, :]
                m.na[here, cols] = (normal * m.gv[0:1, cols] + m.gv[1:2, cols]).astype(BF)
                mlp = normal * m.gv[2:3, cols] + m.gv[3:4, cols]
                m.nm[here, cols] = mlp.astype(BF)
                m.nmt[cols, here] = mlp.T.astype(BF)
            return 0

        lax.fori_loop(0, depth_size, body, 0)

    def place_column(n):
        return jnp.broadcast_to(m.places[pl.ds(n, 1), :], (128, 128)).T

    def make_tables():
        def body(n, _):
            angles = place_column(n) * m.freqs[0:1, :]
            here = pl.ds(pl.multiple_of(n * 128, 128), 128)
            m.tab[here, :] = jnp.cos(angles - jnp.where(lane < ROT, 0.0, math.pi / 2))
            return 0

        lax.fori_loop(0, group * tokens // 128, body, 0)

    def turned(value, here, sign):
        head = value[:, :128]
        left = pltpu.roll(head, 128 - ROT // 2, 1)
        right = pltpu.roll(head, ROT // 2, 1)
        table = m.tab[here, :]
        cosine = jnp.where(lane < ROT, table, 1.0)
        sine = sign * pltpu.roll(table, ROT, 1)
        crossed = jnp.where(lane < ROT // 2, -left, jnp.where(lane < ROT, right, 0.0))
        return head * cosine + crossed * sine

    def project(a):
        return mm(m.na[...], m.wr[a]) + m.biases[a : a + 1, :]

    kv_own = pl.ds(pl.multiple_of(at.slot * tokens, tokens), tokens)
    score_scale = 1.0 / math.sqrt(HD)

    def make_query():
        query = project(0)
        m.q[:, :128] = turned(query, kv_own, 1.0).astype(BF)
        m.q[:, 128:] = query[:, 128:].astype(BF)

    def make_keys():
        keys = project(1)
        m.kv[kv_own, :128] = turned(keys, kv_own, 1.0).astype(BF)
        m.kv[kv_own, 128:HD] = keys[:, 128:].astype(BF)

    def make_values():
        m.kv[kv_own, HD:] = project(2).astype(BF)

    def key_rows(j):
        return pl.ds(pl.multiple_of(j * tokens, tokens), tokens)

    def masked_scores(j):
        scores = mm_nt(m.kv[key_rows(j), :HD], m.q[...]) * score_scale
        count = tokens // 128
        column = jnp.concatenate([place_column(j * count + n)[:, :1] for n in range(count)], 0)
        row = jnp.concatenate([m.places[pl.ds(at.slot * count + n, 1), :] for n in range(count)], 1)
        return jnp.where(column <= row, scores, DROP)

    def attend(j):
        scores = masked_scores(j)
        if j == 0:
            old = jnp.full((1, tokens), -1e20, F32)
        else:
            old = m.stat[0:1, :]
        new = jnp.maximum(old, jnp.max(scores, 0, keepdims=True))
        raw = jnp.exp(scores - new)
        total = jnp.sum(raw, 0, keepdims=True)
        value = mm(m.kv[key_rows(j), HD:].T, raw.astype(BF))
        m.stat[0:1, :] = new
        if j:
            factor = jnp.exp(old - new)
            total = total + m.stat[1:2, :] * factor
            value = value + m.att[...] * factor
        m.stat[1:2, :] = total
        m.att[...] = value
        if j == group - 1:
            m.stat[2:3, :] = new + jnp.log(total)
            value = value / total
            m.att[...] = value
            m.alt[...] = value.astype(BF)
            m.al[...] = value.T.astype(BF)

    def head_grads():
        grad = mm_nt(m.dy[...], m.wc[0])
        low = grad.astype(BF)
        m.hg[...] = low
        m.stat[3:4, :] = jnp.sum(low.astype(F32).T * m.att[...], 0, keepdims=True)

    def attend_back(j):
        probs = jnp.exp(masked_scores(j) - m.stat[2:3, :])
        value_part = mm(probs.astype(BF), m.hg[...])
        prob_grad = mm_nt(m.kv[key_rows(j), HD:], m.hg[...])
        score_grad = (probs * (prob_grad - m.stat[3:4, :]) * score_scale).astype(BF)
        query_part = mm(m.kv[key_rows(j), :HD].T, score_grad)
        key_part = mm(score_grad, m.q[...])
        head_sum = jnp.sum(turned(key_part, key_rows(j), -1.0), 0, keepdims=True)
        rest_sum = jnp.sum(key_part[:, 128:], 0, keepdims=True)
        if j:
            query_part = query_part + m.dqt[...]
            head_sum = head_sum + m.kb[0:1, :128]
            rest_sum = rest_sum + m.kb[0:1, 128:]
        m.dqt[...] = query_part
        m.kb[0:1, :128] = head_sum
        m.kb[0:1, 128:] = rest_sum
        m.kv[key_rows(j), :HD] = key_part.astype(BF)
        m.kv[key_rows(j), HD:] = value_part.astype(BF)

    def small_store(first, row):
        for n in range(row.shape[1] // 128):
            m.ps[0, first + n : first + n + 1, :] = row[:, n * 128 : (n + 1) * 128]

    def attention_grads():
        query = m.dqt[...].T
        head = turned(query, kv_own, -1.0)
        keys = m.kv[kv_own, :HD].astype(F32)
        key_head = turned(keys, kv_own, -1.0)
        m.low[:, :128] = head.astype(BF)
        m.low[:, 128:HD] = query[:, 128:].astype(BF)
        m.low[:, HD : HD + 128] = key_head.astype(BF)
        m.low[:, HD + 128 : 2 * HD] = m.kv[kv_own, 128:HD]
        m.low[:, 2 * HD :] = m.kv[kv_own, HD:]
        small_store(64, jnp.sum(head, 0, keepdims=True))
        small_store(65, jnp.sum(query[:, 128:], 0, keepdims=True))
        small_store(66, m.kb[0:1, :])
        small_store(68, jnp.sum(m.kv[kv_own, HD:].astype(F32), 0, keepdims=True))

        def body(n, _):
            tile = pl.ds(pl.multiple_of(n * ROW_TILE, ROW_TILE), ROW_TILE)
            turned_in = m.na[:, tile].T
            for a in range(3):
                m.gr[a, tile, :] = mm(turned_in, m.low[:, a * HD : (a + 1) * HD]).astype(BF)
            return 0

        lax.fori_loop(0, width // ROW_TILE, body, 0)

    def out_grads():
        def body(n, _):
            tile = pl.ds(pl.multiple_of(n * 512, 512), 512)
            m.gc[0, :, tile] = mm(m.alt[...], m.dy[:, tile]).astype(BF)
            return 0

        lax.fori_loop(0, width // 512, body, 0)

    def feed_forward(i):
        activated, slope = gelu_parts(mm(m.nm[...], m.wr[3 + i]) + m.biases[3 + i : 4 + i, :])
        m.hid[i] = activated.astype(BF)
        up_grad = mm_nt(m.dy[...], m.wc[1 + i]) * slope
        small_store(70 + 2 * i, jnp.sum(up_grad, 0, keepdims=True))
        m.ul[i] = up_grad.astype(BF)
        turned_hidden = activated.T.astype(BF)

        def body(n, _):
            tile = pl.ds(pl.multiple_of(n * 512, 512), 512)
            m.gr[3 + i, tile, :] = mm(m.nmt[tile, :], m.ul[i]).astype(BF)
            m.gc[1 + i, :, tile] = mm(turned_hidden, m.dy[:, tile]).astype(BF)
            return 0

        lax.fori_loop(0, width // 512, body, 0)

    out, back = m.na, m.dy

    def tile_of(n):
        return pl.ds(pl.multiple_of(n * ROW_TILE, ROW_TILE), ROW_TILE)

    def small_add_rows(first, n, value):
        row = jnp.sum(value, 0, keepdims=True)
        for h in range(ROW_TILE // 128):
            m.ps[0, pl.ds(first + n * (ROW_TILE // 128) + h, 1), :] = row[:, h * 128 : (h + 1) * 128]

    def end_out(n):
        tile = tile_of(n)
        total = mm(m.al[...], m.wc[0, :, tile])
        for i in range(ff_chunks):
            total += mm(m.hid[i], m.wc[1 + i, :, tile])
        out[:, tile] = total.astype(BF)

    def end_back(n):
        tile = tile_of(n)
        attn_back = mm_nt(m.low[:, :HD], m.wr[0, tile, :])
        for a in (1, 2):
            attn_back += mm_nt(m.low[:, a * HD : (a + 1) * HD], m.wr[a, tile, :])
        mlp_back = mm_nt(m.ul[0], m.wr[3, tile, :])
        for i in range(1, ff_chunks):
            mlp_back += mm_nt(m.ul[i], m.wr[3 + i, tile, :])
        normal = (m.x[:, tile].astype(F32) - m.mean[...]) * m.inv[...]
        small_add_rows(0, n, attn_back * normal)
        small_add_rows(16, n, attn_back)
        small_add_rows(32, n, mlp_back * normal)
        small_add_rows(48, n, mlp_back)
        small_add_rows(78, n, m.dy[:, tile].astype(F32))
        back[:, tile] = (attn_back * m.gv[0:1, tile] + mlp_back * m.gv[2:3, tile]).astype(BF)

    def end_quarter(piece, which, n):
        count = quarter // ROW_TILE
        odd = at.depth % 2
        first = which * 2 + (odd if n else 1 - odd)

        def body(i, _):
            piece(first * count + i)
            return 0

        lax.fori_loop(0, count, body, 0)

    ends = (out, back)

    def quarter_of(which, n):
        odd = at.depth % 2
        return pl.ds(pl.multiple_of(which * half + (odd if n else 1 - odd) * quarter, quarter), quarter)

    def offer():
        pl.semaphore_signal(m.free, inc=1, device_id=at.twin(), device_id_type=MESH)

    def sum_start(i, n):
        if i == n == 0:
            pl.semaphore_wait(m.free, 1)
        return remote(
            ends[i].at[:, quarter_of(1 - at.tp, n)],
            m.nm.at[:, quarter_of(i, n)],
            m.o_s.at[i, n],
            m.o_r.at[i, n],
            at.twin(),
        )

    def sum_add(i, n):
        mine = ends[i]
        into, source = quarter_of(at.tp, n), quarter_of(i, n)

        def add(z, _):
            block = token_rows(z)
            total = mine[block, into].astype(F32) + m.nm[block, source].astype(F32)
            mine[block, into] = total.astype(BF)
            return 0

        lax.fori_loop(0, depth_size, add, 0)

    def sum_step(i, step, copy):
        received([copy])
        mine = ends[i]
        if step == 0:
            sum_add(i, 0)
            source, into, there = mine.at[her_pair, her_quarter], m.tz.at[i, 0], near
        elif step == 1:
            total = mine[her_pair, my_quarter].astype(F32) + m.tz[i, 0].astype(F32)
            mine[her_pair, my_quarter] = total.astype(BF)
            source, into, there = mine.at[her_pair, my_quarter], m.tz.at[i, 1], far
        elif step == 2:
            total = mine[my_pair, my_quarter].astype(F32) + m.tz[i, 1].astype(F32)
            mine[my_pair, my_quarter] = total.astype(BF)
            source, into, there = mine.at[token_rows(near_depth), my_cols], m.te.at[i], near
        else:
            total = mine[token_rows(at.depth), my_cols].astype(F32) + m.te[i].astype(F32)
            m.fin[i, :, my_cols] = total.astype(BF)
            source, into, there = m.fin.at[i, :, my_cols], m.fin.at[i, :, my_cols], at.twin()
        return remote(source, into, m.o_s.at[i, 2 + step], m.o_r.at[i, 2 + step], there)

    def small_group(stage):
        return remote(m.ps.at[stage], m.pl.at[stage], m.p_s.at[stage], m.p_r.at[stage], at.across(stage))

    def small_add(stage, copy):
        received([copy])
        m.ps[stage + 1] = m.ps[stage] + m.pl[stage]

    def small_depth():
        total = m.ps.at[bits, 0:SMALL_SENT, :]
        copies = [
            remote(total, m.pz.at[at.depth], m.p_s.at[bits + s], m.p_r.at[bits + s], at.along(s))
            for s in range(1, depth_size)
        ]
        m.pz[at.depth] = m.ps[bits, 0:SMALL_SENT, :]
        return copies

    def small_twin(copies):
        received(copies)
        value = m.pz[0]
        for z in range(1, depth_size):
            value = value + m.pz[z]
        m.px[0] = value
        return remote(m.px.at[0], m.px.at[1], m.p_s.at[bits], m.p_r.at[bits], at.twin())

    def small_finish(copy):
        received([copy])
        for v in range(4):
            for b in range(block_count):
                row = v * 16 + b
                into = v * 16 + natural[b]
                m.norm_sums[into : into + 1, :] = m.px[0, row : row + 1, :] + m.px[1, row : row + 1, :]
        for b in range(block_count):
            m.s_dy[natural[b] : natural[b] + 1, :] = m.ps[bits, 78 + b : 79 + b, :]
        for z in range(depth_size):
            m.s_query[2 * z : 2 * z + 2, :] = m.pz[z, 64:66, :]
            m.s_key[2 * z : 2 * z + 2, :] = m.pz[z, 66:68, :]
            m.s_value[2 * z : 2 * z + 2, :] = m.pz[z, 68:70, :]
            m.s_up[8 * z : 8 * z + 8, :] = m.pz[z, 70:78, :]

    z_live, g_live, t_live, k_live, f_live, e_live, x_live, s_live, d_live, p_live = ({} for _ in range(10))
    swapped = {0: [], 1: []}
    buffers = (m.x, m.dy)

    def do_zs(n):
        z_live[n] = z_start(n)

    def do_zy(n):
        z_wait(z_live[n])
        g_live[n] = g_start(n, 0)

    def do_yc(n):
        received(g_live[n])
        g_live[n] = g_start(n, 1)

    def do_cw(n):
        received(g_live[n])

    def do_ta(n):
        t_live[n] = token_step(n, buffers[n], 0, [])

    def do_tb(n):
        token_step(n, buffers[n], 1, t_live[n])

    def do_tc(n):
        token_step(n, buffers[n], 2, t_live[n])

    def do_td(n):
        token_step(n, buffers[n], 3, t_live[n])

    def do_te(n):
        received(swapped[n])

    do_norm, do_vec, do_tab, do_aff = place_rows, place_vectors, make_tables, affine
    do_qq, do_kk, do_val, do_hg = make_query, make_keys, make_values, head_grads
    do_at, do_ag, do_go, do_ff, do_of = attend, attention_grads, out_grads, feed_forward, offer

    def do_ky(n):
        k_live[n] = [kv_start(n, 0)]

    def do_kc(n):
        received(k_live[n])
        k_live[n].append(kv_start(n, 1))

    def do_kw(n):
        received(k_live[n][1:])

    def do_bw(n):
        if n == 0:
            settle(k_live[0] + k_live[1])
        attend_back(n)

    def do_dc():
        d_live[1] = dkv_start(1)

    def do_dy():
        dkv_finish(1, d_live[1])
        d_live[0] = dkv_start(0)

    def do_dw():
        dkv_finish(0, d_live[0])

    def do_fc(n):
        f_live[n] = fold_start(n, 1)

    def do_fy(n):
        fold_add(n, 1, f_live[n])
        f_live[n] = fold_start(n, 0)

    def do_fz(n):
        fold_add(n, 0, f_live[n])
        e_live[n] = end_start(n)

    def do_fq(n):
        f_live[n] = depth_first_start(n, f_live[n])

    def do_fr(n):
        f_live[n] = depth_first_fold(n, f_live[n])

    def do_fs(n):
        e_live[n] = depth_first_end(n, f_live[n])

    def do_ew(n):
        here = depth_size if n in late else 1
        received(e_live[n][:-here])
        for copy in e_live[n][-here:]:
            copy.wait()

    def do_eo(n):
        end_quarter(end_out, at.tp if n >= 2 else 1 - at.tp, n % 2)

    def do_eb(n):
        if n == 0:
            settle(t_live[1] + swapped[1])
        end_quarter(end_back, at.tp if n >= 2 else 1 - at.tp, n % 2)

    def do_sx(n):
        x_live[n] = sum_start(n // 2, n % 2)

    def do_sa(n):
        s_live[n] = sum_step(n, 0, x_live[2 * n])

    def do_sm(n):
        received([x_live[2 * n + 1]])
        sum_add(n, 1)

    def do_sb(n):
        s_live[n] = sum_step(n, 1, s_live[n])

    def do_sc(n):
        s_live[n] = sum_step(n, 2, s_live[n])

    def do_sd(n):
        s_live[n] = sum_step(n, 3, s_live[n])

    def do_sw(n):
        received([s_live[n]])

    def do_pa():
        p_live[0] = small_group(0)

    def do_pb():
        small_add(0, p_live[0])
        p_live[1] = small_group(1)

    def do_pc():
        small_add(1, p_live[1])
        p_live[2] = small_depth()

    def do_pd():
        p_live[3] = small_twin(p_live[2])

    def do_pe():
        small_finish(p_live[3])

    do_zs(1)
    do_zs(2)
    do_norm()
    do_zs(10)
    do_ta(0)
    do_zy(1)
    do_zy(2)
    do_zs(4)
    do_vec()
    do_tb(0)
    do_ta(1)
    do_zy(10)
    do_yc(2)
    do_tab()
    do_zy(4)
    do_zs(3)
    do_tc(0)
    do_zs(0)
    do_zy(3)
    do_zs(9)
    do_td(0)
    do_cw(2)
    do_tb(1)
    do_yc(10)
    do_yc(1)
    do_zy(0)
    do_zs(11)
    do_yc(4)
    do_te(0)
    do_zs(8)
    do_zy(9)
    do_zs(6)
    do_aff()
    do_yc(3)
    do_val()
    do_ky(1)
    do_cw(1)
    do_kk()
    do_tc(1)
    do_ky(0)
    do_zs(7)
    do_yc(0)
    do_cw(0)
    do_kc(1)
    do_qq()
    do_zy(11)
    do_kc(0)
    do_zy(8)
    do_kw(0)
    do_td(1)
    do_yc(9)
    do_kw(1)
    do_at(0)
    do_at(1)
    do_at(2)
    do_cw(3)
    do_zs(5)
    do_zy(6)
    do_yc(11)
    do_cw(4)
    do_at(3)
    do_yc(8)
    do_te(1)
    do_go()
    do_fc(3)
    do_hg()
    do_bw(0)
    do_cw(10)
    do_zy(7)
    do_bw(1)
    do_cw(8)
    do_cw(11)
    do_bw(2)
    do_bw(3)
    do_dc()
    do_zy(5)
    do_ff(3)
    do_yc(6)
    do_fq(3)
    do_cw(9)
    do_ff(2)
    do_fc(9)
    do_cw(6)
    do_yc(7)
    do_dy()
    do_yc(5)
    do_cw(7)
    do_ff(1)
    do_fc(7)
    do_cw(5)
    do_ff(0)
    do_fc(5)
    do_of()
    do_fc(6)
    do_fy(9)
    do_fq(7)
    do_fy(5)
    do_dw()
    do_ag()
    do_fc(0)
    do_eo(0)
    do_fc(4)
    do_sx(0)
    do_eo(1)
    do_sx(1)
    do_fz(9)
    do_eo(2)
    do_eb(0)
    do_fy(0)
    do_eb(1)
    do_eb(3)
    do_fc(1)
    do_fz(5)
    do_eb(2)
    do_pa()
    do_ew(9)
    do_fc(11)
    do_pb()
    do_fc(2)
    do_fy(1)
    do_fc(10)
    do_fy(4)
    do_sx(2)
    do_fz(0)
    do_pc()
    do_fy(10)
    do_eo(3)
    do_sa(0)
    do_fz(1)
    do_fz(4)
    do_sm(0)
    do_pd()
    do_fy(11)
    do_fc(8)
    do_sx(3)
    do_ew(0)
    do_fr(7)
    do_sb(0)
    do_sa(1)
    do_fz(11)
    do_fy(2)
    do_ew(1)
    do_sm(1)
    do_sb(1)
    do_fy(8)
    do_ew(5)
    do_fr(3)
    do_fs(7)
    do_pe()
    do_sc(0)
    do_fy(6)
    do_fz(8)
    do_fz(10)
    do_sc(1)
    do_sd(0)
    do_fs(3)
    do_fz(2)
    do_ew(4)
    do_ew(10)
    do_fz(6)
    do_ew(11)
    do_ew(8)
    do_sd(1)
    do_ew(2)
    do_sw(0)
    do_ew(6)
    do_ew(7)
    do_sw(1)
    do_ew(3)
    for copy in sends:
        if not any(copy is other for other in settled):
            copy.wait_send()


def fits(depth_size, group, depth_rows, rows, width, ff_chunks):
    sizes = layout_of(depth_size, group, depth_rows, rows, width, ff_chunks)
    total = sum(math.prod(shape) * jnp.dtype(kind).itemsize for _, shape, kind in sizes)
    shaped = group == depth_size == ff_chunks == 4 and depth_rows == rows == 128
    return shaped and total < VMEM_BYTES


def fused_shards(
    layer_input,
    block_order,
    attn_gain,
    attn_shift,
    mlp_gain,
    mlp_shift,
    w_query,
    b_query,
    w_key,
    b_key,
    w_value,
    b_value,
    w_out,
    b_out,
    w_up,
    b_up,
    w_down,
    b_down,
    out_grad,
):
    rows, width = layer_input.shape
    tp_size = lax.axis_size("tp")
    depth_size = HEADS // tp_size
    group = lax.axis_size("ctx") // depth_size
    depth_rows = width // (depth_size * group)
    ff_width = w_up.shape[1] // depth_size
    ff_chunks = ff_width // CHUNK
    tokens = depth_size * rows
    at = Place(depth_size, group)

    freqs = (10000.0 ** (-(2.0 * np.arange(ROT // 2, dtype=np.float32)) / ROT)).astype(np.float32)
    freqs = np.tile(freqs, (8, 128 // (ROT // 2)))

    def in_rows(vector):
        return vector.reshape(-1, 128)

    buffers = layout_of(depth_size, group, depth_rows, rows, width, ff_chunks)
    semaphores = semaphores_of(depth_size, group, 4 + 2 * ff_chunks)
    names = tuple(INPUTS) + tuple(OUTPUTS) + tuple(b[0] for b in buffers) + tuple(s[0] for s in semaphores) + ("free",)
    vmem = pl.BlockSpec(memory_space=pltpu.VMEM)
    hbm = pl.BlockSpec(memory_space=pl.ANY)
    shape = jax.ShapeDtypeStruct
    wide, thin = depth_size * HD, depth_size * ff_width
    results = pl.pallas_call(
        functools.partial(fused_kernel, names, depth_size, group),
        out_shape=(
            shape((2, rows, width), BF),
            shape((depth_rows, wide), BF),
            shape((depth_rows, wide), BF),
            shape((depth_rows, wide), BF),
            shape((wide, depth_rows), BF),
            shape((depth_rows, thin), BF),
            shape((thin, depth_rows), BF),
            shape((4 * width // 128, 128), F32),
            shape((wide // 128, 128), F32),
            shape((wide // 128, 128), F32),
            shape((wide // 128, 128), F32),
            shape((thin // 128, 128), F32),
            shape((width // 128, 128), F32),
        ),
        in_specs=[pl.BlockSpec(memory_space=pltpu.SMEM)] + [hbm] * 2 + [vmem] * 9 + [hbm] * 6,
        out_specs=(vmem,) + (hbm,) * 6 + (vmem,) * 6,
        scratch_shapes=[pltpu.VMEM(s, t) for _, s, t in buffers]
        + [pltpu.SemaphoreType.DMA(s) for _, s in semaphores]
        + [pltpu.SemaphoreType.REGULAR],
        compiler_params=pltpu.CompilerParams(
            collective_id=4, has_side_effects=True, vmem_limit_bytes=VMEM_BYTES
        ),
    )(
        block_order,
        layer_input,
        out_grad,
        freqs,
        *[in_rows(v) for v in (attn_gain, attn_shift, mlp_gain, mlp_shift)],
        *[in_rows(v) for v in (b_query, b_key, b_value, b_up)],
        w_query,
        w_key,
        w_value,
        w_out,
        w_up,
        w_down,
    )
    sums, *parts = results
    output, input_grad, *rest = close(
        depth_size, group, layer_input, out_grad, sums, in_rows(b_out), in_rows(b_down), parts
    )
    small = [vector.reshape(-1) for vector in rest[6:]]
    norms, (to_query, to_key, to_value, to_up, to_dy, again) = small[:4], small[4:]
    return (output, input_grad, *rest[:6], to_query, to_key, to_value, to_dy, to_up, again, *norms)


def close_kernel(depth_size, group, x_in, dy_in, sums, b_out, b_down, *refs):
    grads, (norm_sums, *small), results = refs[:6], refs[6:12], refs[12:]
    layer_output, input_grad, wide, norms, others = (
        results[0],
        results[1],
        results[2:8],
        results[8:12],
        results[12:],
    )
    for source, into in zip(grads, wide, strict=True):
        into[...] = source[...].astype(F32)
    for v, into in enumerate(norms):
        count = into.shape[0]
        into[...] = norm_sums[v * count : (v + 1) * count, :]
    for source, into in zip(small + small[-1:], others, strict=True):
        into[...] = source[...]
    x = x_in[...].astype(F32)
    width = x.shape[1]
    natural = natural_blocks(depth_size, group)
    size = width // len(natural)
    centered = x - jnp.mean(x, -1, keepdims=True)
    inverse = lax.rsqrt(jnp.mean(centered * centered, -1, keepdims=True) + norm_epsilon)
    normal = centered * inverse
    total = jnp.zeros((x.shape[0], 1), F32)
    against = jnp.zeros((x.shape[0], 1), F32)
    for b, c in enumerate(natural):
        out_of, into = slice(b * size, (b + 1) * size), slice(c * size, (c + 1) * size)
        bias = b_out[c : c + 1, :] + b_down[c : c + 1, :]
        layer_output[:, into] = (x[:, into] + sums[0, :, out_of].astype(F32) + bias).astype(BF)
        piece = sums[1, :, out_of].astype(F32)
        total += jnp.sum(piece, -1, keepdims=True)
        against += jnp.sum(piece * normal[:, into], -1, keepdims=True)
    total, against = total / width, against / width
    for b, c in enumerate(natural):
        out_of, into = slice(b * size, (b + 1) * size), slice(c * size, (c + 1) * size)
        piece = sums[1, :, out_of].astype(F32) - total - normal[:, into] * against
        input_grad[:, into] = dy_in[:, into].astype(F32) + inverse * piece


def close(depth_size, group, x_in, dy_in, sums, b_out, b_down, parts):
    rows, width = x_in.shape
    steps = rows // 64
    grads, small = parts[:6], parts[6:]
    norms = [jax.ShapeDtypeStruct((width // 128, 128), F32)] * 4
    copies = [jax.ShapeDtypeStruct(s.shape, F32) for s in small[1:] + small[-1:]]

    def by_rows(shape):
        block = shape[:-2] + (shape[-2] // steps, shape[-1])
        return pl.BlockSpec(block, lambda i: (0,) * (len(shape) - 2) + (i, 0))

    def all_of(shape):
        return pl.BlockSpec(shape, lambda i: (0,) * len(shape))

    return pl.pallas_call(
        functools.partial(close_kernel, depth_size, group),
        grid=(steps,),
        out_shape=[
            jax.ShapeDtypeStruct(x_in.shape, BF),
            jax.ShapeDtypeStruct(x_in.shape, F32),
            *[jax.ShapeDtypeStruct(g.shape, F32) for g in grads],
            *norms,
            *copies,
        ],
        in_specs=[by_rows(x_in.shape)] * 2
        + [by_rows(sums.shape), all_of(b_out.shape), all_of(b_down.shape)]
        + [by_rows(g.shape) for g in grads]
        + [all_of(s.shape) for s in small],
        out_specs=[by_rows(x_in.shape)] * 2
        + [by_rows(g.shape) for g in grads]
        + [all_of(s.shape) for s in norms + copies],
        compiler_params=pltpu.CompilerParams(vmem_limit_bytes=VMEM_BYTES),
    )(x_in, dy_in, sums, b_out, b_down, *grads, *small)


def shards(
    layer_input,
    block_order,
    attn_gain,
    attn_shift,
    mlp_gain,
    mlp_shift,
    w_query,
    b_query,
    w_key,
    b_key,
    w_value,
    b_value,
    w_out,
    b_out,
    w_up,
    b_up,
    w_down,
    b_down,
    out_grad,
):
    rows, width = layer_input.shape
    depth_size = HEADS // lax.axis_size("tp")
    group = lax.axis_size("ctx") // depth_size
    ff_chunks = w_up.shape[1] // depth_size // CHUNK
    whole = fits(depth_size, group, width // (depth_size * group), rows, width, ff_chunks)
    chosen = fused_shards if whole else staged_shards
    return chosen(
        layer_input, block_order, attn_gain, attn_shift, mlp_gain, mlp_shift, w_query, b_query, w_key, b_key, w_value, b_value, w_out, b_out, w_up, b_up, w_down, b_down, out_grad
    )


def staged_shards(
    layer_input,
    block_order,
    attn_gain,
    attn_shift,
    mlp_gain,
    mlp_shift,
    w_query,
    b_query,
    w_key,
    b_key,
    w_value,
    b_value,
    w_out,
    b_out,
    w_up,
    b_up,
    w_down,
    b_down,
    out_grad,
):
    rows, width = layer_input.shape
    ctx_size = lax.axis_size("ctx")
    tp_size = lax.axis_size("tp")
    depth_size = HEADS // tp_size
    group = ctx_size // depth_size
    bits = group.bit_length() - 1
    depth_rows = width // ctx_size
    hidden_width = w_up.shape[1] // depth_size
    ff_chunks = hidden_width // CHUNK
    at = Place(depth_size, group)
    block_rows = rows // 2

    def permuted(array):
        lead = array.shape[:-1]
        n = len(lead)
        split = array.reshape(lead + (depth_size,) + (2,) * bits + (depth_rows,))
        order = tuple(range(n)) + tuple(n + 1 + b for b in reversed(range(bits))) + (n, n + 1 + bits)
        return split.transpose(order).reshape(lead + (width,))

    def restored(array):
        lead = array.shape[:-1]
        n = len(lead)
        split = array.reshape(lead + (2,) * bits + (depth_size, depth_rows))
        order = tuple(range(n)) + (n + bits,) + tuple(n + b for b in reversed(range(bits))) + (n + bits + 1,)
        return split.transpose(order).reshape(lead + (width,))

    def slot_members():
        table = []
        for slot in range(group):
            member = 0
            for stage in range(bits):
                member += ((slot >> stage) & 1) << (bits - 1 - stage)
            table.append(member)
        return table

    blocks = block_order.reshape(depth_size, group, 2)
    order = jnp.stack([blocks[:, m] for m in slot_members()], 0)
    place = order[..., None] * block_rows + jnp.arange(block_rows, dtype=jnp.int32)
    key_place = place.reshape(group * depth_size * rows)
    token_total = depth_size * rows
    query_place = lax.dynamic_slice_in_dim(key_place, at.slot * token_total, token_total)
    cosine, sine_table = rope_tables(query_place)

    inputs32 = layer_input.astype(F32)
    centered = inputs32 - jnp.mean(inputs32, -1, keepdims=True)
    inverse = lax.rsqrt(jnp.mean(centered * centered, -1, keepdims=True) + norm_epsilon)
    normal32 = centered * inverse

    def halves(array):
        return permuted(array).reshape(rows, tp_size, width // tp_size).transpose(1, 0, 2)

    def by_head(weight):
        return weight.reshape(depth_rows, depth_size, HD).transpose(1, 0, 2)

    def by_chunk(weight):
        return weight.reshape(depth_rows, depth_size, ff_chunks, CHUNK).transpose(2, 1, 0, 3)

    weights = jnp.concatenate(
        [
            jnp.concatenate([by_head(w_query), by_head(w_key)], -1)[None],
            jnp.concatenate([by_head(w_value), by_head(w_out.T)], -1)[None],
            jnp.concatenate([by_chunk(w_up), by_chunk(w_down.T)], -1),
        ],
        0,
    )
    normal, grad, gathered = gather_all(
        depth_size, group, halves(normal32.astype(BF)), halves(out_grad), weights
    )
    full = gathered.reshape(2 + ff_chunks, width, 2 * HD)
    gain_a, shift_a, gain_m, shift_m = permuted(jnp.stack([attn_gain, attn_shift, mlp_gain, mlp_shift]))
    normal_tokens = normal.astype(F32)
    attn_in = (normal_tokens * gain_a + shift_a).astype(BF)
    mlp_in = (normal_tokens * gain_m + shift_m).astype(BF)

    def own_part(vector, size):
        return lax.dynamic_slice_in_dim(vector, at.depth * size, size)

    query_key = mm(attn_in, full[0])
    query = rotate(query_key[:, :HD] + own_part(b_query, HD), cosine, sine_table).astype(BF)
    keys = rotate(query_key[:, HD:] + own_part(b_key, HD), cosine, sine_table).astype(BF)
    values = (mm(attn_in, full[1, :, :HD]) + own_part(b_value, HD)).astype(BF)
    out_t = full[1, :, HD:]
    shared = share_group(depth_size, group, jnp.concatenate([keys, values], -1))
    shared = shared.reshape(group * token_total, 2 * HD)
    all_keys, all_values = shared[:, :HD], shared[:, HD:]
    score_scale = 1.0 / math.sqrt(HD)
    scores = mm_nt(query, all_keys) * score_scale
    allowed = key_place[None, :] <= query_place[:, None]
    scores = jnp.where(allowed, scores, -1e30)
    top = jnp.max(scores, -1, keepdims=True)
    raw = jnp.exp(scores - top)
    probs = raw / jnp.sum(raw, -1, keepdims=True)
    probs_low = probs.astype(BF)
    attended = mm(probs_low, all_values)
    attn_low = attended.astype(BF)

    head_grad = mm(grad, out_t).astype(BF)
    delta = jnp.sum(head_grad.astype(F32) * attended, -1, keepdims=True)
    value_part = mm_tn(probs_low, head_grad)
    score_grad = (probs * (mm_nt(head_grad, all_values) - delta) * score_scale).astype(BF)
    query_acc = mm(score_grad, all_keys)
    key_part = mm_tn(score_grad, query)
    parts = jnp.concatenate([key_part, value_part], -1).astype(BF)
    folded = fold_group(depth_size, group, parts.reshape(group, token_total, 2 * HD))
    own_grads = lax.dynamic_index_in_dim(folded, at.slot, 0, keepdims=False).astype(F32)
    query_lin = rotate(query_acc, cosine, -sine_table)
    key_lin = rotate(own_grads[:, :HD], cosine, -sine_table)
    value_lin = own_grads[:, HD:]
    query_low, key_low, value_low = query_lin.astype(BF), key_lin.astype(BF), value_lin.astype(BF)
    query_key_low = jnp.concatenate([query_low, key_low], -1)
    attn_back = mm_nt(query_key_low, full[0]) + mm_nt(value_low, full[1, :, :HD])
    grad_chunks = [
        mm_tn(attn_in, query_key_low).astype(BF),
        jnp.concatenate([mm_tn(attn_in, value_low), mm_tn(grad, attn_low)], -1).astype(BF),
    ]

    branches = mm_nt(attn_low, out_t)
    mlp_back = jnp.zeros((token_total, width), F32)
    bias_up = own_part(b_up, hidden_width).reshape(ff_chunks, CHUNK)
    up_sums = []
    for i in range(ff_chunks):
        up, down_t = full[2 + i, :, :CHUNK], full[2 + i, :, CHUNK:]
        activated, slope = gelu_parts(mm(mlp_in, up) + bias_up[i])
        hidden = activated.astype(BF)
        up_grad = mm(grad, down_t) * slope
        up_sums.append(jnp.sum(up_grad, 0))
        up_low = up_grad.astype(BF)
        branches = branches + mm_nt(hidden, down_t)
        mlp_back = mlp_back + mm_nt(up_low, up)
        grad_chunks.append(jnp.concatenate([mm_tn(mlp_in, up_low), mm_tn(grad, hidden)], -1).astype(BF))

    normal_tokens2 = normal.astype(F32)
    back = attn_back * gain_a + mlp_back * gain_m
    grads = jnp.stack(grad_chunks).reshape(2 + ff_chunks, group, depth_size, depth_rows, 2 * HD)
    norm_sums = restored(
        jnp.stack(
            [
                jnp.sum(attn_back * normal_tokens2, 0),
                jnp.sum(attn_back, 0),
                jnp.sum(mlp_back * normal_tokens2, 0),
                jnp.sum(mlp_back, 0),
            ]
        )
    )
    own_biases = jnp.concatenate(
        [jnp.sum(query_lin, 0), jnp.sum(key_lin, 0), jnp.sum(value_lin, 0)] + up_sums
    )
    spread = jnp.where(
        jnp.arange(depth_size, dtype=jnp.int32)[:, None] == at.depth, own_biases[None, :], 0.0
    )
    norm_sums = lax.psum(norm_sums, ("ctx", "tp"))
    grad32 = out_grad.astype(F32)
    spread, bias_grad = lax.psum((spread, jnp.sum(grad32, 0)), "ctx")

    out_sum, back_sum, grad_shares = reduce_all(
        depth_size, group, branches.astype(BF), back.astype(BF), grads
    )
    layer_output = (inputs32 + restored(out_sum).astype(F32) + b_out + b_down).astype(BF)
    back_total = restored(back_sum).astype(F32)
    input_grad = grad32 + inverse * (
        back_total
        - jnp.mean(back_total, -1, keepdims=True)
        - normal32 * jnp.mean(back_total * normal32, -1, keepdims=True)
    )

    def from_head(share):
        return share.transpose(1, 0, 2).reshape(depth_rows, depth_size * HD).astype(F32)

    def from_chunk(share):
        return share.transpose(2, 1, 0, 3).reshape(depth_rows, depth_size * hidden_width).astype(F32)

    return (
        layer_output,
        input_grad,
        from_head(grad_shares[0, :, :, :HD]),
        from_head(grad_shares[0, :, :, HD:]),
        from_head(grad_shares[1, :, :, :HD]),
        from_head(grad_shares[1, :, :, HD:]).T,
        from_chunk(grad_shares[2:, :, :, :CHUNK]),
        from_chunk(grad_shares[2:, :, :, CHUNK:]).T,
        spread[:, :HD].reshape(-1),
        spread[:, HD : 2 * HD].reshape(-1),
        spread[:, 2 * HD : 3 * HD].reshape(-1),
        bias_grad,
        spread[:, 3 * HD :].reshape(-1),
        bias_grad,
        norm_sums[0],
        norm_sums[1],
        norm_sums[2],
        norm_sums[3],
    )


def solution(mesh):
    in_specs = (
        P("ctx", None),
        P(),
        P(),
        P(),
        P(),
        P(),
        P("ctx", "tp"),
        P("tp"),
        P("ctx", "tp"),
        P("tp"),
        P("ctx", "tp"),
        P("tp"),
        P("tp", "ctx"),
        P(),
        P("ctx", "tp"),
        P("tp"),
        P("tp", "ctx"),
        P(),
        P("ctx", None),
    )
    out_specs = (
        P("ctx", None),
        P("ctx", None),
        P("ctx", "tp"),
        P("ctx", "tp"),
        P("ctx", "tp"),
        P("tp", "ctx"),
        P("ctx", "tp"),
        P("tp", "ctx"),
        P("tp"),
        P("tp"),
        P("tp"),
        P(),
        P("tp"),
        P(),
        P(),
        P(),
        P(),
        P(),
    )
    return jax.shard_map(shards, mesh=mesh, in_specs=in_specs, out_specs=out_specs, check_vma=False)
```
